32 devices in a mesh: batch: 4 (over y, core), blk: 8 (over z, x).
Axes of the slice: x: 2, y: 2, z: 4, core: 2. Of those that a mesh axis runs over, the one named last changes fastest.
Arguments:
- tokens: bfloat16 [32, 1024, 1024], P('batch', 'blk'), may hold values from -6 to 6
- cotangent: bfloat16 [32, 1024, 1024], P('batch', 'blk'), may hold values from -6 to 6
- w_query: bfloat16 [1024, 1024], replicated, may hold values from -0.1875 to 0.1875
- w_key: bfloat16 [1024, 1024], replicated, may hold values from -0.1875 to 0.1875
- w_value: bfloat16 [1024, 1024], replicated, may hold values from -0.1875 to 0.1875
- w_gate: bfloat16 [1024, 1024], replicated, may hold values from -0.1875 to 0.1875
- w_out: bfloat16 [1024, 1024], replicated, may hold values from -0.375 to 0.375
- out_gain: float32 [1024], replicated, may hold values from 0.1 to 1.9
- w_first: bfloat16 [1024, 2816], replicated, may hold values from -0.1875 to 0.1875
- w_second: bfloat16 [1024, 2816], replicated, may hold values from -0.1875 to 0.1875
- w_third: bfloat16 [2816, 1024], replicated, may hold values from -0.109375 to 0.109375
Outputs:
- output: bfloat16 [32, 1024, 1024], P('batch', 'blk')
- grad_tokens: float32 [32, 1024, 1024], P('batch', 'blk')
- grad_query: float32 [1024, 1024], P('blk')
- grad_key: float32 [1024, 1024], P('blk')
- grad_value: float32 [1024, 1024], P('blk')
- grad_gate: float32 [1024, 1024], P('blk')
- grad_out: float32 [1024, 1024], P('blk')
- grad_gain: float32 [1024], P('blk')
- grad_first: float32 [1024, 2816], P('blk')
- grad_second: float32 [1024, 2816], P('blk')
- grad_third: float32 [2816, 1024], P('blk')
The draws below stay inside these ranges and needn't reach their ends.
All inputs are finite; a program needn't handle non-finite values.
Results may differ from the reference program's by a relative error of at most 0.014.
Values sent between devices are 32-bit elements; how exact they have to be, the bound alone decides.
A program may use at most 384 MiB of HBM per device.

```python
import math
import jax
import jax.numpy as jnp
from jax import lax

D = 1024
HEADS = 16
HEAD = 64
FF = 2816
LEN = 1024
SPAN = 128
NSEQ = 32
N_BLK = 8


def steps_of(rng, extent, pieces, smallest, largest):
    def one(position, parts):
        steps = jax.random.uniform(jax.random.fold_in(jax.random.fold_in(rng, 6), position), (parts,), jnp.float32, smallest / len(pieces), largest / len(pieces))
        return jnp.repeat(jnp.exp(steps), extent[position] // parts).reshape((-1,) + (1,) * (len(extent) - position - 1))

    level = one(*pieces[0])
    for cut in pieces[1:]:
        level = level * one(*cut)
    return level


def normal_values(rng, extent, spread, reach, cuts=(), held_as=jnp.bfloat16):
    factor_of = steps_of(rng, extent, cuts, -0.22, 0.18) if cuts else 1.0
    values = jax.random.normal(rng, extent, jnp.float32) * spread * factor_of
    return jnp.minimum(jnp.maximum(values, -reach), reach).astype(held_as)


def setup_inputs(seed: int = 0) -> dict:
    key_of = jax.random.split(jax.random.key(seed), 12)
    return {
        "tokens": normal_values(key_of[0], (NSEQ, LEN, D), 1.0, 6.0, ((0, 4), (1, 8))),
        "cotangent": normal_values(key_of[1], (NSEQ, LEN, D), 1.0, 6.0, ((0, 4), (1, 8))),
        "w_query": normal_values(key_of[2], (D, D), D ** -0.5, 0.1875),
        "w_key": normal_values(key_of[3], (D, D), D ** -0.5, 0.1875),
        "w_value": normal_values(key_of[4], (D, D), D ** -0.5, 0.1875),
        "w_gate": normal_values(key_of[5], (D, D), D ** -0.5, 0.1875),
        "w_out": normal_values(key_of[6], (D, D), (D // 4) ** -0.5, 0.375),
        "out_gain": jnp.clip(1.0 + 0.18 * jax.random.normal(key_of[7], (D,), jnp.float32), 0.1, 1.9),
        "w_first": normal_values(key_of[8], (D, FF), D ** -0.5, 0.1875),
        "w_second": normal_values(key_of[9], (D, FF), D ** -0.5, 0.1875),
        "w_third": normal_values(key_of[10], (FF, D), FF ** -0.5, 0.109375),
    }


EPS = 1e-06
HIGH = lax.Precision.HIGHEST

@jax.custom_vjp
def low(v):
    return lax.optimization_barrier(v.astype(jnp.bfloat16)).astype(jnp.float32)

@jax.custom_vjp
def low_back(v):
    return v

def low_keep(v):
    return (low(v), None)

def low_pass(kept, grad):
    return (grad,)

def back_keep(v):
    return (v, None)

def back_low(kept, grad):
    return (low(grad),)
low.defvjp(low_keep, low_pass)
low_back.defvjp(back_keep, back_low)

def matmul(left, weight):
    return jnp.einsum('gtd,df->gtf', left, weight, precision=HIGH)

def forward(params, xf):
    wquery, wkey, wvalue, wgate, wout, gain, wfirst, wsecond, wthird = params
    groups = xf.shape[0]
    rone = lax.rsqrt(lax.optimization_barrier(jnp.mean(xf * xf, axis=-1, keepdims=True)) + EPS)
    normed = low(xf * rone)
    query = low_back(matmul(normed, wquery))
    key = low_back(matmul(normed, wkey))
    value = low_back(matmul(normed, wvalue))
    gate = low_back(matmul(normed, wgate))
    shape5 = (groups, N_BLK, SPAN, HEADS, HEAD)
    fquery = low(jax.nn.silu(query)).reshape(shape5)
    fkey = low(jax.nn.silu(key)).reshape(shape5)
    values = low(value).reshape(shape5)
    causal = (jnp.arange(SPAN)[:, None] >= jnp.arange(SPAN)[None, :]).astype(jnp.float32)
    raw = jnp.einsum('gnthe,gnuhe->gnhtu', fquery, fkey, precision=HIGH) * causal
    scores = low(low_back(raw))
    intra = jnp.einsum('gnhtu,gnuhf->gnthf', scores, values, precision=HIGH)
    states = low_back(jnp.einsum('gnthe,gnthf->gnhef', fkey, values, precision=HIGH))
    totals = jnp.cumsum(states, axis=1)
    prefix = jnp.concatenate([jnp.zeros_like(states[:, :1]), totals[:, :-1]], axis=1)
    inter = jnp.einsum('gnthe,gnhef->gnthf', fquery, low(prefix), precision=HIGH)
    attn = low_back(intra + inter).reshape(groups, LEN, D)
    rattn = lax.rsqrt(lax.optimization_barrier(jnp.mean(attn * attn, axis=-1, keepdims=True)) + EPS)
    mixed = low(attn * rattn * gain * jax.nn.silu(gate))
    resid = xf + low_back(matmul(mixed, wout))
    rtwo = lax.rsqrt(lax.optimization_barrier(jnp.mean(resid * resid, axis=-1, keepdims=True)) + EPS)
    normed2 = low(resid * rtwo)
    first = low_back(matmul(normed2, wfirst))
    second = low_back(matmul(normed2, wsecond))
    inner = low(first * second)
    return resid + low_back(matmul(inner, wthird))

def reference(tokens, cotangent, w_query, w_key, w_value, w_gate, w_out, out_gain, w_first, w_second, w_third):
    params = tuple((a.astype(jnp.float32) for a in (w_query, w_key, w_value, w_gate, w_out, out_gain, w_first, w_second, w_third)))
    group = math.gcd(NSEQ, max(1, 4096 // LEN))
    inputs = tokens.astype(jnp.float32).reshape(NSEQ // group, group, LEN, D)
    grads_in = cotangent.astype(jnp.float32).reshape(NSEQ // group, group, LEN, D)

    def step(acc, pair):
        xgroup, cgroup = pair
        result, pull = jax.vjp(forward, params, xgroup)
        gparams, gx = pull(cgroup)
        acc = jax.tree.map(lambda a, b: a + b, acc, gparams)
        return (acc, (result.astype(jnp.bfloat16), gx))
    zeros = jax.tree.map(jnp.zeros_like, params)
    acc, (results, gxs) = lax.scan(step, zeros, (inputs, grads_in))
    output = results.reshape(NSEQ, LEN, D)
    grad_tokens = gxs.reshape(NSEQ, LEN, D)
    return (output, grad_tokens, acc[0], acc[1], acc[2], acc[3], acc[4], acc[5], acc[6], acc[7], acc[8])
```

```python
import functools

import jax
import jax.numpy as jnp
from jax import lax
from jax.experimental import pallas as pl
from jax.experimental.pallas import tpu as pltpu
from jax.sharding import PartitionSpec as P

HEAD = 64
EPS = 1e-06
MESH = pl.DeviceIdType.MESH
F32 = jnp.float32
BF16 = jnp.bfloat16
MIB = 2**20


def silu_parts(pre):
    sig = jax.nn.sigmoid(pre)
    return (pre * sig, sig * (1.0 + pre * (1.0 - sig)))


def norm_back(grad, value, scale):
    inner = jnp.mean(grad * value, axis=-1, keepdims=True)
    return scale * grad - value * (scale * scale * scale) * inner


def project(left, weight):
    return jnp.dot(left, weight, preferred_element_type=F32)


def weight_grad(left, right):
    return jnp.einsum("td,tf->df", left, right, preferred_element_type=F32)


def back_project(grad, weight):
    return jnp.einsum("tf,df->td", grad, weight, preferred_element_type=F32)


def dot(a, b, ca, cb):
    return lax.dot_general(a, b, (((ca,), (cb,)), ((), ())), preferred_element_type=F32)


def low_lanes(shape):
    return lax.broadcasted_iota(jnp.int32, shape, len(shape) - 1) < HEAD


def two_heads(x):
    low = low_lanes(x.shape)
    zero = jnp.zeros_like(x)
    return jnp.concatenate([jnp.where(low, x, zero), jnp.where(low, zero, x)], axis=0)


def pick_heads(x):
    half = x.shape[0] // 2
    return jnp.where(low_lanes((half, x.shape[1])), x[:half], x[half:])


def causal_pair(span):
    t = lax.broadcasted_iota(jnp.int32, (span, 2 * span), 0)
    u = lax.broadcasted_iota(jnp.int32, (span, 2 * span), 1)
    return t >= u % span


def pair_of(ref, p):
    return ref[:, pl.ds(p * 2 * HEAD, 2 * HEAD)]


def state_kernel(left_ref, right_ref, out_ref):
    for p in range(out_ref.shape[1]):
        out_ref[0, p] = pick_heads(dot(pair_of(left_ref, p), pair_of(right_ref, p), 0, 0))


def attn_kernel(q_ref, k_ref, v_ref, prefix_ref, out_ref):
    span = q_ref.shape[0]
    causal = causal_pair(span)
    for p in range(prefix_ref.shape[1]):
        q, k2, v2 = pair_of(q_ref, p), two_heads(pair_of(k_ref, p)), two_heads(pair_of(v_ref, p))
        scores = jnp.where(causal, dot(q, k2, 1, 1), 0.0).astype(BF16)
        prefix = two_heads(prefix_ref[0, p])
        out_ref[:, pl.ds(p * 2 * HEAD, 2 * HEAD)] = dot(scores, v2, 1, 0) + dot(q, prefix, 1, 0)


def attn_back_kernel(q_ref, k_ref, v_ref, g_ref, prefix_ref, dstate_ref, dq_ref, dk_ref, dv_ref):
    span = q_ref.shape[0]
    causal = causal_pair(span)
    for p in range(prefix_ref.shape[1]):
        q, k, v, g = (pair_of(r, p) for r in (q_ref, k_ref, v_ref, g_ref))
        k2, v2 = two_heads(k), two_heads(v)
        prefix, dstate = two_heads(prefix_ref[0, p]), two_heads(dstate_ref[0, p])
        scores = jnp.where(causal, dot(q, k2, 1, 1), 0.0).astype(BF16)
        dscores = jnp.where(causal, dot(g, v2, 1, 1), 0.0).astype(BF16)
        lanes = pl.ds(p * 2 * HEAD, 2 * HEAD)
        dq_ref[:, lanes] = dot(dscores, k2, 1, 0) + dot(g, prefix, 1, 1)
        dk_ref[:, lanes] = pick_heads(dot(dscores, q, 0, 0)) + dot(v, dstate, 1, 1)
        dv_ref[:, lanes] = pick_heads(dot(scores, g, 0, 0)) + dot(k, dstate, 1, 0)


def rows_spec(span, width):
    return pl.BlockSpec((span, width), lambda s: (s, 0))


def state_spec(pairs):
    return pl.BlockSpec((1, pairs, HEAD, 2 * HEAD), lambda s: (s, 0, 0, 0))


def local_states(left, right, seqs):
    rows, width = left.shape
    span, pairs = rows // seqs, width // (2 * HEAD)
    return pl.pallas_call(
        state_kernel,
        grid=(seqs,),
        in_specs=[rows_spec(span, width)] * 2,
        out_specs=state_spec(pairs),
        out_shape=jax.ShapeDtypeStruct((seqs, pairs, HEAD, 2 * HEAD), F32),
    )(left, right)


def attention(q, k, v, prefix, seqs):
    rows, width = q.shape
    span, pairs = rows // seqs, width // (2 * HEAD)
    return pl.pallas_call(
        attn_kernel,
        grid=(seqs,),
        in_specs=[rows_spec(span, width)] * 3 + [state_spec(pairs)],
        out_specs=rows_spec(span, width),
        out_shape=jax.ShapeDtypeStruct((rows, width), F32),
    )(q, k, v, prefix)


def attention_back(q, k, v, g, prefix, dstate, seqs):
    rows, width = q.shape
    span, pairs = rows // seqs, width // (2 * HEAD)
    return pl.pallas_call(
        attn_back_kernel,
        grid=(seqs,),
        in_specs=[rows_spec(span, width)] * 4 + [state_spec(pairs)] * 2,
        out_specs=[rows_spec(span, width)] * 3,
        out_shape=[jax.ShapeDtypeStruct((rows, width), F32)] * 3,
    )(q, k, v, g, prefix, dstate)


def scan_kernel(outer, reverse, s_ref, out_ref, held, summed, other, zs, zr, xs, xr):
    chunks = s_ref.shape[0]
    k = lax.axis_index("blk")
    z, x = k // 2, k % 2
    if reverse:
        zz, xx = outer - 1 - z, 1 - x
        after, before = jnp.maximum(z - 1, 0), jnp.minimum(z + 1, outer - 1)
    else:
        zz, xx = z, x
        after, before = jnp.minimum(z + 1, outer - 1), jnp.maximum(z - 1, 0)
    nxt, prv, side = {"blk": after * 2 + x}, {"blk": before * 2 + x}, {"blk": z * 2 + 1 - x}
    first, last = zz == 0, zz == outer - 1

    bar = pltpu.get_barrier_semaphore()
    pl.semaphore_signal(bar, inc=1, device_id=side, device_id_type=MESH)
    pl.when(~last)(lambda: pl.semaphore_signal(bar, inc=1, device_id=nxt, device_id_type=MESH))
    pl.when(~first)(lambda: pl.semaphore_signal(bar, inc=1, device_id=prv, device_id_type=MESH))
    pl.semaphore_wait(bar, 1 + jnp.where(last, 0, 1) + jnp.where(first, 0, 1))

    def along(i):
        return pltpu.make_async_remote_copy(
            src_ref=summed.at[i], dst_ref=held.at[i], send_sem=zs.at[i], recv_sem=zr.at[i],
            device_id=nxt, device_id_type=MESH)

    def across(i, src):
        return pltpu.make_async_remote_copy(
            src_ref=src.at[i], dst_ref=other.at[i], send_sem=xs.at[i], recv_sem=xr.at[i],
            device_id=side, device_id_type=MESH)

    def pass_on(i):
        pl.when(~first)(lambda: along(i).wait_recv())

        @pl.when(first)
        def _():
            held[i] = jnp.zeros_like(held[i])

        summed[i] = held[i] + s_ref[i]
        pl.when(~last)(lambda: along(i).start())
        pl.when(xx == 0)(lambda: across(i, summed).start())
        pl.when(xx == 1)(lambda: across(i, held).start())

    def finish(i):
        across(i, held).wait_recv()
        out_ref[i] = (held[i] + other[i]).astype(out_ref.dtype)

    def step(i, carry):
        pl.when(i < chunks)(lambda: pass_on(i))
        pl.when(i > 0)(lambda: finish(i - 1))
        return carry

    lax.fori_loop(0, chunks + 1, step, 0)

    def drain(i, carry):
        pl.when(~last)(lambda: along(i).wait_send())
        across(i, held).wait_send()
        return carry

    lax.fori_loop(0, chunks, drain, 0)


def entering(states, blk, reverse):
    seqs, pairs, head, lanes = states.shape
    per = max(1, pairs // 2)
    shape = (seqs * pairs // per, per, head, lanes)
    vmem = pl.BlockSpec(memory_space=pltpu.VMEM)
    sems = [pltpu.SemaphoreType.DMA((shape[0],))] * 4
    out = pl.pallas_call(
        functools.partial(scan_kernel, blk // 2, reverse),
        out_shape=jax.ShapeDtypeStruct(shape, BF16),
        in_specs=[vmem],
        out_specs=vmem,
        scratch_shapes=[pltpu.VMEM(shape, F32)] * 3 + sems,
        compiler_params=pltpu.CompilerParams(
            collective_id=2 if reverse else 1, has_side_effects=True, vmem_limit_bytes=24 * MIB),
    )(states.reshape(shape))
    return out.reshape(states.shape)


LAND, FIN, ACC = 4, 8, 10
CORE, XA, YA, YB, XB, XC, YC = range(7)


def reduce_kernel(outer, theirs, mine, out, core_rx, acc, xa, ya, yb, xb, xc, yc, zab, zc, fin,
                  ssem, rsem, zss, zrs, lsem, osem, cgs, cgr, ygs, ygr):
    chunks = theirs.shape[0]
    b, k = lax.axis_index("batch"), lax.axis_index("blk")
    y, c = b // 2, b % 2
    z, x = k // 2, k % 2
    ox, oy = 1 - x, 1 - y
    top = outer - 1
    zr = top - z
    to_core, to_y, to_x = {"batch": y * 2 + 1 - c}, {"batch": oy * 2 + c}, {"blk": z * 2 + ox}
    to_up = {"blk": jnp.minimum(z + 1, top) * 2 + x}
    to_down = {"blk": jnp.maximum(z - 1, 0) * 2 + x}

    bar = pltpu.get_barrier_semaphore()
    for d in (to_core, to_y, to_x):
        pl.semaphore_signal(bar, inc=1, device_id=d, device_id_type=MESH)
    pl.when(z < top)(lambda: pl.semaphore_signal(bar, inc=1, device_id=to_up, device_id_type=MESH))
    pl.when(z > 0)(lambda: pl.semaphore_signal(bar, inc=1, device_id=to_down, device_id_type=MESH))
    pl.semaphore_wait(bar, 3 + jnp.where(z < top, 1, 0) + jnp.where(z > 0, 1, 0))

    def remote(src, dst, s, r, dev):
        return pltpu.make_async_remote_copy(
            src_ref=src, dst_ref=dst, send_sem=s, recv_sem=r, device_id=dev, device_id_type=MESH)

    def link(kind, i, src, dst, dev):
        return remote(src, dst.at[i % LAND], ssem.at[kind, i % LAND], rsem.at[kind, i % LAND], dev)

    def at(i, *where):
        return acc.at[(i % ACC,) + where]

    A, B, C = pl.ds(0, 32), pl.ds(32, 16), pl.ds(48, 16)
    every = slice(None)

    def core_copy(i):
        return link(CORE, i, theirs.at[i], core_rx, to_core)

    def mine_copy(i):
        return pltpu.make_async_copy(mine.at[i], at(i), lsem.at[i % LAND])

    def xa_copy(i):
        return link(XA, i, at(i, every, ox, every, A), xa, to_x)

    def ya_copy(i):
        return link(YA, i, at(i, every, x, oy, A), ya, to_y)

    def yb_copy(i):
        return link(YB, i, at(i, every, every, oy, B), yb, to_y)

    def xb_copy(i):
        return link(XB, i, at(i, every, ox, y, B), xb, to_x)

    def xc_copy(i):
        return link(XC, i, at(i, z, ox, every, C), xc, to_x)

    def yc_copy(i):
        return link(YC, i, at(i, z, x, oy, C), yc, to_y)

    def y_share(i):
        f = i % FIN
        return remote(fin.at[f, y], fin.at[f, y], ygs.at[f], ygr.at[f], to_y)

    def core_share(i):
        f = i % FIN
        return remote(fin.at[f], out.at[i, c], cgs.at[f], cgr.at[f], to_core)

    def store(i):
        return pltpu.make_async_copy(fin.at[i % FIN], out.at[i, c], osem.at[i % FIN])

    def part_ab(i, s):
        return at(i, s, x, y, pl.ds(0, 48))

    def part_c(i, s):
        return at(i, s, every, every, C)

    AB, CC = (0, part_ab, zab), (1, part_c, zc)

    def hop(group, i, r, up, s):
        g, part, land = group
        d = 0 if up else 1
        sem = (g, d, r - 1, i % LAND)
        return remote(part(i, s), land.at[i % LAND, d, r - 1], zss.at[sem], zrs.at[sem],
                      to_up if up else to_down)

    def z_each(group, i, r, act):
        up = hop(group, i, r, True, jnp.minimum(outer - r + z, top))
        down = hop(group, i, r, False, jnp.maximum(r - 1 - zr, 0))
        pl.when((z <= r - 1) & (z < top))(lambda: act(up))
        pl.when((zr <= r - 1) & (z > 0))(lambda: act(down))

    def z_send(group, i, r):
        z_each(group, i, r, lambda copy: copy.start())

    def z_sent(group, i, r):
        z_each(group, i, r, lambda copy: copy.wait_send())

    def z_take(group, i, r):
        g, part, land = group

        def take(up, s):
            hop(group, i, r, up, s).wait_recv()
            ref = part(i, s)
            ref[...] = ref[...] + land[i % LAND, 0 if up else 1, r - 1]

        pl.when((z > 0) & (z <= r))(lambda: take(True, jnp.clip(outer - r + z - 1, 0, top)))
        pl.when((z < top) & (zr <= r))(lambda: take(False, jnp.clip(r - zr, 0, top)))

    def add(ref, landed):
        ref[...] = ref[...] + landed

    def begin(i):
        mine_copy(i).start()
        core_copy(i).start()

    def cores(i):
        mine_copy(i).wait()
        core_copy(i).wait_recv()
        core_copy(i).wait_send()
        add(at(i), core_rx[i % LAND])
        xa_copy(i).start()
        yb_copy(i).start()
        z_send(CC, i, 1)

    def second(i):
        yb_copy(i).wait_recv()
        add(at(i, every, every, y, B), yb[i % LAND])
        xb_copy(i).start()
        xa_copy(i).wait_recv()
        add(at(i, every, x, every, A), xa[i % LAND])
        ya_copy(i).start()
        z_take(CC, i, 1)
        z_send(CC, i, 2)
        xa_copy(i).wait_send()
        yb_copy(i).wait_send()
        z_sent(CC, i, 1)

    def third(i):
        xb_copy(i).wait_recv()
        add(at(i, every, x, y, B), xb[i % LAND])
        ya_copy(i).wait_recv()
        add(at(i, every, x, y, A), ya[i % LAND])
        z_send(AB, i, 1)
        z_take(CC, i, 2)
        z_send(CC, i, 3)
        xb_copy(i).wait_send()
        ya_copy(i).wait_send()
        z_sent(CC, i, 2)

    def fourth(i):
        z_take(AB, i, 1)
        z_send(AB, i, 2)
        z_take(CC, i, 3)
        xc_copy(i).start()
        z_sent(AB, i, 1)
        z_sent(CC, i, 3)

    def fifth(i):
        z_take(AB, i, 2)
        z_send(AB, i, 3)
        xc_copy(i).wait_recv()
        add(at(i, z, x, every, C), xc[i % LAND])
        yc_copy(i).start()
        z_sent(AB, i, 2)
        xc_copy(i).wait_send()

    def sixth(i):
        yc_copy(i).wait_recv()
        z_take(AB, i, 3)
        fin[i % FIN, y, pl.ds(0, 48)] = acc[i % ACC, z, x, y, pl.ds(0, 48)]
        fin[i % FIN, y, C] = acc[i % ACC, z, x, y, C] + yc[i % LAND]
        y_share(i).start()
        z_sent(AB, i, 3)
        yc_copy(i).wait_send()

    def seventh(i):
        y_share(i).wait_recv()
        y_share(i).wait_send()
        core_share(i).start()
        store(i).start()

    def last(i):
        core_share(i).wait_send()
        store(i).wait()
        core_share(i).wait_recv()

    stages = (begin, cores, second, third, fourth, fifth, sixth, seventh, last)

    def step(t, carry):
        for n, stage in enumerate(stages):
            i = t - n
            pl.when((i >= 0) & (i < chunks))(functools.partial(stage, i))
        return carry

    lax.fori_loop(0, chunks + len(stages) - 1, step, 0)


def reduce_chunks(theirs, mine):
    chunks = theirs.shape[0]
    anywhere = pl.BlockSpec(memory_space=pl.ANY)

    def v(*shape):
        return pltpu.VMEM(shape, F32)

    def sem(*shape):
        return pltpu.SemaphoreType.DMA(shape)

    return pl.pallas_call(
        functools.partial(reduce_kernel, 4),
        out_shape=jax.ShapeDtypeStruct((chunks, 2, 2, 64, 128), F32),
        in_specs=[anywhere, anywhere],
        out_specs=anywhere,
        scratch_shapes=[
            v(LAND, 4, 2, 2, 64, 128), v(ACC, 4, 2, 2, 64, 128), v(LAND, 4, 2, 32, 128),
            v(LAND, 4, 32, 128), v(LAND, 4, 2, 16, 128), v(LAND, 4, 16, 128), v(LAND, 2, 16, 128),
            v(LAND, 16, 128), v(LAND, 2, 3, 48, 128), v(LAND, 2, 3, 2, 2, 16, 128), v(FIN, 2, 64, 128),
            sem(7, LAND), sem(7, LAND), sem(2, 2, 3, LAND), sem(2, 2, 3, LAND),
            sem(LAND), sem(FIN), sem(FIN), sem(FIN), sem(FIN), sem(FIN),
        ],
        compiler_params=pltpu.CompilerParams(
            collective_id=3, has_side_effects=True, vmem_limit_bytes=32 * MIB),
    )(theirs, mine)


def square_chunks(g):
    g = g.reshape(4, 2, 2, 64, 2, 2, 2, 128)
    g = g.transpose(4, 2, 5, 0, 1, 6, 3, 7)
    return g.reshape(2, 4, 4, 2, 2, 64, 128)


def square_back(out):
    out = out.reshape(2, 2, 2, 2, 64, 128)
    return out.transpose(0, 4, 2, 1, 3, 5).reshape(128, 1024)


def wide_chunks(g1, g2):
    n = g1.shape[1] // 256
    g = jnp.stack([g1, g2])
    g = g.reshape(2, 4, 2, 2, 64, 2, n, 128)
    g = g.transpose(5, 3, 6, 1, 2, 0, 4, 7)
    return g.reshape(2, 2 * n, 4, 2, 2, 64, 128)


def wide_back(out):
    n = out.shape[0] // 2
    out = out.reshape(2, n, 2, 2, 64, 128)
    out = out.transpose(3, 0, 4, 2, 1, 5).reshape(2, 128, 2 * n * 128)
    return out[0], out[1]


def tall_chunks(g):
    n = g.shape[0] // 256
    g = g.reshape(4, 2, n, 32, 2, 2, 2, 128)
    g = g.transpose(4, 2, 0, 1, 5, 6, 3, 7)
    return g.reshape(2, n, 4, 2, 2, 64, 128)


def tall_back(out):
    n = out.shape[0]
    out = out.reshape(n, 2, 2, 2, 32, 128)
    return out.transpose(0, 4, 1, 2, 3, 5).reshape(n * 32, 1024)


def reduce_weights(grads):
    gq, gk, gv, gg, go, g1, g2, g3 = grads
    parts = [tall_chunks(g3), wide_chunks(g1, g2)]
    parts += [square_chunks(g) for g in (go, gg, gq, gk, gv)]
    every = jnp.concatenate(parts, axis=1)
    c = lax.axis_index("batch") % 2
    theirs = lax.dynamic_index_in_dim(every, 1 - c, 0, False)
    mine = lax.dynamic_index_in_dim(every, c, 0, False)
    out = reduce_chunks(theirs, mine)
    n3, n12 = parts[0].shape[1], parts[1].shape[1]
    s3 = tall_back(out[:n3])
    s1, s2 = wide_back(out[n3:n3 + n12])
    at = n3 + n12
    so, sg, sq, sk, sv = (square_back(out[at + 4 * i:at + 4 * i + 4]) for i in range(5))
    return sq, sk, sv, sg, so, s1, s2, s3


def reduce_plain(grads):
    return tuple(
        lax.psum(lax.psum_scatter(g, "blk", scatter_dimension=0, tiled=True), "batch") for g in grads)


def body(
    sizes, tokens, cotangent, w_query, w_key, w_value, w_gate, w_out, out_gain, w_first, w_second, w_third
):
    batch, blk = sizes
    seqs, span, width = tokens.shape
    rows = seqs * span
    xf = tokens.reshape(rows, width).astype(F32)
    rone = lax.rsqrt(jnp.mean(xf * xf, axis=-1, keepdims=True) + EPS)
    normed = (xf * rone).astype(BF16)
    key = project(normed, w_key)
    value = project(normed, w_value)
    fkey, key_der = silu_parts(key)
    k, v = fkey.astype(BF16), value.astype(BF16)
    prefix = entering(local_states(k, v, seqs), blk, False)
    query = project(normed, w_query)
    gate = project(normed, w_gate)
    fquery, query_der = silu_parts(query)
    q = fquery.astype(BF16)
    attn = attention(q, k, v, prefix, seqs)
    rattn = lax.rsqrt(jnp.mean(attn * attn, axis=-1, keepdims=True) + EPS)
    unit_attn = attn * rattn
    scaled = unit_attn * out_gain
    gate_act, gate_der = silu_parts(gate)
    mixed = (scaled * gate_act).astype(BF16)
    resid = xf + project(mixed, w_out)
    rtwo = lax.rsqrt(jnp.mean(resid * resid, axis=-1, keepdims=True) + EPS)
    normed2 = (resid * rtwo).astype(BF16)
    first = project(normed2, w_first)
    second = project(normed2, w_second)
    inner = (first * second).astype(BF16)
    output = (resid + project(inner, w_third)).astype(BF16)
    grad_top = cotangent.reshape(rows, width)
    grad_w3 = weight_grad(inner, grad_top)
    grad_inner = back_project(grad_top, w_third)
    grad_one = (grad_inner * second).astype(BF16)
    grad_two = (grad_inner * first).astype(BF16)
    grad_w1 = weight_grad(normed2, grad_one)
    grad_w2 = weight_grad(normed2, grad_two)
    grad_normed2 = back_project(grad_one, w_first) + back_project(grad_two, w_second)
    grad_resid = grad_top.astype(F32) + norm_back(grad_normed2, resid, rtwo)
    grad_resid_low = grad_resid.astype(BF16)
    grad_wo = weight_grad(mixed, grad_resid_low)
    grad_mixed = back_project(grad_resid_low, w_out)
    grad_scaled = grad_mixed * gate_act
    grad_gate_low = (grad_mixed * scaled * gate_der).astype(BF16)
    grad_gain_local = jnp.sum(grad_scaled * unit_attn, axis=0)
    grad_attn = norm_back(grad_scaled * out_gain, attn, rattn).astype(BF16)
    dstate = entering(local_states(q, grad_attn, seqs), blk, True)
    grad_fq, grad_fk, grad_vv = attention_back(q, k, v, grad_attn, prefix, dstate, seqs)
    grad_query_low = (grad_fq * query_der).astype(BF16)
    grad_key_low = (grad_fk * key_der).astype(BF16)
    grad_value_low = grad_vv.astype(BF16)
    grad_wq = weight_grad(normed, grad_query_low)
    grad_wk = weight_grad(normed, grad_key_low)
    grad_wv = weight_grad(normed, grad_value_low)
    grad_wg = weight_grad(normed, grad_gate_low)
    grad_normed = back_project(grad_query_low, w_query) + back_project(grad_key_low, w_key)
    grad_normed = (
        grad_normed + back_project(grad_value_low, w_value) + back_project(grad_gate_low, w_gate)
    )
    grad_input = grad_resid + norm_back(grad_normed, xf, rone)
    grads = (grad_wq, grad_wk, grad_wv, grad_wg, grad_wo, grad_w1, grad_w2, grad_w3)
    fits = (batch, blk) == (4, 8) and width == 1024 and w_first.shape[1] % 256 == 0
    sq, sk, sv, sg, so, s1, s2, s3 = (reduce_weights if fits else reduce_plain)(grads)
    sgain = lax.psum(
        lax.psum_scatter(grad_gain_local, "blk", scatter_dimension=0, tiled=True), "batch")
    return (
        output.reshape(seqs, span, width),
        grad_input.reshape(seqs, span, width),
        sq, sk, sv, sg, so, sgain, s1, s2, s3,
    )


def solution(mesh):
    rows = P("batch", "blk", None)
    cut = P("blk", None)
    return jax.shard_map(
        functools.partial(body, (mesh.shape["batch"], mesh.shape["blk"])),
        mesh=mesh,
        in_specs=(rows, rows) + (P(),) * 9,
        out_specs=(rows, rows) + (cut,) * 5 + (P("blk"),) + (cut,) * 3,
        check_vma=False,
    )
```

```python
import functools

import jax
import jax.numpy as jnp
from jax import lax
from jax.experimental import pallas as pl
from jax.experimental.pallas import tpu as pltpu
from jax.sharding import PartitionSpec as P

HEAD = 64
EPS = 1e-06
MESH = pl.DeviceIdType.MESH
F32 = jnp.float32
BF16 = jnp.bfloat16
MIB = 2**20


def silu_parts(pre):
    sig = jax.nn.sigmoid(pre)
    return (pre * sig, sig * (1.0 + pre * (1.0 - sig)))


def norm_back(grad, value, scale):
    inner = jnp.mean(grad * value, axis=-1, keepdims=True)
    return scale * grad - value * (scale * scale * scale) * inner


def project(left, weight):
    return jnp.dot(left, weight, preferred_element_type=F32)


def weight_grad(left, right):
    return jnp.einsum("td,tf->df", left, right, preferred_element_type=F32)


def back_project(grad, weight):
    return jnp.einsum("tf,df->td", grad, weight, preferred_element_type=F32)


def dot(a, b, ca, cb):
    return lax.dot_general(a, b, (((ca,), (cb,)), ((), ())), preferred_element_type=F32)


def low_lanes(shape):
    return lax.broadcasted_iota(jnp.int32, shape, len(shape) - 1) < HEAD


def two_heads(x):
    low = low_lanes(x.shape)
    zero = jnp.zeros_like(x)
    return jnp.concatenate([jnp.where(low, x, zero), jnp.where(low, zero, x)], axis=0)


def pick_heads(x):
    half = x.shape[0] // 2
    return jnp.where(low_lanes((half, x.shape[1])), x[:half], x[half:])


def causal_pair(span):
    t = lax.broadcasted_iota(jnp.int32, (span, 2 * span), 0)
    u = lax.broadcasted_iota(jnp.int32, (span, 2 * span), 1)
    return t >= u % span


def pair_of(ref, p):
    return ref[:, pl.ds(p * 2 * HEAD, 2 * HEAD)]


def state_kernel(left_ref, right_ref, out_ref):
    for p in range(out_ref.shape[1]):
        out_ref[0, p] = pick_heads(dot(pair_of(left_ref, p), pair_of(right_ref, p), 0, 0))


def attn_kernel(q_ref, k_ref, v_ref, prefix_ref, out_ref):
    span = q_ref.shape[0]
    causal = causal_pair(span)
    for p in range(prefix_ref.shape[1]):
        q, k2, v2 = pair_of(q_ref, p), two_heads(pair_of(k_ref, p)), two_heads(pair_of(v_ref, p))
        scores = jnp.where(causal, dot(q, k2, 1, 1), 0.0).astype(BF16)
        prefix = two_heads(prefix_ref[0, p])
        out_ref[:, pl.ds(p * 2 * HEAD, 2 * HEAD)] = dot(scores, v2, 1, 0) + dot(q, prefix, 1, 0)


def attn_back_kernel(q_ref, k_ref, v_ref, g_ref, prefix_ref, dstate_ref, dq_ref, dk_ref, dv_ref):
    span = q_ref.shape[0]
    causal = causal_pair(span)
    for p in range(prefix_ref.shape[1]):
        q, k, v, g = (pair_of(r, p) for r in (q_ref, k_ref, v_ref, g_ref))
        k2, v2 = two_heads(k), two_heads(v)
        prefix, dstate = two_heads(prefix_ref[0, p]), two_heads(dstate_ref[0, p])
        scores = jnp.where(causal, dot(q, k2, 1, 1), 0.0).astype(BF16)
        dscores = jnp.where(causal, dot(g, v2, 1, 1), 0.0).astype(BF16)
        lanes = pl.ds(p * 2 * HEAD, 2 * HEAD)
        dq_ref[:, lanes] = dot(dscores, k2, 1, 0) + dot(g, prefix, 1, 1)
        dk_ref[:, lanes] = pick_heads(dot(dscores, q, 0, 0)) + dot(v, dstate, 1, 1)
        dv_ref[:, lanes] = pick_heads(dot(scores, g, 0, 0)) + dot(k, dstate, 1, 0)


def rows_spec(span, width):
    return pl.BlockSpec((span, width), lambda s: (s, 0))


def state_spec(pairs):
    return pl.BlockSpec((1, pairs, HEAD, 2 * HEAD), lambda s: (s, 0, 0, 0))


def local_states(left, right, seqs):
    rows, width = left.shape
    span, pairs = rows // seqs, width // (2 * HEAD)
    return pl.pallas_call(
        state_kernel,
        grid=(seqs,),
        in_specs=[rows_spec(span, width)] * 2,
        out_specs=state_spec(pairs),
        out_shape=jax.ShapeDtypeStruct((seqs, pairs, HEAD, 2 * HEAD), F32),
    )(left, right)


def attention(q, k, v, prefix, seqs):
    rows, width = q.shape
    span, pairs = rows // seqs, width // (2 * HEAD)
    return pl.pallas_call(
        attn_kernel,
        grid=(seqs,),
        in_specs=[rows_spec(span, width)] * 3 + [state_spec(pairs)],
        out_specs=rows_spec(span, width),
        out_shape=jax.ShapeDtypeStruct((rows, width), F32),
    )(q, k, v, prefix)


def attention_back(q, k, v, g, prefix, dstate, seqs):
    rows, width = q.shape
    span, pairs = rows // seqs, width // (2 * HEAD)
    return pl.pallas_call(
        attn_back_kernel,
        grid=(seqs,),
        in_specs=[rows_spec(span, width)] * 4 + [state_spec(pairs)] * 2,
        out_specs=[rows_spec(span, width)] * 3,
        out_shape=[jax.ShapeDtypeStruct((rows, width), F32)] * 3,
    )(q, k, v, g, prefix, dstate)


def scan_kernel(outer, reverse, s_ref, out_ref, held, summed, other, zs, zr, xs, xr):
    chunks = s_ref.shape[0]
    k = lax.axis_index("blk")
    z, x = k // 2, k % 2
    if reverse:
        zz, xx = outer - 1 - z, 1 - x
        after, before = jnp.maximum(z - 1, 0), jnp.minimum(z + 1, outer - 1)
    else:
        zz, xx = z, x
        after, before = jnp.minimum(z + 1, outer - 1), jnp.maximum(z - 1, 0)
    nxt, prv, side = {"blk": after * 2 + x}, {"blk": before * 2 + x}, {"blk": z * 2 + 1 - x}
    first, last = zz == 0, zz == outer - 1

    bar = pltpu.get_barrier_semaphore()
    pl.semaphore_signal(bar, inc=1, device_id=side, device_id_type=MESH)
    pl.when(~last)(lambda: pl.semaphore_signal(bar, inc=1, device_id=nxt, device_id_type=MESH))
    pl.when(~first)(lambda: pl.semaphore_signal(bar, inc=1, device_id=prv, device_id_type=MESH))
    pl.semaphore_wait(bar, 1 + jnp.where(last, 0, 1) + jnp.where(first, 0, 1))

    def along(i):
        return pltpu.make_async_remote_copy(
            src_ref=summed.at[i], dst_ref=held.at[i], send_sem=zs.at[i], recv_sem=zr.at[i],
            device_id=nxt, device_id_type=MESH)

    def across(i, src):
        return pltpu.make_async_remote_copy(
            src_ref=src.at[i], dst_ref=other.at[i], send_sem=xs.at[i], recv_sem=xr.at[i],
            device_id=side, device_id_type=MESH)

    def pass_on(i):
        pl.when(~first)(lambda: along(i).wait_recv())

        @pl.when(first)
        def _():
            held[i] = jnp.zeros_like(held[i])

        summed[i] = held[i] + s_ref[i]
        pl.when(~last)(lambda: along(i).start())
        pl.when(xx == 0)(lambda: across(i, summed).start())
        pl.when(xx == 1)(lambda: across(i, held).start())

    def finish(i):
        across(i, held).wait_recv()
        out_ref[i] = (held[i] + other[i]).astype(out_ref.dtype)

    def step(i, carry):
        pl.when(i < chunks)(lambda: pass_on(i))
        pl.when(i > 0)(lambda: finish(i - 1))
        return carry

    lax.fori_loop(0, chunks + 1, step, 0)

    def drain(i, carry):
        pl.when(~last)(lambda: along(i).wait_send())
        across(i, held).wait_send()
        return carry

    lax.fori_loop(0, chunks, drain, 0)


def entering(states, blk, reverse):
    seqs, pairs, head, lanes = states.shape
    per = max(1, pairs // 2)
    shape = (seqs * pairs // per, per, head, lanes)
    vmem = pl.BlockSpec(memory_space=pltpu.VMEM)
    sems = [pltpu.SemaphoreType.DMA((shape[0],))] * 4
    out = pl.pallas_call(
        functools.partial(scan_kernel, blk // 2, reverse),
        out_shape=jax.ShapeDtypeStruct(shape, BF16),
        in_specs=[vmem],
        out_specs=vmem,
        scratch_shapes=[pltpu.VMEM(shape, F32)] * 3 + sems,
        compiler_params=pltpu.CompilerParams(
            collective_id=2 if reverse else 1, has_side_effects=True, vmem_limit_bytes=24 * MIB),
    )(states.reshape(shape))
    return out.reshape(states.shape)


LAND, FIN, ACC = 4, 8, 10
CORE, XA, YA, YB, XB, XC, YC = range(7)
TILE = 256


class Named:
    def __init__(self, names, refs):
        self.__dict__.update(zip(names, refs))


class Stream:
    def __init__(self, block, buf, sem):
        self.block, self.buf, self.sem = block, buf, sem

    def copy(self, j):
        return pltpu.make_async_copy(self.block(j), self.buf.at[j % 2], self.sem.at[j % 2])

    def start(self, j):
        self.copy(j).start()

    def get(self, j, count):
        self.copy(j).wait()
        pl.when(j + 1 < count)(lambda: self.start(j + 1))
        return self.buf.at[j % 2]


BACK_IN = (
    "tokens", "dy", "innert", "inner", "first", "second", "resid", "gate", "attn", "q", "k", "v",
    "query", "key", "prefix", "normt", "norm2t", "mixedt", "gain", "w_query", "w_key", "w_value",
    "w_gate", "w_out", "w_first", "w_second", "w_third",
)
BACK_OUT = (
    "output", "dtokens", "tall", "wide", "square", "dgain",
)
BACK_SCRATCH = (
    "tbuf", "core_rx", "acc", "xa", "ya", "yb", "xb", "xc", "yc", "zab", "zc", "fin", "ssem",
    "rsem", "zss", "zrs", "osem", "csem", "crem", "ygs", "ygr", "dyv", "dfs", "dn2", "dlow",
    "dgate", "dattn", "at0", "at1", "held", "sums", "other", "dstate", "sz", "rz", "sx", "rx",
    "gacc", "gbuf", "gland", "gs", "gr", "lsem",
)


def back_kernel(outer, seqs, *refs):
    r = Named(BACK_IN + BACK_OUT + BACK_SCRATCH, refs)
    rows, width = r.tokens.shape
    ff = r.first.shape[1]
    span, pairs = rows // seqs, width // (2 * HEAD)
    n_tall, n_wide, n_square = ff // 256, ff // 128, 20
    chunks = n_tall + n_wide + n_square
    at_wide, at_square = n_tall, n_tall + n_wide
    blocks = rows // TILE

    b, k = lax.axis_index("batch"), lax.axis_index("blk")
    y, c = b // 2, b % 2
    z, x = k // 2, k % 2
    ox, oy = 1 - x, 1 - y
    top = outer - 1
    zr = top - z
    to_core, to_y, to_x = {"batch": y * 2 + 1 - c}, {"batch": oy * 2 + c}, {"blk": z * 2 + ox}
    to_up = {"blk": jnp.minimum(z + 1, top) * 2 + x}
    to_down = {"blk": jnp.maximum(z - 1, 0) * 2 + x}
    to_z = [{"blk": (z + d) % outer * 2 + x} for d in range(1, outer)]

    peers = [to_core, to_y, to_x] + to_z
    bar = pltpu.get_barrier_semaphore()
    for d in peers:
        pl.semaphore_signal(bar, inc=1, device_id=d, device_id_type=MESH)
    pl.semaphore_wait(bar, len(peers))

    def remote(src, dst, s, t, dev):
        return pltpu.make_async_remote_copy(
            src_ref=src, dst_ref=dst, send_sem=s, recv_sem=t, device_id=dev, device_id_type=MESH)

    def link(kind, i, src, dst, dev):
        return remote(src, dst.at[i % LAND], r.ssem.at[kind, i % LAND], r.rsem.at[kind, i % LAND], dev)

    def at(i, *where):
        return r.acc.at[(i % ACC,) + where]

    A, B, C = pl.ds(0, 32), pl.ds(32, 16), pl.ds(48, 16)
    every = slice(None)

    def core_copy(i):
        return link(CORE, i, r.tbuf.at[i % 2], r.core_rx, to_core)

    def xa_copy(i):
        return link(XA, i, at(i, every, ox, every, A), r.xa, to_x)

    def ya_copy(i):
        return link(YA, i, at(i, every, x, oy, A), r.ya, to_y)

    def yb_copy(i):
        return link(YB, i, at(i, every, every, oy, B), r.yb, to_y)

    def xb_copy(i):
        return link(XB, i, at(i, every, ox, y, B), r.xb, to_x)

    def xc_copy(i):
        return link(XC, i, at(i, z, ox, every, C), r.xc, to_x)

    def yc_copy(i):
        return link(YC, i, at(i, z, x, oy, C), r.yc, to_y)

    def y_share(i):
        f = i % FIN
        return remote(r.fin.at[f, y], r.fin.at[f, y], r.ygs.at[f], r.ygr.at[f], to_y)

    def part_ab(i, s):
        return at(i, s, x, y, pl.ds(0, 48))

    def part_c(i, s):
        return at(i, s, every, every, C)

    AB, CC = (0, part_ab, r.zab), (1, part_c, r.zc)

    def hop(group, i, n, up, s):
        g, part, land = group
        d = 0 if up else 1
        sem = (g, d, n - 1, i % LAND)
        return remote(part(i, s), land.at[i % LAND, d, n - 1], r.zss.at[sem], r.zrs.at[sem],
                      to_up if up else to_down)

    def z_each(group, i, n, act):
        up = hop(group, i, n, True, jnp.minimum(outer - n + z, top))
        down = hop(group, i, n, False, jnp.maximum(n - 1 - zr, 0))
        pl.when((z <= n - 1) & (z < top))(lambda: act(up))
        pl.when((zr <= n - 1) & (z > 0))(lambda: act(down))

    def z_send(group, i, n):
        z_each(group, i, n, lambda copy: copy.start())

    def z_sent(group, i, n):
        z_each(group, i, n, lambda copy: copy.wait_send())

    def add(ref, landed):
        ref[...] = ref[...] + landed

    def z_take(group, i, n):
        g, part, land = group

        def take(up, s):
            hop(group, i, n, up, s).wait_recv()
            add(part(i, s), land[i % LAND, 0 if up else 1, n - 1])

        pl.when((z > 0) & (z <= n))(lambda: take(True, jnp.clip(outer - n + z - 1, 0, top)))
        pl.when((z < top) & (zr <= n))(lambda: take(False, jnp.clip(n - zr, 0, top)))

    def places(i, act):
        f = r.fin.at[i % FIN]

        @pl.when(i < at_wide)
        def _():
            for yy in range(2):
                for blk in range(2):
                    col = pl.multiple_of(c * (width // 2) + (yy * 2 + blk) * 128, 128)
                    act(f.at[yy, pl.ds(blk * 32, 32)], r.tall.at[pl.ds(i * 32, 32), pl.ds(col, 128)])

        @pl.when((i >= at_wide) & (i < at_square))
        def _():
            j, h = (i - at_wide) // 2, (i - at_wide) % 2
            col = pl.multiple_of(c * (ff // 2) + j * 128, 128)
            for yy in range(2):
                act(f.at[yy], r.wide.at[yy, pl.ds(h * 64, 64), pl.ds(col, 128)])

        @pl.when(i >= at_square)
        def _():
            j = i - at_square
            m, u, h = j // 4, j // 2 % 2, j % 2
            for yy in range(2):
                col = pl.multiple_of(c * (width // 2) + u * 256 + yy * 128, 128)
                act(f.at[yy], r.square.at[m, pl.ds(h * 64, 64), pl.ds(col, 128)])

    def cores(i):
        core_copy(i).wait_recv()
        core_copy(i).wait_send()
        add(at(i), r.core_rx[i % LAND])
        xa_copy(i).start()
        yb_copy(i).start()
        z_send(CC, i, 1)

    def second(i):
        yb_copy(i).wait_recv()
        add(at(i, every, every, y, B), r.yb[i % LAND])
        xb_copy(i).start()
        xa_copy(i).wait_recv()
        add(at(i, every, x, every, A), r.xa[i % LAND])
        ya_copy(i).start()
        z_take(CC, i, 1)
        z_send(CC, i, 2)
        xa_copy(i).wait_send()
        yb_copy(i).wait_send()
        z_sent(CC, i, 1)

    def third(i):
        xb_copy(i).wait_recv()
        add(at(i, every, x, y, B), r.xb[i % LAND])
        ya_copy(i).wait_recv()
        add(at(i, every, x, y, A), r.ya[i % LAND])
        z_send(AB, i, 1)
        z_take(CC, i, 2)
        z_send(CC, i, 3)
        xb_copy(i).wait_send()
        ya_copy(i).wait_send()
        z_sent(CC, i, 2)

    def fourth(i):
        z_take(AB, i, 1)
        z_send(AB, i, 2)
        z_take(CC, i, 3)
        xc_copy(i).start()
        z_sent(AB, i, 1)
        z_sent(CC, i, 3)

    def fifth(i):
        z_take(AB, i, 2)
        z_send(AB, i, 3)
        xc_copy(i).wait_recv()
        add(at(i, z, x, every, C), r.xc[i % LAND])
        yc_copy(i).start()
        z_sent(AB, i, 2)
        xc_copy(i).wait_send()

    def sixth(i):
        yc_copy(i).wait_recv()
        z_take(AB, i, 3)
        f = i % FIN
        r.fin[f, y, pl.ds(0, 48)] = r.acc[i % ACC, z, x, y, pl.ds(0, 48)]
        r.fin[f, y, C] = r.acc[i % ACC, z, x, y, C] + r.yc[i % LAND]
        y_share(i).start()
        z_sent(AB, i, 3)
        yc_copy(i).wait_send()

    def seventh(i):
        y_share(i).wait_recv()
        y_share(i).wait_send()
        f = i % FIN

        def go(src, dst):
            remote(src, dst, r.csem.at[f], r.crem.at[f], to_core).start()
            pltpu.make_async_copy(src, dst, r.osem.at[f]).start()

        places(i, go)

    def last(i):
        f = i % FIN
        whole = r.fin.at[f]
        copy = remote(whole, whole, r.csem.at[f], r.crem.at[f], to_core)
        copy.wait_send()
        copy.wait_recv()
        pltpu.make_async_copy(whole, whole, r.osem.at[f]).wait()

    stages = (None, cores, second, third, fourth, fifth, sixth, seventh, last)

    def move(t):
        for n, stage in enumerate(stages):
            if stage is not None:
                i = t - n
                pl.when((i >= 0) & (i < chunks))(functools.partial(stage, i))

    def make(t, fill):
        fill(1 - c, r.tbuf.at[t % 2])
        core_copy(t).start()
        fill(c, r.acc.at[t % ACC])

    def fill_tall(lhs):
        def fill(half, dst):
            for yy in range(2):
                col = pl.multiple_of(half * (width // 2) + yy * 256, 256)
                res = dot(lhs, r.dyv[:, pl.ds(col, 256)], 1, 0).reshape(4, 2, 32, 256)
                for blk in range(2):
                    dst[:, :, yy, pl.ds(blk * 32, 32), :] = res[..., blk * 128:(blk + 1) * 128]
        return fill

    def left_rows(ref, h):
        return ref[:, h].reshape(8 * 64, rows)

    def fill_two(left, h, take):
        def fill(half, dst):
            res = dot(left_rows(left, h), take(half), 1, 0).reshape(4, 2, 64, 256)
            dst[:, :, 0] = res[..., :128]
            dst[:, :, 1] = res[..., 128:]
        return fill

    def make_wide(t):
        i = t - at_wide
        j, h = i // 2, i % 2

        def take(half):
            col = pl.ds(pl.multiple_of(half * (ff // 2) + j * 128, 128), 128)
            return jnp.concatenate([r.dfs[0, :, col], r.dfs[1, :, col]], axis=1)

        make(t, fill_two(r.at0, h, take))

    def make_square(t, base, left, right):
        i = t - base
        u, h = i // 2, i % 2

        def take(half):
            return right(pl.ds(pl.multiple_of(half * (width // 2) + u * 256, 256), 256))

        make(t, fill_two(left, h, take))

    zz, xx = zr, ox
    n_scan = r.sums.shape[0]
    halves = n_scan // seqs
    scan_at = at_wide + 1

    def along(i):
        return remote(r.sums.at[i], r.held.at[i], r.sz.at[i], r.rz.at[i], to_down)

    def across(i, src):
        return remote(src.at[i], r.other.at[i], r.sx.at[i], r.rx.at[i], to_x)

    def pass_on(i):
        pl.when(zz > 0)(lambda: along(i).wait_recv())

        @pl.when(zz == 0)
        def _():
            r.held[i] = jnp.zeros_like(r.held[i])

        r.sums[i] = r.held[i] + r.sums[i]
        pl.when(zz < top)(lambda: along(i).start())
        pl.when(xx == 0)(lambda: across(i, r.sums).start())
        pl.when(xx == 1)(lambda: across(i, r.held).start())

    def finish(i):
        across(i, r.held).wait_recv()
        r.dstate[i] = (r.held[i] + r.other[i]).astype(BF16)
        pl.when(zz < top)(lambda: along(i).wait_send())
        across(i, r.held).wait_send()

    def scan(t):
        i = t - scan_at - zz
        pl.when((i >= 0) & (i < n_scan))(lambda: pass_on(i))
        pl.when((i >= 2) & (i < n_scan + 2))(lambda: finish(i - 2))

    def tok(j, n=TILE):
        return pl.ds(pl.multiple_of(j * n, n), n)

    def tile_inner(j, w3, w1, w2, first, second):
        def block(m, carry):
            at_rows = tok(m, 512)
            din = dot(r.dyv[at_rows, :], w3[...], 1, 1)
            one = (din * second[at_rows, :].astype(F32)).astype(BF16)
            two = (din * first[at_rows, :].astype(F32)).astype(BF16)
            cols = pl.ds(pl.multiple_of(j * 256, 256), 256)
            r.dfs[0, at_rows, cols] = one
            r.dfs[1, at_rows, cols] = two
            for n in range(width // 256):
                to = pl.ds(n * 256, 256)
                res = dot(one, w1[to, :], 1, 1) + dot(two, w2[to, :], 1, 1)
                r.dn2[at_rows, to] = r.dn2[at_rows, to] + res
            return carry

        lax.fori_loop(0, rows // 512, block, 0)

    def tile_resid(j, resid, gate, attn, q, w_out, gain, dmix):
        def one(m, carry):
            here, sub = pl.ds(pl.multiple_of(j * TILE + m * 32, 32), 32), tok(m, 32)
            value = resid[sub, :]
            grad = r.dn2[here, :]
            scale = lax.rsqrt(jnp.mean(value * value, axis=-1, keepdims=True) + EPS)
            out = r.dyv[here, :].astype(F32) + norm_back(grad, value, scale)
            r.dn2[here, :] = out
            r.dlow[here, :] = out.astype(BF16)
            return carry

        lax.fori_loop(0, TILE // 32, one, 0)
        for n in range(width // 256):
            to = pl.ds(n * 256, 256)
            dmix[:, to] = dot(r.dlow[tok(j), :], w_out[to, :], 1, 1)

        def two(m, carry):
            here, sub = pl.ds(pl.multiple_of(j * TILE + m * 32, 32), 32), tok(m, 32)
            av = attn[sub, :].astype(F32)
            scale = lax.rsqrt(jnp.mean(av * av, axis=-1, keepdims=True) + EPS)
            unit = av * scale
            act, der = silu_parts(gate[sub, :].astype(F32))
            dm = dmix[sub, :]
            ds = dm * act
            r.dgate[here, :] = (dm * (unit * gain[...]) * der).astype(BF16)
            r.gacc[...] = r.gacc[...] + jnp.sum((ds * unit).reshape(4, 8, width), axis=0)
            r.dattn[here, :] = norm_back(ds * gain[...], av, scale).astype(BF16)
            return carry

        lax.fori_loop(0, TILE // 32, two, 0)

        def states(m, carry):
            s = j * (TILE // span) + m
            for p in range(pairs):
                lanes = pl.ds(p * 2 * HEAD, 2 * HEAD)
                grad = r.dattn[tok(s, span), lanes]
                per = pairs // halves
                r.sums[s * halves + p // per, p % per] = pick_heads(dot(q[tok(m, span), lanes], grad, 0, 0))
            return carry

        lax.fori_loop(0, TILE // span, states, 0)

    def tile_attn(s, q_ref, k_ref, v_ref, query, key, prefix_ref):
        causal = causal_pair(span)
        here = tok(s, span)
        for p in range(pairs):
            lanes = pl.ds(p * 2 * HEAD, 2 * HEAD)
            q, k, v, g = q_ref[:, lanes], k_ref[:, lanes], v_ref[:, lanes], r.dattn[here, lanes]
            k2, v2 = two_heads(k), two_heads(v)
            per = pairs // halves
            prefix, dstate = two_heads(prefix_ref[p]), two_heads(r.dstate[s * halves + p // per, p % per])
            scores = jnp.where(causal, dot(q, k2, 1, 1), 0.0).astype(BF16)
            dscores = jnp.where(causal, dot(g, v2, 1, 1), 0.0).astype(BF16)
            dq = dot(dscores, k2, 1, 0) + dot(g, prefix, 1, 1)
            dk = pick_heads(dot(dscores, q, 0, 0)) + dot(v, dstate, 1, 1)
            dv = pick_heads(dot(scores, g, 0, 0)) + dot(k, dstate, 1, 0)
            r.dfs[0, here, lanes] = (dq * silu_parts(query[:, lanes].astype(F32))[1]).astype(BF16)
            r.dfs[0, here, pl.ds(width + p * 2 * HEAD, 2 * HEAD)] = (
                dk * silu_parts(key[:, lanes].astype(F32))[1]).astype(BF16)
            r.dfs[1, here, lanes] = dv.astype(BF16)

    parts = [
        lambda at_rows, cols: r.dfs[0, at_rows, cols],
        lambda at_rows, cols: r.dfs[0, at_rows, pl.ds(width + cols.start, cols.size)],
        lambda at_rows, cols: r.dfs[1, at_rows, cols],
    ]
    dq_cols = lambda cols: r.dfs[0, :, cols]
    dk_cols = lambda cols: r.dfs[0, :, pl.ds(width + cols.start, cols.size)]
    dv_cols = lambda cols: r.dfs[1, :, cols]

    def load(src, dst, n):
        return pltpu.make_async_copy(src, dst, r.lsem.at[n])

    def dma(*shape):
        return pltpu.SemaphoreType.DMA(shape)

    def ring(shape, dtype):
        return pltpu.VMEM((2,) + shape, dtype)

    def steps(count, one):
        def go(j, carry):
            one(j)
            return carry

        lax.fori_loop(0, count, go, 0)

    dy_load = load(r.dy, r.dyv, 0)
    norm2_load = load(r.norm2t, r.at0, 1)
    mixed_load = load(r.mixedt, r.at1, 2)
    norm_load = load(r.normt, r.at0, 3)

    def segment0(left, w3, w1, w2, first, second, sems):
        cols = lambda ref: lambda j: ref.at[:, pl.ds(pl.multiple_of(j * 256, 256), 256)]
        s_left = Stream(lambda j: r.innert.at[:, pl.ds(pl.multiple_of(j * 32, 32), 32)], left, sems.at[0])
        tiles = [
            Stream(lambda j: r.w_third.at[pl.ds(pl.multiple_of(j * 256, 256), 256)], w3, sems.at[1]),
            Stream(cols(r.w_first), w1, sems.at[2]),
            Stream(cols(r.w_second), w2, sems.at[3]),
            Stream(cols(r.first), first, sems.at[4]),
            Stream(cols(r.second), second, sems.at[5]),
        ]
        dy_load.start()
        s_left.start(0)
        for s in tiles:
            s.start(0)
        norm2_load.start()
        r.dn2[...] = jnp.zeros_like(r.dn2)
        r.gacc[...] = jnp.zeros_like(r.gacc)
        dy_load.wait()

        def one(j):
            move(j)
            make(j, fill_tall(s_left.get(j, n_tall)[...].reshape(8 * 32, rows)))
            tile_inner(j, *(s.get(j, n_tall) for s in tiles))

        steps(n_tall, one)
        norm2_load.wait()

    pl.run_scoped(
        segment0, ring((8, 32, rows), BF16), ring((256, width), BF16), ring((width, 256), BF16),
        ring((width, 256), BF16), ring((rows, 256), BF16), ring((rows, 256), BF16), dma(6, 2))

    def segment1(resid, gate, attn, q, w_out, gain, dmix, sems, wsem):
        blk = lambda ref: lambda j: ref.at[tok(j)]
        tiles = [
            Stream(blk(ref), buf, sems.at[n])
            for n, (ref, buf) in enumerate(((r.resid, resid), (r.gate, gate), (r.attn, attn), (r.q, q)))
        ]
        w_load = pltpu.make_async_copy(r.w_out, w_out, wsem.at[0])
        g_load = pltpu.make_async_copy(r.gain, gain, wsem.at[1])
        w_load.start()
        g_load.start()
        for s in tiles:
            s.start(0)
        w_load.wait()
        g_load.wait()

        def one(j):
            t = at_wide + j
            move(t)
            scan(t)
            make_wide(t)
            rs, ga, at_, qs = (s.get(j, blocks) for s in tiles)
            tile_resid(j, rs, ga, at_, qs, w_out, gain, dmix)

        steps(blocks, one)

    pl.run_scoped(
        segment1, ring((TILE, width), F32), ring((TILE, width), BF16), ring((TILE, width), BF16),
        ring((TILE, width), BF16), pltpu.VMEM((width, width), BF16), pltpu.VMEM((1, width), F32),
        pltpu.VMEM((TILE, width), F32), dma(4, 2), dma(2))

    def gain_sum(t):
        base = at_wide + blocks
        hops = [to_core, to_y, to_x]

        def swap(n):
            return remote(r.gbuf, r.gland.at[n], r.gs.at[n], r.gr.at[n], hops[n])

        def spread(d):
            return remote(r.gbuf, r.gland.at[2 + d], r.gs.at[2 + d], r.gr.at[2 + d], to_z[d - 1])

        @pl.when(t == base)
        def _():
            total = jnp.sum(r.gacc[...], axis=0, keepdims=True)
            for n in range(8):
                r.gbuf[pl.ds(n, 1), :] = total[:, n * 128:(n + 1) * 128]
            swap(0).start()

        for n in range(3):
            @pl.when(t == base + 2 + 2 * n)
            def _(n=n):
                swap(n).wait()
                r.gbuf[...] = r.gbuf[...] + r.gland[n]
                if n < 2:
                    swap(n + 1).start()
                else:
                    for d in range(1, outer):
                        spread(d).start()

        @pl.when(t == base + 8)
        def _():
            for d in range(1, outer):
                spread(d).wait()
            for d in range(1, outer):
                r.gbuf[...] = r.gbuf[...] + r.gland[2 + d]
            pltpu.make_async_copy(r.gbuf, r.dgain, r.lsem.at[4]).start()

        pl.when(t == base + 10)(lambda: pltpu.make_async_copy(r.gbuf, r.dgain, r.lsem.at[4]).wait())

    n2 = n_wide - blocks
    n_out = blocks * (width // 256)

    def segment2(w3, inner, resid, out, sems, osem):
        per = width // 256
        cols = lambda j: pl.ds(pl.multiple_of(j % per * 256, 256), 256)
        s_w3 = Stream(lambda j: r.w_third.at[:, cols(j)], w3, sems.at[0])
        s_resid = Stream(lambda j: r.resid.at[tok(j // per), cols(j)], resid, sems.at[1])
        s_inner = Stream(lambda n: r.inner.at[tok(n)], inner, sems.at[2])

        def store(j):
            return pltpu.make_async_copy(out.at[j % 2], r.output.at[tok(j // per), cols(j)], osem.at[j % 2])

        mixed_load.start()
        for s in (s_w3, s_resid, s_inner):
            s.start(0)

        def one(j):
            t = at_wide + blocks + j
            move(t)
            scan(t)
            gain_sum(t)
            make_wide(t)

            @pl.when(j < n_out)
            def _():
                w, res = s_w3.get(j, n_out), s_resid.get(j, n_out)

                @pl.when(j % per == 0)
                def _():
                    s_inner.get(j // per, blocks)

                pl.when(j >= 2)(lambda: store(j - 2).wait())
                prod = dot(inner[j // per % 2], w[...], 1, 0)
                out[j % 2] = (res[...] + prod).astype(BF16)
                store(j).start()

        steps(n2, one)
        store(n_out - 2).wait()
        store(n_out - 1).wait()
        mixed_load.wait()

    pl.run_scoped(
        segment2, ring((ff, 256), BF16), ring((TILE, ff), BF16), ring((TILE, 256), F32),
        ring((TILE, 256), BF16), dma(3, 2), dma(2))

    def segment3(q, k, v, query, key, prefix, sems):
        blk = lambda ref: lambda j: ref.at[tok(j, span)]
        tiles = [
            Stream(blk(ref), buf, sems.at[n])
            for n, (ref, buf) in enumerate(((r.q, q), (r.k, k), (r.v, v), (r.query, query), (r.key, key)))
        ]
        tiles.append(Stream(lambda j: r.prefix.at[j], prefix, sems.at[5]))
        norm_load.start()
        for s in tiles:
            s.start(0)

        def one(j):
            t = at_square + j
            move(t)
            scan(t)
            pl.when(j < 4)(lambda: make_square(t, at_square, r.at1, lambda cols: r.dlow[:, cols]))
            pl.when(j == 4)(lambda: norm_load.wait())
            pl.when(j >= 4)(lambda: make_square(t, at_square + 4, r.at0, lambda cols: r.dgate[:, cols]))
            tile_attn(j, *(s.get(j, seqs) for s in tiles))

        steps(8, one)

    pl.run_scoped(
        segment3, *[ring((span, width), BF16)] * 5, ring((pairs, HEAD, 2 * HEAD), BF16), dma(6, 2))

    def segment4(wq, wk, wv, wg, total, xs, out, sems, xsem, osem):
        nn = width // 256
        rowsblk = lambda ref: lambda n: ref.at[pl.ds(pl.multiple_of(n * 256, 256), 256)]
        weights = [
            Stream(rowsblk(ref), buf, sems.at[n])
            for n, (ref, buf) in enumerate(
                ((r.w_query, wq), (r.w_key, wk), (r.w_value, wv), (r.w_gate, wg)))
        ]
        s_x = Stream(lambda j: r.tokens.at[tok(j)], xs, xsem)
        for s in weights:
            s.start(0)
        s_x.start(0)

        def product(j):
            n, m = j // 2, j % 2
            slot = n % 2

            @pl.when(m == 0)
            def _():
                for s in weights:
                    s.get(n, nn)

            here = tok(m, rows // 2)
            full = pl.ds(0, width)
            res = dot(r.dgate[here, :], wg[slot], 1, 1)
            for part, w in zip(parts, (wq, wk, wv)):
                res = res + dot(part(here, full), w[slot], 1, 1)
            total[here, pl.ds(pl.multiple_of(n * 256, 256), 256)] = res

        def store(j):
            return pltpu.make_async_copy(out.at[j % 2], r.dtokens.at[tok(j)], osem.at[j % 2])

        def finish_rows(j):
            xb = s_x.get(j, blocks)
            pl.when(j >= 2)(lambda: store(j - 2).wait())

            def one(m, carry):
                here, sub = pl.ds(pl.multiple_of(j * TILE + m * 32, 32), 32), tok(m, 32)
                xv = xb[sub, :].astype(F32)
                scale = lax.rsqrt(jnp.mean(xv * xv, axis=-1, keepdims=True) + EPS)
                out[j % 2, sub, :] = r.dn2[here, :] + norm_back(total[here, :], xv, scale)
                return carry

            lax.fori_loop(0, TILE // 32, one, 0)
            store(j).start()

        def one(j):
            t = at_square + 8 + j
            move(t)
            pl.when(j < 4)(lambda: make_square(t, at_square + 8, r.at0, dq_cols))
            pl.when((j >= 4) & (j < 8))(lambda: make_square(t, at_square + 12, r.at0, dk_cols))
            pl.when(j >= 8)(lambda: make_square(t, at_square + 16, r.at0, dv_cols))
            pl.when(j < 2 * nn)(lambda: product(j))
            pl.when(j >= 2 * nn)(lambda: finish_rows(j - 2 * nn))

        steps(12, one)
        store(blocks - 2).wait()
        store(blocks - 1).wait()

    pl.run_scoped(
        segment4, *[ring((256, width), BF16)] * 4, pltpu.VMEM((rows, width), F32),
        ring((TILE, width), BF16), ring((TILE, width), F32), dma(4, 2), dma(2), dma(2))

    steps(len(stages) - 1, lambda j: move(chunks + j))


def back(args, seqs, blk):
    rows, width = args["tokens"].shape
    ff = args["first"].shape[1]
    pairs = width // (2 * HEAD)
    anywhere = pl.BlockSpec(memory_space=pl.ANY)
    cut = 4

    def v(*shape, dtype=F32):
        return pltpu.VMEM(shape, dtype)

    def sem(*shape):
        return pltpu.SemaphoreType.DMA(shape)

    n_scan = seqs * 2
    chunk = (4, 2, 2, 64, 128)
    scratch = dict(
        tbuf=v(2, *chunk), core_rx=v(LAND, *chunk), acc=v(ACC, *chunk), xa=v(LAND, 4, 2, 32, 128),
        ya=v(LAND, 4, 32, 128), yb=v(LAND, 4, 2, 16, 128), xb=v(LAND, 4, 16, 128),
        xc=v(LAND, 2, 16, 128), yc=v(LAND, 16, 128), zab=v(LAND, 2, 3, 48, 128),
        zc=v(LAND, 2, 3, 2, 2, 16, 128), fin=v(FIN, 2, 64, 128),
        ssem=sem(7, LAND), rsem=sem(7, LAND), zss=sem(2, 2, 3, LAND), zrs=sem(2, 2, 3, LAND),
        osem=sem(FIN), csem=sem(FIN), crem=sem(FIN), ygs=sem(FIN), ygr=sem(FIN),
        dyv=v(rows, width, dtype=BF16), dfs=v(2, rows, ff, dtype=BF16), dn2=v(rows, width),
        dlow=v(rows, width, dtype=BF16), dgate=v(rows, width, dtype=BF16),
        dattn=v(rows, width, dtype=BF16), at0=v(8, 2, 64, rows, dtype=BF16),
        at1=v(8, 2, 64, rows, dtype=BF16), held=v(n_scan, cut, HEAD, 128), sums=v(n_scan, cut, HEAD, 128),
        other=v(n_scan, cut, HEAD, 128), dstate=v(n_scan, cut, HEAD, 128, dtype=BF16),
        sz=sem(n_scan), rz=sem(n_scan), sx=sem(n_scan), rx=sem(n_scan),
        gacc=v(8, width), gbuf=v(8, 128), gland=v(6, 8, 128), gs=sem(6), gr=sem(6), lsem=sem(5),
    )
    args = dict(args)
    args["innert"] = args["innert"].reshape(8, ff // 8, rows)
    for name in ("normt", "norm2t", "mixedt"):
        args[name] = args[name].reshape(8, 2, 64, rows)
    args["gain"] = args["gain"].reshape(1, width)
    outs = dict(
        output=((rows, width), BF16), dtokens=((rows, width), F32), tall=((ff // 8, width), F32),
        wide=((2, width // 8, ff), F32), square=((5, width // 8, width), F32), dgain=((8, 128), F32),
    )
    return pl.pallas_call(
        functools.partial(back_kernel, blk // 2, seqs),
        out_shape=[jax.ShapeDtypeStruct(*outs[name]) for name in BACK_OUT],
        in_specs=[anywhere] * len(BACK_IN),
        out_specs=[anywhere] * len(BACK_OUT),
        scratch_shapes=[scratch[name] for name in BACK_SCRATCH],
        compiler_params=pltpu.CompilerParams(
            collective_id=3, has_side_effects=True, vmem_limit_bytes=60 * MIB),
        cost_estimate=pl.CostEstimate(flops=60 * 2**30, bytes_accessed=200 * MIB, transcendentals=0),
    )(*(args[name] for name in BACK_IN))


def rms(value):
    return lax.rsqrt(jnp.mean(value * value, axis=-1, keepdims=True) + EPS)


def forward(blk, seqs, xf, weights):
    w_query, w_key, w_value, w_gate, w_out, out_gain, w_first, w_second, w_third = weights
    normed = (xf * rms(xf)).astype(BF16)
    key = project(normed, w_key)
    value = project(normed, w_value)
    k, v = silu_parts(key)[0].astype(BF16), value.astype(BF16)
    prefix = entering(local_states(k, v, seqs), blk, False)
    query = project(normed, w_query)
    gate = project(normed, w_gate)
    q = silu_parts(query)[0].astype(BF16)
    attn = attention(q, k, v, prefix, seqs)
    mixed = (attn * rms(attn) * out_gain * silu_parts(gate)[0]).astype(BF16)
    resid = xf + project(mixed, w_out)
    normed2 = (resid * rms(resid)).astype(BF16)
    first = project(normed2, w_first)
    second = project(normed2, w_second)
    inner = (first * second).astype(BF16)
    return dict(
        normed=normed, query=query, key=key, gate=gate, q=q, k=k, v=v, prefix=prefix, attn=attn,
        mixed=mixed, resid=resid, normed2=normed2, first=first, second=second, inner=inner)


def backward_plain(blk, seqs, xf, grad_top, f, weights):
    w_query, w_key, w_value, w_gate, w_out, out_gain, w_first, w_second, w_third = weights
    output = (f["resid"] + project(f["inner"], w_third)).astype(BF16)
    grad_w3 = weight_grad(f["inner"], grad_top)
    grad_inner = back_project(grad_top, w_third)
    grad_one = (grad_inner * f["second"]).astype(BF16)
    grad_two = (grad_inner * f["first"]).astype(BF16)
    grad_w1 = weight_grad(f["normed2"], grad_one)
    grad_w2 = weight_grad(f["normed2"], grad_two)
    grad_normed2 = back_project(grad_one, w_first) + back_project(grad_two, w_second)
    resid, attn = f["resid"], f["attn"]
    grad_resid = grad_top.astype(F32) + norm_back(grad_normed2, resid, rms(resid))
    grad_resid_low = grad_resid.astype(BF16)
    grad_wo = weight_grad(f["mixed"], grad_resid_low)
    grad_mixed = back_project(grad_resid_low, w_out)
    gate_act, gate_der = silu_parts(f["gate"])
    rattn = rms(attn)
    unit_attn = attn * rattn
    grad_scaled = grad_mixed * gate_act
    grad_gate_low = (grad_mixed * (unit_attn * out_gain) * gate_der).astype(BF16)
    grad_gain = jnp.sum(grad_scaled * unit_attn, axis=0)
    grad_attn = norm_back(grad_scaled * out_gain, attn, rattn).astype(BF16)
    q, k, v, prefix = f["q"], f["k"], f["v"], f["prefix"]
    dstate = entering(local_states(q, grad_attn, seqs), blk, True)
    grad_fq, grad_fk, grad_vv = attention_back(q, k, v, grad_attn, prefix, dstate, seqs)
    grad_query_low = (grad_fq * silu_parts(f["query"])[1]).astype(BF16)
    grad_key_low = (grad_fk * silu_parts(f["key"])[1]).astype(BF16)
    grad_value_low = grad_vv.astype(BF16)
    normed = f["normed"]
    grads = [weight_grad(normed, g) for g in (grad_query_low, grad_key_low, grad_value_low, grad_gate_low)]
    grads += [grad_wo, grad_gain, grad_w1, grad_w2, grad_w3]
    grad_normed = back_project(grad_query_low, w_query) + back_project(grad_key_low, w_key)
    grad_normed = (
        grad_normed + back_project(grad_value_low, w_value) + back_project(grad_gate_low, w_gate)
    )
    grad_input = grad_resid + norm_back(grad_normed, xf, rms(xf))
    summed = [
        lax.psum(lax.psum_scatter(g, "blk", scatter_dimension=0, tiled=True), "batch") for g in grads]
    return output, grad_input, summed


WEIGHTS = (
    "w_query", "w_key", "w_value", "w_gate", "w_out", "gain", "w_first", "w_second", "w_third",
)
SAVED = (
    "inner", "first", "second", "gate", "attn", "query", "key", "q", "k", "v", "prefix",
)


def backward(blk, seqs, tokens, grad_top, f, weights):
    names = WEIGHTS
    args = dict(zip(names, weights), tokens=tokens, dy=grad_top)
    for name in SAVED:
        args[name] = f[name].astype(BF16)
    args["resid"] = f["resid"]
    args["innert"] = f["inner"].T
    args["normt"], args["norm2t"], args["mixedt"] = f["normed"].T, f["normed2"].T, f["mixed"].T
    output, grad_input, tall, wide, square, dgain = back(args, seqs, blk)
    so, sg, sq, sk, sv = (square[n] for n in range(5))
    sgain = lax.dynamic_index_in_dim(dgain, lax.axis_index("blk"), 0, False)
    return output, grad_input, [sq, sk, sv, sg, so, sgain, wide[0], wide[1], tall]


def body(sizes, tokens, cotangent, *weights):
    batch, blk = sizes
    seqs, span, width = tokens.shape
    rows = seqs * span
    low = tokens.reshape(rows, width)
    xf = low.astype(F32)
    grad_top = cotangent.reshape(rows, width)
    f = forward(blk, seqs, xf, weights)
    ff = weights[-1].shape[0]
    if (batch, blk, rows, span, width, ff % 256) == (4, 8, 1024, 128, 1024, 0):
        output, grad_input, grads = backward(blk, seqs, low, grad_top, f, weights)
    else:
        output, grad_input, grads = backward_plain(blk, seqs, xf, grad_top, f, weights)
    shape = (seqs, span, width)
    return (output.reshape(shape), grad_input.reshape(shape), *grads)


def solution(mesh):
    rows = P("batch", "blk", None)
    cut = P("blk", None)
    return jax.shard_map(
        functools.partial(body, (mesh.shape["batch"], mesh.shape["blk"])),
        mesh=mesh,
        in_specs=(rows, rows) + (P(),) * 9,
        out_specs=(rows, rows) + (cut,) * 5 + (P("blk"),) + (cut,) * 3,
        check_vma=False,
    )
```

```python
import functools

import jax
import jax.numpy as jnp
from jax import lax
from jax.experimental import pallas as pl
from jax.experimental.pallas import tpu as pltpu
from jax.sharding import PartitionSpec as P

HEAD = 64
EPS = 1e-06
MESH = pl.DeviceIdType.MESH
F32 = jnp.float32
BF16 = jnp.bfloat16
MIB = 2**20


def silu_parts(pre):
    sig = jax.nn.sigmoid(pre)
    return (pre * sig, sig * (1.0 + pre * (1.0 - sig)))


def norm_back(grad, value, scale):
    inner = jnp.mean(grad * value, axis=-1, keepdims=True)
    return scale * grad - value * (scale * scale * scale) * inner


def project(left, weight):
    return jnp.dot(left, weight, preferred_element_type=F32)


def weight_grad(left, right):
    return jnp.einsum("td,tf->df", left, right, preferred_element_type=F32)


def back_project(grad, weight):
    return jnp.einsum("tf,df->td", grad, weight, preferred_element_type=F32)


def dot(a, b, ca, cb):
    return lax.dot_general(a, b, (((ca,), (cb,)), ((), ())), preferred_element_type=F32)


def low_lanes(shape):
    return lax.broadcasted_iota(jnp.int32, shape, len(shape) - 1) < HEAD


def two_heads(x):
    low = low_lanes(x.shape)
    zero = jnp.zeros_like(x)
    return jnp.concatenate([jnp.where(low, x, zero), jnp.where(low, zero, x)], axis=0)


def pick_heads(x):
    half = x.shape[0] // 2
    return jnp.where(low_lanes((half, x.shape[1])), x[:half], x[half:])


def causal_pair(span):
    t = lax.broadcasted_iota(jnp.int32, (span, 2 * span), 0)
    u = lax.broadcasted_iota(jnp.int32, (span, 2 * span), 1)
    return t >= u % span


def pair_of(ref, p):
    return ref[:, pl.ds(p * 2 * HEAD, 2 * HEAD)]


def state_kernel(left_ref, right_ref, out_ref):
    for p in range(out_ref.shape[1]):
        out_ref[0, p] = pick_heads(dot(pair_of(left_ref, p), pair_of(right_ref, p), 0, 0))


def attn_kernel(q_ref, k_ref, v_ref, prefix_ref, out_ref):
    span = q_ref.shape[0]
    causal = causal_pair(span)
    for p in range(prefix_ref.shape[1]):
        q, k2, v2 = pair_of(q_ref, p), two_heads(pair_of(k_ref, p)), two_heads(pair_of(v_ref, p))
        scores = jnp.where(causal, dot(q, k2, 1, 1), 0.0).astype(BF16)
        prefix = two_heads(prefix_ref[0, p])
        out_ref[:, pl.ds(p * 2 * HEAD, 2 * HEAD)] = dot(scores, v2, 1, 0) + dot(q, prefix, 1, 0)


def attn_back_kernel(q_ref, k_ref, v_ref, g_ref, prefix_ref, dstate_ref, dq_ref, dk_ref, dv_ref):
    span = q_ref.shape[0]
    causal = causal_pair(span)
    for p in range(prefix_ref.shape[1]):
        q, k, v, g = (pair_of(r, p) for r in (q_ref, k_ref, v_ref, g_ref))
        k2, v2 = two_heads(k), two_heads(v)
        prefix, dstate = two_heads(prefix_ref[0, p]), two_heads(dstate_ref[0, p])
        scores = jnp.where(causal, dot(q, k2, 1, 1), 0.0).astype(BF16)
        dscores = jnp.where(causal, dot(g, v2, 1, 1), 0.0).astype(BF16)
        lanes = pl.ds(p * 2 * HEAD, 2 * HEAD)
        dq_ref[:, lanes] = dot(dscores, k2, 1, 0) + dot(g, prefix, 1, 1)
        dk_ref[:, lanes] = pick_heads(dot(dscores, q, 0, 0)) + dot(v, dstate, 1, 1)
        dv_ref[:, lanes] = pick_heads(dot(scores, g, 0, 0)) + dot(k, dstate, 1, 0)


def rows_spec(span, width):
    return pl.BlockSpec((span, width), lambda s: (s, 0))


def state_spec(pairs):
    return pl.BlockSpec((1, pairs, HEAD, 2 * HEAD), lambda s: (s, 0, 0, 0))


def local_states(left, right, seqs):
    rows, width = left.shape
    span, pairs = rows // seqs, width // (2 * HEAD)
    return pl.pallas_call(
        state_kernel,
        grid=(seqs,),
        in_specs=[rows_spec(span, width)] * 2,
        out_specs=state_spec(pairs),
        out_shape=jax.ShapeDtypeStruct((seqs, pairs, HEAD, 2 * HEAD), F32),
    )(left, right)


def attention(q, k, v, prefix, seqs):
    rows, width = q.shape
    span, pairs = rows // seqs, width // (2 * HEAD)
    return pl.pallas_call(
        attn_kernel,
        grid=(seqs,),
        in_specs=[rows_spec(span, width)] * 3 + [state_spec(pairs)],
        out_specs=rows_spec(span, width),
        out_shape=jax.ShapeDtypeStruct((rows, width), F32),
    )(q, k, v, prefix)


def attention_back(q, k, v, g, prefix, dstate, seqs):
    rows, width = q.shape
    span, pairs = rows // seqs, width // (2 * HEAD)
    return pl.pallas_call(
        attn_back_kernel,
        grid=(seqs,),
        in_specs=[rows_spec(span, width)] * 4 + [state_spec(pairs)] * 2,
        out_specs=[rows_spec(span, width)] * 3,
        out_shape=[jax.ShapeDtypeStruct((rows, width), F32)] * 3,
    )(q, k, v, g, prefix, dstate)


def scan_kernel(outer, reverse, s_ref, out_ref, held, summed, other, zs, zr, xs, xr):
    chunks = s_ref.shape[0]
    k = lax.axis_index("blk")
    z, x = k // 2, k % 2
    if reverse:
        zz, xx = outer - 1 - z, 1 - x
        after, before = jnp.maximum(z - 1, 0), jnp.minimum(z + 1, outer - 1)
    else:
        zz, xx = z, x
        after, before = jnp.minimum(z + 1, outer - 1), jnp.maximum(z - 1, 0)
    nxt, prv, side = {"blk": after * 2 + x}, {"blk": before * 2 + x}, {"blk": z * 2 + 1 - x}
    first, last = zz == 0, zz == outer - 1

    bar = pltpu.get_barrier_semaphore()
    pl.semaphore_signal(bar, inc=1, device_id=side, device_id_type=MESH)
    pl.when(~last)(lambda: pl.semaphore_signal(bar, inc=1, device_id=nxt, device_id_type=MESH))
    pl.when(~first)(lambda: pl.semaphore_signal(bar, inc=1, device_id=prv, device_id_type=MESH))
    pl.semaphore_wait(bar, 1 + jnp.where(last, 0, 1) + jnp.where(first, 0, 1))

    def along(i):
        return pltpu.make_async_remote_copy(
            src_ref=summed.at[i], dst_ref=held.at[i], send_sem=zs.at[i], recv_sem=zr.at[i],
            device_id=nxt, device_id_type=MESH)

    def across(i, src):
        return pltpu.make_async_remote_copy(
            src_ref=src.at[i], dst_ref=other.at[i], send_sem=xs.at[i], recv_sem=xr.at[i],
            device_id=side, device_id_type=MESH)

    def pass_on(i):
        pl.when(~first)(lambda: along(i).wait_recv())

        @pl.when(first)
        def _():
            held[i] = jnp.zeros_like(held[i])

        summed[i] = held[i] + s_ref[i]
        pl.when(~last)(lambda: along(i).start())
        pl.when(xx == 0)(lambda: across(i, summed).start())
        pl.when(xx == 1)(lambda: across(i, held).start())

    def finish(i):
        across(i, held).wait_recv()
        out_ref[i] = (held[i] + other[i]).astype(out_ref.dtype)

    def step(i, carry):
        pl.when(i < chunks)(lambda: pass_on(i))
        pl.when(i > 0)(lambda: finish(i - 1))
        return carry

    lax.fori_loop(0, chunks + 1, step, 0)

    def drain(i, carry):
        pl.when(~last)(lambda: along(i).wait_send())
        across(i, held).wait_send()
        return carry

    lax.fori_loop(0, chunks, drain, 0)


def entering(states, blk, reverse):
    seqs, pairs, head, lanes = states.shape
    per = max(1, pairs // 2)
    shape = (seqs * pairs // per, per, head, lanes)
    vmem = pl.BlockSpec(memory_space=pltpu.VMEM)
    sems = [pltpu.SemaphoreType.DMA((shape[0],))] * 4
    out = pl.pallas_call(
        functools.partial(scan_kernel, blk // 2, reverse),
        out_shape=jax.ShapeDtypeStruct(shape, BF16),
        in_specs=[vmem],
        out_specs=vmem,
        scratch_shapes=[pltpu.VMEM(shape, F32)] * 3 + sems,
        compiler_params=pltpu.CompilerParams(
            collective_id=2 if reverse else 1, has_side_effects=True, vmem_limit_bytes=24 * MIB),
    )(states.reshape(shape))
    return out.reshape(states.shape)


LAND, FIN, ACC = 4, 8, 10
CORE, XA, YA, YB, XB, XC, YC = range(7)
TILE = 256


class Named:
    def __init__(self, names, refs):
        self.__dict__.update(zip(names, refs))


class Stream:
    def __init__(self, block, buf, sem):
        self.block, self.buf, self.sem = block, buf, sem

    def copy(self, j):
        return pltpu.make_async_copy(self.block(j), self.buf.at[j % 2], self.sem.at[j % 2])

    def start(self, j):
        self.copy(j).start()

    def get(self, j, count):
        self.copy(j).wait()
        pl.when(j + 1 < count)(lambda: self.start(j + 1))
        return self.buf.at[j % 2]


BACK_IN = (
    "tokens", "dy", "innert", "inner", "first", "second", "resid", "gate", "attn", "q", "k", "v",
    "query", "key", "prefix", "normt", "norm2t", "mixedt", "gain", "w_query", "w_key", "w_value",
    "w_gate", "w_out", "w_first", "w_second", "w_third",
)
BACK_OUT = (
    "output", "dtokens", "tall", "wide", "square", "dgain",
)
BACK_SCRATCH = (
    "tbuf", "core_rx", "acc", "xa", "ya", "yb", "xb", "xc", "yc", "zab", "zc", "fin", "ssem",
    "rsem", "zss", "zrs", "osem", "csem", "crem", "ygs", "ygr", "dyv", "dfs", "dn2", "dlow",
    "dgate", "dattn", "at0", "at1", "held", "sums", "other", "dstate", "sz", "rz", "sx", "rx",
    "gacc", "gbuf", "gland", "gs", "gr", "lsem",
)


FWD_IN = (
    "tokens", "gain", "w_query", "w_key", "w_value", "w_gate", "w_out", "w_first", "w_second",
)
FWD_OUT = (
    "k", "v", "key", "normt", "q", "gate", "query", "attn", "mixedt", "resid", "norm2t", "first",
    "second", "inner", "innert", "prefix",
)
FWD_SCRATCH = (
    "xv", "gv", "wq", "wk", "wv", "wg", "wo", "w1", "w2", "nrm", "kb", "vb", "qb", "gb", "intra",
    "keyb", "queryb", "attnb", "mixb", "residb", "n2b", "firstb", "secondb", "innerb", "tb0", "tb1",
    "tb2", "innertb", "held", "sums", "other", "pre", "sz", "rz", "sx", "rx", "lsem", "xsem", "osem",
)


def forward_kernel(outer, seqs, *refs):
    r = Named(FWD_IN + FWD_OUT + FWD_SCRATCH, refs)
    rows, width = r.tokens.shape
    ff = r.w_first.shape[1]
    span, pairs = rows // seqs, width // (2 * HEAD)
    blocks, per_block = rows // TILE, TILE // span
    n_scan, cut = r.sums.shape[:2]
    per_seq = pairs // cut

    k = lax.axis_index("blk")
    z, x = k // 2, k % 2
    top = outer - 1
    side = {"blk": z * 2 + 1 - x}
    above, below = {"blk": jnp.minimum(z + 1, top) * 2 + x}, {"blk": jnp.maximum(z - 1, 0) * 2 + x}
    bar = pltpu.get_barrier_semaphore()
    pl.semaphore_signal(bar, inc=1, device_id=side, device_id_type=MESH)
    pl.when(z < top)(lambda: pl.semaphore_signal(bar, inc=1, device_id=above, device_id_type=MESH))
    pl.when(z > 0)(lambda: pl.semaphore_signal(bar, inc=1, device_id=below, device_id_type=MESH))

    def tok(j, n=TILE):
        return pl.ds(pl.multiple_of(j * n, n), n)

    loads = [
        pltpu.make_async_copy(src, dst, r.lsem.at[n])
        for n, (src, dst) in enumerate((
            (r.w_key, r.wk), (r.w_value, r.wv), (r.w_query, r.wq), (r.w_gate, r.wg), (r.gain, r.gv),
            (r.w_out, r.wo), (r.w_first, r.w1), (r.w_second, r.w2)))
    ]

    def x_load(j):
        return pltpu.make_async_copy(r.tokens.at[tok(j)], r.xv.at[tok(j)], r.xsem.at[j])

    by_rows = dict(
        k=lambda j: r.kb.at[tok(j)], v=lambda j: r.vb.at[tok(j)], q=lambda j: r.qb.at[tok(j)],
        gate=lambda j: r.gb.at[tok(j)], key=lambda j: r.keyb, query=lambda j: r.queryb,
        attn=lambda j: r.attnb, resid=lambda j: r.residb, first=lambda j: r.firstb,
        second=lambda j: r.secondb, inner=lambda j: r.innerb)
    by_cols = dict(normt=r.tb0, mixedt=r.tb1, norm2t=r.tb2, innert=r.innertb)

    def store(name, j):
        sem = r.osem.at[FWD_OUT.index(name)]
        out = getattr(r, name)
        if name in by_rows:
            return pltpu.make_async_copy(by_rows[name](j), out.at[tok(j)], sem)
        return pltpu.make_async_copy(by_cols[name], out.at[:, tok(j)], sem)

    def free(name, j):
        pl.when(j > 0)(lambda: store(name, j - 1).wait())

    def remote(src, dst, s, t, dev):
        return pltpu.make_async_remote_copy(
            src_ref=src, dst_ref=dst, send_sem=s, recv_sem=t, device_id=dev, device_id_type=MESH)

    def along(i):
        return remote(r.sums.at[i], r.held.at[i], r.sz.at[i], r.rz.at[i], above)

    def across(i, src):
        return remote(src.at[i], r.other.at[i], r.sx.at[i], r.rx.at[i], side)

    def pass_on(i):
        pl.when(z > 0)(lambda: along(i).wait_recv())

        @pl.when(z == 0)
        def _():
            r.held[i] = jnp.zeros_like(r.held[i])

        r.sums[i] = r.held[i] + r.sums[i]
        pl.when(z < top)(lambda: along(i).start())
        pl.when(x == 0)(lambda: across(i, r.sums).start())
        pl.when(x == 1)(lambda: across(i, r.held).start())

    def finish(i):
        across(i, r.held).wait_recv()
        r.pre[i] = (r.held[i] + r.other[i]).astype(BF16)
        pl.when(z < top)(lambda: along(i).wait_send())
        across(i, r.held).wait_send()

    LAG = 2

    def scan(n):
        i = n - LAG * z
        pl.when((i >= 0) & (i < n_scan))(lambda: pass_on(i))
        pl.when((i >= LAG) & (i < n_scan + LAG))(lambda: finish(i - LAG))

    def transposed(src, dst):
        def one(n, carry):
            cols = pl.ds(pl.multiple_of(n * 128, 128), 128)
            dst[cols, :] = src[:, cols].T
            return carry

        lax.fori_loop(0, dst.shape[0] // 128, one, 0)

    def norm_rows(value):
        return (value * lax.rsqrt(jnp.mean(value * value, axis=-1, keepdims=True) + EPS)).astype(BF16)

    def each(count, one):
        def go(m, carry):
            one(m)
            return carry

        lax.fori_loop(0, count, go, 0)

    def rows_of(j, m):
        return pl.ds(pl.multiple_of(j * TILE + m * 32, 32), 32)

    def col(n):
        return pl.ds(pl.multiple_of(n * 256, 256), 256)

    def tile_keys(j):
        x_load(j).wait()

        @pl.when(j == 0)
        def _():
            loads[0].wait()
            loads[1].wait()

        for name in ("key", "k", "v", "normt"):
            free(name, j)

        def one(m):
            r.nrm[rows_of(j, m), :] = norm_rows(r.xv[rows_of(j, m), :].astype(F32))

        each(TILE // 32, one)

        def product(n):
            key = dot(r.nrm[tok(j), :], r.wk[:, col(n)], 1, 0)
            r.keyb[:, col(n)] = key.astype(BF16)
            r.kb[tok(j), col(n)] = silu_parts(key)[0].astype(BF16)
            r.vb[tok(j), col(n)] = dot(r.nrm[tok(j), :], r.wv[:, col(n)], 1, 0).astype(BF16)

        each(width // 256, product)

        def states(m):
            s = j * per_block + m
            for p in range(pairs):
                lanes = pl.ds(p * 2 * HEAD, 2 * HEAD)
                here = tok(s, span)
                r.sums[s * per_seq + p // cut, p % cut] = pick_heads(dot(r.kb[here, lanes], r.vb[here, lanes], 0, 0))

        each(per_block, states)
        transposed(r.nrm.at[tok(j)], r.tb0)
        for name in ("key", "k", "v", "normt"):
            store(name, j).start()

    def tile_query(j):
        @pl.when(j == 0)
        def _():
            loads[2].wait()
            loads[3].wait()

        for name in ("query", "q", "gate"):
            free(name, j)

        def product(n):
            query = dot(r.nrm[tok(j), :], r.wq[:, col(n)], 1, 0)
            r.queryb[:, col(n)] = query.astype(BF16)
            r.qb[tok(j), col(n)] = silu_parts(query)[0].astype(BF16)
            r.gb[tok(j), col(n)] = dot(r.nrm[tok(j), :], r.wg[:, col(n)], 1, 0).astype(BF16)

        each(width // 256, product)
        for name in ("query", "q", "gate"):
            store(name, j).start()

    def tile_scores(s):
        causal = causal_pair(span)
        here = tok(s, span)
        for p in range(pairs):
            lanes = pl.ds(p * 2 * HEAD, 2 * HEAD)
            q, k2, v2 = r.qb[here, lanes], two_heads(r.kb[here, lanes]), two_heads(r.vb[here, lanes])
            scores = jnp.where(causal, dot(q, k2, 1, 1), 0.0).astype(BF16)
            r.intra[here, lanes] = dot(scores, v2, 1, 0)

    def tile_mixed(j):
        pl.when(j == 0)(lambda: loads[4].wait())
        for name in ("attn", "mixedt"):
            free(name, j)

        def inter(m):
            s = j * per_block + m
            here = tok(s, span)
            for p in range(pairs):
                lanes = pl.ds(p * 2 * HEAD, 2 * HEAD)
                prefix = two_heads(r.pre[s * per_seq + p // cut, p % cut])
                r.intra[here, lanes] = r.intra[here, lanes] + dot(r.qb[here, lanes], prefix, 1, 0)

        each(per_block, inter)

        def one(m):
            av = r.intra[rows_of(j, m), :]
            scale = lax.rsqrt(jnp.mean(av * av, axis=-1, keepdims=True) + EPS)
            act = silu_parts(r.gb[rows_of(j, m), :].astype(F32))[0]
            r.attnb[tok(m, 32), :] = av.astype(BF16)
            r.mixb[tok(m, 32), :] = (av * scale * r.gv[...] * act).astype(BF16)

        each(TILE // 32, one)
        transposed(r.mixb, r.tb1)
        for name in ("attn", "mixedt"):
            store(name, j).start()

    def tile_resid(j):
        pl.when(j == 0)(lambda: loads[5].wait())
        for name in ("resid", "norm2t"):
            free(name, j)

        def product(n):
            r.residb[:, col(n)] = r.xv[tok(j), col(n)].astype(F32) + dot(r.mixb[...], r.wo[:, col(n)], 1, 0)

        each(width // 256, product)

        def one(m):
            r.n2b[tok(m, 32), :] = norm_rows(r.residb[tok(m, 32), :])

        each(TILE // 32, one)
        transposed(r.n2b, r.tb2)
        for name in ("resid", "norm2t"):
            store(name, j).start()

    def tile_inner(j, lo, hi):
        def one(n):
            n = n + lo
            first = dot(r.n2b[...], r.w1[:, col(n)], 1, 0)
            second = dot(r.n2b[...], r.w2[:, col(n)], 1, 0)
            inner = (first * second).astype(BF16)
            r.firstb[:, col(n)] = first.astype(BF16)
            r.secondb[:, col(n)] = second.astype(BF16)
            r.innerb[:, col(n)] = inner
            r.innertb[col(n), :] = inner.T

        each(hi - lo, one)

    def tile_up(j):
        @pl.when(j == 0)
        def _():
            loads[6].wait()
            loads[7].wait()

        for name in ("first", "second", "inner", "innert"):
            free(name, j)
        tile_inner(j, 0, ff // 512)

    def tile_up2(j):
        tile_inner(j, ff // 512, ff // 256)
        for name in ("first", "second", "inner", "innert"):
            store(name, j).start()

    for n in range(2):
        x_load(n).start()
        loads[n].start()
    for n in range(2, blocks):
        x_load(n).start()
    for copy in loads[2:]:
        copy.start()
    pl.semaphore_wait(bar, 1 + jnp.where(z < top, 1, 0) + jnp.where(z > 0, 1, 0))

    per = n_scan // blocks
    late = (tile_mixed, tile_resid, tile_up, tile_up2)
    n_query = 1 + per_block

    def slot(n, carry):
        pl.when(n < blocks)(lambda: tile_keys(n))
        q = n - blocks

        @pl.when((q >= 0) & (q < blocks * n_query))
        def _():
            j, m = q // n_query, q % n_query
            pl.when(m == 0)(lambda: tile_query(j))
            pl.when(m > 0)(lambda: tile_scores(j * per_block + m - 1))

        scan(n)
        w = n - LAG * z - LAG - per + 1
        j, m = w // per, w % per
        for step, tile in enumerate(late):
            pl.when((w >= 0) & (j < blocks) & (m == step))(functools.partial(tile, j))
        return carry

    lax.fori_loop(0, n_scan + LAG * (top + 1) + len(late), slot, 0)
    whole = pltpu.make_async_copy(r.pre, r.prefix, r.osem.at[FWD_OUT.index("prefix")])
    whole.start()
    for name in FWD_OUT[:-1]:
        store(name, blocks - 1).wait()
    whole.wait()


def forward_fast(blk, seqs, tokens, weights):
    w_query, w_key, w_value, w_gate, w_out, out_gain, w_first, w_second, w_third = weights
    rows, width = tokens.shape
    ff = w_first.shape[1]
    pairs = width // (2 * HEAD)
    cut = 2
    n_scan = seqs * pairs // cut

    def v(*shape, dtype=BF16):
        return pltpu.VMEM(shape, dtype)

    def sem(*shape):
        return pltpu.SemaphoreType.DMA(shape)

    wide, tall = (rows, width), (width, ff)
    chunks = (n_scan, cut, HEAD, 2 * HEAD)
    scratch = dict(
        xv=v(*wide), gv=v(1, width, dtype=F32), wq=v(width, width), wk=v(width, width), wv=v(width, width),
        wg=v(width, width), wo=v(width, width), w1=v(*tall), w2=v(*tall), nrm=v(*wide), kb=v(*wide),
        vb=v(*wide), qb=v(*wide), gb=v(*wide), intra=v(*wide, dtype=F32), keyb=v(TILE, width),
        queryb=v(TILE, width), attnb=v(TILE, width), mixb=v(TILE, width), residb=v(TILE, width, dtype=F32),
        n2b=v(TILE, width), firstb=v(TILE, ff), secondb=v(TILE, ff), innerb=v(TILE, ff),
        tb0=v(width, TILE), tb1=v(width, TILE), tb2=v(width, TILE), innertb=v(ff, TILE),
        held=v(*chunks, dtype=F32), sums=v(*chunks, dtype=F32), other=v(*chunks, dtype=F32), pre=v(*chunks),
        sz=sem(n_scan), rz=sem(n_scan), sx=sem(n_scan), rx=sem(n_scan), lsem=sem(8),
        xsem=sem(rows // TILE), osem=sem(len(FWD_OUT)),
    )
    shapes = dict(
        normt=(width, rows), mixedt=(width, rows), norm2t=(width, rows), first=(rows, ff), second=(rows, ff),
        inner=(rows, ff), innert=(ff, rows), prefix=chunks)
    anywhere = pl.BlockSpec(memory_space=pl.ANY)
    outs = pl.pallas_call(
        functools.partial(forward_kernel, blk // 2, seqs),
        out_shape=[
            jax.ShapeDtypeStruct(shapes.get(name, wide), F32 if name == "resid" else BF16)
            for name in FWD_OUT
        ],
        in_specs=[anywhere] * len(FWD_IN),
        out_specs=[anywhere] * len(FWD_OUT),
        scratch_shapes=[scratch[name] for name in FWD_SCRATCH],
        compiler_params=pltpu.CompilerParams(
            collective_id=4, has_side_effects=True, vmem_limit_bytes=60 * MIB),
        cost_estimate=pl.CostEstimate(flops=26 * 2**30, bytes_accessed=80 * MIB, transcendentals=0),
    )(tokens, out_gain.reshape(1, width), w_query, w_key, w_value, w_gate, w_out, w_first, w_second)
    f = dict(zip(FWD_OUT, outs))
    f["prefix"] = f["prefix"].reshape(seqs, pairs, HEAD, 2 * HEAD)
    return f


def back_kernel(outer, seqs, *refs):
    r = Named(BACK_IN + BACK_OUT + BACK_SCRATCH, refs)
    rows, width = r.tokens.shape
    ff = r.first.shape[1]
    span, pairs = rows // seqs, width // (2 * HEAD)
    n_tall, n_wide, n_square = ff // 256, ff // 128, 20
    chunks = n_tall + n_wide + n_square
    at_wide, at_square = n_tall, n_tall + n_wide
    blocks = rows // TILE

    b, k = lax.axis_index("batch"), lax.axis_index("blk")
    y, c = b // 2, b % 2
    z, x = k // 2, k % 2
    ox, oy = 1 - x, 1 - y
    top = outer - 1
    zr = top - z
    to_core, to_y, to_x = {"batch": y * 2 + 1 - c}, {"batch": oy * 2 + c}, {"blk": z * 2 + ox}
    to_up = {"blk": jnp.minimum(z + 1, top) * 2 + x}
    to_down = {"blk": jnp.maximum(z - 1, 0) * 2 + x}
    to_z = [{"blk": (z + d) % outer * 2 + x} for d in range(1, outer)]

    peers = [to_core, to_y, to_x] + to_z
    bar = pltpu.get_barrier_semaphore()
    for d in peers:
        pl.semaphore_signal(bar, inc=1, device_id=d, device_id_type=MESH)
    pl.semaphore_wait(bar, len(peers))

    def remote(src, dst, s, t, dev):
        return pltpu.make_async_remote_copy(
            src_ref=src, dst_ref=dst, send_sem=s, recv_sem=t, device_id=dev, device_id_type=MESH)

    def link(kind, i, src, dst, dev):
        return remote(src, dst.at[i % LAND], r.ssem.at[kind, i % LAND], r.rsem.at[kind, i % LAND], dev)

    def at(i, *where):
        return r.acc.at[(i % ACC,) + where]

    A, B, C = pl.ds(0, 32), pl.ds(32, 16), pl.ds(48, 16)
    every = slice(None)

    def core_copy(i):
        return link(CORE, i, r.tbuf.at[i % 2], r.core_rx, to_core)

    def xa_copy(i):
        return link(XA, i, at(i, every, ox, every, A), r.xa, to_x)

    def ya_copy(i):
        return link(YA, i, at(i, every, x, oy, A), r.ya, to_y)

    def yb_copy(i):
        return link(YB, i, at(i, every, every, oy, B), r.yb, to_y)

    def xb_copy(i):
        return link(XB, i, at(i, every, ox, y, B), r.xb, to_x)

    def xc_copy(i):
        return link(XC, i, at(i, z, ox, every, C), r.xc, to_x)

    def yc_copy(i):
        return link(YC, i, at(i, z, x, oy, C), r.yc, to_y)

    def y_share(i):
        f = i % FIN
        return remote(r.fin.at[f, y], r.fin.at[f, y], r.ygs.at[f], r.ygr.at[f], to_y)

    def part_ab(i, s):
        return at(i, s, x, y, pl.ds(0, 48))

    def part_c(i, s):
        return at(i, s, every, every, C)

    AB, CC = (0, part_ab, r.zab), (1, part_c, r.zc)

    def hop(group, i, n, up, s):
        g, part, land = group
        d = 0 if up else 1
        sem = (g, d, n - 1, i % LAND)
        return remote(part(i, s), land.at[i % LAND, d, n - 1], r.zss.at[sem], r.zrs.at[sem],
                      to_up if up else to_down)

    def z_each(group, i, n, act):
        up = hop(group, i, n, True, jnp.minimum(outer - n + z, top))
        down = hop(group, i, n, False, jnp.maximum(n - 1 - zr, 0))
        pl.when((z <= n - 1) & (z < top))(lambda: act(up))
        pl.when((zr <= n - 1) & (z > 0))(lambda: act(down))

    def z_send(group, i, n):
        z_each(group, i, n, lambda copy: copy.start())

    def z_sent(group, i, n):
        z_each(group, i, n, lambda copy: copy.wait_send())

    def add(ref, landed):
        ref[...] = ref[...] + landed

    def z_take(group, i, n):
        g, part, land = group

        def take(up, s):
            hop(group, i, n, up, s).wait_recv()
            add(part(i, s), land[i % LAND, 0 if up else 1, n - 1])

        pl.when((z > 0) & (z <= n))(lambda: take(True, jnp.clip(outer - n + z - 1, 0, top)))
        pl.when((z < top) & (zr <= n))(lambda: take(False, jnp.clip(n - zr, 0, top)))

    def places(i, act):
        f = r.fin.at[i % FIN]

        @pl.when(i < at_wide)
        def _():
            for yy in range(2):
                for blk in range(2):
                    col = pl.multiple_of(c * (width // 2) + (yy * 2 + blk) * 128, 128)
                    act(f.at[yy, pl.ds(blk * 32, 32)], r.tall.at[pl.ds(i * 32, 32), pl.ds(col, 128)])

        @pl.when((i >= at_wide) & (i < at_square))
        def _():
            j, h = (i - at_wide) // 2, (i - at_wide) % 2
            col = pl.multiple_of(c * (ff // 2) + j * 128, 128)
            for yy in range(2):
                act(f.at[yy], r.wide.at[yy, pl.ds(h * 64, 64), pl.ds(col, 128)])

        @pl.when(i >= at_square)
        def _():
            j = i - at_square
            m, u, h = j // 4, j // 2 % 2, j % 2
            for yy in range(2):
                col = pl.multiple_of(c * (width // 2) + u * 256 + yy * 128, 128)
                act(f.at[yy], r.square.at[m, pl.ds(h * 64, 64), pl.ds(col, 128)])

    def cores(i):
        core_copy(i).wait_recv()
        core_copy(i).wait_send()
        add(at(i), r.core_rx[i % LAND])
        xa_copy(i).start()
        yb_copy(i).start()
        z_send(CC, i, 1)

    def second(i):
        yb_copy(i).wait_recv()
        add(at(i, every, every, y, B), r.yb[i % LAND])
        xb_copy(i).start()
        xa_copy(i).wait_recv()
        add(at(i, every, x, every, A), r.xa[i % LAND])
        ya_copy(i).start()
        z_take(CC, i, 1)
        z_send(CC, i, 2)
        xa_copy(i).wait_send()
        yb_copy(i).wait_send()
        z_sent(CC, i, 1)

    def third(i):
        xb_copy(i).wait_recv()
        add(at(i, every, x, y, B), r.xb[i % LAND])
        ya_copy(i).wait_recv()
        add(at(i, every, x, y, A), r.ya[i % LAND])
        z_send(AB, i, 1)
        z_take(CC, i, 2)
        z_send(CC, i, 3)
        xb_copy(i).wait_send()
        ya_copy(i).wait_send()
        z_sent(CC, i, 2)

    def fourth(i):
        z_take(AB, i, 1)
        z_send(AB, i, 2)
        z_take(CC, i, 3)
        xc_copy(i).start()
        z_sent(AB, i, 1)
        z_sent(CC, i, 3)

    def fifth(i):
        z_take(AB, i, 2)
        z_send(AB, i, 3)
        xc_copy(i).wait_recv()
        add(at(i, z, x, every, C), r.xc[i % LAND])
        yc_copy(i).start()
        z_sent(AB, i, 2)
        xc_copy(i).wait_send()

    def sixth(i):
        yc_copy(i).wait_recv()
        z_take(AB, i, 3)
        f = i % FIN
        r.fin[f, y, pl.ds(0, 48)] = r.acc[i % ACC, z, x, y, pl.ds(0, 48)]
        r.fin[f, y, C] = r.acc[i % ACC, z, x, y, C] + r.yc[i % LAND]
        y_share(i).start()
        z_sent(AB, i, 3)
        yc_copy(i).wait_send()

    def seventh(i):
        y_share(i).wait_recv()
        y_share(i).wait_send()
        f = i % FIN

        def go(src, dst):
            remote(src, dst, r.csem.at[f], r.crem.at[f], to_core).start()
            pltpu.make_async_copy(src, dst, r.osem.at[f]).start()

        places(i, go)

    def last(i):
        f = i % FIN
        whole = r.fin.at[f]
        copy = remote(whole, whole, r.csem.at[f], r.crem.at[f], to_core)
        copy.wait_send()
        copy.wait_recv()
        pltpu.make_async_copy(whole, whole, r.osem.at[f]).wait()

    stages = (None, cores, second, third, fourth, fifth, sixth, seventh, last)

    def move(t):
        for n, stage in enumerate(stages):
            if stage is not None:
                i = t - n
                pl.when((i >= 0) & (i < chunks))(functools.partial(stage, i))

    def make(t, fill):
        fill(1 - c, r.tbuf.at[t % 2])
        core_copy(t).start()
        fill(c, r.acc.at[t % ACC])

    def fill_tall(lhs):
        def fill(half, dst):
            for yy in range(2):
                col = pl.multiple_of(half * (width // 2) + yy * 256, 256)
                res = dot(lhs, r.dyv[:, pl.ds(col, 256)], 1, 0).reshape(4, 2, 32, 256)
                for blk in range(2):
                    dst[:, :, yy, pl.ds(blk * 32, 32), :] = res[..., blk * 128:(blk + 1) * 128]
        return fill

    def left_rows(ref, h):
        return ref[:, h].reshape(8 * 64, rows)

    def fill_two(left, h, take):
        def fill(half, dst):
            res = dot(left_rows(left, h), take(half), 1, 0).reshape(4, 2, 64, 256)
            dst[:, :, 0] = res[..., :128]
            dst[:, :, 1] = res[..., 128:]
        return fill

    def make_wide(t):
        i = t - at_wide
        j, h = i // 2, i % 2

        def take(half):
            col = pl.ds(pl.multiple_of(half * (ff // 2) + j * 128, 128), 128)
            return jnp.concatenate([r.dfs[0, :, col], r.dfs[1, :, col]], axis=1)

        make(t, fill_two(r.at0, h, take))

    def make_square(t, base, left, right):
        i = t - base
        u, h = i // 2, i % 2

        def take(half):
            return right(pl.ds(pl.multiple_of(half * (width // 2) + u * 256, 256), 256))

        make(t, fill_two(left, h, take))

    zz, xx = zr, ox
    n_scan = r.sums.shape[0]
    halves = n_scan // seqs
    scan_at = at_wide + 1

    def along(i):
        return remote(r.sums.at[i], r.held.at[i], r.sz.at[i], r.rz.at[i], to_down)

    def across(i, src):
        return remote(src.at[i], r.other.at[i], r.sx.at[i], r.rx.at[i], to_x)

    def pass_on(i):
        pl.when(zz > 0)(lambda: along(i).wait_recv())

        @pl.when(zz == 0)
        def _():
            r.held[i] = jnp.zeros_like(r.held[i])

        r.sums[i] = r.held[i] + r.sums[i]
        pl.when(zz < top)(lambda: along(i).start())
        pl.when(xx == 0)(lambda: across(i, r.sums).start())
        pl.when(xx == 1)(lambda: across(i, r.held).start())

    def finish(i):
        across(i, r.held).wait_recv()
        r.dstate[i] = (r.held[i] + r.other[i]).astype(BF16)
        pl.when(zz < top)(lambda: along(i).wait_send())
        across(i, r.held).wait_send()

    def scan(t):
        i = t - scan_at - zz
        pl.when((i >= 0) & (i < n_scan))(lambda: pass_on(i))
        pl.when((i >= 2) & (i < n_scan + 2))(lambda: finish(i - 2))

    def tok(j, n=TILE):
        return pl.ds(pl.multiple_of(j * n, n), n)

    def tile_inner(j, w3, w1, w2, first, second):
        def block(m, carry):
            at_rows = tok(m, 512)
            din = dot(r.dyv[at_rows, :], w3[...], 1, 1)
            one = (din * second[at_rows, :].astype(F32)).astype(BF16)
            two = (din * first[at_rows, :].astype(F32)).astype(BF16)
            cols = pl.ds(pl.multiple_of(j * 256, 256), 256)
            r.dfs[0, at_rows, cols] = one
            r.dfs[1, at_rows, cols] = two
            for n in range(width // 256):
                to = pl.ds(n * 256, 256)
                res = dot(one, w1[to, :], 1, 1) + dot(two, w2[to, :], 1, 1)
                r.dn2[at_rows, to] = r.dn2[at_rows, to] + res
            return carry

        lax.fori_loop(0, rows // 512, block, 0)

    def tile_resid(j, resid, gate, attn, q, w_out, gain, dmix):
        def one(m, carry):
            here, sub = pl.ds(pl.multiple_of(j * TILE + m * 32, 32), 32), tok(m, 32)
            value = resid[sub, :]
            grad = r.dn2[here, :]
            scale = lax.rsqrt(jnp.mean(value * value, axis=-1, keepdims=True) + EPS)
            out = r.dyv[here, :].astype(F32) + norm_back(grad, value, scale)
            r.dn2[here, :] = out
            r.dlow[here, :] = out.astype(BF16)
            return carry

        lax.fori_loop(0, TILE // 32, one, 0)
        for n in range(width // 256):
            to = pl.ds(n * 256, 256)
            dmix[:, to] = dot(r.dlow[tok(j), :], w_out[to, :], 1, 1)

        def two(m, carry):
            here, sub = pl.ds(pl.multiple_of(j * TILE + m * 32, 32), 32), tok(m, 32)
            av = attn[sub, :].astype(F32)
            scale = lax.rsqrt(jnp.mean(av * av, axis=-1, keepdims=True) + EPS)
            unit = av * scale
            act, der = silu_parts(gate[sub, :].astype(F32))
            dm = dmix[sub, :]
            ds = dm * act
            r.dgate[here, :] = (dm * (unit * gain[...]) * der).astype(BF16)
            r.gacc[...] = r.gacc[...] + jnp.sum((ds * unit).reshape(4, 8, width), axis=0)
            r.dattn[here, :] = norm_back(ds * gain[...], av, scale).astype(BF16)
            return carry

        lax.fori_loop(0, TILE // 32, two, 0)

        def states(m, carry):
            s = j * (TILE // span) + m
            for p in range(pairs):
                lanes = pl.ds(p * 2 * HEAD, 2 * HEAD)
                grad = r.dattn[tok(s, span), lanes]
                per = pairs // halves
                r.sums[s * halves + p // per, p % per] = pick_heads(dot(q[tok(m, span), lanes], grad, 0, 0))
            return carry

        lax.fori_loop(0, TILE // span, states, 0)

    def tile_attn(s, q_ref, k_ref, v_ref, query, key, prefix_ref):
        causal = causal_pair(span)
        here = tok(s, span)
        for p in range(pairs):
            lanes = pl.ds(p * 2 * HEAD, 2 * HEAD)
            q, k, v, g = q_ref[:, lanes], k_ref[:, lanes], v_ref[:, lanes], r.dattn[here, lanes]
            k2, v2 = two_heads(k), two_heads(v)
            per = pairs // halves
            prefix, dstate = two_heads(prefix_ref[p]), two_heads(r.dstate[s * halves + p // per, p % per])
            scores = jnp.where(causal, dot(q, k2, 1, 1), 0.0).astype(BF16)
            dscores = jnp.where(causal, dot(g, v2, 1, 1), 0.0).astype(BF16)
            dq = dot(dscores, k2, 1, 0) + dot(g, prefix, 1, 1)
            dk = pick_heads(dot(dscores, q, 0, 0)) + dot(v, dstate, 1, 1)
            dv = pick_heads(dot(scores, g, 0, 0)) + dot(k, dstate, 1, 0)
            r.dfs[0, here, lanes] = (dq * silu_parts(query[:, lanes].astype(F32))[1]).astype(BF16)
            r.dfs[0, here, pl.ds(width + p * 2 * HEAD, 2 * HEAD)] = (
                dk * silu_parts(key[:, lanes].astype(F32))[1]).astype(BF16)
            r.dfs[1, here, lanes] = dv.astype(BF16)

    parts = [
        lambda at_rows, cols: r.dfs[0, at_rows, cols],
        lambda at_rows, cols: r.dfs[0, at_rows, pl.ds(width + cols.start, cols.size)],
        lambda at_rows, cols: r.dfs[1, at_rows, cols],
    ]
    dq_cols = lambda cols: r.dfs[0, :, cols]
    dk_cols = lambda cols: r.dfs[0, :, pl.ds(width + cols.start, cols.size)]
    dv_cols = lambda cols: r.dfs[1, :, cols]

    def load(src, dst, n):
        return pltpu.make_async_copy(src, dst, r.lsem.at[n])

    def dma(*shape):
        return pltpu.SemaphoreType.DMA(shape)

    def ring(shape, dtype):
        return pltpu.VMEM((2,) + shape, dtype)

    def steps(count, one):
        def go(j, carry):
            one(j)
            return carry

        lax.fori_loop(0, count, go, 0)

    dy_load = load(r.dy, r.dyv, 0)
    norm2_load = load(r.norm2t, r.at0, 1)
    mixed_load = load(r.mixedt, r.at1, 2)
    norm_load = load(r.normt, r.at0, 3)

    def segment0(left, w3, w1, w2, first, second, sems):
        cols = lambda ref: lambda j: ref.at[:, pl.ds(pl.multiple_of(j * 256, 256), 256)]
        s_left = Stream(lambda j: r.innert.at[:, pl.ds(pl.multiple_of(j * 32, 32), 32)], left, sems.at[0])
        tiles = [
            Stream(lambda j: r.w_third.at[pl.ds(pl.multiple_of(j * 256, 256), 256)], w3, sems.at[1]),
            Stream(cols(r.w_first), w1, sems.at[2]),
            Stream(cols(r.w_second), w2, sems.at[3]),
            Stream(cols(r.first), first, sems.at[4]),
            Stream(cols(r.second), second, sems.at[5]),
        ]
        dy_load.start()
        s_left.start(0)
        for s in tiles:
            s.start(0)
        norm2_load.start()
        r.dn2[...] = jnp.zeros_like(r.dn2)
        r.gacc[...] = jnp.zeros_like(r.gacc)
        dy_load.wait()

        def one(j):
            move(j)
            make(j, fill_tall(s_left.get(j, n_tall)[...].reshape(8 * 32, rows)))
            tile_inner(j, *(s.get(j, n_tall) for s in tiles))

        steps(n_tall, one)
        norm2_load.wait()

    pl.run_scoped(
        segment0, ring((8, 32, rows), BF16), ring((256, width), BF16), ring((width, 256), BF16),
        ring((width, 256), BF16), ring((rows, 256), BF16), ring((rows, 256), BF16), dma(6, 2))

    def segment1(resid, gate, attn, q, w_out, gain, dmix, sems, wsem):
        blk = lambda ref: lambda j: ref.at[tok(j)]
        tiles = [
            Stream(blk(ref), buf, sems.at[n])
            for n, (ref, buf) in enumerate(((r.resid, resid), (r.gate, gate), (r.attn, attn), (r.q, q)))
        ]
        w_load = pltpu.make_async_copy(r.w_out, w_out, wsem.at[0])
        g_load = pltpu.make_async_copy(r.gain, gain, wsem.at[1])
        w_load.start()
        g_load.start()
        for s in tiles:
            s.start(0)
        w_load.wait()
        g_load.wait()

        def one(j):
            t = at_wide + j
            move(t)
            scan(t)
            make_wide(t)
            rs, ga, at_, qs = (s.get(j, blocks) for s in tiles)
            tile_resid(j, rs, ga, at_, qs, w_out, gain, dmix)

        steps(blocks, one)

    pl.run_scoped(
        segment1, ring((TILE, width), F32), ring((TILE, width), BF16), ring((TILE, width), BF16),
        ring((TILE, width), BF16), pltpu.VMEM((width, width), BF16), pltpu.VMEM((1, width), F32),
        pltpu.VMEM((TILE, width), F32), dma(4, 2), dma(2))

    def gain_sum(t):
        base = at_wide + blocks
        hops = [to_core, to_y, to_x]

        def swap(n):
            return remote(r.gbuf, r.gland.at[n], r.gs.at[n], r.gr.at[n], hops[n])

        def spread(d):
            return remote(r.gbuf, r.gland.at[2 + d], r.gs.at[2 + d], r.gr.at[2 + d], to_z[d - 1])

        @pl.when(t == base)
        def _():
            total = jnp.sum(r.gacc[...], axis=0, keepdims=True)
            for n in range(8):
                r.gbuf[pl.ds(n, 1), :] = total[:, n * 128:(n + 1) * 128]
            swap(0).start()

        for n in range(3):
            @pl.when(t == base + 2 + 2 * n)
            def _(n=n):
                swap(n).wait()
                r.gbuf[...] = r.gbuf[...] + r.gland[n]
                if n < 2:
                    swap(n + 1).start()
                else:
                    for d in range(1, outer):
                        spread(d).start()

        @pl.when(t == base + 8)
        def _():
            for d in range(1, outer):
                spread(d).wait()
            for d in range(1, outer):
                r.gbuf[...] = r.gbuf[...] + r.gland[2 + d]
            pltpu.make_async_copy(r.gbuf, r.dgain, r.lsem.at[4]).start()

        pl.when(t == base + 10)(lambda: pltpu.make_async_copy(r.gbuf, r.dgain, r.lsem.at[4]).wait())

    n2 = n_wide - blocks
    n_out = blocks * (width // 256)

    def segment2(w3, inner, resid, out, sems, osem):
        per = width // 256
        cols = lambda j: pl.ds(pl.multiple_of(j % per * 256, 256), 256)
        s_w3 = Stream(lambda j: r.w_third.at[:, cols(j)], w3, sems.at[0])
        s_resid = Stream(lambda j: r.resid.at[tok(j // per), cols(j)], resid, sems.at[1])
        s_inner = Stream(lambda n: r.inner.at[tok(n)], inner, sems.at[2])

        def store(j):
            return pltpu.make_async_copy(out.at[j % 2], r.output.at[tok(j // per), cols(j)], osem.at[j % 2])

        mixed_load.start()
        for s in (s_w3, s_resid, s_inner):
            s.start(0)

        def one(j):
            t = at_wide + blocks + j
            move(t)
            scan(t)
            gain_sum(t)
            make_wide(t)

            @pl.when(j < n_out)
            def _():
                w, res = s_w3.get(j, n_out), s_resid.get(j, n_out)

                @pl.when(j % per == 0)
                def _():
                    s_inner.get(j // per, blocks)

                pl.when(j >= 2)(lambda: store(j - 2).wait())
                prod = dot(inner[j // per % 2], w[...], 1, 0)
                out[j % 2] = (res[...] + prod).astype(BF16)
                store(j).start()

        steps(n2, one)
        store(n_out - 2).wait()
        store(n_out - 1).wait()
        mixed_load.wait()

    pl.run_scoped(
        segment2, ring((ff, 256), BF16), ring((TILE, ff), BF16), ring((TILE, 256), F32),
        ring((TILE, 256), BF16), dma(3, 2), dma(2))

    def segment3(q, k, v, query, key, prefix, sems):
        blk = lambda ref: lambda j: ref.at[tok(j, span)]
        tiles = [
            Stream(blk(ref), buf, sems.at[n])
            for n, (ref, buf) in enumerate(((r.q, q), (r.k, k), (r.v, v), (r.query, query), (r.key, key)))
        ]
        tiles.append(Stream(lambda j: r.prefix.at[j], prefix, sems.at[5]))
        norm_load.start()
        for s in tiles:
            s.start(0)

        def one(j):
            t = at_square + j
            move(t)
            scan(t)
            pl.when(j < 4)(lambda: make_square(t, at_square, r.at1, lambda cols: r.dlow[:, cols]))
            pl.when(j == 4)(lambda: norm_load.wait())
            pl.when(j >= 4)(lambda: make_square(t, at_square + 4, r.at0, lambda cols: r.dgate[:, cols]))
            tile_attn(j, *(s.get(j, seqs) for s in tiles))

        steps(8, one)

    pl.run_scoped(
        segment3, *[ring((span, width), BF16)] * 5, ring((pairs, HEAD, 2 * HEAD), BF16), dma(6, 2))

    def segment4(wq, wk, wv, wg, total, xs, out, sems, xsem, osem):
        nn = width // 256
        rowsblk = lambda ref: lambda n: ref.at[pl.ds(pl.multiple_of(n * 256, 256), 256)]
        weights = [
            Stream(rowsblk(ref), buf, sems.at[n])
            for n, (ref, buf) in enumerate(
                ((r.w_query, wq), (r.w_key, wk), (r.w_value, wv), (r.w_gate, wg)))
        ]
        s_x = Stream(lambda j: r.tokens.at[tok(j)], xs, xsem)
        for s in weights:
            s.start(0)
        s_x.start(0)

        def product(j):
            n, m = j // 2, j % 2
            slot = n % 2

            @pl.when(m == 0)
            def _():
                for s in weights:
                    s.get(n, nn)

            here = tok(m, rows // 2)
            full = pl.ds(0, width)
            res = dot(r.dgate[here, :], wg[slot], 1, 1)
            for part, w in zip(parts, (wq, wk, wv)):
                res = res + dot(part(here, full), w[slot], 1, 1)
            total[here, pl.ds(pl.multiple_of(n * 256, 256), 256)] = res

        def store(j):
            return pltpu.make_async_copy(out.at[j % 2], r.dtokens.at[tok(j)], osem.at[j % 2])

        def finish_rows(j):
            xb = s_x.get(j, blocks)
            pl.when(j >= 2)(lambda: store(j - 2).wait())

            def one(m, carry):
                here, sub = pl.ds(pl.multiple_of(j * TILE + m * 32, 32), 32), tok(m, 32)
                xv = xb[sub, :].astype(F32)
                scale = lax.rsqrt(jnp.mean(xv * xv, axis=-1, keepdims=True) + EPS)
                out[j % 2, sub, :] = r.dn2[here, :] + norm_back(total[here, :], xv, scale)
                return carry

            lax.fori_loop(0, TILE // 32, one, 0)
            store(j).start()

        def one(j):
            t = at_square + 8 + j
            move(t)
            pl.when(j < 4)(lambda: make_square(t, at_square + 8, r.at0, dq_cols))
            pl.when((j >= 4) & (j < 8))(lambda: make_square(t, at_square + 12, r.at0, dk_cols))
            pl.when(j >= 8)(lambda: make_square(t, at_square + 16, r.at0, dv_cols))
            pl.when(j < 2 * nn)(lambda: product(j))
            pl.when(j >= 2 * nn)(lambda: finish_rows(j - 2 * nn))

        steps(12, one)
        store(blocks - 2).wait()
        store(blocks - 1).wait()

    pl.run_scoped(
        segment4, *[ring((256, width), BF16)] * 4, pltpu.VMEM((rows, width), F32),
        ring((TILE, width), BF16), ring((TILE, width), F32), dma(4, 2), dma(2), dma(2))

    steps(len(stages) - 1, lambda j: move(chunks + j))


def back(args, seqs, blk):
    rows, width = args["tokens"].shape
    ff = args["first"].shape[1]
    pairs = width // (2 * HEAD)
    anywhere = pl.BlockSpec(memory_space=pl.ANY)
    cut = 4

    def v(*shape, dtype=F32):
        return pltpu.VMEM(shape, dtype)

    def sem(*shape):
        return pltpu.SemaphoreType.DMA(shape)

    n_scan = seqs * 2
    chunk = (4, 2, 2, 64, 128)
    scratch = dict(
        tbuf=v(2, *chunk), core_rx=v(LAND, *chunk), acc=v(ACC, *chunk), xa=v(LAND, 4, 2, 32, 128),
        ya=v(LAND, 4, 32, 128), yb=v(LAND, 4, 2, 16, 128), xb=v(LAND, 4, 16, 128),
        xc=v(LAND, 2, 16, 128), yc=v(LAND, 16, 128), zab=v(LAND, 2, 3, 48, 128),
        zc=v(LAND, 2, 3, 2, 2, 16, 128), fin=v(FIN, 2, 64, 128),
        ssem=sem(7, LAND), rsem=sem(7, LAND), zss=sem(2, 2, 3, LAND), zrs=sem(2, 2, 3, LAND),
        osem=sem(FIN), csem=sem(FIN), crem=sem(FIN), ygs=sem(FIN), ygr=sem(FIN),
        dyv=v(rows, width, dtype=BF16), dfs=v(2, rows, ff, dtype=BF16), dn2=v(rows, width),
        dlow=v(rows, width, dtype=BF16), dgate=v(rows, width, dtype=BF16),
        dattn=v(rows, width, dtype=BF16), at0=v(8, 2, 64, rows, dtype=BF16),
        at1=v(8, 2, 64, rows, dtype=BF16), held=v(n_scan, cut, HEAD, 128), sums=v(n_scan, cut, HEAD, 128),
        other=v(n_scan, cut, HEAD, 128), dstate=v(n_scan, cut, HEAD, 128, dtype=BF16),
        sz=sem(n_scan), rz=sem(n_scan), sx=sem(n_scan), rx=sem(n_scan),
        gacc=v(8, width), gbuf=v(8, 128), gland=v(6, 8, 128), gs=sem(6), gr=sem(6), lsem=sem(5),
    )
    args = dict(args)
    args["innert"] = args["innert"].reshape(8, ff // 8, rows)
    for name in ("normt", "norm2t", "mixedt"):
        args[name] = args[name].reshape(8, 2, 64, rows)
    args["gain"] = args["gain"].reshape(1, width)
    outs = dict(
        output=((rows, width), BF16), dtokens=((rows, width), F32), tall=((ff // 8, width), F32),
        wide=((2, width // 8, ff), F32), square=((5, width // 8, width), F32), dgain=((8, 128), F32),
    )
    return pl.pallas_call(
        functools.partial(back_kernel, blk // 2, seqs),
        out_shape=[jax.ShapeDtypeStruct(*outs[name]) for name in BACK_OUT],
        in_specs=[anywhere] * len(BACK_IN),
        out_specs=[anywhere] * len(BACK_OUT),
        scratch_shapes=[scratch[name] for name in BACK_SCRATCH],
        compiler_params=pltpu.CompilerParams(
            collective_id=3, has_side_effects=True, vmem_limit_bytes=60 * MIB),
        cost_estimate=pl.CostEstimate(flops=60 * 2**30, bytes_accessed=200 * MIB, transcendentals=0),
    )(*(args[name] for name in BACK_IN))


def rms(value):
    return lax.rsqrt(jnp.mean(value * value, axis=-1, keepdims=True) + EPS)


def forward(blk, seqs, xf, weights):
    w_query, w_key, w_value, w_gate, w_out, out_gain, w_first, w_second, w_third = weights
    normed = (xf * rms(xf)).astype(BF16)
    key = project(normed, w_key)
    value = project(normed, w_value)
    k, v = silu_parts(key)[0].astype(BF16), value.astype(BF16)
    prefix = entering(local_states(k, v, seqs), blk, False)
    query = project(normed, w_query)
    gate = project(normed, w_gate)
    q = silu_parts(query)[0].astype(BF16)
    attn = attention(q, k, v, prefix, seqs)
    mixed = (attn * rms(attn) * out_gain * silu_parts(gate)[0]).astype(BF16)
    resid = xf + project(mixed, w_out)
    normed2 = (resid * rms(resid)).astype(BF16)
    first = project(normed2, w_first)
    second = project(normed2, w_second)
    inner = (first * second).astype(BF16)
    return dict(
        normed=normed, query=query, key=key, gate=gate, q=q, k=k, v=v, prefix=prefix, attn=attn,
        mixed=mixed, resid=resid, normed2=normed2, first=first, second=second, inner=inner)


def backward_plain(blk, seqs, xf, grad_top, f, weights):
    w_query, w_key, w_value, w_gate, w_out, out_gain, w_first, w_second, w_third = weights
    output = (f["resid"] + project(f["inner"], w_third)).astype(BF16)
    grad_w3 = weight_grad(f["inner"], grad_top)
    grad_inner = back_project(grad_top, w_third)
    grad_one = (grad_inner * f["second"]).astype(BF16)
    grad_two = (grad_inner * f["first"]).astype(BF16)
    grad_w1 = weight_grad(f["normed2"], grad_one)
    grad_w2 = weight_grad(f["normed2"], grad_two)
    grad_normed2 = back_project(grad_one, w_first) + back_project(grad_two, w_second)
    resid, attn = f["resid"], f["attn"]
    grad_resid = grad_top.astype(F32) + norm_back(grad_normed2, resid, rms(resid))
    grad_resid_low = grad_resid.astype(BF16)
    grad_wo = weight_grad(f["mixed"], grad_resid_low)
    grad_mixed = back_project(grad_resid_low, w_out)
    gate_act, gate_der = silu_parts(f["gate"])
    rattn = rms(attn)
    unit_attn = attn * rattn
    grad_scaled = grad_mixed * gate_act
    grad_gate_low = (grad_mixed * (unit_attn * out_gain) * gate_der).astype(BF16)
    grad_gain = jnp.sum(grad_scaled * unit_attn, axis=0)
    grad_attn = norm_back(grad_scaled * out_gain, attn, rattn).astype(BF16)
    q, k, v, prefix = f["q"], f["k"], f["v"], f["prefix"]
    dstate = entering(local_states(q, grad_attn, seqs), blk, True)
    grad_fq, grad_fk, grad_vv = attention_back(q, k, v, grad_attn, prefix, dstate, seqs)
    grad_query_low = (grad_fq * silu_parts(f["query"])[1]).astype(BF16)
    grad_key_low = (grad_fk * silu_parts(f["key"])[1]).astype(BF16)
    grad_value_low = grad_vv.astype(BF16)
    normed = f["normed"]
    grads = [weight_grad(normed, g) for g in (grad_query_low, grad_key_low, grad_value_low, grad_gate_low)]
    grads += [grad_wo, grad_gain, grad_w1, grad_w2, grad_w3]
    grad_normed = back_project(grad_query_low, w_query) + back_project(grad_key_low, w_key)
    grad_normed = (
        grad_normed + back_project(grad_value_low, w_value) + back_project(grad_gate_low, w_gate)
    )
    grad_input = grad_resid + norm_back(grad_normed, xf, rms(xf))
    summed = [
        lax.psum(lax.psum_scatter(g, "blk", scatter_dimension=0, tiled=True), "batch") for g in grads]
    return output, grad_input, summed


WEIGHTS = (
    "w_query", "w_key", "w_value", "w_gate", "w_out", "gain", "w_first", "w_second", "w_third",
)


def backward(blk, seqs, tokens, grad_top, f, weights):
    names = WEIGHTS
    args = dict(zip(names, weights), tokens=tokens, dy=grad_top)
    args.update(f)
    output, grad_input, tall, wide, square, dgain = back(args, seqs, blk)
    so, sg, sq, sk, sv = (square[n] for n in range(5))
    sgain = lax.dynamic_index_in_dim(dgain, lax.axis_index("blk"), 0, False)
    return output, grad_input, [sq, sk, sv, sg, so, sgain, wide[0], wide[1], tall]


def body(sizes, tokens, cotangent, *weights):
    batch, blk = sizes
    seqs, span, width = tokens.shape
    rows = seqs * span
    low = tokens.reshape(rows, width)
    xf = low.astype(F32)
    grad_top = cotangent.reshape(rows, width)
    ff = weights[-1].shape[0]
    if (batch, blk, rows, span, width, ff % 256) == (4, 8, 1024, 128, 1024, 0):
        f = forward_fast(blk, seqs, low, weights)
        output, grad_input, grads = backward(blk, seqs, low, grad_top, f, weights)
    else:
        f = forward(blk, seqs, xf, weights)
        output, grad_input, grads = backward_plain(blk, seqs, xf, grad_top, f, weights)
    shape = (seqs, span, width)
    return (output.reshape(shape), grad_input.reshape(shape), *grads)


def solution(mesh):
    rows = P("batch", "blk", None)
    cut = P("blk", None)
    return jax.shard_map(
        functools.partial(body, (mesh.shape["batch"], mesh.shape["blk"])),
        mesh=mesh,
        in_specs=(rows, rows) + (P(),) * 9,
        out_specs=(rows, rows) + (cut,) * 5 + (P("blk"),) + (cut,) * 3,
        check_vma=False,
    )
```

```python
import functools

import jax
import jax.numpy as jnp
from jax import lax
from jax.experimental import pallas as pl
from jax.experimental.pallas import tpu as pltpu
from jax.sharding import PartitionSpec as P

HEAD = 64
EPS = 1e-06
MESH = pl.DeviceIdType.MESH
F32 = jnp.float32
BF16 = jnp.bfloat16
MIB = 2**20


def silu_parts(pre):
    sig = jax.nn.sigmoid(pre)
    return (pre * sig, sig * (1.0 + pre * (1.0 - sig)))


def norm_back(grad, value, scale):
    inner = jnp.mean(grad * value, axis=-1, keepdims=True)
    return scale * grad - value * (scale * scale * scale) * inner


def project(left, weight):
    return jnp.dot(left, weight, preferred_element_type=F32)


def weight_grad(left, right):
    return jnp.einsum("td,tf->df", left, right, preferred_element_type=F32)


def back_project(grad, weight):
    return jnp.einsum("tf,df->td", grad, weight, preferred_element_type=F32)


def dot(a, b, ca, cb):
    return lax.dot_general(a, b, (((ca,), (cb,)), ((), ())), preferred_element_type=F32)


def low_lanes(shape):
    return lax.broadcasted_iota(jnp.int32, shape, len(shape) - 1) < HEAD


def two_heads(x):
    low = low_lanes(x.shape)
    zero = jnp.zeros_like(x)
    return jnp.concatenate([jnp.where(low, x, zero), jnp.where(low, zero, x)], axis=0)


def pick_heads(x):
    half = x.shape[0] // 2
    return jnp.where(low_lanes((half, x.shape[1])), x[:half], x[half:])


def causal_pair(span):
    t = lax.broadcasted_iota(jnp.int32, (span, 2 * span), 0)
    u = lax.broadcasted_iota(jnp.int32, (span, 2 * span), 1)
    return t >= u % span


def pair_of(ref, p):
    return ref[:, pl.ds(p * 2 * HEAD, 2 * HEAD)]


def state_kernel(left_ref, right_ref, out_ref):
    for p in range(out_ref.shape[1]):
        out_ref[0, p] = pick_heads(dot(pair_of(left_ref, p), pair_of(right_ref, p), 0, 0))


def attn_kernel(q_ref, k_ref, v_ref, prefix_ref, out_ref):
    span = q_ref.shape[0]
    causal = causal_pair(span)
    for p in range(prefix_ref.shape[1]):
        q, k2, v2 = pair_of(q_ref, p), two_heads(pair_of(k_ref, p)), two_heads(pair_of(v_ref, p))
        scores = jnp.where(causal, dot(q, k2, 1, 1), 0.0).astype(BF16)
        prefix = two_heads(prefix_ref[0, p])
        out_ref[:, pl.ds(p * 2 * HEAD, 2 * HEAD)] = dot(scores, v2, 1, 0) + dot(q, prefix, 1, 0)


def attn_back_kernel(q_ref, k_ref, v_ref, g_ref, prefix_ref, dstate_ref, dq_ref, dk_ref, dv_ref):
    span = q_ref.shape[0]
    causal = causal_pair(span)
    for p in range(prefix_ref.shape[1]):
        q, k, v, g = (pair_of(r, p) for r in (q_ref, k_ref, v_ref, g_ref))
        k2, v2 = two_heads(k), two_heads(v)
        prefix, dstate = two_heads(prefix_ref[0, p]), two_heads(dstate_ref[0, p])
        scores = jnp.where(causal, dot(q, k2, 1, 1), 0.0).astype(BF16)
        dscores = jnp.where(causal, dot(g, v2, 1, 1), 0.0).astype(BF16)
        lanes = pl.ds(p * 2 * HEAD, 2 * HEAD)
        dq_ref[:, lanes] = dot(dscores, k2, 1, 0) + dot(g, prefix, 1, 1)
        dk_ref[:, lanes] = pick_heads(dot(dscores, q, 0, 0)) + dot(v, dstate, 1, 1)
        dv_ref[:, lanes] = pick_heads(dot(scores, g, 0, 0)) + dot(k, dstate, 1, 0)


def rows_spec(span, width):
    return pl.BlockSpec((span, width), lambda s: (s, 0))


def state_spec(pairs):
    return pl.BlockSpec((1, pairs, HEAD, 2 * HEAD), lambda s: (s, 0, 0, 0))


def local_states(left, right, seqs):
    rows, width = left.shape
    span, pairs = rows // seqs, width // (2 * HEAD)
    return pl.pallas_call(
        state_kernel,
        grid=(seqs,),
        in_specs=[rows_spec(span, width)] * 2,
        out_specs=state_spec(pairs),
        out_shape=jax.ShapeDtypeStruct((seqs, pairs, HEAD, 2 * HEAD), F32),
    )(left, right)


def attention(q, k, v, prefix, seqs):
    rows, width = q.shape
    span, pairs = rows // seqs, width // (2 * HEAD)
    return pl.pallas_call(
        attn_kernel,
        grid=(seqs,),
        in_specs=[rows_spec(span, width)] * 3 + [state_spec(pairs)],
        out_specs=rows_spec(span, width),
        out_shape=jax.ShapeDtypeStruct((rows, width), F32),
    )(q, k, v, prefix)


def attention_back(q, k, v, g, prefix, dstate, seqs):
    rows, width = q.shape
    span, pairs = rows // seqs, width // (2 * HEAD)
    return pl.pallas_call(
        attn_back_kernel,
        grid=(seqs,),
        in_specs=[rows_spec(span, width)] * 4 + [state_spec(pairs)] * 2,
        out_specs=[rows_spec(span, width)] * 3,
        out_shape=[jax.ShapeDtypeStruct((rows, width), F32)] * 3,
    )(q, k, v, g, prefix, dstate)


def scan_kernel(outer, reverse, s_ref, out_ref, held, summed, other, zs, zr, xs, xr):
    chunks = s_ref.shape[0]
    k = lax.axis_index("blk")
    z, x = k // 2, k % 2
    if reverse:
        zz, xx = outer - 1 - z, 1 - x
        after, before = jnp.maximum(z - 1, 0), jnp.minimum(z + 1, outer - 1)
    else:
        zz, xx = z, x
        after, before = jnp.minimum(z + 1, outer - 1), jnp.maximum(z - 1, 0)
    nxt, prv, side = {"blk": after * 2 + x}, {"blk": before * 2 + x}, {"blk": z * 2 + 1 - x}
    first, last = zz == 0, zz == outer - 1

    bar = pltpu.get_barrier_semaphore()
    pl.semaphore_signal(bar, inc=1, device_id=side, device_id_type=MESH)
    pl.when(~last)(lambda: pl.semaphore_signal(bar, inc=1, device_id=nxt, device_id_type=MESH))
    pl.when(~first)(lambda: pl.semaphore_signal(bar, inc=1, device_id=prv, device_id_type=MESH))
    pl.semaphore_wait(bar, 1 + jnp.where(last, 0, 1) + jnp.where(first, 0, 1))

    def along(i):
        return pltpu.make_async_remote_copy(
            src_ref=summed.at[i], dst_ref=held.at[i], send_sem=zs.at[i], recv_sem=zr.at[i],
            device_id=nxt, device_id_type=MESH)

    def across(i, src):
        return pltpu.make_async_remote_copy(
            src_ref=src.at[i], dst_ref=other.at[i], send_sem=xs.at[i], recv_sem=xr.at[i],
            device_id=side, device_id_type=MESH)

    def pass_on(i):
        pl.when(~first)(lambda: along(i).wait_recv())

        @pl.when(first)
        def _():
            held[i] = jnp.zeros_like(held[i])

        summed[i] = held[i] + s_ref[i]
        pl.when(~last)(lambda: along(i).start())
        pl.when(xx == 0)(lambda: across(i, summed).start())
        pl.when(xx == 1)(lambda: across(i, held).start())

    def finish(i):
        across(i, held).wait_recv()
        out_ref[i] = (held[i] + other[i]).astype(out_ref.dtype)

    def step(i, carry):
        pl.when(i < chunks)(lambda: pass_on(i))
        pl.when(i > 0)(lambda: finish(i - 1))
        return carry

    lax.fori_loop(0, chunks + 1, step, 0)

    def drain(i, carry):
        pl.when(~last)(lambda: along(i).wait_send())
        across(i, held).wait_send()
        return carry

    lax.fori_loop(0, chunks, drain, 0)


def entering(states, blk, reverse):
    seqs, pairs, head, lanes = states.shape
    per = max(1, pairs // 2)
    shape = (seqs * pairs // per, per, head, lanes)
    vmem = pl.BlockSpec(memory_space=pltpu.VMEM)
    sems = [pltpu.SemaphoreType.DMA((shape[0],))] * 4
    out = pl.pallas_call(
        functools.partial(scan_kernel, blk // 2, reverse),
        out_shape=jax.ShapeDtypeStruct(shape, BF16),
        in_specs=[vmem],
        out_specs=vmem,
        scratch_shapes=[pltpu.VMEM(shape, F32)] * 3 + sems,
        compiler_params=pltpu.CompilerParams(
            collective_id=2 if reverse else 1, has_side_effects=True, vmem_limit_bytes=24 * MIB),
    )(states.reshape(shape))
    return out.reshape(states.shape)


LAND, FIN, ACC = 4, 8, 10
CORE, XA, YA, YB, XB, XC, YC = range(7)
TILE = 256


class Named:
    def __init__(self, names, refs):
        self.__dict__.update(zip(names, refs))


class Stream:
    def __init__(self, block, buf, sem):
        self.block, self.buf, self.sem = block, buf, sem

    def copy(self, j):
        return pltpu.make_async_copy(self.block(j), self.buf.at[j % 2], self.sem.at[j % 2])

    def start(self, j):
        self.copy(j).start()

    def get(self, j, count):
        self.copy(j).wait()
        pl.when(j + 1 < count)(lambda: self.start(j + 1))
        return self.buf.at[j % 2]


BACK_IN = (
    "tokens", "dy", "innert", "inner", "first", "second", "resid", "gate", "attn", "q", "k", "v",
    "query", "key", "prefix", "normt", "norm2t", "mixedt", "gain", "w_query", "w_key", "w_value",
    "w_gate", "w_out", "w_first", "w_second", "w_third",
)
BACK_OUT = (
    "output", "dtokens", "tall", "wide", "square", "dgain",
)
BACK_SCRATCH = (
    "tbuf", "core_rx", "acc", "xa", "ya", "yb", "xb", "xc", "yc", "zab", "zc", "fin", "ssem",
    "rsem", "zss", "zrs", "osem", "csem", "crem", "ygs", "ygr", "dyv", "dfs", "dn2", "dlow",
    "dgate", "dattn", "at0", "at1", "held", "sums", "other", "dstate", "sz", "rz", "sx", "rx",
    "gacc", "gbuf", "gland", "gs", "gr", "lsem",
)


FWD_IN = (
    "tokens", "gain", "w_query", "w_key", "w_value", "w_gate", "w_out", "w_first", "w_second",
)
FWD_OUT = (
    "k", "v", "key", "normt", "q", "gate", "query", "attn", "mixedt", "resid", "norm2t", "first",
    "second", "inner", "innert", "prefix",
)
FWD_SCRATCH = (
    "xv", "gv", "wq", "wk", "wv", "wg", "wo", "w1", "w2", "nrm", "kb", "vb", "qb", "gb", "intra",
    "keyb", "queryb", "attnb", "mixb", "residb", "n2b", "firstb", "secondb", "innerb", "tb0", "tb1",
    "tb2", "innertb", "held", "sums", "other", "pre", "sz", "rz", "sx", "rx", "lsem", "xsem", "osem",
)


def forward_kernel(outer, seqs, *refs):
    r = Named(FWD_IN + FWD_OUT + FWD_SCRATCH, refs)
    rows, width = r.tokens.shape
    ff = r.w_first.shape[1]
    span, pairs = rows // seqs, width // (2 * HEAD)
    blocks, per_block = rows // TILE, TILE // span
    n_scan, cut = r.sums.shape[:2]
    per_seq = pairs // cut

    k = lax.axis_index("blk")
    z, x = k // 2, k % 2
    top = outer - 1
    side = {"blk": z * 2 + 1 - x}
    above, below = {"blk": jnp.minimum(z + 1, top) * 2 + x}, {"blk": jnp.maximum(z - 1, 0) * 2 + x}
    bar = pltpu.get_barrier_semaphore()
    pl.semaphore_signal(bar, inc=1, device_id=side, device_id_type=MESH)
    pl.when(z < top)(lambda: pl.semaphore_signal(bar, inc=1, device_id=above, device_id_type=MESH))
    pl.when(z > 0)(lambda: pl.semaphore_signal(bar, inc=1, device_id=below, device_id_type=MESH))

    def span_of(start, size, step):
        return pl.ds(start if isinstance(start, int) else pl.multiple_of(start, step), size)

    def tok(j, n=TILE):
        return span_of(j * n, n, n)

    loads = [
        pltpu.make_async_copy(src, dst, r.lsem.at[n])
        for n, (src, dst) in enumerate((
            (r.w_key, r.wk), (r.w_value, r.wv), (r.w_query, r.wq), (r.w_gate, r.wg), (r.gain, r.gv),
            (r.w_out, r.wo), (r.w_first, r.w1), (r.w_second, r.w2)))
    ]

    def x_load(j):
        return pltpu.make_async_copy(r.tokens.at[tok(j)], r.xv.at[tok(j)], r.xsem.at[j])

    by_rows = dict(
        k=lambda j: r.kb.at[tok(j)], v=lambda j: r.vb.at[tok(j)], q=lambda j: r.qb.at[tok(j)],
        gate=lambda j: r.gb.at[tok(j)], key=lambda j: r.keyb, query=lambda j: r.queryb,
        attn=lambda j: r.attnb, resid=lambda j: r.residb, first=lambda j: r.firstb,
        second=lambda j: r.secondb, inner=lambda j: r.innerb)
    by_cols = dict(normt=r.tb0, mixedt=r.tb1, norm2t=r.tb2, innert=r.innertb)

    def store(name, j):
        sem = r.osem.at[FWD_OUT.index(name)]
        out = getattr(r, name)
        if name in by_rows:
            return pltpu.make_async_copy(by_rows[name](j), out.at[tok(j)], sem)
        return pltpu.make_async_copy(by_cols[name], out.at[:, tok(j)], sem)

    def free(name, j):
        pl.when(j > 0)(lambda: store(name, j - 1).wait())

    def remote(src, dst, s, t, dev):
        return pltpu.make_async_remote_copy(
            src_ref=src, dst_ref=dst, send_sem=s, recv_sem=t, device_id=dev, device_id_type=MESH)

    def along(i):
        return remote(r.sums.at[i], r.held.at[i], r.sz.at[i], r.rz.at[i], above)

    def across(i, src):
        return remote(src.at[i], r.other.at[i], r.sx.at[i], r.rx.at[i], side)

    def pass_on(i):
        pl.when(z > 0)(lambda: along(i).wait_recv())

        @pl.when(z == 0)
        def _():
            r.held[i] = jnp.zeros_like(r.held[i])

        r.sums[i] = r.held[i] + r.sums[i]
        pl.when(z < top)(lambda: along(i).start())
        pl.when(x == 0)(lambda: across(i, r.sums).start())
        pl.when(x == 1)(lambda: across(i, r.held).start())

    def finish(i):
        across(i, r.held).wait_recv()
        r.pre[i] = (r.held[i] + r.other[i]).astype(BF16)
        pl.when(z < top)(lambda: along(i).wait_send())
        across(i, r.held).wait_send()

    LAG = 2

    def scan(n):
        i = n - LAG * z
        pl.when((i >= 0) & (i < n_scan))(lambda: pass_on(i))
        pl.when((i >= LAG) & (i < n_scan + LAG))(lambda: finish(i - LAG))

    def transposed(src, dst):
        for n in range(dst.shape[0] // 128):
            cols = pl.ds(n * 128, 128)
            dst[cols, :] = src[:, cols].T

    def norm_rows(value):
        return (value * lax.rsqrt(jnp.mean(value * value, axis=-1, keepdims=True) + EPS)).astype(BF16)

    def each(count, one):
        for m in range(count):
            one(m)

    def rows_of(j, m):
        return span_of(j * TILE + m * 32, 32, 32)

    def col(n):
        return span_of(n * 256, 256, 256)

    def tile_keys(j):
        x_load(j).wait()

        @pl.when(j == 0)
        def _():
            loads[0].wait()
            loads[1].wait()

        for name in ("key", "k", "v", "normt"):
            free(name, j)

        def one(m):
            r.nrm[rows_of(j, m), :] = norm_rows(r.xv[rows_of(j, m), :].astype(F32))

        each(TILE // 32, one)

        def product(n):
            key = dot(r.nrm[tok(j), :], r.wk[:, col(n)], 1, 0)
            r.keyb[:, col(n)] = key.astype(BF16)
            r.kb[tok(j), col(n)] = silu_parts(key)[0].astype(BF16)
            r.vb[tok(j), col(n)] = dot(r.nrm[tok(j), :], r.wv[:, col(n)], 1, 0).astype(BF16)

        each(width // 256, product)

        def states(m):
            s = j * per_block + m
            for p in range(pairs):
                lanes = pl.ds(p * 2 * HEAD, 2 * HEAD)
                here = tok(s, span)
                r.sums[s * per_seq + p // cut, p % cut] = pick_heads(dot(r.kb[here, lanes], r.vb[here, lanes], 0, 0))

        each(per_block, states)
        transposed(r.nrm.at[tok(j)], r.tb0)
        for name in ("key", "k", "v", "normt"):
            store(name, j).start()

    def tile_query(j):
        @pl.when(j == 0)
        def _():
            loads[2].wait()
            loads[3].wait()

        for name in ("query", "q", "gate"):
            free(name, j)

        def product(n):
            query = dot(r.nrm[tok(j), :], r.wq[:, col(n)], 1, 0)
            r.queryb[:, col(n)] = query.astype(BF16)
            r.qb[tok(j), col(n)] = silu_parts(query)[0].astype(BF16)
            r.gb[tok(j), col(n)] = dot(r.nrm[tok(j), :], r.wg[:, col(n)], 1, 0).astype(BF16)

        each(width // 256, product)
        for name in ("query", "q", "gate"):
            store(name, j).start()

    def tile_scores(s):
        causal = causal_pair(span)
        here = tok(s, span)
        for p in range(pairs):
            lanes = pl.ds(p * 2 * HEAD, 2 * HEAD)
            q, k2, v2 = r.qb[here, lanes], two_heads(r.kb[here, lanes]), two_heads(r.vb[here, lanes])
            scores = jnp.where(causal, dot(q, k2, 1, 1), 0.0).astype(BF16)
            r.intra[here, lanes] = dot(scores, v2, 1, 0)

    def tile_mixed(j):
        pl.when(j == 0)(lambda: loads[4].wait())
        for name in ("attn", "mixedt"):
            free(name, j)

        def inter(m):
            s = j * per_block + m
            here = tok(s, span)
            for p in range(pairs):
                lanes = pl.ds(p * 2 * HEAD, 2 * HEAD)
                prefix = two_heads(r.pre[s * per_seq + p // cut, p % cut])
                r.intra[here, lanes] = r.intra[here, lanes] + dot(r.qb[here, lanes], prefix, 1, 0)

        each(per_block, inter)

        def one(m):
            av = r.intra[rows_of(j, m), :]
            scale = lax.rsqrt(jnp.mean(av * av, axis=-1, keepdims=True) + EPS)
            act = silu_parts(r.gb[rows_of(j, m), :].astype(F32))[0]
            r.attnb[tok(m, 32), :] = av.astype(BF16)
            r.mixb[tok(m, 32), :] = (av * scale * r.gv[...] * act).astype(BF16)

        each(TILE // 32, one)
        transposed(r.mixb, r.tb1)
        for name in ("attn", "mixedt"):
            store(name, j).start()

    def tile_resid(j):
        pl.when(j == 0)(lambda: loads[5].wait())
        for name in ("resid", "norm2t"):
            free(name, j)

        def product(n):
            r.residb[:, col(n)] = r.xv[tok(j), col(n)].astype(F32) + dot(r.mixb[...], r.wo[:, col(n)], 1, 0)

        each(width // 256, product)

        def one(m):
            r.n2b[tok(m, 32), :] = norm_rows(r.residb[tok(m, 32), :])

        each(TILE // 32, one)
        transposed(r.n2b, r.tb2)
        for name in ("resid", "norm2t"):
            store(name, j).start()

    def tile_inner(j, lo, hi):
        def one(n):
            n = n + lo
            first = dot(r.n2b[...], r.w1[:, col(n)], 1, 0)
            second = dot(r.n2b[...], r.w2[:, col(n)], 1, 0)
            inner = (first * second).astype(BF16)
            r.firstb[:, col(n)] = first.astype(BF16)
            r.secondb[:, col(n)] = second.astype(BF16)
            r.innerb[:, col(n)] = inner
            r.innertb[col(n), :] = inner.T

        each(hi - lo, one)

    def tile_up(j):
        @pl.when(j == 0)
        def _():
            loads[6].wait()
            loads[7].wait()

        for name in ("first", "second", "inner", "innert"):
            free(name, j)
        tile_inner(j, 0, ff // 512)

    def tile_up2(j):
        tile_inner(j, ff // 512, ff // 256)
        for name in ("first", "second", "inner", "innert"):
            store(name, j).start()

    for n in range(2):
        x_load(n).start()
        loads[n].start()
    for n in range(2, blocks):
        x_load(n).start()
    for copy in loads[2:]:
        copy.start()
    pl.semaphore_wait(bar, 1 + jnp.where(z < top, 1, 0) + jnp.where(z > 0, 1, 0))

    per = n_scan // blocks
    late = (tile_mixed, tile_resid, tile_up, tile_up2)
    n_query = 1 + per_block

    def slot(n, carry):
        pl.when(n < blocks)(lambda: tile_keys(n))
        q = n - blocks

        @pl.when((q >= 0) & (q < blocks * n_query))
        def _():
            j, m = q // n_query, q % n_query
            pl.when(m == 0)(lambda: tile_query(j))
            pl.when(m > 0)(lambda: tile_scores(j * per_block + m - 1))

        scan(n)
        w = n - LAG * z - LAG - per + 1
        j, m = w // per, w % per
        for step, tile in enumerate(late):
            pl.when((w >= 0) & (j < blocks) & (m == step))(functools.partial(tile, j))
        return carry

    lax.fori_loop(0, n_scan + LAG * (top + 1) + len(late), slot, 0)
    whole = pltpu.make_async_copy(r.pre, r.prefix, r.osem.at[FWD_OUT.index("prefix")])
    whole.start()
    for name in FWD_OUT[:-1]:
        store(name, blocks - 1).wait()
    whole.wait()


def forward_fast(blk, seqs, tokens, weights):
    w_query, w_key, w_value, w_gate, w_out, out_gain, w_first, w_second, w_third = weights
    rows, width = tokens.shape
    ff = w_first.shape[1]
    pairs = width // (2 * HEAD)
    cut = 2
    n_scan = seqs * pairs // cut

    def v(*shape, dtype=BF16):
        return pltpu.VMEM(shape, dtype)

    def sem(*shape):
        return pltpu.SemaphoreType.DMA(shape)

    wide, tall = (rows, width), (width, ff)
    chunks = (n_scan, cut, HEAD, 2 * HEAD)
    scratch = dict(
        xv=v(*wide), gv=v(1, width, dtype=F32), wq=v(width, width), wk=v(width, width), wv=v(width, width),
        wg=v(width, width), wo=v(width, width), w1=v(*tall), w2=v(*tall), nrm=v(*wide), kb=v(*wide),
        vb=v(*wide), qb=v(*wide), gb=v(*wide), intra=v(*wide, dtype=F32), keyb=v(TILE, width),
        queryb=v(TILE, width), attnb=v(TILE, width), mixb=v(TILE, width), residb=v(TILE, width, dtype=F32),
        n2b=v(TILE, width), firstb=v(TILE, ff), secondb=v(TILE, ff), innerb=v(TILE, ff),
        tb0=v(width, TILE), tb1=v(width, TILE), tb2=v(width, TILE), innertb=v(ff, TILE),
        held=v(*chunks, dtype=F32), sums=v(*chunks, dtype=F32), other=v(*chunks, dtype=F32), pre=v(*chunks),
        sz=sem(n_scan), rz=sem(n_scan), sx=sem(n_scan), rx=sem(n_scan), lsem=sem(8),
        xsem=sem(rows // TILE), osem=sem(len(FWD_OUT)),
    )
    shapes = dict(
        normt=(width, rows), mixedt=(width, rows), norm2t=(width, rows), first=(rows, ff), second=(rows, ff),
        inner=(rows, ff), innert=(ff, rows), prefix=chunks)
    anywhere = pl.BlockSpec(memory_space=pl.ANY)
    outs = pl.pallas_call(
        functools.partial(forward_kernel, blk // 2, seqs),
        out_shape=[
            jax.ShapeDtypeStruct(shapes.get(name, wide), F32 if name == "resid" else BF16)
            for name in FWD_OUT
        ],
        in_specs=[anywhere] * len(FWD_IN),
        out_specs=[anywhere] * len(FWD_OUT),
        scratch_shapes=[scratch[name] for name in FWD_SCRATCH],
        compiler_params=pltpu.CompilerParams(
            collective_id=4, has_side_effects=True, vmem_limit_bytes=60 * MIB),
        cost_estimate=pl.CostEstimate(flops=26 * 2**30, bytes_accessed=80 * MIB, transcendentals=0),
    )(tokens, out_gain.reshape(1, width), w_query, w_key, w_value, w_gate, w_out, w_first, w_second)
    f = dict(zip(FWD_OUT, outs))
    f["prefix"] = f["prefix"].reshape(seqs, pairs, HEAD, 2 * HEAD)
    return f


def back_kernel(outer, seqs, *refs):
    r = Named(BACK_IN + BACK_OUT + BACK_SCRATCH, refs)
    rows, width = r.tokens.shape
    ff = r.first.shape[1]
    span, pairs = rows // seqs, width // (2 * HEAD)
    n_tall, n_wide, n_square = ff // 256, ff // 128, 20
    chunks = n_tall + n_wide + n_square
    at_wide, at_square = n_tall, n_tall + n_wide
    blocks = rows // TILE

    b, k = lax.axis_index("batch"), lax.axis_index("blk")
    y, c = b // 2, b % 2
    z, x = k // 2, k % 2
    ox, oy = 1 - x, 1 - y
    top = outer - 1
    zr = top - z
    to_core, to_y, to_x = {"batch": y * 2 + 1 - c}, {"batch": oy * 2 + c}, {"blk": z * 2 + ox}
    to_up = {"blk": jnp.minimum(z + 1, top) * 2 + x}
    to_down = {"blk": jnp.maximum(z - 1, 0) * 2 + x}
    to_z = [{"blk": (z + d) % outer * 2 + x} for d in range(1, outer)]

    peers = [to_core, to_y, to_x] + to_z
    bar = pltpu.get_barrier_semaphore()
    for d in peers:
        pl.semaphore_signal(bar, inc=1, device_id=d, device_id_type=MESH)
    pl.semaphore_wait(bar, len(peers))

    def remote(src, dst, s, t, dev):
        return pltpu.make_async_remote_copy(
            src_ref=src, dst_ref=dst, send_sem=s, recv_sem=t, device_id=dev, device_id_type=MESH)

    def link(kind, i, src, dst, dev):
        return remote(src, dst.at[i % LAND], r.ssem.at[kind, i % LAND], r.rsem.at[kind, i % LAND], dev)

    def at(i, *where):
        return r.acc.at[(i % ACC,) + where]

    A, B, C = pl.ds(0, 32), pl.ds(32, 16), pl.ds(48, 16)
    every = slice(None)

    def core_copy(i):
        return link(CORE, i, r.tbuf.at[i % 2], r.core_rx, to_core)

    def xa_copy(i):
        return link(XA, i, at(i, every, ox, every, A), r.xa, to_x)

    def ya_copy(i):
        return link(YA, i, at(i, every, x, oy, A), r.ya, to_y)

    def yb_copy(i):
        return link(YB, i, at(i, every, every, oy, B), r.yb, to_y)

    def xb_copy(i):
        return link(XB, i, at(i, every, ox, y, B), r.xb, to_x)

    def xc_copy(i):
        return link(XC, i, at(i, z, ox, every, C), r.xc, to_x)

    def yc_copy(i):
        return link(YC, i, at(i, z, x, oy, C), r.yc, to_y)

    def y_share(i):
        f = i % FIN
        return remote(r.fin.at[f, y], r.fin.at[f, y], r.ygs.at[f], r.ygr.at[f], to_y)

    def part_ab(i, s):
        return at(i, s, x, y, pl.ds(0, 48))

    def part_c(i, s):
        return at(i, s, every, every, C)

    AB, CC = (0, part_ab, r.zab), (1, part_c, r.zc)

    def hop(group, i, n, up, s):
        g, part, land = group
        d = 0 if up else 1
        sem = (g, d, n - 1, i % LAND)
        return remote(part(i, s), land.at[i % LAND, d, n - 1], r.zss.at[sem], r.zrs.at[sem],
                      to_up if up else to_down)

    def z_each(group, i, n, act):
        up = hop(group, i, n, True, jnp.minimum(outer - n + z, top))
        down = hop(group, i, n, False, jnp.maximum(n - 1 - zr, 0))
        pl.when((z <= n - 1) & (z < top))(lambda: act(up))
        pl.when((zr <= n - 1) & (z > 0))(lambda: act(down))

    def z_send(group, i, n):
        z_each(group, i, n, lambda copy: copy.start())

    def z_sent(group, i, n):
        z_each(group, i, n, lambda copy: copy.wait_send())

    def add(ref, landed):
        ref[...] = ref[...] + landed

    def z_take(group, i, n):
        g, part, land = group

        def take(up, s):
            hop(group, i, n, up, s).wait_recv()
            add(part(i, s), land[i % LAND, 0 if up else 1, n - 1])

        pl.when((z > 0) & (z <= n))(lambda: take(True, jnp.clip(outer - n + z - 1, 0, top)))
        pl.when((z < top) & (zr <= n))(lambda: take(False, jnp.clip(n - zr, 0, top)))

    def places(i, act):
        f = r.fin.at[i % FIN]

        @pl.when(i < at_wide)
        def _():
            for yy in range(2):
                for blk in range(2):
                    col = pl.multiple_of(c * (width // 2) + (yy * 2 + blk) * 128, 128)
                    act(f.at[yy, pl.ds(blk * 32, 32)], r.tall.at[pl.ds(i * 32, 32), pl.ds(col, 128)])

        @pl.when((i >= at_wide) & (i < at_square))
        def _():
            j, h = (i - at_wide) // 2, (i - at_wide) % 2
            col = pl.multiple_of(c * (ff // 2) + j * 128, 128)
            for yy in range(2):
                act(f.at[yy], r.wide.at[yy, pl.ds(h * 64, 64), pl.ds(col, 128)])

        @pl.when(i >= at_square)
        def _():
            j = i - at_square
            m, u, h = j // 4, j // 2 % 2, j % 2
            for yy in range(2):
                col = pl.multiple_of(c * (width // 2) + u * 256 + yy * 128, 128)
                act(f.at[yy], r.square.at[m, pl.ds(h * 64, 64), pl.ds(col, 128)])

    def cores(i):
        core_copy(i).wait_recv()
        core_copy(i).wait_send()
        add(at(i), r.core_rx[i % LAND])
        xa_copy(i).start()
        yb_copy(i).start()
        z_send(CC, i, 1)

    def second(i):
        yb_copy(i).wait_recv()
        add(at(i, every, every, y, B), r.yb[i % LAND])
        xb_copy(i).start()
        xa_copy(i).wait_recv()
        add(at(i, every, x, every, A), r.xa[i % LAND])
        ya_copy(i).start()
        z_take(CC, i, 1)
        z_send(CC, i, 2)
        xa_copy(i).wait_send()
        yb_copy(i).wait_send()
        z_sent(CC, i, 1)

    def third(i):
        xb_copy(i).wait_recv()
        add(at(i, every, x, y, B), r.xb[i % LAND])
        ya_copy(i).wait_recv()
        add(at(i, every, x, y, A), r.ya[i % LAND])
        z_send(AB, i, 1)
        z_take(CC, i, 2)
        z_send(CC, i, 3)
        xb_copy(i).wait_send()
        ya_copy(i).wait_send()
        z_sent(CC, i, 2)

    def fourth(i):
        z_take(AB, i, 1)
        z_send(AB, i, 2)
        z_take(CC, i, 3)
        xc_copy(i).start()
        z_sent(AB, i, 1)
        z_sent(CC, i, 3)

    def fifth(i):
        z_take(AB, i, 2)
        z_send(AB, i, 3)
        xc_copy(i).wait_recv()
        add(at(i, z, x, every, C), r.xc[i % LAND])
        yc_copy(i).start()
        z_sent(AB, i, 2)
        xc_copy(i).wait_send()

    def sixth(i):
        yc_copy(i).wait_recv()
        z_take(AB, i, 3)
        f = i % FIN
        r.fin[f, y, pl.ds(0, 48)] = r.acc[i % ACC, z, x, y, pl.ds(0, 48)]
        r.fin[f, y, C] = r.acc[i % ACC, z, x, y, C] + r.yc[i % LAND]
        y_share(i).start()
        z_sent(AB, i, 3)
        yc_copy(i).wait_send()

    def seventh(i):
        y_share(i).wait_recv()
        y_share(i).wait_send()
        f = i % FIN

        def go(src, dst):
            remote(src, dst, r.csem.at[f], r.crem.at[f], to_core).start()
            pltpu.make_async_copy(src, dst, r.osem.at[f]).start()

        places(i, go)

    def last(i):
        f = i % FIN
        whole = r.fin.at[f]
        copy = remote(whole, whole, r.csem.at[f], r.crem.at[f], to_core)
        copy.wait_send()
        copy.wait_recv()
        pltpu.make_async_copy(whole, whole, r.osem.at[f]).wait()

    stages = (None, cores, second, third, fourth, fifth, sixth, seventh, last)

    def move(t):
        for n, stage in enumerate(stages):
            if stage is not None:
                i = t - n
                pl.when((i >= 0) & (i < chunks))(functools.partial(stage, i))

    def make(t, fill):
        fill(1 - c, r.tbuf.at[t % 2])
        core_copy(t).start()
        fill(c, r.acc.at[t % ACC])

    def fill_tall(lhs):
        def fill(half, dst):
            for yy in range(2):
                col = pl.multiple_of(half * (width // 2) + yy * 256, 256)
                res = dot(lhs, r.dyv[:, pl.ds(col, 256)], 1, 0).reshape(4, 2, 32, 256)
                for blk in range(2):
                    dst[:, :, yy, pl.ds(blk * 32, 32), :] = res[..., blk * 128:(blk + 1) * 128]
        return fill

    def left_rows(ref, h):
        return ref[:, h].reshape(8 * 64, rows)

    def fill_two(left, h, take):
        def fill(half, dst):
            res = dot(left_rows(left, h), take(half), 1, 0).reshape(4, 2, 64, 256)
            dst[:, :, 0] = res[..., :128]
            dst[:, :, 1] = res[..., 128:]
        return fill

    def make_wide(t):
        i = t - at_wide
        j, h = i // 2, i % 2

        def take(half):
            col = pl.ds(pl.multiple_of(half * (ff // 2) + j * 128, 128), 128)
            return jnp.concatenate([r.dfs[0, :, col], r.dfs[1, :, col]], axis=1)

        make(t, fill_two(r.at0, h, take))

    def make_square(t, base, left, right):
        i = t - base
        u, h = i // 2, i % 2

        def take(half):
            return right(pl.ds(pl.multiple_of(half * (width // 2) + u * 256, 256), 256))

        make(t, fill_two(left, h, take))

    zz, xx = zr, ox
    n_scan = r.sums.shape[0]
    halves = n_scan // seqs
    scan_at = at_wide + 1

    def along(i):
        return remote(r.sums.at[i], r.held.at[i], r.sz.at[i], r.rz.at[i], to_down)

    def across(i, src):
        return remote(src.at[i], r.other.at[i], r.sx.at[i], r.rx.at[i], to_x)

    def pass_on(i):
        pl.when(zz > 0)(lambda: along(i).wait_recv())

        @pl.when(zz == 0)
        def _():
            r.held[i] = jnp.zeros_like(r.held[i])

        r.sums[i] = r.held[i] + r.sums[i]
        pl.when(zz < top)(lambda: along(i).start())
        pl.when(xx == 0)(lambda: across(i, r.sums).start())
        pl.when(xx == 1)(lambda: across(i, r.held).start())

    def finish(i):
        across(i, r.held).wait_recv()
        r.dstate[i] = (r.held[i] + r.other[i]).astype(BF16)
        pl.when(zz < top)(lambda: along(i).wait_send())
        across(i, r.held).wait_send()

    def scan(t):
        i = t - scan_at - zz
        pl.when((i >= 0) & (i < n_scan))(lambda: pass_on(i))
        pl.when((i >= 2) & (i < n_scan + 2))(lambda: finish(i - 2))

    def span_of(start, size, step):
        return pl.ds(start if isinstance(start, int) else pl.multiple_of(start, step), size)

    def tok(j, n=TILE):
        return span_of(j * n, n, n)

    def tile_inner(j, w3, w1, w2, first, second):
        def block(m, carry):
            at_rows = tok(m, 512)
            din = dot(r.dyv[at_rows, :], w3[...], 1, 1)
            one = (din * second[at_rows, :].astype(F32)).astype(BF16)
            two = (din * first[at_rows, :].astype(F32)).astype(BF16)
            cols = pl.ds(pl.multiple_of(j * 256, 256), 256)
            r.dfs[0, at_rows, cols] = one
            r.dfs[1, at_rows, cols] = two
            for n in range(width // 256):
                to = pl.ds(n * 256, 256)
                res = dot(one, w1[to, :], 1, 1) + dot(two, w2[to, :], 1, 1)
                r.dn2[at_rows, to] = r.dn2[at_rows, to] + res
            return carry

        for m in range(rows // 512):
            block(m, 0)

    def tile_resid(j, resid, gate, attn, q, w_out, gain, dmix):
        def one(m, carry):
            here, sub = pl.ds(pl.multiple_of(j * TILE + m * 32, 32), 32), tok(m, 32)
            value = resid[sub, :]
            grad = r.dn2[here, :]
            scale = lax.rsqrt(jnp.mean(value * value, axis=-1, keepdims=True) + EPS)
            out = r.dyv[here, :].astype(F32) + norm_back(grad, value, scale)
            r.dn2[here, :] = out
            r.dlow[here, :] = out.astype(BF16)
            return carry

        for m in range(TILE // 32):
            one(m, 0)
        for n in range(width // 256):
            to = pl.ds(n * 256, 256)
            dmix[:, to] = dot(r.dlow[tok(j), :], w_out[to, :], 1, 1)

        def two(m, carry):
            here, sub = pl.ds(pl.multiple_of(j * TILE + m * 32, 32), 32), tok(m, 32)
            av = attn[sub, :].astype(F32)
            scale = lax.rsqrt(jnp.mean(av * av, axis=-1, keepdims=True) + EPS)
            unit = av * scale
            act, der = silu_parts(gate[sub, :].astype(F32))
            dm = dmix[sub, :]
            ds = dm * act
            r.dgate[here, :] = (dm * (unit * gain[...]) * der).astype(BF16)
            r.gacc[...] = r.gacc[...] + jnp.sum((ds * unit).reshape(4, 8, width), axis=0)
            r.dattn[here, :] = norm_back(ds * gain[...], av, scale).astype(BF16)
            return carry

        for m in range(TILE // 32):
            two(m, 0)

        def states(m, carry):
            s = j * (TILE // span) + m
            for p in range(pairs):
                lanes = pl.ds(p * 2 * HEAD, 2 * HEAD)
                grad = r.dattn[tok(s, span), lanes]
                per = pairs // halves
                r.sums[s * halves + p // per, p % per] = pick_heads(dot(q[tok(m, span), lanes], grad, 0, 0))
            return carry

        for m in range(TILE // span):
            states(m, 0)

    def tile_attn(s, q_ref, k_ref, v_ref, query, key, prefix_ref):
        causal = causal_pair(span)
        here = tok(s, span)
        for p in range(pairs):
            lanes = pl.ds(p * 2 * HEAD, 2 * HEAD)
            q, k, v, g = q_ref[:, lanes], k_ref[:, lanes], v_ref[:, lanes], r.dattn[here, lanes]
            k2, v2 = two_heads(k), two_heads(v)
            per = pairs // halves
            prefix, dstate = two_heads(prefix_ref[p]), two_heads(r.dstate[s * halves + p // per, p % per])
            scores = jnp.where(causal, dot(q, k2, 1, 1), 0.0).astype(BF16)
            dscores = jnp.where(causal, dot(g, v2, 1, 1), 0.0).astype(BF16)
            dq = dot(dscores, k2, 1, 0) + dot(g, prefix, 1, 1)
            dk = pick_heads(dot(dscores, q, 0, 0)) + dot(v, dstate, 1, 1)
            dv = pick_heads(dot(scores, g, 0, 0)) + dot(k, dstate, 1, 0)
            r.dfs[0, here, lanes] = (dq * silu_parts(query[:, lanes].astype(F32))[1]).astype(BF16)
            r.dfs[0, here, pl.ds(width + p * 2 * HEAD, 2 * HEAD)] = (
                dk * silu_parts(key[:, lanes].astype(F32))[1]).astype(BF16)
            r.dfs[1, here, lanes] = dv.astype(BF16)

    parts = [
        lambda at_rows, cols: r.dfs[0, at_rows, cols],
        lambda at_rows, cols: r.dfs[0, at_rows, pl.ds(width + cols.start, cols.size)],
        lambda at_rows, cols: r.dfs[1, at_rows, cols],
    ]
    dq_cols = lambda cols: r.dfs[0, :, cols]
    dk_cols = lambda cols: r.dfs[0, :, pl.ds(width + cols.start, cols.size)]
    dv_cols = lambda cols: r.dfs[1, :, cols]

    def load(src, dst, n):
        return pltpu.make_async_copy(src, dst, r.lsem.at[n])

    def dma(*shape):
        return pltpu.SemaphoreType.DMA(shape)

    def ring(shape, dtype):
        return pltpu.VMEM((2,) + shape, dtype)

    def steps(count, one):
        def go(j, carry):
            one(j)
            return carry

        lax.fori_loop(0, count, go, 0)

    dy_load = load(r.dy, r.dyv, 0)
    norm2_load = load(r.norm2t, r.at0, 1)
    mixed_load = load(r.mixedt, r.at1, 2)
    norm_load = load(r.normt, r.at0, 3)

    def segment0(left, w3, w1, w2, first, second, sems):
        cols = lambda ref: lambda j: ref.at[:, pl.ds(pl.multiple_of(j * 256, 256), 256)]
        s_left = Stream(lambda j: r.innert.at[:, pl.ds(pl.multiple_of(j * 32, 32), 32)], left, sems.at[0])
        tiles = [
            Stream(lambda j: r.w_third.at[pl.ds(pl.multiple_of(j * 256, 256), 256)], w3, sems.at[1]),
            Stream(cols(r.w_first), w1, sems.at[2]),
            Stream(cols(r.w_second), w2, sems.at[3]),
            Stream(cols(r.first), first, sems.at[4]),
            Stream(cols(r.second), second, sems.at[5]),
        ]
        dy_load.start()
        s_left.start(0)
        for s in tiles:
            s.start(0)
        norm2_load.start()
        r.dn2[...] = jnp.zeros_like(r.dn2)
        r.gacc[...] = jnp.zeros_like(r.gacc)
        dy_load.wait()

        def one(j):
            move(j)
            make(j, fill_tall(s_left.get(j, n_tall)[...].reshape(8 * 32, rows)))
            tile_inner(j, *(s.get(j, n_tall) for s in tiles))

        steps(n_tall, one)
        norm2_load.wait()

    pl.run_scoped(
        segment0, ring((8, 32, rows), BF16), ring((256, width), BF16), ring((width, 256), BF16),
        ring((width, 256), BF16), ring((rows, 256), BF16), ring((rows, 256), BF16), dma(6, 2))

    def segment1(resid, gate, attn, q, w_out, gain, dmix, sems, wsem):
        blk = lambda ref: lambda j: ref.at[tok(j)]
        tiles = [
            Stream(blk(ref), buf, sems.at[n])
            for n, (ref, buf) in enumerate(((r.resid, resid), (r.gate, gate), (r.attn, attn), (r.q, q)))
        ]
        w_load = pltpu.make_async_copy(r.w_out, w_out, wsem.at[0])
        g_load = pltpu.make_async_copy(r.gain, gain, wsem.at[1])
        w_load.start()
        g_load.start()
        for s in tiles:
            s.start(0)
        w_load.wait()
        g_load.wait()

        def one(j):
            t = at_wide + j
            move(t)
            scan(t)
            make_wide(t)
            rs, ga, at_, qs = (s.get(j, blocks) for s in tiles)
            tile_resid(j, rs, ga, at_, qs, w_out, gain, dmix)

        steps(blocks, one)

    pl.run_scoped(
        segment1, ring((TILE, width), F32), ring((TILE, width), BF16), ring((TILE, width), BF16),
        ring((TILE, width), BF16), pltpu.VMEM((width, width), BF16), pltpu.VMEM((1, width), F32),
        pltpu.VMEM((TILE, width), F32), dma(4, 2), dma(2))

    def gain_sum(t):
        base = at_wide + blocks
        hops = [to_core, to_y, to_x]

        def swap(n):
            return remote(r.gbuf, r.gland.at[n], r.gs.at[n], r.gr.at[n], hops[n])

        def spread(d):
            return remote(r.gbuf, r.gland.at[2 + d], r.gs.at[2 + d], r.gr.at[2 + d], to_z[d - 1])

        @pl.when(t == base)
        def _():
            total = jnp.sum(r.gacc[...], axis=0, keepdims=True)
            for n in range(8):
                r.gbuf[pl.ds(n, 1), :] = total[:, n * 128:(n + 1) * 128]
            swap(0).start()

        for n in range(3):
            @pl.when(t == base + 2 + 2 * n)
            def _(n=n):
                swap(n).wait()
                r.gbuf[...] = r.gbuf[...] + r.gland[n]
                if n < 2:
                    swap(n + 1).start()
                else:
                    for d in range(1, outer):
                        spread(d).start()

        @pl.when(t == base + 8)
        def _():
            for d in range(1, outer):
                spread(d).wait()
            for d in range(1, outer):
                r.gbuf[...] = r.gbuf[...] + r.gland[2 + d]
            pltpu.make_async_copy(r.gbuf, r.dgain, r.lsem.at[4]).start()

        pl.when(t == base + 10)(lambda: pltpu.make_async_copy(r.gbuf, r.dgain, r.lsem.at[4]).wait())

    n2 = n_wide - blocks
    n_out = blocks * (width // 256)

    def segment2(w3, inner, resid, out, sems, osem):
        per = width // 256
        cols = lambda j: pl.ds(pl.multiple_of(j % per * 256, 256), 256)
        s_w3 = Stream(lambda j: r.w_third.at[:, cols(j)], w3, sems.at[0])
        s_resid = Stream(lambda j: r.resid.at[tok(j // per), cols(j)], resid, sems.at[1])
        s_inner = Stream(lambda n: r.inner.at[tok(n)], inner, sems.at[2])

        def store(j):
            return pltpu.make_async_copy(out.at[j % 2], r.output.at[tok(j // per), cols(j)], osem.at[j % 2])

        mixed_load.start()
        for s in (s_w3, s_resid, s_inner):
            s.start(0)

        def one(j):
            t = at_wide + blocks + j
            move(t)
            scan(t)
            gain_sum(t)
            make_wide(t)

            @pl.when(j < n_out)
            def _():
                w, res = s_w3.get(j, n_out), s_resid.get(j, n_out)

                @pl.when(j % per == 0)
                def _():
                    s_inner.get(j // per, blocks)

                pl.when(j >= 2)(lambda: store(j - 2).wait())
                prod = dot(inner[j // per % 2], w[...], 1, 0)
                out[j % 2] = (res[...] + prod).astype(BF16)
                store(j).start()

        steps(n2, one)
        store(n_out - 2).wait()
        store(n_out - 1).wait()
        mixed_load.wait()

    pl.run_scoped(
        segment2, ring((ff, 256), BF16), ring((TILE, ff), BF16), ring((TILE, 256), F32),
        ring((TILE, 256), BF16), dma(3, 2), dma(2))

    def segment3(q, k, v, query, key, prefix, sems):
        blk = lambda ref: lambda j: ref.at[tok(j, span)]
        tiles = [
            Stream(blk(ref), buf, sems.at[n])
            for n, (ref, buf) in enumerate(((r.q, q), (r.k, k), (r.v, v), (r.query, query), (r.key, key)))
        ]
        tiles.append(Stream(lambda j: r.prefix.at[j], prefix, sems.at[5]))
        norm_load.start()
        for s in tiles:
            s.start(0)

        def one(j):
            t = at_square + j
            move(t)
            scan(t)
            pl.when(j < 4)(lambda: make_square(t, at_square, r.at1, lambda cols: r.dlow[:, cols]))
            pl.when(j == 4)(lambda: norm_load.wait())
            pl.when(j >= 4)(lambda: make_square(t, at_square + 4, r.at0, lambda cols: r.dgate[:, cols]))
            tile_attn(j, *(s.get(j, seqs) for s in tiles))

        steps(8, one)

    pl.run_scoped(
        segment3, *[ring((span, width), BF16)] * 5, ring((pairs, HEAD, 2 * HEAD), BF16), dma(6, 2))

    def segment4(wq, wk, wv, wg, total, xs, out, sems, xsem, osem):
        nn = width // 256
        rowsblk = lambda ref: lambda n: ref.at[pl.ds(pl.multiple_of(n * 256, 256), 256)]
        weights = [
            Stream(rowsblk(ref), buf, sems.at[n])
            for n, (ref, buf) in enumerate(
                ((r.w_query, wq), (r.w_key, wk), (r.w_value, wv), (r.w_gate, wg)))
        ]
        s_x = Stream(lambda j: r.tokens.at[tok(j)], xs, xsem)
        for s in weights:
            s.start(0)
        s_x.start(0)

        def product(j):
            n, m = j // 2, j % 2
            slot = n % 2

            @pl.when(m == 0)
            def _():
                for s in weights:
                    s.get(n, nn)

            here = tok(m, rows // 2)
            full = pl.ds(0, width)
            res = dot(r.dgate[here, :], wg[slot], 1, 1)
            for part, w in zip(parts, (wq, wk, wv)):
                res = res + dot(part(here, full), w[slot], 1, 1)
            total[here, pl.ds(pl.multiple_of(n * 256, 256), 256)] = res

        def store(j):
            return pltpu.make_async_copy(out.at[j % 2], r.dtokens.at[tok(j)], osem.at[j % 2])

        def finish_rows(j):
            xb = s_x.get(j, blocks)
            pl.when(j >= 2)(lambda: store(j - 2).wait())

            def one(m, carry):
                here, sub = pl.ds(pl.multiple_of(j * TILE + m * 32, 32), 32), tok(m, 32)
                xv = xb[sub, :].astype(F32)
                scale = lax.rsqrt(jnp.mean(xv * xv, axis=-1, keepdims=True) + EPS)
                out[j % 2, sub, :] = r.dn2[here, :] + norm_back(total[here, :], xv, scale)
                return carry

            for m in range(TILE // 32):
                one(m, 0)
            store(j).start()

        def one(j):
            t = at_square + 8 + j
            move(t)
            pl.when(j < 4)(lambda: make_square(t, at_square + 8, r.at0, dq_cols))
            pl.when((j >= 4) & (j < 8))(lambda: make_square(t, at_square + 12, r.at0, dk_cols))
            pl.when(j >= 8)(lambda: make_square(t, at_square + 16, r.at0, dv_cols))
            pl.when(j < 2 * nn)(lambda: product(j))
            pl.when(j >= 2 * nn)(lambda: finish_rows(j - 2 * nn))

        steps(12, one)
        store(blocks - 2).wait()
        store(blocks - 1).wait()

    pl.run_scoped(
        segment4, *[ring((256, width), BF16)] * 4, pltpu.VMEM((rows, width), F32),
        ring((TILE, width), BF16), ring((TILE, width), F32), dma(4, 2), dma(2), dma(2))

    steps(len(stages) - 1, lambda j: move(chunks + j))


def back(args, seqs, blk):
    rows, width = args["tokens"].shape
    ff = args["first"].shape[1]
    pairs = width // (2 * HEAD)
    anywhere = pl.BlockSpec(memory_space=pl.ANY)
    cut = 4

    def v(*shape, dtype=F32):
        return pltpu.VMEM(shape, dtype)

    def sem(*shape):
        return pltpu.SemaphoreType.DMA(shape)

    n_scan = seqs * 2
    chunk = (4, 2, 2, 64, 128)
    scratch = dict(
        tbuf=v(2, *chunk), core_rx=v(LAND, *chunk), acc=v(ACC, *chunk), xa=v(LAND, 4, 2, 32, 128),
        ya=v(LAND, 4, 32, 128), yb=v(LAND, 4, 2, 16, 128), xb=v(LAND, 4, 16, 128),
        xc=v(LAND, 2, 16, 128), yc=v(LAND, 16, 128), zab=v(LAND, 2, 3, 48, 128),
        zc=v(LAND, 2, 3, 2, 2, 16, 128), fin=v(FIN, 2, 64, 128),
        ssem=sem(7, LAND), rsem=sem(7, LAND), zss=sem(2, 2, 3, LAND), zrs=sem(2, 2, 3, LAND),
        osem=sem(FIN), csem=sem(FIN), crem=sem(FIN), ygs=sem(FIN), ygr=sem(FIN),
        dyv=v(rows, width, dtype=BF16), dfs=v(2, rows, ff, dtype=BF16), dn2=v(rows, width),
        dlow=v(rows, width, dtype=BF16), dgate=v(rows, width, dtype=BF16),
        dattn=v(rows, width, dtype=BF16), at0=v(8, 2, 64, rows, dtype=BF16),
        at1=v(8, 2, 64, rows, dtype=BF16), held=v(n_scan, cut, HEAD, 128), sums=v(n_scan, cut, HEAD, 128),
        other=v(n_scan, cut, HEAD, 128), dstate=v(n_scan, cut, HEAD, 128, dtype=BF16),
        sz=sem(n_scan), rz=sem(n_scan), sx=sem(n_scan), rx=sem(n_scan),
        gacc=v(8, width), gbuf=v(8, 128), gland=v(6, 8, 128), gs=sem(6), gr=sem(6), lsem=sem(5),
    )
    args = dict(args)
    args["innert"] = args["innert"].reshape(8, ff // 8, rows)
    for name in ("normt", "norm2t", "mixedt"):
        args[name] = args[name].reshape(8, 2, 64, rows)
    args["gain"] = args["gain"].reshape(1, width)
    outs = dict(
        output=((rows, width), BF16), dtokens=((rows, width), F32), tall=((ff // 8, width), F32),
        wide=((2, width // 8, ff), F32), square=((5, width // 8, width), F32), dgain=((8, 128), F32),
    )
    return pl.pallas_call(
        functools.partial(back_kernel, blk // 2, seqs),
        out_shape=[jax.ShapeDtypeStruct(*outs[name]) for name in BACK_OUT],
        in_specs=[anywhere] * len(BACK_IN),
        out_specs=[anywhere] * len(BACK_OUT),
        scratch_shapes=[scratch[name] for name in BACK_SCRATCH],
        compiler_params=pltpu.CompilerParams(
            collective_id=3, has_side_effects=True, vmem_limit_bytes=60 * MIB),
        cost_estimate=pl.CostEstimate(flops=60 * 2**30, bytes_accessed=200 * MIB, transcendentals=0),
    )(*(args[name] for name in BACK_IN))


def rms(value):
    return lax.rsqrt(jnp.mean(value * value, axis=-1, keepdims=True) + EPS)


def forward(blk, seqs, xf, weights):
    w_query, w_key, w_value, w_gate, w_out, out_gain, w_first, w_second, w_third = weights
    normed = (xf * rms(xf)).astype(BF16)
    key = project(normed, w_key)
    value = project(normed, w_value)
    k, v = silu_parts(key)[0].astype(BF16), value.astype(BF16)
    prefix = entering(local_states(k, v, seqs), blk, False)
    query = project(normed, w_query)
    gate = project(normed, w_gate)
    q = silu_parts(query)[0].astype(BF16)
    attn = attention(q, k, v, prefix, seqs)
    mixed = (attn * rms(attn) * out_gain * silu_parts(gate)[0]).astype(BF16)
    resid = xf + project(mixed, w_out)
    normed2 = (resid * rms(resid)).astype(BF16)
    first = project(normed2, w_first)
    second = project(normed2, w_second)
    inner = (first * second).astype(BF16)
    return dict(
        normed=normed, query=query, key=key, gate=gate, q=q, k=k, v=v, prefix=prefix, attn=attn,
        mixed=mixed, resid=resid, normed2=normed2, first=first, second=second, inner=inner)


def backward_plain(blk, seqs, xf, grad_top, f, weights):
    w_query, w_key, w_value, w_gate, w_out, out_gain, w_first, w_second, w_third = weights
    output = (f["resid"] + project(f["inner"], w_third)).astype(BF16)
    grad_w3 = weight_grad(f["inner"], grad_top)
    grad_inner = back_project(grad_top, w_third)
    grad_one = (grad_inner * f["second"]).astype(BF16)
    grad_two = (grad_inner * f["first"]).astype(BF16)
    grad_w1 = weight_grad(f["normed2"], grad_one)
    grad_w2 = weight_grad(f["normed2"], grad_two)
    grad_normed2 = back_project(grad_one, w_first) + back_project(grad_two, w_second)
    resid, attn = f["resid"], f["attn"]
    grad_resid = grad_top.astype(F32) + norm_back(grad_normed2, resid, rms(resid))
    grad_resid_low = grad_resid.astype(BF16)
    grad_wo = weight_grad(f["mixed"], grad_resid_low)
    grad_mixed = back_project(grad_resid_low, w_out)
    gate_act, gate_der = silu_parts(f["gate"])
    rattn = rms(attn)
    unit_attn = attn * rattn
    grad_scaled = grad_mixed * gate_act
    grad_gate_low = (grad_mixed * (unit_attn * out_gain) * gate_der).astype(BF16)
    grad_gain = jnp.sum(grad_scaled * unit_attn, axis=0)
    grad_attn = norm_back(grad_scaled * out_gain, attn, rattn).astype(BF16)
    q, k, v, prefix = f["q"], f["k"], f["v"], f["prefix"]
    dstate = entering(local_states(q, grad_attn, seqs), blk, True)
    grad_fq, grad_fk, grad_vv = attention_back(q, k, v, grad_attn, prefix, dstate, seqs)
    grad_query_low = (grad_fq * silu_parts(f["query"])[1]).astype(BF16)
    grad_key_low = (grad_fk * silu_parts(f["key"])[1]).astype(BF16)
    grad_value_low = grad_vv.astype(BF16)
    normed = f["normed"]
    grads = [weight_grad(normed, g) for g in (grad_query_low, grad_key_low, grad_value_low, grad_gate_low)]
    grads += [grad_wo, grad_gain, grad_w1, grad_w2, grad_w3]
    grad_normed = back_project(grad_query_low, w_query) + back_project(grad_key_low, w_key)
    grad_normed = (
        grad_normed + back_project(grad_value_low, w_value) + back_project(grad_gate_low, w_gate)
    )
    grad_input = grad_resid + norm_back(grad_normed, xf, rms(xf))
    summed = [
        lax.psum(lax.psum_scatter(g, "blk", scatter_dimension=0, tiled=True), "batch") for g in grads]
    return output, grad_input, summed


WEIGHTS = (
    "w_query", "w_key", "w_value", "w_gate", "w_out", "gain", "w_first", "w_second", "w_third",
)


def backward(blk, seqs, tokens, grad_top, f, weights):
    names = WEIGHTS
    args = dict(zip(names, weights), tokens=tokens, dy=grad_top)
    args.update(f)
    output, grad_input, tall, wide, square, dgain = back(args, seqs, blk)
    so, sg, sq, sk, sv = (square[n] for n in range(5))
    sgain = lax.dynamic_index_in_dim(dgain, lax.axis_index("blk"), 0, False)
    return output, grad_input, [sq, sk, sv, sg, so, sgain, wide[0], wide[1], tall]


def body(sizes, tokens, cotangent, *weights):
    batch, blk = sizes
    seqs, span, width = tokens.shape
    rows = seqs * span
    low = tokens.reshape(rows, width)
    xf = low.astype(F32)
    grad_top = cotangent.reshape(rows, width)
    ff = weights[-1].shape[0]
    if (batch, blk, rows, span, width, ff % 256) == (4, 8, 1024, 128, 1024, 0):
        f = forward_fast(blk, seqs, low, weights)
        output, grad_input, grads = backward(blk, seqs, low, grad_top, f, weights)
    else:
        f = forward(blk, seqs, xf, weights)
        output, grad_input, grads = backward_plain(blk, seqs, xf, grad_top, f, weights)
    shape = (seqs, span, width)
    return (output.reshape(shape), grad_input.reshape(shape), *grads)


def solution(mesh):
    rows = P("batch", "blk", None)
    cut = P("blk", None)
    return jax.shard_map(
        functools.partial(body, (mesh.shape["batch"], mesh.shape["blk"])),
        mesh=mesh,
        in_specs=(rows, rows) + (P(),) * 9,
        out_specs=(rows, rows) + (cut,) * 5 + (P("blk"),) + (cut,) * 3,
        check_vma=False,
    )
```

```python
import functools

import jax
import jax.numpy as jnp
from jax import lax
from jax.experimental import pallas as pl
from jax.experimental.pallas import tpu as pltpu
from jax.sharding import PartitionSpec as P

HEAD = 64
EPS = 1e-06
MESH = pl.DeviceIdType.MESH
F32 = jnp.float32
BF16 = jnp.bfloat16
MIB = 2**20


def silu_parts(pre):
    sig = jax.nn.sigmoid(pre)
    return (pre * sig, sig * (1.0 + pre * (1.0 - sig)))


def norm_back(grad, value, scale):
    inner = jnp.mean(grad * value, axis=-1, keepdims=True)
    return scale * grad - value * (scale * scale * scale) * inner


def project(left, weight):
    return jnp.dot(left, weight, preferred_element_type=F32)


def weight_grad(left, right):
    return jnp.einsum("td,tf->df", left, right, preferred_element_type=F32)


def back_project(grad, weight):
    return jnp.einsum("tf,df->td", grad, weight, preferred_element_type=F32)


def dot(a, b, ca, cb):
    return lax.dot_general(a, b, (((ca,), (cb,)), ((), ())), preferred_element_type=F32)


def low_lanes(shape):
    return lax.broadcasted_iota(jnp.int32, shape, len(shape) - 1) < HEAD


def two_heads(x):
    low = low_lanes(x.shape)
    zero = jnp.zeros_like(x)
    return jnp.concatenate([jnp.where(low, x, zero), jnp.where(low, zero, x)], axis=0)


def pick_heads(x):
    half = x.shape[0] // 2
    return jnp.where(low_lanes((half, x.shape[1])), x[:half], x[half:])


def causal_pair(span):
    t = lax.broadcasted_iota(jnp.int32, (span, 2 * span), 0)
    u = lax.broadcasted_iota(jnp.int32, (span, 2 * span), 1)
    return t >= u % span


def pair_of(ref, p):
    return ref[:, pl.ds(p * 2 * HEAD, 2 * HEAD)]


def state_kernel(left_ref, right_ref, out_ref):
    for p in range(out_ref.shape[1]):
        out_ref[0, p] = pick_heads(dot(pair_of(left_ref, p), pair_of(right_ref, p), 0, 0))


def attn_kernel(q_ref, k_ref, v_ref, prefix_ref, out_ref):
    span = q_ref.shape[0]
    causal = causal_pair(span)
    for p in range(prefix_ref.shape[1]):
        q, k2, v2 = pair_of(q_ref, p), two_heads(pair_of(k_ref, p)), two_heads(pair_of(v_ref, p))
        scores = jnp.where(causal, dot(q, k2, 1, 1), 0.0).astype(BF16)
        prefix = two_heads(prefix_ref[0, p])
        out_ref[:, pl.ds(p * 2 * HEAD, 2 * HEAD)] = dot(scores, v2, 1, 0) + dot(q, prefix, 1, 0)


def attn_back_kernel(q_ref, k_ref, v_ref, g_ref, prefix_ref, dstate_ref, dq_ref, dk_ref, dv_ref):
    span = q_ref.shape[0]
    causal = causal_pair(span)
    for p in range(prefix_ref.shape[1]):
        q, k, v, g = (pair_of(r, p) for r in (q_ref, k_ref, v_ref, g_ref))
        k2, v2 = two_heads(k), two_heads(v)
        prefix, dstate = two_heads(prefix_ref[0, p]), two_heads(dstate_ref[0, p])
        scores = jnp.where(causal, dot(q, k2, 1, 1), 0.0).astype(BF16)
        dscores = jnp.where(causal, dot(g, v2, 1, 1), 0.0).astype(BF16)
        lanes = pl.ds(p * 2 * HEAD, 2 * HEAD)
        dq_ref[:, lanes] = dot(dscores, k2, 1, 0) + dot(g, prefix, 1, 1)
        dk_ref[:, lanes] = pick_heads(dot(dscores, q, 0, 0)) + dot(v, dstate, 1, 1)
        dv_ref[:, lanes] = pick_heads(dot(scores, g, 0, 0)) + dot(k, dstate, 1, 0)


def rows_spec(span, width):
    return pl.BlockSpec((span, width), lambda s: (s, 0))


def state_spec(pairs):
    return pl.BlockSpec((1, pairs, HEAD, 2 * HEAD), lambda s: (s, 0, 0, 0))


def local_states(left, right, seqs):
    rows, width = left.shape
    span, pairs = rows // seqs, width // (2 * HEAD)
    return pl.pallas_call(
        state_kernel,
        grid=(seqs,),
        in_specs=[rows_spec(span, width)] * 2,
        out_specs=state_spec(pairs),
        out_shape=jax.ShapeDtypeStruct((seqs, pairs, HEAD, 2 * HEAD), F32),
    )(left, right)


def attention(q, k, v, prefix, seqs):
    rows, width = q.shape
    span, pairs = rows // seqs, width // (2 * HEAD)
    return pl.pallas_call(
        attn_kernel,
        grid=(seqs,),
        in_specs=[rows_spec(span, width)] * 3 + [state_spec(pairs)],
        out_specs=rows_spec(span, width),
        out_shape=jax.ShapeDtypeStruct((rows, width), F32),
    )(q, k, v, prefix)


def attention_back(q, k, v, g, prefix, dstate, seqs):
    rows, width = q.shape
    span, pairs = rows // seqs, width // (2 * HEAD)
    return pl.pallas_call(
        attn_back_kernel,
        grid=(seqs,),
        in_specs=[rows_spec(span, width)] * 4 + [state_spec(pairs)] * 2,
        out_specs=[rows_spec(span, width)] * 3,
        out_shape=[jax.ShapeDtypeStruct((rows, width), F32)] * 3,
    )(q, k, v, g, prefix, dstate)


def scan_kernel(outer, reverse, s_ref, out_ref, held, summed, other, zs, zr, xs, xr):
    chunks = s_ref.shape[0]
    k = lax.axis_index("blk")
    z, x = k // 2, k % 2
    if reverse:
        zz, xx = outer - 1 - z, 1 - x
        after, before = jnp.maximum(z - 1, 0), jnp.minimum(z + 1, outer - 1)
    else:
        zz, xx = z, x
        after, before = jnp.minimum(z + 1, outer - 1), jnp.maximum(z - 1, 0)
    nxt, prv, side = {"blk": after * 2 + x}, {"blk": before * 2 + x}, {"blk": z * 2 + 1 - x}
    first, last = zz == 0, zz == outer - 1

    bar = pltpu.get_barrier_semaphore()
    pl.semaphore_signal(bar, inc=1, device_id=side, device_id_type=MESH)
    pl.when(~last)(lambda: pl.semaphore_signal(bar, inc=1, device_id=nxt, device_id_type=MESH))
    pl.when(~first)(lambda: pl.semaphore_signal(bar, inc=1, device_id=prv, device_id_type=MESH))
    pl.semaphore_wait(bar, 1 + jnp.where(last, 0, 1) + jnp.where(first, 0, 1))

    def along(i):
        return pltpu.make_async_remote_copy(
            src_ref=summed.at[i], dst_ref=held.at[i], send_sem=zs.at[i], recv_sem=zr.at[i],
            device_id=nxt, device_id_type=MESH)

    def across(i, src):
        return pltpu.make_async_remote_copy(
            src_ref=src.at[i], dst_ref=other.at[i], send_sem=xs.at[i], recv_sem=xr.at[i],
            device_id=side, device_id_type=MESH)

    def pass_on(i):
        pl.when(~first)(lambda: along(i).wait_recv())

        @pl.when(first)
        def _():
            held[i] = jnp.zeros_like(held[i])

        summed[i] = held[i] + s_ref[i]
        pl.when(~last)(lambda: along(i).start())
        pl.when(xx == 0)(lambda: across(i, summed).start())
        pl.when(xx == 1)(lambda: across(i, held).start())

    def finish(i):
        across(i, held).wait_recv()
        out_ref[i] = (held[i] + other[i]).astype(out_ref.dtype)

    def step(i, carry):
        pl.when(i < chunks)(lambda: pass_on(i))
        pl.when(i > 0)(lambda: finish(i - 1))
        return carry

    lax.fori_loop(0, chunks + 1, step, 0)

    def drain(i, carry):
        pl.when(~last)(lambda: along(i).wait_send())
        across(i, held).wait_send()
        return carry

    lax.fori_loop(0, chunks, drain, 0)


def entering(states, blk, reverse):
    seqs, pairs, head, lanes = states.shape
    per = max(1, pairs // 2)
    shape = (seqs * pairs // per, per, head, lanes)
    vmem = pl.BlockSpec(memory_space=pltpu.VMEM)
    sems = [pltpu.SemaphoreType.DMA((shape[0],))] * 4
    out = pl.pallas_call(
        functools.partial(scan_kernel, blk // 2, reverse),
        out_shape=jax.ShapeDtypeStruct(shape, BF16),
        in_specs=[vmem],
        out_specs=vmem,
        scratch_shapes=[pltpu.VMEM(shape, F32)] * 3 + sems,
        compiler_params=pltpu.CompilerParams(
            collective_id=2 if reverse else 1, has_side_effects=True, vmem_limit_bytes=24 * MIB),
    )(states.reshape(shape))
    return out.reshape(states.shape)


LAND, FIN, ACC = 4, 8, 10
CORE, XA, YA, YB, XB, XC, YC = range(7)
TILE = 256


SPARE = (2, 18)


class Way:
    def __init__(self, a, b, c):
        self.a = pl.ds(0, a) if a else None
        self.b, self.c = pl.ds(a, b), pl.ds(a + b, c)
        self.ab, self.top_b, self.top_c = pl.ds(0, a + b), pl.ds(0, b), pl.ds(0, c)


class Named:
    def __init__(self, names, refs):
        self.__dict__.update(zip(names, refs))


class Stream:
    def __init__(self, block, buf, sem):
        self.block, self.buf, self.sem = block, buf, sem

    def copy(self, j):
        return pltpu.make_async_copy(self.block(j), self.buf.at[j % 2], self.sem.at[j % 2])

    def start(self, j):
        self.copy(j).start()

    def get(self, j, count):
        self.copy(j).wait()
        pl.when(j + 1 < count)(lambda: self.start(j + 1))
        return self.buf.at[j % 2]


BACK_IN = (
    "tokens", "dy", "innert", "inner", "first", "second", "resid", "gate", "attn", "q", "k", "v",
    "query", "key", "prefix", "normt", "norm2t", "mixedt", "gain", "w_query", "w_key", "w_value",
    "w_gate", "w_out", "w_first", "w_second", "w_third",
)
BACK_OUT = (
    "output", "dtokens", "tall", "wide", "square", "dgain",
)
BACK_SCRATCH = (
    "tbuf", "core_rx", "acc", "xa", "ya", "yb", "xb", "xc", "yc", "zab", "zc", "fin", "ssem",
    "rsem", "zss", "zrs", "osem", "csem", "crem", "ygs", "ygr", "dyv", "dfs", "dn2", "dlow",
    "dgate", "dattn", "at0", "at1", "held", "sums", "other", "dstate", "sz", "rz", "sx", "rx",
    "gacc", "gbuf", "gland", "gs", "gr", "lsem",
)


FWD_IN = (
    "tokens", "gain", "w_query", "w_key", "w_value", "w_gate", "w_out", "w_first", "w_second",
)
FWD_OUT = (
    "k", "v", "key", "normt", "q", "gate", "query", "attn", "mixedt", "resid", "norm2t", "first",
    "second", "inner", "innert", "prefix",
)
FWD_SCRATCH = (
    "xv", "gv", "wq", "wk", "wv", "wg", "wo", "w1", "w2", "nrm", "kb", "vb", "qb", "gb", "intra",
    "keyb", "queryb", "attnb", "mixb", "residb", "n2b", "firstb", "secondb", "innerb", "tb0", "tb1",
    "tb2", "innertb", "held", "sums", "other", "pre", "sz", "rz", "sx", "rx", "lsem", "xsem", "osem",
)


LAG, WAIT = 1, 2


def forward_kernel(outer, seqs, *refs):
    r = Named(FWD_IN + FWD_OUT + FWD_SCRATCH, refs)
    rows, width = r.tokens.shape
    ff = r.w_first.shape[1]
    span, pairs = rows // seqs, width // (2 * HEAD)
    blocks, per_block = rows // TILE, TILE // span
    n_scan, cut = r.sums.shape[:2]
    per_seq = pairs // cut

    k = lax.axis_index("blk")
    z, x = k // 2, k % 2
    top = outer - 1
    side = {"blk": z * 2 + 1 - x}
    above, below = {"blk": jnp.minimum(z + 1, top) * 2 + x}, {"blk": jnp.maximum(z - 1, 0) * 2 + x}
    bar = pltpu.get_barrier_semaphore()
    pl.semaphore_signal(bar, inc=1, device_id=side, device_id_type=MESH)
    pl.when(z < top)(lambda: pl.semaphore_signal(bar, inc=1, device_id=above, device_id_type=MESH))
    pl.when(z > 0)(lambda: pl.semaphore_signal(bar, inc=1, device_id=below, device_id_type=MESH))

    def span_of(start, size, step):
        return pl.ds(start if isinstance(start, int) else pl.multiple_of(start, step), size)

    def tok(j, n=TILE):
        return span_of(j * n, n, n)

    loads = [
        pltpu.make_async_copy(src, dst, r.lsem.at[n])
        for n, (src, dst) in enumerate((
            (r.w_key, r.wk), (r.w_value, r.wv), (r.w_query, r.wq), (r.w_gate, r.wg), (r.gain, r.gv),
            (r.w_out, r.wo), (r.w_first, r.w1), (r.w_second, r.w2)))
    ]

    def x_load(j):
        return pltpu.make_async_copy(r.tokens.at[tok(j)], r.xv.at[tok(j)], r.xsem.at[j])

    by_rows = dict(
        k=lambda j: r.kb.at[tok(j)], v=lambda j: r.vb.at[tok(j)], q=lambda j: r.qb.at[tok(j)],
        gate=lambda j: r.gb.at[tok(j)], key=lambda j: r.keyb, query=lambda j: r.queryb,
        attn=lambda j: r.attnb, resid=lambda j: r.residb, first=lambda j: r.firstb,
        second=lambda j: r.secondb, inner=lambda j: r.innerb)
    by_cols = dict(normt=r.tb0, mixedt=r.tb1, norm2t=r.tb2, innert=r.innertb)

    def store(name, j):
        sem = r.osem.at[FWD_OUT.index(name)]
        out = getattr(r, name)
        if name in by_rows:
            return pltpu.make_async_copy(by_rows[name](j), out.at[tok(j)], sem)
        return pltpu.make_async_copy(by_cols[name], out.at[:, tok(j)], sem)

    def free(name, j):
        pl.when(j > 0)(lambda: store(name, j - 1).wait())

    def remote(src, dst, s, t, dev):
        return pltpu.make_async_remote_copy(
            src_ref=src, dst_ref=dst, send_sem=s, recv_sem=t, device_id=dev, device_id_type=MESH)

    def along(i):
        return remote(r.sums.at[i], r.held.at[i], r.sz.at[i], r.rz.at[i], above)

    def across(i, src):
        return remote(src.at[i], r.other.at[i], r.sx.at[i], r.rx.at[i], side)

    def pass_on(i):
        pl.when(z > 0)(lambda: along(i).wait_recv())

        @pl.when(z == 0)
        def _():
            r.held[i] = jnp.zeros_like(r.held[i])

        r.sums[i] = r.held[i] + r.sums[i]
        pl.when(z < top)(lambda: along(i).start())
        pl.when(x == 0)(lambda: across(i, r.sums).start())
        pl.when(x == 1)(lambda: across(i, r.held).start())

    def finish(i):
        across(i, r.held).wait_recv()
        r.pre[i] = (r.held[i] + r.other[i]).astype(BF16)
        pl.when(z < top)(lambda: along(i).wait_send())
        across(i, r.held).wait_send()

    def scan(n):
        i = n - LAG * z
        pl.when((i >= 0) & (i < n_scan))(lambda: pass_on(i))
        pl.when((i >= WAIT) & (i < n_scan + WAIT))(lambda: finish(i - WAIT))

    def transposed(src, dst):
        for n in range(dst.shape[0] // 128):
            cols = pl.ds(n * 128, 128)
            dst[cols, :] = src[:, cols].T

    def norm_rows(value):
        return (value * lax.rsqrt(jnp.mean(value * value, axis=-1, keepdims=True) + EPS)).astype(BF16)

    def each(count, one):
        for m in range(count):
            one(m)

    def rows_of(j, m):
        return span_of(j * TILE + m * 32, 32, 32)

    def col(n):
        return span_of(n * 256, 256, 256)

    def tile_keys(j):
        x_load(j).wait()

        @pl.when(j == 0)
        def _():
            loads[0].wait()
            loads[1].wait()

        for name in ("key", "k", "v", "normt"):
            free(name, j)

        def one(m):
            r.nrm[rows_of(j, m), :] = norm_rows(r.xv[rows_of(j, m), :].astype(F32))

        each(TILE // 32, one)

        def product(n):
            key = dot(r.nrm[tok(j), :], r.wk[:, col(n)], 1, 0)
            r.keyb[:, col(n)] = key.astype(BF16)
            r.kb[tok(j), col(n)] = silu_parts(key)[0].astype(BF16)
            r.vb[tok(j), col(n)] = dot(r.nrm[tok(j), :], r.wv[:, col(n)], 1, 0).astype(BF16)

        each(width // 256, product)

        def states(m):
            s = j * per_block + m
            for p in range(pairs):
                lanes = pl.ds(p * 2 * HEAD, 2 * HEAD)
                here = tok(s, span)
                r.sums[s * per_seq + p // cut, p % cut] = pick_heads(dot(r.kb[here, lanes], r.vb[here, lanes], 0, 0))

        each(per_block, states)
        transposed(r.nrm.at[tok(j)], r.tb0)
        for name in ("key", "k", "v", "normt"):
            store(name, j).start()

    def tile_query(j):
        @pl.when(j == 0)
        def _():
            loads[2].wait()
            loads[3].wait()

        for name in ("query", "q", "gate"):
            free(name, j)

        def product(n):
            query = dot(r.nrm[tok(j), :], r.wq[:, col(n)], 1, 0)
            r.queryb[:, col(n)] = query.astype(BF16)
            r.qb[tok(j), col(n)] = silu_parts(query)[0].astype(BF16)
            r.gb[tok(j), col(n)] = dot(r.nrm[tok(j), :], r.wg[:, col(n)], 1, 0).astype(BF16)

        each(width // 256, product)
        for name in ("query", "q", "gate"):
            store(name, j).start()

    def tile_scores(s):
        causal = causal_pair(span)
        here = tok(s, span)
        for p in range(pairs):
            lanes = pl.ds(p * 2 * HEAD, 2 * HEAD)
            q, k2, v2 = r.qb[here, lanes], two_heads(r.kb[here, lanes]), two_heads(r.vb[here, lanes])
            scores = jnp.where(causal, dot(q, k2, 1, 1), 0.0).astype(BF16)
            r.intra[here, lanes] = dot(scores, v2, 1, 0)

    def tile_mixed(j):
        pl.when(j == 0)(lambda: loads[4].wait())
        for name in ("attn", "mixedt"):
            free(name, j)

        def inter(m):
            s = j * per_block + m
            here = tok(s, span)
            for p in range(pairs):
                lanes = pl.ds(p * 2 * HEAD, 2 * HEAD)
                prefix = two_heads(r.pre[s * per_seq + p // cut, p % cut])
                r.intra[here, lanes] = r.intra[here, lanes] + dot(r.qb[here, lanes], prefix, 1, 0)

        each(per_block, inter)

        def one(m):
            av = r.intra[rows_of(j, m), :]
            scale = lax.rsqrt(jnp.mean(av * av, axis=-1, keepdims=True) + EPS)
            act = silu_parts(r.gb[rows_of(j, m), :].astype(F32))[0]
            r.attnb[tok(m, 32), :] = av.astype(BF16)
            r.mixb[tok(m, 32), :] = (av * scale * r.gv[...] * act).astype(BF16)

        each(TILE // 32, one)
        transposed(r.mixb, r.tb1)
        for name in ("attn", "mixedt"):
            store(name, j).start()

    def tile_resid(j):
        pl.when(j == 0)(lambda: loads[5].wait())
        for name in ("resid", "norm2t"):
            free(name, j)

        def product(n):
            r.residb[:, col(n)] = r.xv[tok(j), col(n)].astype(F32) + dot(r.mixb[...], r.wo[:, col(n)], 1, 0)

        each(width // 256, product)

        def one(m):
            r.n2b[tok(m, 32), :] = norm_rows(r.residb[tok(m, 32), :])

        each(TILE // 32, one)
        transposed(r.n2b, r.tb2)
        for name in ("resid", "norm2t"):
            store(name, j).start()

    def tile_inner(j, lo, hi):
        def one(n):
            n = n + lo
            first = dot(r.n2b[...], r.w1[:, col(n)], 1, 0)
            second = dot(r.n2b[...], r.w2[:, col(n)], 1, 0)
            inner = (first * second).astype(BF16)
            r.firstb[:, col(n)] = first.astype(BF16)
            r.secondb[:, col(n)] = second.astype(BF16)
            r.innerb[:, col(n)] = inner
            r.innertb[col(n), :] = inner.T

        each(hi - lo, one)

    def tile_up(j):
        @pl.when(j == 0)
        def _():
            loads[6].wait()
            loads[7].wait()

        for name in ("first", "second", "inner", "innert"):
            free(name, j)
        tile_inner(j, 0, ff // 512)

    def tile_up2(j):
        tile_inner(j, ff // 512, ff // 256)
        for name in ("first", "second", "inner", "innert"):
            store(name, j).start()

    for n in range(2):
        x_load(n).start()
        loads[n].start()
    for n in range(2, blocks):
        x_load(n).start()
    for copy in loads[2:]:
        copy.start()
    pl.semaphore_wait(bar, 1 + jnp.where(z < top, 1, 0) + jnp.where(z > 0, 1, 0))

    per = n_scan // blocks
    late = (tile_mixed, tile_resid, tile_up, tile_up2)

    def slot(n, carry):
        pl.when(n < blocks)(lambda: tile_keys(n))

        @pl.when((n >= blocks) & (n < 2 * blocks))
        def _():
            tile_query(n - blocks)
            for m in range(per_block):
                tile_scores((n - blocks) * per_block + m)

        scan(n)
        w = n - LAG * z - WAIT - per + 1
        j, m = w // per, w % per
        for step, tile in enumerate(late):
            pl.when((w >= 0) & (j < blocks) & (m == step))(functools.partial(tile, j))
        return carry

    lax.fori_loop(0, n_scan + LAG * top + WAIT + len(late), slot, 0)
    whole = pltpu.make_async_copy(r.pre, r.prefix, r.osem.at[FWD_OUT.index("prefix")])
    whole.start()
    for name in FWD_OUT[:-1]:
        store(name, blocks - 1).wait()
    whole.wait()


def forward_fast(blk, seqs, tokens, weights):
    w_query, w_key, w_value, w_gate, w_out, out_gain, w_first, w_second, w_third = weights
    rows, width = tokens.shape
    ff = w_first.shape[1]
    pairs = width // (2 * HEAD)
    cut = 4
    n_scan = seqs * pairs // cut

    def v(*shape, dtype=BF16):
        return pltpu.VMEM(shape, dtype)

    def sem(*shape):
        return pltpu.SemaphoreType.DMA(shape)

    wide, tall = (rows, width), (width, ff)
    chunks = (n_scan, cut, HEAD, 2 * HEAD)
    scratch = dict(
        xv=v(*wide), gv=v(1, width, dtype=F32), wq=v(width, width), wk=v(width, width), wv=v(width, width),
        wg=v(width, width), wo=v(width, width), w1=v(*tall), w2=v(*tall), nrm=v(*wide), kb=v(*wide),
        vb=v(*wide), qb=v(*wide), gb=v(*wide), intra=v(*wide, dtype=F32), keyb=v(TILE, width),
        queryb=v(TILE, width), attnb=v(TILE, width), mixb=v(TILE, width), residb=v(TILE, width, dtype=F32),
        n2b=v(TILE, width), firstb=v(TILE, ff), secondb=v(TILE, ff), innerb=v(TILE, ff),
        tb0=v(width, TILE), tb1=v(width, TILE), tb2=v(width, TILE), innertb=v(ff, TILE),
        held=v(*chunks, dtype=F32), sums=v(*chunks, dtype=F32), other=v(*chunks, dtype=F32), pre=v(*chunks),
        sz=sem(n_scan), rz=sem(n_scan), sx=sem(n_scan), rx=sem(n_scan), lsem=sem(8),
        xsem=sem(rows // TILE), osem=sem(len(FWD_OUT)),
    )
    shapes = dict(
        normt=(width, rows), mixedt=(width, rows), norm2t=(width, rows), first=(rows, ff), second=(rows, ff),
        inner=(rows, ff), innert=(ff, rows), prefix=chunks)
    anywhere = pl.BlockSpec(memory_space=pl.ANY)
    outs = pl.pallas_call(
        functools.partial(forward_kernel, blk // 2, seqs),
        out_shape=[
            jax.ShapeDtypeStruct(shapes.get(name, wide), F32 if name == "resid" else BF16)
            for name in FWD_OUT
        ],
        in_specs=[anywhere] * len(FWD_IN),
        out_specs=[anywhere] * len(FWD_OUT),
        scratch_shapes=[scratch[name] for name in FWD_SCRATCH],
        compiler_params=pltpu.CompilerParams(
            collective_id=4, has_side_effects=True, vmem_limit_bytes=60 * MIB),
        cost_estimate=pl.CostEstimate(flops=26 * 2**30, bytes_accessed=80 * MIB, transcendentals=0),
    )(tokens, out_gain.reshape(1, width), w_query, w_key, w_value, w_gate, w_out, w_first, w_second)
    f = dict(zip(FWD_OUT, outs))
    f["prefix"] = f["prefix"].reshape(seqs, pairs, HEAD, 2 * HEAD)
    return f


def back_kernel(outer, seqs, *refs):
    r = Named(BACK_IN + BACK_OUT + BACK_SCRATCH, refs)
    rows, width = r.tokens.shape
    ff = r.first.shape[1]
    span, pairs = rows // seqs, width // (2 * HEAD)
    n_tall, n_wide, n_square = ff // 256, ff // 128, 20
    chunks = n_tall + n_wide + n_square
    at_wide, at_square = n_tall, n_tall + n_wide
    blocks = rows // TILE

    b, k = lax.axis_index("batch"), lax.axis_index("blk")
    y, c = b // 2, b % 2
    z, x = k // 2, k % 2
    ox, oy = 1 - x, 1 - y
    top = outer - 1
    zr = top - z
    to_core, to_y, to_x = {"batch": y * 2 + 1 - c}, {"batch": oy * 2 + c}, {"blk": z * 2 + ox}
    to_up = {"blk": jnp.minimum(z + 1, top) * 2 + x}
    to_down = {"blk": jnp.maximum(z - 1, 0) * 2 + x}
    to_z = [{"blk": (z + d) % outer * 2 + x} for d in range(1, outer)]

    peers = [to_core, to_y, to_x] + to_z
    bar = pltpu.get_barrier_semaphore()
    for d in peers:
        pl.semaphore_signal(bar, inc=1, device_id=d, device_id_type=MESH)
    pl.semaphore_wait(bar, len(peers))

    def remote(src, dst, s, t, dev):
        return pltpu.make_async_remote_copy(
            src_ref=src, dst_ref=dst, send_sem=s, recv_sem=t, device_id=dev, device_id_type=MESH)

    def link(kind, i, src, dst, dev):
        return remote(src, dst.at[i % LAND], r.ssem.at[kind, i % LAND], r.rsem.at[kind, i % LAND], dev)

    def at(i, *where):
        return r.acc.at[(i % ACC,) + where]

    every = slice(None)

    def core_copy(i):
        return link(CORE, i, r.tbuf.at[i % 2], r.core_rx, to_core)

    def xa_copy(w, i):
        return link(XA, i, at(i, every, ox, every, w.a), r.xa, to_x)

    def ya_copy(w, i):
        return link(YA, i, at(i, every, x, oy, w.a), r.ya, to_y)

    def yb_copy(w, i):
        return link(YB, i, at(i, every, every, oy, w.b), r.yb.at[:, :, :, w.top_b], to_y)

    def xb_copy(w, i):
        return link(XB, i, at(i, every, ox, y, w.b), r.xb.at[:, :, w.top_b], to_x)

    def xc_copy(w, i):
        return link(XC, i, at(i, z, ox, every, w.c), r.xc.at[:, :, w.top_c], to_x)

    def yc_copy(w, i):
        return link(YC, i, at(i, z, x, oy, w.c), r.yc.at[:, w.top_c], to_y)

    def y_share(i):
        f = i % FIN
        return remote(r.fin.at[f, y], r.fin.at[f, y], r.ygs.at[f], r.ygr.at[f], to_y)

    def part_ab(w, i, s):
        return at(i, s, x, y, w.ab)

    def part_c(w, i, s):
        return at(i, s, every, every, w.c)

    def land_ab(w, i, d, n):
        return r.zab.at[i % LAND, d, n - 1, w.ab]

    def land_c(w, i, d, n):
        return r.zc.at[i % LAND, d, n - 1, :, :, w.top_c]

    AB, CC = (0, part_ab, land_ab), (1, part_c, land_c)

    def hop(group, w, i, n, up, s):
        g, part, land = group
        d = 0 if up else 1
        sem = (g, d, n - 1, i % LAND)
        return remote(part(w, i, s), land(w, i, d, n), r.zss.at[sem], r.zrs.at[sem],
                      to_up if up else to_down)

    def z_each(group, w, i, n, act):
        up = hop(group, w, i, n, True, jnp.minimum(outer - n + z, top))
        down = hop(group, w, i, n, False, jnp.maximum(n - 1 - zr, 0))
        pl.when((z <= n - 1) & (z < top))(lambda: act(up))
        pl.when((zr <= n - 1) & (z > 0))(lambda: act(down))

    def z_send(group, w, i, n):
        z_each(group, w, i, n, lambda copy: copy.start())

    def z_sent(group, w, i, n):
        z_each(group, w, i, n, lambda copy: copy.wait_send())

    def add(ref, landed):
        ref[...] = ref[...] + landed[...]

    def z_take(group, w, i, n):
        g, part, land = group

        def take(up, s):
            hop(group, w, i, n, up, s).wait_recv()
            add(part(w, i, s), land(w, i, 0 if up else 1, n))

        pl.when((z > 0) & (z <= n))(lambda: take(True, jnp.clip(outer - n + z - 1, 0, top)))
        pl.when((z < top) & (zr <= n))(lambda: take(False, jnp.clip(n - zr, 0, top)))

    BOTH = (Way(32, 16, 16), Way(0, 56, 8))
    spare = (at_wide + SPARE[0], at_wide + SPARE[1])

    def places(i, act):
        f = r.fin.at[i % FIN]

        @pl.when(i < at_wide)
        def _():
            for yy in range(2):
                for blk in range(2):
                    col = pl.multiple_of(c * (width // 2) + (yy * 2 + blk) * 128, 128)
                    act(f.at[yy, pl.ds(blk * 32, 32)], r.tall.at[pl.ds(i * 32, 32), pl.ds(col, 128)])

        @pl.when((i >= at_wide) & (i < at_square))
        def _():
            j, h = (i - at_wide) // 2, (i - at_wide) % 2
            col = pl.multiple_of(c * (ff // 2) + j * 128, 128)
            for yy in range(2):
                act(f.at[yy], r.wide.at[yy, pl.ds(h * 64, 64), pl.ds(col, 128)])

        @pl.when(i >= at_square)
        def _():
            j = i - at_square
            m, u, h = j // 4, j // 2 % 2, j % 2
            for yy in range(2):
                col = pl.multiple_of(c * (width // 2) + u * 256 + yy * 128, 128)
                act(f.at[yy], r.square.at[m, pl.ds(h * 64, 64), pl.ds(col, 128)])

    def cores(w, i):
        core_copy(i).wait_recv()
        core_copy(i).wait_send()
        add(at(i), r.core_rx.at[i % LAND])
        if w.a is not None:
            xa_copy(w, i).start()
        yb_copy(w, i).start()
        z_send(CC, w, i, 1)

    def second(w, i):
        yb_copy(w, i).wait_recv()
        add(at(i, every, every, y, w.b), r.yb.at[i % LAND, :, :, w.top_b])
        xb_copy(w, i).start()
        if w.a is not None:
            xa_copy(w, i).wait_recv()
            add(at(i, every, x, every, w.a), r.xa.at[i % LAND])
            ya_copy(w, i).start()
        z_take(CC, w, i, 1)
        z_send(CC, w, i, 2)
        if w.a is not None:
            xa_copy(w, i).wait_send()
        yb_copy(w, i).wait_send()
        z_sent(CC, w, i, 1)

    def third(w, i):
        xb_copy(w, i).wait_recv()
        add(at(i, every, x, y, w.b), r.xb.at[i % LAND, :, w.top_b])
        if w.a is not None:
            ya_copy(w, i).wait_recv()
            add(at(i, every, x, y, w.a), r.ya.at[i % LAND])
        z_send(AB, w, i, 1)
        z_take(CC, w, i, 2)
        z_send(CC, w, i, 3)
        xb_copy(w, i).wait_send()
        if w.a is not None:
            ya_copy(w, i).wait_send()
        z_sent(CC, w, i, 2)

    def fourth(w, i):
        z_take(AB, w, i, 1)
        z_send(AB, w, i, 2)
        z_take(CC, w, i, 3)
        xc_copy(w, i).start()
        z_sent(AB, w, i, 1)
        z_sent(CC, w, i, 3)

    def fifth(w, i):
        z_take(AB, w, i, 2)
        z_send(AB, w, i, 3)
        xc_copy(w, i).wait_recv()
        add(at(i, z, x, every, w.c), r.xc.at[i % LAND, :, w.top_c])
        yc_copy(w, i).start()
        z_sent(AB, w, i, 2)
        xc_copy(w, i).wait_send()

    def sixth(w, i):
        yc_copy(w, i).wait_recv()
        z_take(AB, w, i, 3)
        f = i % FIN
        r.fin[f, y, w.ab] = r.acc[i % ACC, z, x, y, w.ab]
        r.fin[f, y, w.c] = r.acc[i % ACC, z, x, y, w.c] + r.yc[i % LAND, w.top_c]
        y_share(i).start()
        z_sent(AB, w, i, 3)
        yc_copy(w, i).wait_send()

    def seventh(w, i):
        y_share(i).wait_recv()
        y_share(i).wait_send()
        f = i % FIN

        def go(src, dst):
            remote(src, dst, r.csem.at[f], r.crem.at[f], to_core).start()
            pltpu.make_async_copy(src, dst, r.osem.at[f]).start()

        places(i, go)

    def last(w, i):
        f = i % FIN
        whole = r.fin.at[f]
        copy = remote(whole, whole, r.csem.at[f], r.crem.at[f], to_core)
        copy.wait_send()
        copy.wait_recv()
        pltpu.make_async_copy(whole, whole, r.osem.at[f]).wait()

    stages = (None, cores, second, third, fourth, fifth, sixth, seventh, last)

    def advance(t, some, ways):
        for n in some:
            i = t - n
            live = (i >= 0) & (i < chunks)
            if n >= 7 or len(ways) == 1:
                pl.when(live)(functools.partial(stages[n], ways[0], i))
            else:
                spared = (i >= spare[0]) & (i < spare[1])
                pl.when(live & ~spared)(functools.partial(stages[n], ways[0], i))
                pl.when(spared)(functools.partial(stages[n], ways[1], i))

    def send_first(t, ways=BOTH):
        advance(t, (1,), ways)

    def move(t, ways=BOTH):
        advance(t, range(2, len(stages)), ways)

    def make(t, fill):
        fill(1 - c, r.tbuf.at[t % 2])
        core_copy(t).start()
        fill(c, r.acc.at[t % ACC])

    def fill_tall(lhs):
        def fill(half, dst):
            for yy in range(2):
                col = pl.multiple_of(half * (width // 2) + yy * 256, 256)
                res = dot(lhs, r.dyv[:, pl.ds(col, 256)], 1, 0).reshape(4, 2, 32, 256)
                for blk in range(2):
                    dst[:, :, yy, pl.ds(blk * 32, 32), :] = res[..., blk * 128:(blk + 1) * 128]
        return fill

    def left_rows(ref, h):
        return ref[:, h].reshape(8 * 64, rows)

    def fill_two(left, h, take):
        def fill(half, dst):
            res = dot(left_rows(left, h), take(half), 1, 0).reshape(4, 2, 64, 256)
            dst[:, :, 0] = res[..., :128]
            dst[:, :, 1] = res[..., 128:]
        return fill

    def make_wide(t):
        i = t - at_wide
        j, h = i // 2, i % 2

        def take(half):
            col = pl.ds(pl.multiple_of(half * (ff // 2) + j * 128, 128), 128)
            return jnp.concatenate([r.dfs[0, :, col], r.dfs[1, :, col]], axis=1)

        make(t, fill_two(r.at0, h, take))

    def make_square(t, base, left, right):
        i = t - base
        u, h = i // 2, i % 2

        def take(half):
            return right(pl.ds(pl.multiple_of(half * (width // 2) + u * 256, 256), 256))

        make(t, fill_two(left, h, take))

    zz, xx = zr, ox
    n_scan = r.sums.shape[0]
    halves = n_scan // seqs
    scan_at = at_wide

    def along(i):
        return remote(r.sums.at[i], r.held.at[i], r.sz.at[i], r.rz.at[i], to_down)

    def across(i, src):
        return remote(src.at[i], r.other.at[i], r.sx.at[i], r.rx.at[i], to_x)

    def pass_on(i):
        pl.when(zz > 0)(lambda: along(i).wait_recv())

        @pl.when(zz == 0)
        def _():
            r.held[i] = jnp.zeros_like(r.held[i])

        r.sums[i] = r.held[i] + r.sums[i]
        pl.when(zz < top)(lambda: along(i).start())
        pl.when(xx == 0)(lambda: across(i, r.sums).start())
        pl.when(xx == 1)(lambda: across(i, r.held).start())

    def finish(i):
        across(i, r.held).wait_recv()
        r.dstate[i] = (r.held[i] + r.other[i]).astype(BF16)
        pl.when(zz < top)(lambda: along(i).wait_send())
        across(i, r.held).wait_send()

    def scan(t):
        i = t - scan_at - zz
        pl.when((i >= 0) & (i < n_scan))(lambda: pass_on(i))
        pl.when((i >= 2) & (i < n_scan + 2))(lambda: finish(i - 2))

    def span_of(start, size, step):
        return pl.ds(start if isinstance(start, int) else pl.multiple_of(start, step), size)

    def tok(j, n=TILE):
        return span_of(j * n, n, n)

    def tile_inner(j, w3, w1, w2, first, second):
        def block(m, carry):
            at_rows = tok(m, 512)
            din = dot(r.dyv[at_rows, :], w3[...], 1, 1)
            one = (din * second[at_rows, :].astype(F32)).astype(BF16)
            two = (din * first[at_rows, :].astype(F32)).astype(BF16)
            cols = pl.ds(pl.multiple_of(j * 256, 256), 256)
            r.dfs[0, at_rows, cols] = one
            r.dfs[1, at_rows, cols] = two
            for n in range(width // 256):
                to = pl.ds(n * 256, 256)
                res = dot(one, w1[to, :], 1, 1) + dot(two, w2[to, :], 1, 1)
                r.dn2[at_rows, to] = r.dn2[at_rows, to] + res
            return carry

        for m in range(rows // 512):
            block(m, 0)

    def tile_resid(j, resid, gate, attn, q, w_out, gain, dmix):
        def one(m, carry):
            here, sub = pl.ds(pl.multiple_of(j * TILE + m * 32, 32), 32), tok(m, 32)
            value = resid[sub, :]
            grad = r.dn2[here, :]
            scale = lax.rsqrt(jnp.mean(value * value, axis=-1, keepdims=True) + EPS)
            out = r.dyv[here, :].astype(F32) + norm_back(grad, value, scale)
            r.dn2[here, :] = out
            r.dlow[here, :] = out.astype(BF16)
            return carry

        for m in range(TILE // 32):
            one(m, 0)
        for n in range(width // 256):
            to = pl.ds(n * 256, 256)
            dmix[:, to] = dot(r.dlow[tok(j), :], w_out[to, :], 1, 1)

        def two(m, carry):
            here, sub = pl.ds(pl.multiple_of(j * TILE + m * 32, 32), 32), tok(m, 32)
            av = attn[sub, :].astype(F32)
            scale = lax.rsqrt(jnp.mean(av * av, axis=-1, keepdims=True) + EPS)
            unit = av * scale
            act, der = silu_parts(gate[sub, :].astype(F32))
            dm = dmix[sub, :]
            ds = dm * act
            r.dgate[here, :] = (dm * (unit * gain[...]) * der).astype(BF16)
            r.gacc[...] = r.gacc[...] + jnp.sum((ds * unit).reshape(4, 8, width), axis=0)
            r.dattn[here, :] = norm_back(ds * gain[...], av, scale).astype(BF16)
            return carry

        for m in range(TILE // 32):
            two(m, 0)

        def states(m, carry):
            s = j * (TILE // span) + m
            for p in range(pairs):
                lanes = pl.ds(p * 2 * HEAD, 2 * HEAD)
                grad = r.dattn[tok(s, span), lanes]
                per = pairs // halves
                r.sums[s * halves + p // per, p % per] = pick_heads(dot(q[tok(m, span), lanes], grad, 0, 0))
            return carry

        for m in range(TILE // span):
            states(m, 0)

    def tile_attn(s, q_ref, k_ref, v_ref, query, key, prefix_ref):
        causal = causal_pair(span)
        here = tok(s, span)
        for p in range(pairs):
            lanes = pl.ds(p * 2 * HEAD, 2 * HEAD)
            q, k, v, g = q_ref[:, lanes], k_ref[:, lanes], v_ref[:, lanes], r.dattn[here, lanes]
            k2, v2 = two_heads(k), two_heads(v)
            per = pairs // halves
            prefix, dstate = two_heads(prefix_ref[p]), two_heads(r.dstate[s * halves + p // per, p % per])
            scores = jnp.where(causal, dot(q, k2, 1, 1), 0.0).astype(BF16)
            dscores = jnp.where(causal, dot(g, v2, 1, 1), 0.0).astype(BF16)
            dq = dot(dscores, k2, 1, 0) + dot(g, prefix, 1, 1)
            dk = pick_heads(dot(dscores, q, 0, 0)) + dot(v, dstate, 1, 1)
            dv = pick_heads(dot(scores, g, 0, 0)) + dot(k, dstate, 1, 0)
            r.dfs[0, here, lanes] = (dq * silu_parts(query[:, lanes].astype(F32))[1]).astype(BF16)
            r.dfs[0, here, pl.ds(width + p * 2 * HEAD, 2 * HEAD)] = (
                dk * silu_parts(key[:, lanes].astype(F32))[1]).astype(BF16)
            r.dfs[1, here, lanes] = dv.astype(BF16)

    parts = [
        lambda at_rows, cols: r.dfs[0, at_rows, cols],
        lambda at_rows, cols: r.dfs[0, at_rows, pl.ds(width + cols.start, cols.size)],
        lambda at_rows, cols: r.dfs[1, at_rows, cols],
    ]
    dq_cols = lambda cols: r.dfs[0, :, cols]
    dk_cols = lambda cols: r.dfs[0, :, pl.ds(width + cols.start, cols.size)]
    dv_cols = lambda cols: r.dfs[1, :, cols]

    def load(src, dst, n):
        return pltpu.make_async_copy(src, dst, r.lsem.at[n])

    def dma(*shape):
        return pltpu.SemaphoreType.DMA(shape)

    def ring(shape, dtype):
        return pltpu.VMEM((2,) + shape, dtype)

    def steps(count, one):
        def go(j, carry):
            one(j)
            return carry

        lax.fori_loop(0, count, go, 0)

    dy_load = load(r.dy, r.dyv, 0)
    norm2_load = load(r.norm2t, r.at0, 1)
    mixed_load = load(r.mixedt, r.at1, 2)
    norm_load = load(r.normt, r.at0, 3)

    def segment0(left, w3, w1, w2, first, second, sems):
        cols = lambda ref: lambda j: ref.at[:, pl.ds(pl.multiple_of(j * 256, 256), 256)]
        s_left = Stream(lambda j: r.innert.at[:, pl.ds(pl.multiple_of(j * 32, 32), 32)], left, sems.at[0])
        tiles = [
            Stream(lambda j: r.w_third.at[pl.ds(pl.multiple_of(j * 256, 256), 256)], w3, sems.at[1]),
            Stream(cols(r.w_first), w1, sems.at[2]),
            Stream(cols(r.w_second), w2, sems.at[3]),
            Stream(cols(r.first), first, sems.at[4]),
            Stream(cols(r.second), second, sems.at[5]),
        ]
        dy_load.start()
        s_left.start(0)
        for s in tiles:
            s.start(0)
        norm2_load.start()
        r.dn2[...] = jnp.zeros_like(r.dn2)
        r.gacc[...] = jnp.zeros_like(r.gacc)
        dy_load.wait()

        def one(j):
            send_first(j, BOTH[:1])
            make(j, fill_tall(s_left.get(j, n_tall)[...].reshape(8 * 32, rows)))
            tile_inner(j, *(s.get(j, n_tall) for s in tiles))
            move(j, BOTH[:1])

        steps(n_tall, one)
        norm2_load.wait()

    pl.run_scoped(
        segment0, ring((8, 32, rows), BF16), ring((256, width), BF16), ring((width, 256), BF16),
        ring((width, 256), BF16), ring((rows, 256), BF16), ring((rows, 256), BF16), dma(6, 2))

    def segment1(resid, gate, attn, q, w_out, gain, dmix, sems, wsem):
        blk = lambda ref: lambda j: ref.at[tok(j)]
        tiles = [
            Stream(blk(ref), buf, sems.at[n])
            for n, (ref, buf) in enumerate(((r.resid, resid), (r.gate, gate), (r.attn, attn), (r.q, q)))
        ]
        w_load = pltpu.make_async_copy(r.w_out, w_out, wsem.at[0])
        g_load = pltpu.make_async_copy(r.gain, gain, wsem.at[1])
        w_load.start()
        g_load.start()
        for s in tiles:
            s.start(0)
        w_load.wait()
        g_load.wait()

        def one(j):
            t = at_wide + j
            send_first(t)
            make_wide(t)
            rs, ga, at_, qs = (s.get(j, blocks) for s in tiles)
            tile_resid(j, rs, ga, at_, qs, w_out, gain, dmix)
            move(t)
            scan(t)

        steps(blocks, one)

    pl.run_scoped(
        segment1, ring((TILE, width), F32), ring((TILE, width), BF16), ring((TILE, width), BF16),
        ring((TILE, width), BF16), pltpu.VMEM((width, width), BF16), pltpu.VMEM((1, width), F32),
        pltpu.VMEM((TILE, width), F32), dma(4, 2), dma(2))

    def gain_sum(t):
        base = at_wide + blocks
        hops = [to_core, to_y, to_x]

        def swap(n):
            return remote(r.gbuf, r.gland.at[n], r.gs.at[n], r.gr.at[n], hops[n])

        def spread(d):
            return remote(r.gbuf, r.gland.at[2 + d], r.gs.at[2 + d], r.gr.at[2 + d], to_z[d - 1])

        @pl.when(t == base)
        def _():
            total = jnp.sum(r.gacc[...], axis=0, keepdims=True)
            for n in range(8):
                r.gbuf[pl.ds(n, 1), :] = total[:, n * 128:(n + 1) * 128]
            swap(0).start()

        for n in range(3):
            @pl.when(t == base + 2 + 2 * n)
            def _(n=n):
                swap(n).wait()
                r.gbuf[...] = r.gbuf[...] + r.gland[n]
                if n < 2:
                    swap(n + 1).start()
                else:
                    for d in range(1, outer):
                        spread(d).start()

        @pl.when(t == base + 8)
        def _():
            for d in range(1, outer):
                spread(d).wait()
            for d in range(1, outer):
                r.gbuf[...] = r.gbuf[...] + r.gland[2 + d]
            pltpu.make_async_copy(r.gbuf, r.dgain, r.lsem.at[4]).start()

        pl.when(t == base + 10)(lambda: pltpu.make_async_copy(r.gbuf, r.dgain, r.lsem.at[4]).wait())

    n2 = n_wide - blocks
    n_out = blocks * (width // 256)

    def segment2(w3, inner, resid, out, sems, osem):
        per = width // 256
        cols = lambda j: pl.ds(pl.multiple_of(j % per * 256, 256), 256)
        s_w3 = Stream(lambda j: r.w_third.at[:, cols(j)], w3, sems.at[0])
        s_resid = Stream(lambda j: r.resid.at[tok(j // per), cols(j)], resid, sems.at[1])
        s_inner = Stream(lambda n: r.inner.at[tok(n)], inner, sems.at[2])

        def store(j):
            return pltpu.make_async_copy(out.at[j % 2], r.output.at[tok(j // per), cols(j)], osem.at[j % 2])

        mixed_load.start()
        for s in (s_w3, s_resid, s_inner):
            s.start(0)

        def one(j):
            t = at_wide + blocks + j
            send_first(t)
            make_wide(t)

            @pl.when(j < n_out)
            def _():
                w, res = s_w3.get(j, n_out), s_resid.get(j, n_out)

                @pl.when(j % per == 0)
                def _():
                    s_inner.get(j // per, blocks)

                pl.when(j >= 2)(lambda: store(j - 2).wait())
                prod = dot(inner[j // per % 2], w[...], 1, 0)
                out[j % 2] = (res[...] + prod).astype(BF16)
                store(j).start()

            move(t)
            scan(t)
            gain_sum(t)

        steps(n2, one)
        store(n_out - 2).wait()
        store(n_out - 1).wait()
        mixed_load.wait()

    pl.run_scoped(
        segment2, ring((ff, 256), BF16), ring((TILE, ff), BF16), ring((TILE, 256), F32),
        ring((TILE, 256), BF16), dma(3, 2), dma(2))

    def segment3(q, k, v, query, key, prefix, sems):
        blk = lambda ref: lambda j: ref.at[tok(j, span)]
        tiles = [
            Stream(blk(ref), buf, sems.at[n])
            for n, (ref, buf) in enumerate(((r.q, q), (r.k, k), (r.v, v), (r.query, query), (r.key, key)))
        ]
        tiles.append(Stream(lambda j: r.prefix.at[j], prefix, sems.at[5]))
        norm_load.start()
        for s in tiles:
            s.start(0)

        def one(j):
            t = at_square + j
            send_first(t)
            pl.when(j < 4)(lambda: make_square(t, at_square, r.at1, lambda cols: r.dlow[:, cols]))
            pl.when(j == 4)(lambda: norm_load.wait())
            pl.when(j >= 4)(lambda: make_square(t, at_square + 4, r.at0, lambda cols: r.dgate[:, cols]))
            tile_attn(j, *(s.get(j, seqs) for s in tiles))
            move(t)

        steps(8, one)

    pl.run_scoped(
        segment3, *[ring((span, width), BF16)] * 5, ring((pairs, HEAD, 2 * HEAD), BF16), dma(6, 2))

    def segment4(wq, wk, wv, wg, total, xs, out, sems, xsem, osem):
        nn = width // 256
        rowsblk = lambda ref: lambda n: ref.at[pl.ds(pl.multiple_of(n * 256, 256), 256)]
        weights = [
            Stream(rowsblk(ref), buf, sems.at[n])
            for n, (ref, buf) in enumerate(
                ((r.w_query, wq), (r.w_key, wk), (r.w_value, wv), (r.w_gate, wg)))
        ]
        s_x = Stream(lambda j: r.tokens.at[tok(j)], xs, xsem)
        for s in weights:
            s.start(0)
        s_x.start(0)

        def product(j):
            n, m = j // 2, j % 2
            slot = n % 2

            @pl.when(m == 0)
            def _():
                for s in weights:
                    s.get(n, nn)

            here = tok(m, rows // 2)
            full = pl.ds(0, width)
            res = dot(r.dgate[here, :], wg[slot], 1, 1)
            for part, w in zip(parts, (wq, wk, wv)):
                res = res + dot(part(here, full), w[slot], 1, 1)
            total[here, pl.ds(pl.multiple_of(n * 256, 256), 256)] = res

        def store(j):
            return pltpu.make_async_copy(out.at[j % 2], r.dtokens.at[tok(j)], osem.at[j % 2])

        def finish_rows(j):
            xb = s_x.get(j, blocks)
            pl.when(j >= 2)(lambda: store(j - 2).wait())

            def one(m, carry):
                here, sub = pl.ds(pl.multiple_of(j * TILE + m * 32, 32), 32), tok(m, 32)
                xv = xb[sub, :].astype(F32)
                scale = lax.rsqrt(jnp.mean(xv * xv, axis=-1, keepdims=True) + EPS)
                out[j % 2, sub, :] = r.dn2[here, :] + norm_back(total[here, :], xv, scale)
                return carry

            for m in range(TILE // 32):
                one(m, 0)
            store(j).start()

        def one(j):
            t = at_square + 8 + j
            send_first(t, BOTH[:1])
            pl.when(j < 4)(lambda: make_square(t, at_square + 8, r.at0, dq_cols))
            pl.when((j >= 4) & (j < 8))(lambda: make_square(t, at_square + 12, r.at0, dk_cols))
            pl.when(j >= 8)(lambda: make_square(t, at_square + 16, r.at0, dv_cols))
            pl.when(j < 2 * nn)(lambda: product(j))
            pl.when(j >= 2 * nn)(lambda: finish_rows(j - 2 * nn))
            move(t, BOTH[:1])

        steps(12, one)
        store(blocks - 2).wait()
        store(blocks - 1).wait()

    pl.run_scoped(
        segment4, *[ring((256, width), BF16)] * 4, pltpu.VMEM((rows, width), F32),
        ring((TILE, width), BF16), ring((TILE, width), F32), dma(4, 2), dma(2), dma(2))

    def rest(j):
        send_first(chunks + j, BOTH[:1])
        move(chunks + j, BOTH[:1])

    steps(len(stages) - 1, rest)


def back(args, seqs, blk):
    rows, width = args["tokens"].shape
    ff = args["first"].shape[1]
    pairs = width // (2 * HEAD)
    anywhere = pl.BlockSpec(memory_space=pl.ANY)
    cut = 4

    def v(*shape, dtype=F32):
        return pltpu.VMEM(shape, dtype)

    def sem(*shape):
        return pltpu.SemaphoreType.DMA(shape)

    n_scan = seqs * 2
    chunk = (4, 2, 2, 64, 128)
    scratch = dict(
        tbuf=v(2, *chunk), core_rx=v(LAND, *chunk), acc=v(ACC, *chunk), xa=v(LAND, 4, 2, 32, 128),
        ya=v(LAND, 4, 32, 128), yb=v(LAND, 4, 2, 56, 128), xb=v(LAND, 4, 56, 128),
        xc=v(LAND, 2, 16, 128), yc=v(LAND, 16, 128), zab=v(LAND, 2, 3, 56, 128),
        zc=v(LAND, 2, 3, 2, 2, 16, 128), fin=v(FIN, 2, 64, 128),
        ssem=sem(7, LAND), rsem=sem(7, LAND), zss=sem(2, 2, 3, LAND), zrs=sem(2, 2, 3, LAND),
        osem=sem(FIN), csem=sem(FIN), crem=sem(FIN), ygs=sem(FIN), ygr=sem(FIN),
        dyv=v(rows, width, dtype=BF16), dfs=v(2, rows, ff, dtype=BF16), dn2=v(rows, width),
        dlow=v(rows, width, dtype=BF16), dgate=v(rows, width, dtype=BF16),
        dattn=v(rows, width, dtype=BF16), at0=v(8, 2, 64, rows, dtype=BF16),
        at1=v(8, 2, 64, rows, dtype=BF16), held=v(n_scan, cut, HEAD, 128), sums=v(n_scan, cut, HEAD, 128),
        other=v(n_scan, cut, HEAD, 128), dstate=v(n_scan, cut, HEAD, 128, dtype=BF16),
        sz=sem(n_scan), rz=sem(n_scan), sx=sem(n_scan), rx=sem(n_scan),
        gacc=v(8, width), gbuf=v(8, 128), gland=v(6, 8, 128), gs=sem(6), gr=sem(6), lsem=sem(5),
    )
    args = dict(args)
    args["innert"] = args["innert"].reshape(8, ff // 8, rows)
    for name in ("normt", "norm2t", "mixedt"):
        args[name] = args[name].reshape(8, 2, 64, rows)
    args["gain"] = args["gain"].reshape(1, width)
    outs = dict(
        output=((rows, width), BF16), dtokens=((rows, width), F32), tall=((ff // 8, width), F32),
        wide=((2, width // 8, ff), F32), square=((5, width // 8, width), F32), dgain=((8, 128), F32),
    )
    return pl.pallas_call(
        functools.partial(back_kernel, blk // 2, seqs),
        out_shape=[jax.ShapeDtypeStruct(*outs[name]) for name in BACK_OUT],
        in_specs=[anywhere] * len(BACK_IN),
        out_specs=[anywhere] * len(BACK_OUT),
        scratch_shapes=[scratch[name] for name in BACK_SCRATCH],
        compiler_params=pltpu.CompilerParams(
            collective_id=3, has_side_effects=True, vmem_limit_bytes=60 * MIB),
        cost_estimate=pl.CostEstimate(flops=60 * 2**30, bytes_accessed=200 * MIB, transcendentals=0),
    )(*(args[name] for name in BACK_IN))


def rms(value):
    return lax.rsqrt(jnp.mean(value * value, axis=-1, keepdims=True) + EPS)


def forward(blk, seqs, xf, weights):
    w_query, w_key, w_value, w_gate, w_out, out_gain, w_first, w_second, w_third = weights
    normed = (xf * rms(xf)).astype(BF16)
    key = project(normed, w_key)
    value = project(normed, w_value)
    k, v = silu_parts(key)[0].astype(BF16), value.astype(BF16)
    prefix = entering(local_states(k, v, seqs), blk, False)
    query = project(normed, w_query)
    gate = project(normed, w_gate)
    q = silu_parts(query)[0].astype(BF16)
    attn = attention(q, k, v, prefix, seqs)
    mixed = (attn * rms(attn) * out_gain * silu_parts(gate)[0]).astype(BF16)
    resid = xf + project(mixed, w_out)
    normed2 = (resid * rms(resid)).astype(BF16)
    first = project(normed2, w_first)
    second = project(normed2, w_second)
    inner = (first * second).astype(BF16)
    return dict(
        normed=normed, query=query, key=key, gate=gate, q=q, k=k, v=v, prefix=prefix, attn=attn,
        mixed=mixed, resid=resid, normed2=normed2, first=first, second=second, inner=inner)


def backward_plain(blk, seqs, xf, grad_top, f, weights):
    w_query, w_key, w_value, w_gate, w_out, out_gain, w_first, w_second, w_third = weights
    output = (f["resid"] + project(f["inner"], w_third)).astype(BF16)
    grad_w3 = weight_grad(f["inner"], grad_top)
    grad_inner = back_project(grad_top, w_third)
    grad_one = (grad_inner * f["second"]).astype(BF16)
    grad_two = (grad_inner * f["first"]).astype(BF16)
    grad_w1 = weight_grad(f["normed2"], grad_one)
    grad_w2 = weight_grad(f["normed2"], grad_two)
    grad_normed2 = back_project(grad_one, w_first) + back_project(grad_two, w_second)
    resid, attn = f["resid"], f["attn"]
    grad_resid = grad_top.astype(F32) + norm_back(grad_normed2, resid, rms(resid))
    grad_resid_low = grad_resid.astype(BF16)
    grad_wo = weight_grad(f["mixed"], grad_resid_low)
    grad_mixed = back_project(grad_resid_low, w_out)
    gate_act, gate_der = silu_parts(f["gate"])
    rattn = rms(attn)
    unit_attn = attn * rattn
    grad_scaled = grad_mixed * gate_act
    grad_gate_low = (grad_mixed * (unit_attn * out_gain) * gate_der).astype(BF16)
    grad_gain = jnp.sum(grad_scaled * unit_attn, axis=0)
    grad_attn = norm_back(grad_scaled * out_gain, attn, rattn).astype(BF16)
    q, k, v, prefix = f["q"], f["k"], f["v"], f["prefix"]
    dstate = entering(local_states(q, grad_attn, seqs), blk, True)
    grad_fq, grad_fk, grad_vv = attention_back(q, k, v, grad_attn, prefix, dstate, seqs)
    grad_query_low = (grad_fq * silu_parts(f["query"])[1]).astype(BF16)
    grad_key_low = (grad_fk * silu_parts(f["key"])[1]).astype(BF16)
    grad_value_low = grad_vv.astype(BF16)
    normed = f["normed"]
    grads = [weight_grad(normed, g) for g in (grad_query_low, grad_key_low, grad_value_low, grad_gate_low)]
    grads += [grad_wo, grad_gain, grad_w1, grad_w2, grad_w3]
    grad_normed = back_project(grad_query_low, w_query) + back_project(grad_key_low, w_key)
    grad_normed = (
        grad_normed + back_project(grad_value_low, w_value) + back_project(grad_gate_low, w_gate)
    )
    grad_input = grad_resid + norm_back(grad_normed, xf, rms(xf))
    summed = [
        lax.psum(lax.psum_scatter(g, "blk", scatter_dimension=0, tiled=True), "batch") for g in grads]
    return output, grad_input, summed


WEIGHTS = (
    "w_query", "w_key", "w_value", "w_gate", "w_out", "gain", "w_first", "w_second", "w_third",
)


def backward(blk, seqs, tokens, grad_top, f, weights):
    names = WEIGHTS
    args = dict(zip(names, weights), tokens=tokens, dy=grad_top)
    args.update(f)
    output, grad_input, tall, wide, square, dgain = back(args, seqs, blk)
    so, sg, sq, sk, sv = (square[n] for n in range(5))
    sgain = lax.dynamic_index_in_dim(dgain, lax.axis_index("blk"), 0, False)
    return output, grad_input, [sq, sk, sv, sg, so, sgain, wide[0], wide[1], tall]


def body(sizes, tokens, cotangent, *weights):
    batch, blk = sizes
    seqs, span, width = tokens.shape
    rows = seqs * span
    low = tokens.reshape(rows, width)
    xf = low.astype(F32)
    grad_top = cotangent.reshape(rows, width)
    ff = weights[-1].shape[0]
    if (batch, blk, rows, span, width, ff % 256) == (4, 8, 1024, 128, 1024, 0):
        f = forward_fast(blk, seqs, low, weights)
        output, grad_input, grads = backward(blk, seqs, low, grad_top, f, weights)
    else:
        f = forward(blk, seqs, xf, weights)
        output, grad_input, grads = backward_plain(blk, seqs, xf, grad_top, f, weights)
    shape = (seqs, span, width)
    return (output.reshape(shape), grad_input.reshape(shape), *grads)


def solution(mesh):
    rows = P("batch", "blk", None)
    cut = P("blk", None)
    return jax.shard_map(
        functools.partial(body, (mesh.shape["batch"], mesh.shape["blk"])),
        mesh=mesh,
        in_specs=(rows, rows) + (P(),) * 9,
        out_specs=(rows, rows) + (cut,) * 5 + (P("blk"),) + (cut,) * 3,
        check_vma=False,
    )
```

```python
import functools

import jax
import jax.numpy as jnp
from jax import lax
from jax.experimental import pallas as pl
from jax.experimental.pallas import tpu as pltpu
from jax.sharding import PartitionSpec as P

HEAD = 64
EPS = 1e-06
MESH = pl.DeviceIdType.MESH
F32 = jnp.float32
BF16 = jnp.bfloat16
MIB = 2**20


def silu_parts(pre):
    sig = jax.nn.sigmoid(pre)
    return (pre * sig, sig * (1.0 + pre * (1.0 - sig)))


def norm_back(grad, value, scale):
    inner = jnp.mean(grad * value, axis=-1, keepdims=True)
    return scale * grad - value * (scale * scale * scale) * inner


def project(left, weight):
    return jnp.dot(left, weight, preferred_element_type=F32)


def weight_grad(left, right):
    return jnp.einsum("td,tf->df", left, right, preferred_element_type=F32)


def back_project(grad, weight):
    return jnp.einsum("tf,df->td", grad, weight, preferred_element_type=F32)


def dot(a, b, ca, cb):
    return lax.dot_general(a, b, (((ca,), (cb,)), ((), ())), preferred_element_type=F32)


def low_lanes(shape):
    return lax.broadcasted_iota(jnp.int32, shape, len(shape) - 1) < HEAD


def two_heads(x):
    low = low_lanes(x.shape)
    zero = jnp.zeros_like(x)
    return jnp.concatenate([jnp.where(low, x, zero), jnp.where(low, zero, x)], axis=0)


def pick_heads(x):
    half = x.shape[0] // 2
    return jnp.where(low_lanes((half, x.shape[1])), x[:half], x[half:])


def causal_pair(span):
    t = lax.broadcasted_iota(jnp.int32, (span, 2 * span), 0)
    u = lax.broadcasted_iota(jnp.int32, (span, 2 * span), 1)
    return t >= u % span


def pair_of(ref, p):
    return ref[:, pl.ds(p * 2 * HEAD, 2 * HEAD)]


def state_kernel(left_ref, right_ref, out_ref):
    for p in range(out_ref.shape[1]):
        out_ref[0, p] = pick_heads(dot(pair_of(left_ref, p), pair_of(right_ref, p), 0, 0))


def attn_kernel(q_ref, k_ref, v_ref, prefix_ref, out_ref):
    span = q_ref.shape[0]
    causal = causal_pair(span)
    for p in range(prefix_ref.shape[1]):
        q, k2, v2 = pair_of(q_ref, p), two_heads(pair_of(k_ref, p)), two_heads(pair_of(v_ref, p))
        scores = jnp.where(causal, dot(q, k2, 1, 1), 0.0).astype(BF16)
        prefix = two_heads(prefix_ref[0, p])
        out_ref[:, pl.ds(p * 2 * HEAD, 2 * HEAD)] = dot(scores, v2, 1, 0) + dot(q, prefix, 1, 0)


def attn_back_kernel(q_ref, k_ref, v_ref, g_ref, prefix_ref, dstate_ref, dq_ref, dk_ref, dv_ref):
    span = q_ref.shape[0]
    causal = causal_pair(span)
    for p in range(prefix_ref.shape[1]):
        q, k, v, g = (pair_of(r, p) for r in (q_ref, k_ref, v_ref, g_ref))
        k2, v2 = two_heads(k), two_heads(v)
        prefix, dstate = two_heads(prefix_ref[0, p]), two_heads(dstate_ref[0, p])
        scores = jnp.where(causal, dot(q, k2, 1, 1), 0.0).astype(BF16)
        dscores = jnp.where(causal, dot(g, v2, 1, 1), 0.0).astype(BF16)
        lanes = pl.ds(p * 2 * HEAD, 2 * HEAD)
        dq_ref[:, lanes] = dot(dscores, k2, 1, 0) + dot(g, prefix, 1, 1)
        dk_ref[:, lanes] = pick_heads(dot(dscores, q, 0, 0)) + dot(v, dstate, 1, 1)
        dv_ref[:, lanes] = pick_heads(dot(scores, g, 0, 0)) + dot(k, dstate, 1, 0)


def rows_spec(span, width):
    return pl.BlockSpec((span, width), lambda s: (s, 0))


def state_spec(pairs):
    return pl.BlockSpec((1, pairs, HEAD, 2 * HEAD), lambda s: (s, 0, 0, 0))


def local_states(left, right, seqs):
    rows, width = left.shape
    span, pairs = rows // seqs, width // (2 * HEAD)
    return pl.pallas_call(
        state_kernel,
        grid=(seqs,),
        in_specs=[rows_spec(span, width)] * 2,
        out_specs=state_spec(pairs),
        out_shape=jax.ShapeDtypeStruct((seqs, pairs, HEAD, 2 * HEAD), F32),
    )(left, right)


def attention(q, k, v, prefix, seqs):
    rows, width = q.shape
    span, pairs = rows // seqs, width // (2 * HEAD)
    return pl.pallas_call(
        attn_kernel,
        grid=(seqs,),
        in_specs=[rows_spec(span, width)] * 3 + [state_spec(pairs)],
        out_specs=rows_spec(span, width),
        out_shape=jax.ShapeDtypeStruct((rows, width), F32),
    )(q, k, v, prefix)


def attention_back(q, k, v, g, prefix, dstate, seqs):
    rows, width = q.shape
    span, pairs = rows // seqs, width // (2 * HEAD)
    return pl.pallas_call(
        attn_back_kernel,
        grid=(seqs,),
        in_specs=[rows_spec(span, width)] * 4 + [state_spec(pairs)] * 2,
        out_specs=[rows_spec(span, width)] * 3,
        out_shape=[jax.ShapeDtypeStruct((rows, width), F32)] * 3,
    )(q, k, v, g, prefix, dstate)


def scan_kernel(outer, reverse, s_ref, out_ref, held, summed, other, zs, zr, xs, xr):
    chunks = s_ref.shape[0]
    k = lax.axis_index("blk")
    z, x = k // 2, k % 2
    if reverse:
        zz, xx = outer - 1 - z, 1 - x
        after, before = jnp.maximum(z - 1, 0), jnp.minimum(z + 1, outer - 1)
    else:
        zz, xx = z, x
        after, before = jnp.minimum(z + 1, outer - 1), jnp.maximum(z - 1, 0)
    nxt, prv, side = {"blk": after * 2 + x}, {"blk": before * 2 + x}, {"blk": z * 2 + 1 - x}
    first, last = zz == 0, zz == outer - 1

    bar = pltpu.get_barrier_semaphore()
    pl.semaphore_signal(bar, inc=1, device_id=side, device_id_type=MESH)
    pl.when(~last)(lambda: pl.semaphore_signal(bar, inc=1, device_id=nxt, device_id_type=MESH))
    pl.when(~first)(lambda: pl.semaphore_signal(bar, inc=1, device_id=prv, device_id_type=MESH))
    pl.semaphore_wait(bar, 1 + jnp.where(last, 0, 1) + jnp.where(first, 0, 1))

    def along(i):
        return pltpu.make_async_remote_copy(
            src_ref=summed.at[i], dst_ref=held.at[i], send_sem=zs.at[i], recv_sem=zr.at[i],
            device_id=nxt, device_id_type=MESH)

    def across(i, src):
        return pltpu.make_async_remote_copy(
            src_ref=src.at[i], dst_ref=other.at[i], send_sem=xs.at[i], recv_sem=xr.at[i],
            device_id=side, device_id_type=MESH)

    def pass_on(i):
        pl.when(~first)(lambda: along(i).wait_recv())

        @pl.when(first)
        def _():
            held[i] = jnp.zeros_like(held[i])

        summed[i] = held[i] + s_ref[i]
        pl.when(~last)(lambda: along(i).start())
        pl.when(xx == 0)(lambda: across(i, summed).start())
        pl.when(xx == 1)(lambda: across(i, held).start())

    def finish(i):
        across(i, held).wait_recv()
        out_ref[i] = (held[i] + other[i]).astype(out_ref.dtype)

    def step(i, carry):
        pl.when(i < chunks)(lambda: pass_on(i))
        pl.when(i > 0)(lambda: finish(i - 1))
        return carry

    lax.fori_loop(0, chunks + 1, step, 0)

    def drain(i, carry):
        pl.when(~last)(lambda: along(i).wait_send())
        across(i, held).wait_send()
        return carry

    lax.fori_loop(0, chunks, drain, 0)


def entering(states, blk, reverse):
    seqs, pairs, head, lanes = states.shape
    per = max(1, pairs // 2)
    shape = (seqs * pairs // per, per, head, lanes)
    vmem = pl.BlockSpec(memory_space=pltpu.VMEM)
    sems = [pltpu.SemaphoreType.DMA((shape[0],))] * 4
    out = pl.pallas_call(
        functools.partial(scan_kernel, blk // 2, reverse),
        out_shape=jax.ShapeDtypeStruct(shape, BF16),
        in_specs=[vmem],
        out_specs=vmem,
        scratch_shapes=[pltpu.VMEM(shape, F32)] * 3 + sems,
        compiler_params=pltpu.CompilerParams(
            collective_id=2 if reverse else 1, has_side_effects=True, vmem_limit_bytes=24 * MIB),
    )(states.reshape(shape))
    return out.reshape(states.shape)


LAND, FIN, ACC = 4, 8, 10
CORE, XA, YA, YB, XB, XC, YC = range(7)
TILE = 256


SPARE = (2, 18)


class Way:
    def __init__(self, a, b, c):
        self.a = pl.ds(0, a) if a else None
        self.b, self.c = pl.ds(a, b), pl.ds(a + b, c)
        self.ab, self.top_b, self.top_c = pl.ds(0, a + b), pl.ds(0, b), pl.ds(0, c)


class Named:
    def __init__(self, names, refs):
        self.__dict__.update(zip(names, refs))


class Stream:
    def __init__(self, block, buf, sem):
        self.block, self.buf, self.sem = block, buf, sem

    def copy(self, j):
        return pltpu.make_async_copy(self.block(j), self.buf.at[j % 2], self.sem.at[j % 2])

    def start(self, j):
        self.copy(j).start()

    def get(self, j, count):
        self.copy(j).wait()
        pl.when(j + 1 < count)(lambda: self.start(j + 1))
        return self.buf.at[j % 2]


BACK_IN = (
    "tokens", "dy", "innert", "inner", "first", "second", "resid", "gate", "attn", "q", "k", "v",
    "query", "key", "prefix", "normt", "norm2t", "mixedt", "gain", "w_query", "w_key", "w_value",
    "w_gate", "w_out", "w_first", "w_second", "w_third",
)
BACK_OUT = (
    "output", "dtokens", "tall", "wide", "square", "dgain",
)
BACK_SCRATCH = (
    "tbuf", "core_rx", "acc", "xa", "ya", "yb", "xb", "xc", "yc", "zab", "zc", "fin", "ssem",
    "rsem", "zss", "zrs", "osem", "csem", "crem", "ygs", "ygr", "dyv", "dfs", "dn2", "dlow",
    "dgate", "dattn", "at0", "at1", "held", "sums", "other", "dstate", "sz", "rz", "sx", "rx",
    "gacc", "gbuf", "gland", "gs", "gr", "lsem",
)


FWD_IN = (
    "tokens", "gain", "w_query", "w_key", "w_value", "w_gate", "w_out", "w_first", "w_second",
)
FWD_OUT = (
    "k", "v", "key", "normt", "q", "gate", "query", "attn", "mixedt", "resid", "norm2t", "first",
    "second", "inner", "innert", "prefix",
)
FWD_SCRATCH = (
    "xv", "gv", "wq", "wk", "wv", "wg", "wo", "w1", "w2", "nrm", "kb", "vb", "qb", "gb", "intra",
    "keyb", "queryb", "attnb", "mixb", "residb", "n2b", "firstb", "secondb", "innerb", "tb0", "tb1",
    "tb2", "innertb", "held", "sums", "other", "pre", "sz", "rz", "sx", "rx", "lsem", "xsem", "osem",
)


LAG, WAIT, GROUP = 1, 3, 2


def forward_kernel(outer, seqs, *refs):
    r = Named(FWD_IN + FWD_OUT + FWD_SCRATCH, refs)
    rows, width = r.tokens.shape
    ff = r.w_first.shape[1]
    span, pairs = rows // seqs, width // (2 * HEAD)
    blocks, per_block = rows // TILE, TILE // span
    n_scan, cut = r.sums.shape[:2]
    per_seq = pairs // cut

    k = lax.axis_index("blk")
    z, x = k // 2, k % 2
    top = outer - 1
    side = {"blk": z * 2 + 1 - x}
    above, below = {"blk": jnp.minimum(z + 1, top) * 2 + x}, {"blk": jnp.maximum(z - 1, 0) * 2 + x}
    bar = pltpu.get_barrier_semaphore()
    pl.semaphore_signal(bar, inc=1, device_id=side, device_id_type=MESH)
    pl.when(z < top)(lambda: pl.semaphore_signal(bar, inc=1, device_id=above, device_id_type=MESH))
    pl.when(z > 0)(lambda: pl.semaphore_signal(bar, inc=1, device_id=below, device_id_type=MESH))

    def span_of(start, size, step):
        return pl.ds(start if isinstance(start, int) else pl.multiple_of(start, step), size)

    def tok(j, n=TILE):
        return span_of(j * n, n, n)

    loads = [
        pltpu.make_async_copy(src, dst, r.lsem.at[n])
        for n, (src, dst) in enumerate((
            (r.w_key, r.wk), (r.w_value, r.wv), (r.w_query, r.wq), (r.w_gate, r.wg), (r.gain, r.gv),
            (r.w_out, r.wo), (r.w_first, r.w1), (r.w_second, r.w2)))
    ]

    def x_load(j):
        return pltpu.make_async_copy(r.tokens.at[tok(j)], r.xv.at[tok(j)], r.xsem.at[j])

    by_rows = dict(
        k=lambda j: r.kb.at[tok(j)], v=lambda j: r.vb.at[tok(j)], q=lambda j: r.qb.at[tok(j)],
        gate=lambda j: r.gb.at[tok(j)], key=lambda j: r.keyb, query=lambda j: r.queryb,
        attn=lambda j: r.attnb, resid=lambda j: r.residb, first=lambda j: r.firstb,
        second=lambda j: r.secondb, inner=lambda j: r.innerb)
    by_cols = dict(normt=r.tb0, mixedt=r.tb1, norm2t=r.tb2, innert=r.innertb)

    def store(name, j):
        sem = r.osem.at[FWD_OUT.index(name)]
        out = getattr(r, name)
        if name in by_rows:
            return pltpu.make_async_copy(by_rows[name](j), out.at[tok(j)], sem)
        return pltpu.make_async_copy(by_cols[name], out.at[:, tok(j)], sem)

    def free(name, j):
        pl.when(j > 0)(lambda: store(name, j - 1).wait())

    def remote(src, dst, s, t, dev):
        return pltpu.make_async_remote_copy(
            src_ref=src, dst_ref=dst, send_sem=s, recv_sem=t, device_id=dev, device_id_type=MESH)

    def along(i):
        return remote(r.sums.at[i], r.held.at[i], r.sz.at[i], r.rz.at[i], above)

    def across(i, src):
        return remote(src.at[i], r.other.at[i], r.sx.at[i], r.rx.at[i], side)

    def pass_on(i):
        pl.when(z > 0)(lambda: along(i).wait_recv())

        @pl.when(z == 0)
        def _():
            r.held[i] = jnp.zeros_like(r.held[i])

        r.sums[i] = r.held[i] + r.sums[i]
        pl.when(z < top)(lambda: along(i).start())
        pl.when(x == 0)(lambda: across(i, r.sums).start())
        pl.when(x == 1)(lambda: across(i, r.held).start())

    def finish(i):
        across(i, r.held).wait_recv()
        r.pre[i] = (r.held[i] + r.other[i]).astype(BF16)
        pl.when(z < top)(lambda: along(i).wait_send())
        across(i, r.held).wait_send()

    def scan(n):
        i = (n - LAG * z) * GROUP

        @pl.when((i >= 0) & (i < n_scan))
        def _():
            for g in range(GROUP):
                pass_on(i + g)

        @pl.when((i >= WAIT * GROUP) & (i < n_scan + WAIT * GROUP))
        def _():
            for g in range(GROUP):
                finish(i - WAIT * GROUP + g)

    def transposed(src, dst):
        for n in range(dst.shape[0] // 128):
            cols = pl.ds(n * 128, 128)
            dst[cols, :] = src[:, cols].T

    def norm_rows(value):
        return (value * lax.rsqrt(jnp.mean(value * value, axis=-1, keepdims=True) + EPS)).astype(BF16)

    def each(count, one):
        for m in range(count):
            one(m)

    def rows_of(j, m):
        return span_of(j * TILE + m * 32, 32, 32)

    def col(n):
        return span_of(n * 256, 256, 256)

    def tile_keys(j):
        x_load(j).wait()

        @pl.when(j == 0)
        def _():
            loads[0].wait()
            loads[1].wait()

        for name in ("key", "k", "v", "normt"):
            free(name, j)

        def one(m):
            r.nrm[rows_of(j, m), :] = norm_rows(r.xv[rows_of(j, m), :].astype(F32))

        each(TILE // 32, one)

        def product(n):
            key = dot(r.nrm[tok(j), :], r.wk[:, col(n)], 1, 0)
            r.keyb[:, col(n)] = key.astype(BF16)
            r.kb[tok(j), col(n)] = silu_parts(key)[0].astype(BF16)
            r.vb[tok(j), col(n)] = dot(r.nrm[tok(j), :], r.wv[:, col(n)], 1, 0).astype(BF16)

        each(width // 256, product)

        def states(m):
            s = j * per_block + m
            for p in range(pairs):
                lanes = pl.ds(p * 2 * HEAD, 2 * HEAD)
                here = tok(s, span)
                r.sums[s * per_seq + p // cut, p % cut] = pick_heads(dot(r.kb[here, lanes], r.vb[here, lanes], 0, 0))

        each(per_block, states)
        transposed(r.nrm.at[tok(j)], r.tb0)
        for name in ("key", "k", "v", "normt"):
            store(name, j).start()

    def tile_query(j):
        @pl.when(j == 0)
        def _():
            loads[2].wait()
            loads[3].wait()

        for name in ("query", "q", "gate"):
            free(name, j)

        def product(n):
            query = dot(r.nrm[tok(j), :], r.wq[:, col(n)], 1, 0)
            r.queryb[:, col(n)] = query.astype(BF16)
            r.qb[tok(j), col(n)] = silu_parts(query)[0].astype(BF16)
            r.gb[tok(j), col(n)] = dot(r.nrm[tok(j), :], r.wg[:, col(n)], 1, 0).astype(BF16)

        each(width // 256, product)
        for name in ("query", "q", "gate"):
            store(name, j).start()

    def tile_scores(s):
        causal = causal_pair(span)
        here = tok(s, span)
        for p in range(pairs):
            lanes = pl.ds(p * 2 * HEAD, 2 * HEAD)
            q, k2, v2 = r.qb[here, lanes], two_heads(r.kb[here, lanes]), two_heads(r.vb[here, lanes])
            scores = jnp.where(causal, dot(q, k2, 1, 1), 0.0).astype(BF16)
            r.intra[here, lanes] = dot(scores, v2, 1, 0)

    def tile_mixed(j, m):
        if m == 0:
            pl.when(j == 0)(lambda: loads[4].wait())
            for name in ("attn", "mixedt"):
                free(name, j)
        s = j * per_block + m
        here = tok(s, span)
        for p in range(pairs):
            lanes = pl.ds(p * 2 * HEAD, 2 * HEAD)
            prefix = two_heads(r.pre[s * per_seq + p // cut, p % cut])
            r.intra[here, lanes] = r.intra[here, lanes] + dot(r.qb[here, lanes], prefix, 1, 0)
        for n in range(m * span // 32, (m + 1) * span // 32):
            av = r.intra[rows_of(j, n), :]
            scale = lax.rsqrt(jnp.mean(av * av, axis=-1, keepdims=True) + EPS)
            act = silu_parts(r.gb[rows_of(j, n), :].astype(F32))[0]
            r.attnb[tok(n, 32), :] = av.astype(BF16)
            r.mixb[tok(n, 32), :] = (av * scale * r.gv[...] * act).astype(BF16)
        for n in range(width // 128):
            r.tb1[pl.ds(n * 128, 128), tok(m, span)] = r.mixb[tok(m, span), pl.ds(n * 128, 128)].T
        if m == per_block - 1:
            for name in ("attn", "mixedt"):
                store(name, j).start()

    def tile_resid(j):
        pl.when(j == 0)(lambda: loads[5].wait())
        for name in ("resid", "norm2t"):
            free(name, j)

        def product(n):
            r.residb[:, col(n)] = r.xv[tok(j), col(n)].astype(F32) + dot(r.mixb[...], r.wo[:, col(n)], 1, 0)

        each(width // 256, product)

        def one(m):
            r.n2b[tok(m, 32), :] = norm_rows(r.residb[tok(m, 32), :])

        each(TILE // 32, one)
        transposed(r.n2b, r.tb2)
        for name in ("resid", "norm2t"):
            store(name, j).start()

    def tile_inner(j, lo, hi):
        def one(n):
            n = n + lo
            first = dot(r.n2b[...], r.w1[:, col(n)], 1, 0)
            second = dot(r.n2b[...], r.w2[:, col(n)], 1, 0)
            inner = (first * second).astype(BF16)
            r.firstb[:, col(n)] = first.astype(BF16)
            r.secondb[:, col(n)] = second.astype(BF16)
            r.innerb[:, col(n)] = inner
            r.innertb[col(n), :] = inner.T

        each(hi - lo, one)

    half = ff // 512 * 256
    halves = (pl.ds(0, half), pl.ds(half, ff - half))

    def up_stores(j, h):
        cols = halves[h]
        sem = lambda name: r.osem.at[FWD_OUT.index(name)]
        copies = [
            pltpu.make_async_copy(by_rows[name](j).at[:, cols], getattr(r, name).at[tok(j), cols], sem(name))
            for name in ("first", "second", "inner")]
        return copies + [
            pltpu.make_async_copy(r.innertb.at[cols], r.innert.at[cols, tok(j)], sem("innert"))]

    def tile_up(j, h):
        if h == 0:
            @pl.when(j == 0)
            def _():
                loads[6].wait()
                loads[7].wait()

            for name in ("first", "second", "inner", "innert"):
                free(name, j)
        tile_inner(j, (0, half // 256)[h], (half // 256, ff // 256)[h])
        for copy in up_stores(j, h):
            copy.start()

    for n in range(2):
        x_load(n).start()
        loads[n].start()
    for n in range(2, blocks):
        x_load(n).start()
    for copy in loads[2:]:
        copy.start()
    pl.semaphore_wait(bar, 1 + jnp.where(z < top, 1, 0) + jnp.where(z > 0, 1, 0))

    per = n_scan // blocks // GROUP

    def slot(n, carry):
        pl.when(n < blocks)(lambda: tile_keys(n))

        @pl.when((n >= blocks) & (n < 2 * blocks))
        def _():
            tile_query(n - blocks)
            for m in range(per_block):
                tile_scores((n - blocks) * per_block + m)

        scan(n)
        w = n - LAG * z - WAIT - per // 2 + 1
        j, m = w // per, w % per
        live = (w >= 0) & (j < blocks)
        pl.when((w >= per) & (j <= blocks) & (m == 0))(lambda: tile_up(j - 1, 1))
        pl.when(live & (m == 0))(lambda: tile_mixed(j, 0))

        @pl.when(live & (m == 2))
        def _():
            tile_mixed(j, 1)
            tile_resid(j)

        pl.when(live & (m == 3))(lambda: tile_up(j, 0))
        return carry

    lax.fori_loop(0, n_scan // GROUP + LAG * top + WAIT + 3, slot, 0)
    whole = pltpu.make_async_copy(r.pre, r.prefix, r.osem.at[FWD_OUT.index("prefix")])
    whole.start()
    for name in FWD_OUT[:-1]:
        store(name, blocks - 1).wait()
    whole.wait()


def forward_fast(blk, seqs, tokens, weights):
    w_query, w_key, w_value, w_gate, w_out, out_gain, w_first, w_second, w_third = weights
    rows, width = tokens.shape
    ff = w_first.shape[1]
    pairs = width // (2 * HEAD)
    cut = 2
    n_scan = seqs * pairs // cut

    def v(*shape, dtype=BF16):
        return pltpu.VMEM(shape, dtype)

    def sem(*shape):
        return pltpu.SemaphoreType.DMA(shape)

    wide, tall = (rows, width), (width, ff)
    chunks = (n_scan, cut, HEAD, 2 * HEAD)
    scratch = dict(
        xv=v(*wide), gv=v(1, width, dtype=F32), wq=v(width, width), wk=v(width, width), wv=v(width, width),
        wg=v(width, width), wo=v(width, width), w1=v(*tall), w2=v(*tall), nrm=v(*wide), kb=v(*wide),
        vb=v(*wide), qb=v(*wide), gb=v(*wide), intra=v(*wide, dtype=F32), keyb=v(TILE, width),
        queryb=v(TILE, width), attnb=v(TILE, width), mixb=v(TILE, width), residb=v(TILE, width, dtype=F32),
        n2b=v(TILE, width), firstb=v(TILE, ff), secondb=v(TILE, ff), innerb=v(TILE, ff),
        tb0=v(width, TILE), tb1=v(width, TILE), tb2=v(width, TILE), innertb=v(ff, TILE),
        held=v(*chunks, dtype=F32), sums=v(*chunks, dtype=F32), other=v(*chunks, dtype=F32), pre=v(*chunks),
        sz=sem(n_scan), rz=sem(n_scan), sx=sem(n_scan), rx=sem(n_scan), lsem=sem(8),
        xsem=sem(rows // TILE), osem=sem(len(FWD_OUT)),
    )
    shapes = dict(
        normt=(width, rows), mixedt=(width, rows), norm2t=(width, rows), first=(rows, ff), second=(rows, ff),
        inner=(rows, ff), innert=(ff, rows), prefix=chunks)
    anywhere = pl.BlockSpec(memory_space=pl.ANY)
    outs = pl.pallas_call(
        functools.partial(forward_kernel, blk // 2, seqs),
        out_shape=[
            jax.ShapeDtypeStruct(shapes.get(name, wide), F32 if name == "resid" else BF16)
            for name in FWD_OUT
        ],
        in_specs=[anywhere] * len(FWD_IN),
        out_specs=[anywhere] * len(FWD_OUT),
        scratch_shapes=[scratch[name] for name in FWD_SCRATCH],
        compiler_params=pltpu.CompilerParams(
            collective_id=4, has_side_effects=True, vmem_limit_bytes=60 * MIB),
        cost_estimate=pl.CostEstimate(flops=26 * 2**30, bytes_accessed=80 * MIB, transcendentals=0),
    )(tokens, out_gain.reshape(1, width), w_query, w_key, w_value, w_gate, w_out, w_first, w_second)
    f = dict(zip(FWD_OUT, outs))
    f["prefix"] = f["prefix"].reshape(seqs, pairs, HEAD, 2 * HEAD)
    return f


def back_kernel(outer, seqs, *refs):
    r = Named(BACK_IN + BACK_OUT + BACK_SCRATCH, refs)
    rows, width = r.tokens.shape
    ff = r.first.shape[1]
    span, pairs = rows // seqs, width // (2 * HEAD)
    n_tall, n_wide, n_square = ff // 256, ff // 128, 20
    chunks = n_tall + n_wide + n_square
    at_wide, at_square = n_tall, n_tall + n_wide
    blocks = rows // TILE

    b, k = lax.axis_index("batch"), lax.axis_index("blk")
    y, c = b // 2, b % 2
    z, x = k // 2, k % 2
    ox, oy = 1 - x, 1 - y
    top = outer - 1
    zr = top - z
    to_core, to_y, to_x = {"batch": y * 2 + 1 - c}, {"batch": oy * 2 + c}, {"blk": z * 2 + ox}
    to_up = {"blk": jnp.minimum(z + 1, top) * 2 + x}
    to_down = {"blk": jnp.maximum(z - 1, 0) * 2 + x}
    to_z = [{"blk": (z + d) % outer * 2 + x} for d in range(1, outer)]

    peers = [to_core, to_y, to_x] + to_z
    bar = pltpu.get_barrier_semaphore()
    for d in peers:
        pl.semaphore_signal(bar, inc=1, device_id=d, device_id_type=MESH)

    def remote(src, dst, s, t, dev):
        return pltpu.make_async_remote_copy(
            src_ref=src, dst_ref=dst, send_sem=s, recv_sem=t, device_id=dev, device_id_type=MESH)

    def link(kind, i, src, dst, dev):
        return remote(src, dst.at[i % LAND], r.ssem.at[kind, i % LAND], r.rsem.at[kind, i % LAND], dev)

    def at(i, *where):
        return r.acc.at[(i % ACC,) + where]

    every = slice(None)

    def core_copy(i):
        return link(CORE, i, r.tbuf.at[i % 2], r.core_rx, to_core)

    def xa_copy(w, i):
        return link(XA, i, at(i, every, ox, every, w.a), r.xa, to_x)

    def ya_copy(w, i):
        return link(YA, i, at(i, every, x, oy, w.a), r.ya, to_y)

    def yb_copy(w, i):
        return link(YB, i, at(i, every, every, oy, w.b), r.yb.at[:, :, :, w.top_b], to_y)

    def xb_copy(w, i):
        return link(XB, i, at(i, every, ox, y, w.b), r.xb.at[:, :, w.top_b], to_x)

    def xc_copy(w, i):
        return link(XC, i, at(i, z, ox, every, w.c), r.xc.at[:, :, w.top_c], to_x)

    def yc_copy(w, i):
        return link(YC, i, at(i, z, x, oy, w.c), r.yc.at[:, w.top_c], to_y)

    def y_share(i):
        f = i % FIN
        return remote(r.fin.at[f, y], r.fin.at[f, y], r.ygs.at[f], r.ygr.at[f], to_y)

    def part_ab(w, i, s):
        return at(i, s, x, y, w.ab)

    def part_c(w, i, s):
        return at(i, s, every, every, w.c)

    def land_ab(w, i, d, n):
        return r.zab.at[i % LAND, d, n - 1, w.ab]

    def land_c(w, i, d, n):
        return r.zc.at[i % LAND, d, n - 1, :, :, w.top_c]

    AB, CC = (0, part_ab, land_ab), (1, part_c, land_c)

    def hop(group, w, i, n, up, s):
        g, part, land = group
        d = 0 if up else 1
        sem = (g, d, n - 1, i % LAND)
        return remote(part(w, i, s), land(w, i, d, n), r.zss.at[sem], r.zrs.at[sem],
                      to_up if up else to_down)

    def z_each(group, w, i, n, act):
        up = hop(group, w, i, n, True, jnp.minimum(outer - n + z, top))
        down = hop(group, w, i, n, False, jnp.maximum(n - 1 - zr, 0))
        pl.when((z <= n - 1) & (z < top))(lambda: act(up))
        pl.when((zr <= n - 1) & (z > 0))(lambda: act(down))

    def z_send(group, w, i, n):
        z_each(group, w, i, n, lambda copy: copy.start())

    def z_sent(group, w, i, n):
        z_each(group, w, i, n, lambda copy: copy.wait_send())

    def add(ref, landed):
        ref[...] = ref[...] + landed[...]

    def z_take(group, w, i, n):
        g, part, land = group

        def take(up, s):
            hop(group, w, i, n, up, s).wait_recv()
            add(part(w, i, s), land(w, i, 0 if up else 1, n))

        pl.when((z > 0) & (z <= n))(lambda: take(True, jnp.clip(outer - n + z - 1, 0, top)))
        pl.when((z < top) & (zr <= n))(lambda: take(False, jnp.clip(n - zr, 0, top)))

    BOTH = (Way(32, 16, 16), Way(0, 56, 8))
    spare = (at_wide + SPARE[0], at_wide + SPARE[1])

    def places(i, act):
        f = r.fin.at[i % FIN]

        @pl.when(i < at_wide)
        def _():
            for yy in range(2):
                for blk in range(2):
                    col = pl.multiple_of(c * (width // 2) + (yy * 2 + blk) * 128, 128)
                    act(f.at[yy, pl.ds(blk * 32, 32)], r.tall.at[pl.ds(i * 32, 32), pl.ds(col, 128)])

        @pl.when((i >= at_wide) & (i < at_square))
        def _():
            j, h = (i - at_wide) // 2, (i - at_wide) % 2
            col = pl.multiple_of(c * (ff // 2) + j * 128, 128)
            for yy in range(2):
                act(f.at[yy], r.wide.at[yy, pl.ds(h * 64, 64), pl.ds(col, 128)])

        @pl.when(i >= at_square)
        def _():
            j = i - at_square
            m, u, h = j // 4, j // 2 % 2, j % 2
            for yy in range(2):
                col = pl.multiple_of(c * (width // 2) + u * 256 + yy * 128, 128)
                act(f.at[yy], r.square.at[m, pl.ds(h * 64, 64), pl.ds(col, 128)])

    def cores(w, i):
        core_copy(i).wait_recv()
        core_copy(i).wait_send()
        add(at(i), r.core_rx.at[i % LAND])
        if w.a is not None:
            xa_copy(w, i).start()
        yb_copy(w, i).start()
        z_send(CC, w, i, 1)

    def second(w, i):
        yb_copy(w, i).wait_recv()
        add(at(i, every, every, y, w.b), r.yb.at[i % LAND, :, :, w.top_b])
        xb_copy(w, i).start()
        if w.a is not None:
            xa_copy(w, i).wait_recv()
            add(at(i, every, x, every, w.a), r.xa.at[i % LAND])
            ya_copy(w, i).start()
        z_take(CC, w, i, 1)
        z_send(CC, w, i, 2)
        if w.a is not None:
            xa_copy(w, i).wait_send()
        yb_copy(w, i).wait_send()
        z_sent(CC, w, i, 1)

    def third(w, i):
        xb_copy(w, i).wait_recv()
        add(at(i, every, x, y, w.b), r.xb.at[i % LAND, :, w.top_b])
        if w.a is not None:
            ya_copy(w, i).wait_recv()
            add(at(i, every, x, y, w.a), r.ya.at[i % LAND])
        z_send(AB, w, i, 1)
        z_take(CC, w, i, 2)
        z_send(CC, w, i, 3)
        xb_copy(w, i).wait_send()
        if w.a is not None:
            ya_copy(w, i).wait_send()
        z_sent(CC, w, i, 2)

    def fourth(w, i):
        z_take(AB, w, i, 1)
        z_send(AB, w, i, 2)
        z_take(CC, w, i, 3)
        xc_copy(w, i).start()
        z_sent(AB, w, i, 1)
        z_sent(CC, w, i, 3)

    def fifth(w, i):
        z_take(AB, w, i, 2)
        z_send(AB, w, i, 3)
        xc_copy(w, i).wait_recv()
        add(at(i, z, x, every, w.c), r.xc.at[i % LAND, :, w.top_c])
        yc_copy(w, i).start()
        z_sent(AB, w, i, 2)
        xc_copy(w, i).wait_send()

    def sixth(w, i):
        yc_copy(w, i).wait_recv()
        z_take(AB, w, i, 3)
        f = i % FIN
        r.fin[f, y, w.ab] = r.acc[i % ACC, z, x, y, w.ab]
        r.fin[f, y, w.c] = r.acc[i % ACC, z, x, y, w.c] + r.yc[i % LAND, w.top_c]
        y_share(i).start()
        z_sent(AB, w, i, 3)
        yc_copy(w, i).wait_send()

    def seventh(w, i):
        y_share(i).wait_recv()
        y_share(i).wait_send()
        f = i % FIN

        def go(src, dst):
            remote(src, dst, r.csem.at[f], r.crem.at[f], to_core).start()
            pltpu.make_async_copy(src, dst, r.osem.at[f]).start()

        places(i, go)

    def last(w, i):
        f = i % FIN
        whole = r.fin.at[f]
        copy = remote(whole, whole, r.csem.at[f], r.crem.at[f], to_core)
        copy.wait_send()
        copy.wait_recv()
        pltpu.make_async_copy(whole, whole, r.osem.at[f]).wait()

    ORDER = range(2, 9)
    stages = (None, cores, second, third, fourth, fifth, sixth, seventh, last)

    def advance(t, some, ways):
        for n in some:
            i = t - n
            live = (i >= 0) & (i < chunks)
            if n >= 7 or len(ways) == 1:
                pl.when(live)(functools.partial(stages[n], ways[0], i))
            else:
                spared = (i >= spare[0]) & (i < spare[1])
                pl.when(live & ~spared)(functools.partial(stages[n], ways[0], i))
                pl.when(spared)(functools.partial(stages[n], ways[1], i))

    def send_first(t, ways=BOTH):
        advance(t, (1,), ways)

    def move(t, ways=BOTH):
        advance(t, ORDER, ways)

    def make(t, fill):
        fill(1 - c, r.tbuf.at[t % 2])
        core_copy(t).start()
        fill(c, r.acc.at[t % ACC])

    def fill_tall(lhs):
        def fill(half, dst):
            for yy in range(2):
                col = pl.multiple_of(half * (width // 2) + yy * 256, 256)
                res = dot(lhs, r.dyv[:, pl.ds(col, 256)], 1, 0).reshape(4, 2, 32, 256)
                for blk in range(2):
                    dst[:, :, yy, pl.ds(blk * 32, 32), :] = res[..., blk * 128:(blk + 1) * 128]
        return fill

    def left_rows(ref, h):
        return ref[:, h].reshape(8 * 64, rows)

    def fill_two(left, h, take):
        def fill(half, dst):
            res = dot(left_rows(left, h), take(half), 1, 0).reshape(4, 2, 64, 256)
            dst[:, :, 0] = res[..., :128]
            dst[:, :, 1] = res[..., 128:]
        return fill

    def make_wide(t):
        i = t - at_wide
        j, h = i // 2, i % 2

        def take(half):
            col = pl.ds(pl.multiple_of(half * (ff // 2) + j * 128, 128), 128)
            return jnp.concatenate([r.dfs[0, :, col], r.dfs[1, :, col]], axis=1)

        make(t, fill_two(r.at0, h, take))

    def make_square(t, base, left, right):
        i = t - base
        u, h = i // 2, i % 2

        def take(half):
            return right(pl.ds(pl.multiple_of(half * (width // 2) + u * 256, 256), 256))

        make(t, fill_two(left, h, take))

    zz, xx = zr, ox
    n_scan = r.sums.shape[0]
    halves = n_scan // seqs
    scan_at = at_wide

    def along(i):
        return remote(r.sums.at[i], r.held.at[i], r.sz.at[i], r.rz.at[i], to_down)

    def across(i, src):
        return remote(src.at[i], r.other.at[i], r.sx.at[i], r.rx.at[i], to_x)

    def pass_on(i):
        pl.when(zz > 0)(lambda: along(i).wait_recv())

        @pl.when(zz == 0)
        def _():
            r.held[i] = jnp.zeros_like(r.held[i])

        r.sums[i] = r.held[i] + r.sums[i]
        pl.when(zz < top)(lambda: along(i).start())
        pl.when(xx == 0)(lambda: across(i, r.sums).start())
        pl.when(xx == 1)(lambda: across(i, r.held).start())

    def finish(i):
        across(i, r.held).wait_recv()
        r.dstate[i] = (r.held[i] + r.other[i]).astype(BF16)
        pl.when(zz < top)(lambda: along(i).wait_send())
        across(i, r.held).wait_send()

    def scan(t):
        i = t - scan_at - zz
        pl.when((i >= 0) & (i < n_scan))(lambda: pass_on(i))
        pl.when((i >= 2) & (i < n_scan + 2))(lambda: finish(i - 2))

    def span_of(start, size, step):
        return pl.ds(start if isinstance(start, int) else pl.multiple_of(start, step), size)

    def tok(j, n=TILE):
        return span_of(j * n, n, n)

    def tile_inner(j, w3, w1, w2, first, second):
        def block(m, carry):
            at_rows = tok(m, 512)
            din = dot(r.dyv[at_rows, :], w3[...], 1, 1)
            one = (din * second[at_rows, :].astype(F32)).astype(BF16)
            two = (din * first[at_rows, :].astype(F32)).astype(BF16)
            cols = pl.ds(pl.multiple_of(j * 256, 256), 256)
            r.dfs[0, at_rows, cols] = one
            r.dfs[1, at_rows, cols] = two
            for n in range(width // 256):
                to = pl.ds(n * 256, 256)
                res = dot(one, w1[to, :], 1, 1) + dot(two, w2[to, :], 1, 1)
                r.dn2[at_rows, to] = r.dn2[at_rows, to] + res
            return carry

        for m in range(rows // 512):
            block(m, 0)

    def tile_resid(j, resid, gate, attn, q, w_out, gain, dmix):
        def one(m, carry):
            here, sub = pl.ds(pl.multiple_of(j * TILE + m * 32, 32), 32), tok(m, 32)
            value = resid[sub, :]
            grad = r.dn2[here, :]
            scale = lax.rsqrt(jnp.mean(value * value, axis=-1, keepdims=True) + EPS)
            out = r.dyv[here, :].astype(F32) + norm_back(grad, value, scale)
            r.dn2[here, :] = out
            r.dlow[here, :] = out.astype(BF16)
            return carry

        for m in range(TILE // 32):
            one(m, 0)
        for n in range(width // 256):
            to = pl.ds(n * 256, 256)
            dmix[:, to] = dot(r.dlow[tok(j), :], w_out[to, :], 1, 1)

        def two(m, carry):
            here, sub = pl.ds(pl.multiple_of(j * TILE + m * 32, 32), 32), tok(m, 32)
            av = attn[sub, :].astype(F32)
            scale = lax.rsqrt(jnp.mean(av * av, axis=-1, keepdims=True) + EPS)
            unit = av * scale
            act, der = silu_parts(gate[sub, :].astype(F32))
            dm = dmix[sub, :]
            ds = dm * act
            r.dgate[here, :] = (dm * (unit * gain[...]) * der).astype(BF16)
            r.gacc[...] = r.gacc[...] + jnp.sum((ds * unit).reshape(4, 8, width), axis=0)
            r.dattn[here, :] = norm_back(ds * gain[...], av, scale).astype(BF16)
            return carry

        for m in range(TILE // 32):
            two(m, 0)

        def states(m, carry):
            s = j * (TILE // span) + m
            for p in range(pairs):
                lanes = pl.ds(p * 2 * HEAD, 2 * HEAD)
                grad = r.dattn[tok(s, span), lanes]
                per = pairs // halves
                r.sums[s * halves + p // per, p % per] = pick_heads(dot(q[tok(m, span), lanes], grad, 0, 0))
            return carry

        for m in range(TILE // span):
            states(m, 0)

    def tile_attn(s, q_ref, k_ref, v_ref, query, key, prefix_ref):
        causal = causal_pair(span)
        here = tok(s, span)
        for p in range(pairs):
            lanes = pl.ds(p * 2 * HEAD, 2 * HEAD)
            q, k, v, g = q_ref[:, lanes], k_ref[:, lanes], v_ref[:, lanes], r.dattn[here, lanes]
            k2, v2 = two_heads(k), two_heads(v)
            per = pairs // halves
            prefix, dstate = two_heads(prefix_ref[p]), two_heads(r.dstate[s * halves + p // per, p % per])
            scores = jnp.where(causal, dot(q, k2, 1, 1), 0.0).astype(BF16)
            dscores = jnp.where(causal, dot(g, v2, 1, 1), 0.0).astype(BF16)
            dq = dot(dscores, k2, 1, 0) + dot(g, prefix, 1, 1)
            dk = pick_heads(dot(dscores, q, 0, 0)) + dot(v, dstate, 1, 1)
            dv = pick_heads(dot(scores, g, 0, 0)) + dot(k, dstate, 1, 0)
            r.dfs[0, here, lanes] = (dq * silu_parts(query[:, lanes].astype(F32))[1]).astype(BF16)
            r.dfs[0, here, pl.ds(width + p * 2 * HEAD, 2 * HEAD)] = (
                dk * silu_parts(key[:, lanes].astype(F32))[1]).astype(BF16)
            r.dfs[1, here, lanes] = dv.astype(BF16)

    parts = [
        lambda at_rows, cols: r.dfs[0, at_rows, cols],
        lambda at_rows, cols: r.dfs[0, at_rows, pl.ds(width + cols.start, cols.size)],
        lambda at_rows, cols: r.dfs[1, at_rows, cols],
    ]
    dq_cols = lambda cols: r.dfs[0, :, cols]
    dk_cols = lambda cols: r.dfs[0, :, pl.ds(width + cols.start, cols.size)]
    dv_cols = lambda cols: r.dfs[1, :, cols]

    def load(src, dst, n):
        return pltpu.make_async_copy(src, dst, r.lsem.at[n])

    def dma(*shape):
        return pltpu.SemaphoreType.DMA(shape)

    def ring(shape, dtype):
        return pltpu.VMEM((2,) + shape, dtype)

    def steps(count, one):
        def go(j, carry):
            one(j)
            return carry

        lax.fori_loop(0, count, go, 0)

    dy_load = load(r.dy, r.dyv, 0)
    norm2_load = load(r.norm2t, r.at0, 1)
    mixed_load = load(r.mixedt, r.at1, 2)
    norm_load = load(r.normt, r.at0, 3)

    def segment0(left, w3, w1, w2, first, second, sems):
        cols = lambda ref: lambda j: ref.at[:, pl.ds(pl.multiple_of(j * 256, 256), 256)]
        s_left = Stream(lambda j: r.innert.at[:, pl.ds(pl.multiple_of(j * 32, 32), 32)], left, sems.at[0])
        tiles = [
            Stream(lambda j: r.w_third.at[pl.ds(pl.multiple_of(j * 256, 256), 256)], w3, sems.at[1]),
            Stream(cols(r.w_first), w1, sems.at[2]),
            Stream(cols(r.w_second), w2, sems.at[3]),
            Stream(cols(r.first), first, sems.at[4]),
            Stream(cols(r.second), second, sems.at[5]),
        ]
        dy_load.start()
        s_left.start(0)
        for s in tiles:
            s.start(0)
        norm2_load.start()
        r.dn2[...] = jnp.zeros_like(r.dn2)
        r.gacc[...] = jnp.zeros_like(r.gacc)
        dy_load.wait()
        pl.semaphore_wait(bar, len(peers))

        def one(j):
            send_first(j, BOTH[:1])
            make(j, fill_tall(s_left.get(j, n_tall)[...].reshape(8 * 32, rows)))
            tile_inner(j, *(s.get(j, n_tall) for s in tiles))
            move(j, BOTH[:1])

        steps(n_tall, one)
        norm2_load.wait()

    pl.run_scoped(
        segment0, ring((8, 32, rows), BF16), ring((256, width), BF16), ring((width, 256), BF16),
        ring((width, 256), BF16), ring((rows, 256), BF16), ring((rows, 256), BF16), dma(6, 2))

    def segment1(resid, gate, attn, q, w_out, gain, dmix, sems, wsem):
        blk = lambda ref: lambda j: ref.at[tok(j)]
        tiles = [
            Stream(blk(ref), buf, sems.at[n])
            for n, (ref, buf) in enumerate(((r.resid, resid), (r.gate, gate), (r.attn, attn), (r.q, q)))
        ]
        w_load = pltpu.make_async_copy(r.w_out, w_out, wsem.at[0])
        g_load = pltpu.make_async_copy(r.gain, gain, wsem.at[1])
        w_load.start()
        g_load.start()
        for s in tiles:
            s.start(0)
        w_load.wait()
        g_load.wait()

        def one(j):
            t = at_wide + j
            send_first(t)
            make_wide(t)
            rs, ga, at_, qs = (s.get(j, blocks) for s in tiles)
            tile_resid(j, rs, ga, at_, qs, w_out, gain, dmix)
            move(t)
            scan(t)

        steps(blocks, one)

    pl.run_scoped(
        segment1, ring((TILE, width), F32), ring((TILE, width), BF16), ring((TILE, width), BF16),
        ring((TILE, width), BF16), pltpu.VMEM((width, width), BF16), pltpu.VMEM((1, width), F32),
        pltpu.VMEM((TILE, width), F32), dma(4, 2), dma(2))

    def gain_sum(t):
        base = at_wide + blocks
        hops = [to_core, to_y, to_x]

        def swap(n):
            return remote(r.gbuf, r.gland.at[n], r.gs.at[n], r.gr.at[n], hops[n])

        def spread(d):
            return remote(r.gbuf, r.gland.at[2 + d], r.gs.at[2 + d], r.gr.at[2 + d], to_z[d - 1])

        @pl.when(t == base)
        def _():
            total = jnp.sum(r.gacc[...], axis=0, keepdims=True)
            for n in range(8):
                r.gbuf[pl.ds(n, 1), :] = total[:, n * 128:(n + 1) * 128]
            swap(0).start()

        for n in range(3):
            @pl.when(t == base + 2 + 2 * n)
            def _(n=n):
                swap(n).wait()
                r.gbuf[...] = r.gbuf[...] + r.gland[n]
                if n < 2:
                    swap(n + 1).start()
                else:
                    for d in range(1, outer):
                        spread(d).start()

        @pl.when(t == base + 8)
        def _():
            for d in range(1, outer):
                spread(d).wait()
            for d in range(1, outer):
                r.gbuf[...] = r.gbuf[...] + r.gland[2 + d]
            pltpu.make_async_copy(r.gbuf, r.dgain, r.lsem.at[4]).start()

        pl.when(t == base + 10)(lambda: pltpu.make_async_copy(r.gbuf, r.dgain, r.lsem.at[4]).wait())

    n2 = n_wide - blocks
    n_out = blocks * (width // 256)

    def segment2(w3, inner, resid, out, sems, osem):
        per = width // 256
        cols = lambda j: pl.ds(pl.multiple_of(j % per * 256, 256), 256)
        s_w3 = Stream(lambda j: r.w_third.at[:, cols(j)], w3, sems.at[0])
        s_resid = Stream(lambda j: r.resid.at[tok(j // per), cols(j)], resid, sems.at[1])
        s_inner = Stream(lambda n: r.inner.at[tok(n)], inner, sems.at[2])

        def store(j):
            return pltpu.make_async_copy(out.at[j % 2], r.output.at[tok(j // per), cols(j)], osem.at[j % 2])

        mixed_load.start()
        for s in (s_w3, s_resid, s_inner):
            s.start(0)

        def one(j):
            t = at_wide + blocks + j
            send_first(t)
            make_wide(t)

            @pl.when(j < n_out)
            def _():
                w, res = s_w3.get(j, n_out), s_resid.get(j, n_out)

                @pl.when(j % per == 0)
                def _():
                    s_inner.get(j // per, blocks)

                pl.when(j >= 2)(lambda: store(j - 2).wait())
                prod = dot(inner[j // per % 2], w[...], 1, 0)
                out[j % 2] = (res[...] + prod).astype(BF16)
                store(j).start()

            move(t)
            scan(t)
            gain_sum(t)

        steps(n2, one)
        store(n_out - 2).wait()
        store(n_out - 1).wait()
        mixed_load.wait()

    pl.run_scoped(
        segment2, ring((ff, 256), BF16), ring((TILE, ff), BF16), ring((TILE, 256), F32),
        ring((TILE, 256), BF16), dma(3, 2), dma(2))

    def segment3(q, k, v, query, key, prefix, sems):
        blk = lambda ref: lambda j: ref.at[tok(j, span)]
        tiles = [
            Stream(blk(ref), buf, sems.at[n])
            for n, (ref, buf) in enumerate(((r.q, q), (r.k, k), (r.v, v), (r.query, query), (r.key, key)))
        ]
        tiles.append(Stream(lambda j: r.prefix.at[j], prefix, sems.at[5]))
        norm_load.start()
        for s in tiles:
            s.start(0)

        def one(j):
            t = at_square + j
            send_first(t)
            pl.when(j < 4)(lambda: make_square(t, at_square, r.at1, lambda cols: r.dlow[:, cols]))
            pl.when(j == 4)(lambda: norm_load.wait())
            pl.when(j >= 4)(lambda: make_square(t, at_square + 4, r.at0, lambda cols: r.dgate[:, cols]))
            tile_attn(j, *(s.get(j, seqs) for s in tiles))
            move(t)

        steps(8, one)

    pl.run_scoped(
        segment3, *[ring((span, width), BF16)] * 5, ring((pairs, HEAD, 2 * HEAD), BF16), dma(6, 2))

    def segment4(wq, wk, wv, wg, total, xs, out, sems, xsem, osem):
        nn = width // 256
        rowsblk = lambda ref: lambda n: ref.at[pl.ds(pl.multiple_of(n * 256, 256), 256)]
        weights = [
            Stream(rowsblk(ref), buf, sems.at[n])
            for n, (ref, buf) in enumerate(
                ((r.w_query, wq), (r.w_key, wk), (r.w_value, wv), (r.w_gate, wg)))
        ]
        s_x = Stream(lambda j: r.tokens.at[tok(j)], xs, xsem)
        for s in weights:
            s.start(0)
        s_x.start(0)

        def product(j):
            n, m = j // 2, j % 2
            slot = n % 2

            @pl.when(m == 0)
            def _():
                for s in weights:
                    s.get(n, nn)

            here = tok(m, rows // 2)
            full = pl.ds(0, width)
            res = dot(r.dgate[here, :], wg[slot], 1, 1)
            for part, w in zip(parts, (wq, wk, wv)):
                res = res + dot(part(here, full), w[slot], 1, 1)
            total[here, pl.ds(pl.multiple_of(n * 256, 256), 256)] = res

        def store(j):
            return pltpu.make_async_copy(out.at[j % 2], r.dtokens.at[tok(j)], osem.at[j % 2])

        def finish_rows(j):
            xb = s_x.get(j, blocks)
            pl.when(j >= 2)(lambda: store(j - 2).wait())

            def one(m, carry):
                here, sub = pl.ds(pl.multiple_of(j * TILE + m * 32, 32), 32), tok(m, 32)
                xv = xb[sub, :].astype(F32)
                scale = lax.rsqrt(jnp.mean(xv * xv, axis=-1, keepdims=True) + EPS)
                out[j % 2, sub, :] = r.dn2[here, :] + norm_back(total[here, :], xv, scale)
                return carry

            for m in range(TILE // 32):
                one(m, 0)
            store(j).start()

        def one(j):
            t = at_square + 8 + j
            send_first(t, BOTH[:1])
            pl.when(j < 4)(lambda: make_square(t, at_square + 8, r.at0, dq_cols))
            pl.when((j >= 4) & (j < 8))(lambda: make_square(t, at_square + 12, r.at0, dk_cols))
            pl.when(j >= 8)(lambda: make_square(t, at_square + 16, r.at0, dv_cols))
            pl.when(j < 2 * nn)(lambda: product(j))
            pl.when(j >= 2 * nn)(lambda: finish_rows(j - 2 * nn))
            move(t, BOTH[:1])

        steps(12, one)
        store(blocks - 2).wait()
        store(blocks - 1).wait()

    pl.run_scoped(
        segment4, *[ring((256, width), BF16)] * 4, pltpu.VMEM((rows, width), F32),
        ring((TILE, width), BF16), ring((TILE, width), F32), dma(4, 2), dma(2), dma(2))

    def rest(j):
        send_first(chunks + j, BOTH[:1])
        move(chunks + j, BOTH[:1])

    steps(len(stages) - 1, rest)


def back(args, seqs, blk):
    rows, width = args["tokens"].shape
    ff = args["first"].shape[1]
    pairs = width // (2 * HEAD)
    anywhere = pl.BlockSpec(memory_space=pl.ANY)
    cut = 4

    def v(*shape, dtype=F32):
        return pltpu.VMEM(shape, dtype)

    def sem(*shape):
        return pltpu.SemaphoreType.DMA(shape)

    n_scan = seqs * 2
    chunk = (4, 2, 2, 64, 128)
    scratch = dict(
        tbuf=v(2, *chunk), core_rx=v(LAND, *chunk), acc=v(ACC, *chunk), xa=v(LAND, 4, 2, 32, 128),
        ya=v(LAND, 4, 32, 128), yb=v(LAND, 4, 2, 56, 128), xb=v(LAND, 4, 56, 128),
        xc=v(LAND, 2, 16, 128), yc=v(LAND, 16, 128), zab=v(LAND, 2, 3, 56, 128),
        zc=v(LAND, 2, 3, 2, 2, 16, 128), fin=v(FIN, 2, 64, 128),
        ssem=sem(7, LAND), rsem=sem(7, LAND), zss=sem(2, 2, 3, LAND), zrs=sem(2, 2, 3, LAND),
        osem=sem(FIN), csem=sem(FIN), crem=sem(FIN), ygs=sem(FIN), ygr=sem(FIN),
        dyv=v(rows, width, dtype=BF16), dfs=v(2, rows, ff, dtype=BF16), dn2=v(rows, width),
        dlow=v(rows, width, dtype=BF16), dgate=v(rows, width, dtype=BF16),
        dattn=v(rows, width, dtype=BF16), at0=v(8, 2, 64, rows, dtype=BF16),
        at1=v(8, 2, 64, rows, dtype=BF16), held=v(n_scan, cut, HEAD, 128), sums=v(n_scan, cut, HEAD, 128),
        other=v(n_scan, cut, HEAD, 128), dstate=v(n_scan, cut, HEAD, 128, dtype=BF16),
        sz=sem(n_scan), rz=sem(n_scan), sx=sem(n_scan), rx=sem(n_scan),
        gacc=v(8, width), gbuf=v(8, 128), gland=v(6, 8, 128), gs=sem(6), gr=sem(6), lsem=sem(5),
    )
    args = dict(args)
    args["innert"] = args["innert"].reshape(8, ff // 8, rows)
    for name in ("normt", "norm2t", "mixedt"):
        args[name] = args[name].reshape(8, 2, 64, rows)
    args["gain"] = args["gain"].reshape(1, width)
    outs = dict(
        output=((rows, width), BF16), dtokens=((rows, width), F32), tall=((ff // 8, width), F32),
        wide=((2, width // 8, ff), F32), square=((5, width // 8, width), F32), dgain=((8, 128), F32),
    )
    return pl.pallas_call(
        functools.partial(back_kernel, blk // 2, seqs),
        out_shape=[jax.ShapeDtypeStruct(*outs[name]) for name in BACK_OUT],
        in_specs=[anywhere] * len(BACK_IN),
        out_specs=[anywhere] * len(BACK_OUT),
        scratch_shapes=[scratch[name] for name in BACK_SCRATCH],
        compiler_params=pltpu.CompilerParams(
            collective_id=3, has_side_effects=True, vmem_limit_bytes=60 * MIB),
        cost_estimate=pl.CostEstimate(flops=60 * 2**30, bytes_accessed=200 * MIB, transcendentals=0),
    )(*(args[name] for name in BACK_IN))


def rms(value):
    return lax.rsqrt(jnp.mean(value * value, axis=-1, keepdims=True) + EPS)


def forward(blk, seqs, xf, weights):
    w_query, w_key, w_value, w_gate, w_out, out_gain, w_first, w_second, w_third = weights
    normed = (xf * rms(xf)).astype(BF16)
    key = project(normed, w_key)
    value = project(normed, w_value)
    k, v = silu_parts(key)[0].astype(BF16), value.astype(BF16)
    prefix = entering(local_states(k, v, seqs), blk, False)
    query = project(normed, w_query)
    gate = project(normed, w_gate)
    q = silu_parts(query)[0].astype(BF16)
    attn = attention(q, k, v, prefix, seqs)
    mixed = (attn * rms(attn) * out_gain * silu_parts(gate)[0]).astype(BF16)
    resid = xf + project(mixed, w_out)
    normed2 = (resid * rms(resid)).astype(BF16)
    first = project(normed2, w_first)
    second = project(normed2, w_second)
    inner = (first * second).astype(BF16)
    return dict(
        normed=normed, query=query, key=key, gate=gate, q=q, k=k, v=v, prefix=prefix, attn=attn,
        mixed=mixed, resid=resid, normed2=normed2, first=first, second=second, inner=inner)


def backward_plain(blk, seqs, xf, grad_top, f, weights):
    w_query, w_key, w_value, w_gate, w_out, out_gain, w_first, w_second, w_third = weights
    output = (f["resid"] + project(f["inner"], w_third)).astype(BF16)
    grad_w3 = weight_grad(f["inner"], grad_top)
    grad_inner = back_project(grad_top, w_third)
    grad_one = (grad_inner * f["second"]).astype(BF16)
    grad_two = (grad_inner * f["first"]).astype(BF16)
    grad_w1 = weight_grad(f["normed2"], grad_one)
    grad_w2 = weight_grad(f["normed2"], grad_two)
    grad_normed2 = back_project(grad_one, w_first) + back_project(grad_two, w_second)
    resid, attn = f["resid"], f["attn"]
    grad_resid = grad_top.astype(F32) + norm_back(grad_normed2, resid, rms(resid))
    grad_resid_low = grad_resid.astype(BF16)
    grad_wo = weight_grad(f["mixed"], grad_resid_low)
    grad_mixed = back_project(grad_resid_low, w_out)
    gate_act, gate_der = silu_parts(f["gate"])
    rattn = rms(attn)
    unit_attn = attn * rattn
    grad_scaled = grad_mixed * gate_act
    grad_gate_low = (grad_mixed * (unit_attn * out_gain) * gate_der).astype(BF16)
    grad_gain = jnp.sum(grad_scaled * unit_attn, axis=0)
    grad_attn = norm_back(grad_scaled * out_gain, attn, rattn).astype(BF16)
    q, k, v, prefix = f["q"], f["k"], f["v"], f["prefix"]
    dstate = entering(local_states(q, grad_attn, seqs), blk, True)
    grad_fq, grad_fk, grad_vv = attention_back(q, k, v, grad_attn, prefix, dstate, seqs)
    grad_query_low = (grad_fq * silu_parts(f["query"])[1]).astype(BF16)
    grad_key_low = (grad_fk * silu_parts(f["key"])[1]).astype(BF16)
    grad_value_low = grad_vv.astype(BF16)
    normed = f["normed"]
    grads = [weight_grad(normed, g) for g in (grad_query_low, grad_key_low, grad_value_low, grad_gate_low)]
    grads += [grad_wo, grad_gain, grad_w1, grad_w2, grad_w3]
    grad_normed = back_project(grad_query_low, w_query) + back_project(grad_key_low, w_key)
    grad_normed = (
        grad_normed + back_project(grad_value_low, w_value) + back_project(grad_gate_low, w_gate)
    )
    grad_input = grad_resid + norm_back(grad_normed, xf, rms(xf))
    summed = [
        lax.psum(lax.psum_scatter(g, "blk", scatter_dimension=0, tiled=True), "batch") for g in grads]
    return output, grad_input, summed


WEIGHTS = (
    "w_query", "w_key", "w_value", "w_gate", "w_out", "gain", "w_first", "w_second", "w_third",
)


def laid_out(output, grad_input, tall, wide, square, dgain):
    arrays = (output, grad_input, tall, wide, square, dgain)
    squares, wides = square.shape[0], wide.shape[0]
    shapes = [square.shape[1:]] * squares + [wide.shape[1:]] * wides + [(1, dgain.shape[1])]
    types = [F32] * len(shapes) + [output.dtype, grad_input.dtype, F32]
    shapes += [output.shape, grad_input.shape, tall.shape]
    cuts = [2] * squares + [4] * wides + [1, 4, 8, 4]

    def kernel(output, grad_input, tall, wide, square, dgain, *rest):
        outs, bufs = rest[:len(shapes)], rest[len(shapes):2 * len(shapes)]
        sem_in, sem_out = rest[2 * len(shapes):]
        k = lax.axis_index("blk")
        ins = [square.at[n] for n in range(squares)] + [wide.at[n] for n in range(wides)]
        ins += [dgain.at[pl.ds(k, 1)], output, grad_input, tall]
        loads, stores = [], []
        for src, buf, dst, cut in zip(ins, bufs, outs, cuts):
            step = dst.shape[0] // cut
            for n in range(cut):
                part = pl.ds(n * step, step)
                m = len(loads)
                loads.append(pltpu.make_async_copy(src.at[part], buf.at[part], sem_in.at[m]))
                stores.append(pltpu.make_async_copy(buf.at[part], dst.at[part], sem_out.at[m]))
        for copy in loads:
            copy.start()
        for load, store in zip(loads, stores):
            load.wait()
            store.start()
        for copy in stores:
            copy.wait()

    anywhere = pl.BlockSpec(memory_space=pl.ANY)
    outs = pl.pallas_call(
        kernel,
        out_shape=[jax.ShapeDtypeStruct(*of) for of in zip(shapes, types)],
        in_specs=[anywhere] * len(arrays),
        out_specs=[anywhere] * len(shapes),
        scratch_shapes=[pltpu.VMEM(*of) for of in zip(shapes, types)]
        + [pltpu.SemaphoreType.DMA((sum(cuts),))] * 2,
        compiler_params=pltpu.CompilerParams(vmem_limit_bytes=60 * MIB),
    )(*arrays)
    return outs[:squares], outs[squares:squares + wides], *outs[squares + wides:]


def backward(blk, seqs, tokens, grad_top, f, weights):
    names = WEIGHTS
    args = dict(zip(names, weights), tokens=tokens, dy=grad_top)
    args.update(f)
    output, grad_input, tall, wide, square, dgain = back(args, seqs, blk)
    (so, sg, sq, sk, sv), (s1, s2), sgain, output, grad_input, tall = laid_out(
        output, grad_input, tall, wide, square, dgain)
    return output, grad_input, [sq, sk, sv, sg, so, sgain.reshape(-1), s1, s2, tall]


def body(sizes, tokens, cotangent, *weights):
    batch, blk = sizes
    seqs, span, width = tokens.shape
    rows = seqs * span
    low = tokens.reshape(rows, width)
    xf = low.astype(F32)
    grad_top = cotangent.reshape(rows, width)
    ff = weights[-1].shape[0]
    if (batch, blk, rows, span, width, ff % 256) == (4, 8, 1024, 128, 1024, 0):
        f = forward_fast(blk, seqs, low, weights)
        output, grad_input, grads = backward(blk, seqs, low, grad_top, f, weights)
    else:
        f = forward(blk, seqs, xf, weights)
        output, grad_input, grads = backward_plain(blk, seqs, xf, grad_top, f, weights)
    shape = (seqs, span, width)
    return (output.reshape(shape), grad_input.reshape(shape), *grads)


def solution(mesh):
    rows = P("batch", "blk", None)
    cut = P("blk", None)
    return jax.shard_map(
        functools.partial(body, (mesh.shape["batch"], mesh.shape["blk"])),
        mesh=mesh,
        in_specs=(rows, rows) + (P(),) * 9,
        out_specs=(rows, rows) + (cut,) * 5 + (P("blk"),) + (cut,) * 3,
        check_vma=False,
    )
```

```python
import functools

import jax
import jax.numpy as jnp
from jax import lax
from jax.experimental import pallas as pl
from jax.experimental.pallas import tpu as pltpu
from jax.sharding import PartitionSpec as P

HEAD = 64
EPS = 1e-06
MESH = pl.DeviceIdType.MESH
F32 = jnp.float32
BF16 = jnp.bfloat16
MIB = 2**20


def silu_parts(pre):
    sig = jax.nn.sigmoid(pre)
    return (pre * sig, sig * (1.0 + pre * (1.0 - sig)))


def norm_back(grad, value, scale):
    inner = jnp.mean(grad * value, axis=-1, keepdims=True)
    return scale * grad - value * (scale * scale * scale) * inner


def project(left, weight):
    return jnp.dot(left, weight, preferred_element_type=F32)


def weight_grad(left, right):
    return jnp.einsum("td,tf->df", left, right, preferred_element_type=F32)


def back_project(grad, weight):
    return jnp.einsum("tf,df->td", grad, weight, preferred_element_type=F32)


def dot(a, b, ca, cb):
    return lax.dot_general(a, b, (((ca,), (cb,)), ((), ())), preferred_element_type=F32)


def low_lanes(shape):
    return lax.broadcasted_iota(jnp.int32, shape, len(shape) - 1) < HEAD


def two_heads(x):
    low = low_lanes(x.shape)
    zero = jnp.zeros_like(x)
    return jnp.concatenate([jnp.where(low, x, zero), jnp.where(low, zero, x)], axis=0)


def pick_heads(x):
    half = x.shape[0] // 2
    return jnp.where(low_lanes((half, x.shape[1])), x[:half], x[half:])


def causal_pair(span):
    t = lax.broadcasted_iota(jnp.int32, (span, 2 * span), 0)
    u = lax.broadcasted_iota(jnp.int32, (span, 2 * span), 1)
    return t >= u % span


def pair_of(ref, p):
    return ref[:, pl.ds(p * 2 * HEAD, 2 * HEAD)]


def state_kernel(left_ref, right_ref, out_ref):
    for p in range(out_ref.shape[1]):
        out_ref[0, p] = pick_heads(dot(pair_of(left_ref, p), pair_of(right_ref, p), 0, 0))


def attn_kernel(q_ref, k_ref, v_ref, prefix_ref, out_ref):
    span = q_ref.shape[0]
    causal = causal_pair(span)
    for p in range(prefix_ref.shape[1]):
        q, k2, v2 = pair_of(q_ref, p), two_heads(pair_of(k_ref, p)), two_heads(pair_of(v_ref, p))
        scores = jnp.where(causal, dot(q, k2, 1, 1), 0.0).astype(BF16)
        prefix = two_heads(prefix_ref[0, p])
        out_ref[:, pl.ds(p * 2 * HEAD, 2 * HEAD)] = dot(scores, v2, 1, 0) + dot(q, prefix, 1, 0)


def attn_back_kernel(q_ref, k_ref, v_ref, g_ref, prefix_ref, dstate_ref, dq_ref, dk_ref, dv_ref):
    span = q_ref.shape[0]
    causal = causal_pair(span)
    for p in range(prefix_ref.shape[1]):
        q, k, v, g = (pair_of(r, p) for r in (q_ref, k_ref, v_ref, g_ref))
        k2, v2 = two_heads(k), two_heads(v)
        prefix, dstate = two_heads(prefix_ref[0, p]), two_heads(dstate_ref[0, p])
        scores = jnp.where(causal, dot(q, k2, 1, 1), 0.0).astype(BF16)
        dscores = jnp.where(causal, dot(g, v2, 1, 1), 0.0).astype(BF16)
        lanes = pl.ds(p * 2 * HEAD, 2 * HEAD)
        dq_ref[:, lanes] = dot(dscores, k2, 1, 0) + dot(g, prefix, 1, 1)
        dk_ref[:, lanes] = pick_heads(dot(dscores, q, 0, 0)) + dot(v, dstate, 1, 1)
        dv_ref[:, lanes] = pick_heads(dot(scores, g, 0, 0)) + dot(k, dstate, 1, 0)


def rows_spec(span, width):
    return pl.BlockSpec((span, width), lambda s: (s, 0))


def state_spec(pairs):
    return pl.BlockSpec((1, pairs, HEAD, 2 * HEAD), lambda s: (s, 0, 0, 0))


def local_states(left, right, seqs):
    rows, width = left.shape
    span, pairs = rows // seqs, width // (2 * HEAD)
    return pl.pallas_call(
        state_kernel,
        grid=(seqs,),
        in_specs=[rows_spec(span, width)] * 2,
        out_specs=state_spec(pairs),
        out_shape=jax.ShapeDtypeStruct((seqs, pairs, HEAD, 2 * HEAD), F32),
    )(left, right)


def attention(q, k, v, prefix, seqs):
    rows, width = q.shape
    span, pairs = rows // seqs, width // (2 * HEAD)
    return pl.pallas_call(
        attn_kernel,
        grid=(seqs,),
        in_specs=[rows_spec(span, width)] * 3 + [state_spec(pairs)],
        out_specs=rows_spec(span, width),
        out_shape=jax.ShapeDtypeStruct((rows, width), F32),
    )(q, k, v, prefix)


def attention_back(q, k, v, g, prefix, dstate, seqs):
    rows, width = q.shape
    span, pairs = rows // seqs, width // (2 * HEAD)
    return pl.pallas_call(
        attn_back_kernel,
        grid=(seqs,),
        in_specs=[rows_spec(span, width)] * 4 + [state_spec(pairs)] * 2,
        out_specs=[rows_spec(span, width)] * 3,
        out_shape=[jax.ShapeDtypeStruct((rows, width), F32)] * 3,
    )(q, k, v, g, prefix, dstate)


def scan_kernel(outer, reverse, s_ref, out_ref, held, summed, other, zs, zr, xs, xr):
    chunks = s_ref.shape[0]
    k = lax.axis_index("blk")
    z, x = k // 2, k % 2
    if reverse:
        zz, xx = outer - 1 - z, 1 - x
        after, before = jnp.maximum(z - 1, 0), jnp.minimum(z + 1, outer - 1)
    else:
        zz, xx = z, x
        after, before = jnp.minimum(z + 1, outer - 1), jnp.maximum(z - 1, 0)
    nxt, prv, side = {"blk": after * 2 + x}, {"blk": before * 2 + x}, {"blk": z * 2 + 1 - x}
    first, last = zz == 0, zz == outer - 1

    bar = pltpu.get_barrier_semaphore()
    pl.semaphore_signal(bar, inc=1, device_id=side, device_id_type=MESH)
    pl.when(~last)(lambda: pl.semaphore_signal(bar, inc=1, device_id=nxt, device_id_type=MESH))
    pl.when(~first)(lambda: pl.semaphore_signal(bar, inc=1, device_id=prv, device_id_type=MESH))
    pl.semaphore_wait(bar, 1 + jnp.where(last, 0, 1) + jnp.where(first, 0, 1))

    def along(i):
        return pltpu.make_async_remote_copy(
            src_ref=summed.at[i], dst_ref=held.at[i], send_sem=zs.at[i], recv_sem=zr.at[i],
            device_id=nxt, device_id_type=MESH)

    def across(i, src):
        return pltpu.make_async_remote_copy(
            src_ref=src.at[i], dst_ref=other.at[i], send_sem=xs.at[i], recv_sem=xr.at[i],
            device_id=side, device_id_type=MESH)

    def pass_on(i):
        pl.when(~first)(lambda: along(i).wait_recv())

        @pl.when(first)
        def _():
            held[i] = jnp.zeros_like(held[i])

        summed[i] = held[i] + s_ref[i]
        pl.when(~last)(lambda: along(i).start())
        pl.when(xx == 0)(lambda: across(i, summed).start())
        pl.when(xx == 1)(lambda: across(i, held).start())

    def finish(i):
        across(i, held).wait_recv()
        out_ref[i] = (held[i] + other[i]).astype(out_ref.dtype)

    def step(i, carry):
        pl.when(i < chunks)(lambda: pass_on(i))
        pl.when(i > 0)(lambda: finish(i - 1))
        return carry

    lax.fori_loop(0, chunks + 1, step, 0)

    def drain(i, carry):
        pl.when(~last)(lambda: along(i).wait_send())
        across(i, held).wait_send()
        return carry

    lax.fori_loop(0, chunks, drain, 0)


def entering(states, blk, reverse):
    seqs, pairs, head, lanes = states.shape
    per = max(1, pairs // 2)
    shape = (seqs * pairs // per, per, head, lanes)
    vmem = pl.BlockSpec(memory_space=pltpu.VMEM)
    sems = [pltpu.SemaphoreType.DMA((shape[0],))] * 4
    out = pl.pallas_call(
        functools.partial(scan_kernel, blk // 2, reverse),
        out_shape=jax.ShapeDtypeStruct(shape, BF16),
        in_specs=[vmem],
        out_specs=vmem,
        scratch_shapes=[pltpu.VMEM(shape, F32)] * 3 + sems,
        compiler_params=pltpu.CompilerParams(
            collective_id=2 if reverse else 1, has_side_effects=True, vmem_limit_bytes=24 * MIB),
    )(states.reshape(shape))
    return out.reshape(states.shape)


LAND, FIN, ACC = 4, 8, 10
CORE, XA, YA, YB, XB, XC, YC = range(7)
TILE = 256


SPARE = (2, 19)
QUICK = 2


class Way:
    def __init__(self, a, b, c):
        self.a = pl.ds(0, a) if a else None
        self.b, self.c = pl.ds(a, b), pl.ds(a + b, c)
        self.ab, self.top_a = pl.ds(0, a + b), pl.ds(0, max(a, 8))
        self.top_b, self.top_c = pl.ds(0, b), pl.ds(0, c)


class Named:
    def __init__(self, names, refs):
        self.__dict__.update(zip(names, refs))


class Stream:
    def __init__(self, block, buf, sem):
        self.block, self.buf, self.sem = block, buf, sem

    def copy(self, j):
        return pltpu.make_async_copy(self.block(j), self.buf.at[j % 2], self.sem.at[j % 2])

    def start(self, j):
        self.copy(j).start()

    def get(self, j, count):
        self.copy(j).wait()
        pl.when(j + 1 < count)(lambda: self.start(j + 1))
        return self.buf.at[j % 2]


LAG, WAIT, OFFER = 1, 8, (0, 1, 4, 8)


def forward_kernel(outer, seqs, names, results, *refs):
    r = Named(names, refs)
    rows, width = r.tokens.shape
    ff = r.w_first.shape[1]
    span, pairs = rows // seqs, width // (2 * HEAD)
    blocks, per_block = rows // TILE, TILE // span
    n_scan, cut = r.sums.shape[:2]
    per_seq = pairs // cut

    k = lax.axis_index("blk")
    z, x = k // 2, k % 2
    top = outer - 1
    side = {"blk": z * 2 + 1 - x}
    above, below = {"blk": jnp.minimum(z + 1, top) * 2 + x}, {"blk": jnp.maximum(z - 1, 0) * 2 + x}
    bar = pltpu.get_barrier_semaphore()
    pl.semaphore_signal(bar, inc=1, device_id=side, device_id_type=MESH)
    pl.when(z < top)(lambda: pl.semaphore_signal(bar, inc=1, device_id=above, device_id_type=MESH))
    pl.when(z > 0)(lambda: pl.semaphore_signal(bar, inc=1, device_id=below, device_id_type=MESH))

    def span_of(start, size, step):
        return pl.ds(start if isinstance(start, int) else pl.multiple_of(start, step), size)

    def tok(j, n=TILE):
        return span_of(j * n, n, n)

    loads = [
        pltpu.make_async_copy(src, dst, r.lsem.at[n])
        for n, (src, dst) in enumerate((
            (r.w_key, r.wk), (r.w_value, r.wv), (r.w_query, r.wq), (r.w_gate, r.wg), (r.gain, r.gv),
            (r.w_out, r.wo), (r.w_first, r.w1), (r.w_second, r.w2)))
    ]

    def x_load(j):
        return pltpu.make_async_copy(r.tokens.at[tok(j)], r.xv.at[tok(j)], r.xsem.at[j])

    by_rows = dict(
        k=lambda j: r.kb.at[tok(j)], v=lambda j: r.vb.at[tok(j)], q=lambda j: r.qb.at[tok(j)],
        gate=lambda j: r.gb.at[tok(j)], key=lambda j: r.keyb, query=lambda j: r.queryb,
        attn=lambda j: r.attnb, resid=lambda j: r.residb, first=lambda j: r.firstb,
        second=lambda j: r.secondb, inner=lambda j: r.innerb)
    by_cols = dict(normt=r.tb0, mixedt=r.tb1, norm2t=r.tb2, innert=r.innertb)

    def store(name, j):
        sem = r.osem.at[results.index(name)]
        out = getattr(r, name)
        if name in by_rows:
            return pltpu.make_async_copy(by_rows[name](j), out.at[tok(j)], sem)
        return pltpu.make_async_copy(by_cols[name], out.at[:, tok(j)], sem)

    def free(name, j):
        pl.when(j > 0)(lambda: store(name, j - 1).wait())

    def remote(src, dst, s, t, dev):
        return pltpu.make_async_remote_copy(
            src_ref=src, dst_ref=dst, send_sem=s, recv_sem=t, device_id=dev, device_id_type=MESH)

    def along(i):
        return remote(r.sums.at[i], r.held.at[i], r.sz.at[i], r.rz.at[i], above)

    def across(i, src):
        return remote(src.at[i], r.other.at[i], r.sx.at[i], r.rx.at[i], side)

    def owned(i):
        return i % 2 == x

    def pass_on(i):
        across(i, r.other).wait_recv()
        pl.when(z > 0)(lambda: along(i).wait_recv())

        @pl.when(z == 0)
        def _():
            r.held[i] = jnp.zeros_like(r.held[i])

        @pl.when(x == 0)
        def _():
            mine = r.held[i] + r.sums[i]
            r.pre[i] = r.held[i].astype(BF16)
            r.sums[i] = mine + r.other[i]
            r.other[i] = mine
            across(i, r.other).start()

        @pl.when(x == 1)
        def _():
            mine = r.held[i] + r.other[i]
            r.pre[i] = mine.astype(BF16)
            r.sums[i] = mine + r.sums[i]
            across(i, r.held).start()

        pl.when(z < top)(lambda: along(i).start())

    def finish(i):
        @pl.when(owned(i))
        def _():
            pl.when(z < top)(lambda: along(i).wait_send())

        @pl.when(~owned(i))
        def _():
            across(i, r.sums).wait_recv()
            r.pre[i] = r.other[i].astype(BF16)

        across(i, r.sums).wait_send()

    def scan(n):
        per_tile = n_scan // blocks
        for j in range(blocks):
            @pl.when(n == OFFER[j])
            def _(j=j):
                for g in range(per_tile):
                    i = j * per_tile + g
                    pl.when(~owned(i))(lambda: across(i, r.sums).start())

        i = (n - 1 - LAG * z) * 2

        @pl.when((i >= 0) & (i < n_scan))
        def _():
            for g in range(2):
                pl.when(owned(i + g))(lambda: pass_on(i + g))

        q = (n - WAIT) * 2

        @pl.when((q >= 0) & (q < n_scan))
        def _():
            for g in range(2):
                finish(q + g)

    def transposed(src, dst):
        for n in range(dst.shape[0] // 128):
            cols = pl.ds(n * 128, 128)
            dst[cols, :] = src[:, cols].T

    def norm_rows(value):
        return (value * lax.rsqrt(jnp.mean(value * value, axis=-1, keepdims=True) + EPS)).astype(BF16)

    def each(count, one):
        for m in range(count):
            one(m)

    def rows_of(j, m):
        return span_of(j * TILE + m * 32, 32, 32)

    def col(n):
        return span_of(n * 256, 256, 256)

    def tile_keys(j):
        x_load(j).wait()

        @pl.when(j == 0)
        def _():
            loads[0].wait()
            loads[1].wait()
            for n in range(1, blocks):
                x_load(n).start()
            for copy in loads[2:]:
                copy.start()

        for name in ("key", "k", "v", "normt"):
            free(name, j)

        def one(m):
            r.nrm[rows_of(j, m), :] = norm_rows(r.xv[rows_of(j, m), :].astype(F32))

        each(TILE // 32, one)

        def product(n):
            key = dot(r.nrm[tok(j), :], r.wk[:, col(n)], 1, 0)
            r.keyb[:, col(n)] = key.astype(BF16)
            r.kb[tok(j), col(n)] = silu_parts(key)[0].astype(BF16)
            r.vb[tok(j), col(n)] = dot(r.nrm[tok(j), :], r.wv[:, col(n)], 1, 0).astype(BF16)

        each(width // 256, product)

        def states(m):
            s = j * per_block + m
            for p in range(pairs):
                lanes = pl.ds(p * 2 * HEAD, 2 * HEAD)
                here = tok(s, span)
                r.sums[s * per_seq + p // cut, p % cut] = pick_heads(dot(r.kb[here, lanes], r.vb[here, lanes], 0, 0))

        each(per_block, states)
        transposed(r.nrm.at[tok(j)], r.tb0)
        for name in ("key", "k", "v", "normt"):
            store(name, j).start()

    def tile_query(j):
        @pl.when(j == 0)
        def _():
            loads[2].wait()
            loads[3].wait()

        for name in ("query", "q", "gate"):
            free(name, j)

        def product(n):
            query = dot(r.nrm[tok(j), :], r.wq[:, col(n)], 1, 0)
            r.queryb[:, col(n)] = query.astype(BF16)
            r.qb[tok(j), col(n)] = silu_parts(query)[0].astype(BF16)
            r.gb[tok(j), col(n)] = dot(r.nrm[tok(j), :], r.wg[:, col(n)], 1, 0).astype(BF16)

        each(width // 256, product)
        for name in ("query", "q", "gate"):
            store(name, j).start()

    def tile_scores(s):
        causal = causal_pair(span)
        here = tok(s, span)
        for p in range(pairs):
            lanes = pl.ds(p * 2 * HEAD, 2 * HEAD)
            q, k2, v2 = r.qb[here, lanes], two_heads(r.kb[here, lanes]), two_heads(r.vb[here, lanes])
            scores = jnp.where(causal, dot(q, k2, 1, 1), 0.0).astype(BF16)
            r.intra[here, lanes] = dot(scores, v2, 1, 0)

    def tile_mixed(j, m):
        if m == 0:
            pl.when(j == 0)(lambda: loads[4].wait())
            for name in ("attn", "mixedt"):
                free(name, j)
        s = j * per_block + m
        here = tok(s, span)
        for p in range(pairs):
            lanes = pl.ds(p * 2 * HEAD, 2 * HEAD)
            prefix = two_heads(r.pre[s * per_seq + p // cut, p % cut])
            r.intra[here, lanes] = r.intra[here, lanes] + dot(r.qb[here, lanes], prefix, 1, 0)
        for n in range(m * span // 32, (m + 1) * span // 32):
            av = r.intra[rows_of(j, n), :]
            scale = lax.rsqrt(jnp.mean(av * av, axis=-1, keepdims=True) + EPS)
            act = silu_parts(r.gb[rows_of(j, n), :].astype(F32))[0]
            r.attnb[tok(n, 32), :] = av.astype(BF16)
            r.mixb[tok(n, 32), :] = (av * scale * r.gv[...] * act).astype(BF16)
        for n in range(width // 128):
            r.tb1[pl.ds(n * 128, 128), tok(m, span)] = r.mixb[tok(m, span), pl.ds(n * 128, 128)].T
        if m == per_block - 1:
            for name in ("attn", "mixedt"):
                store(name, j).start()

    def tile_resid(j):
        pl.when(j == 0)(lambda: loads[5].wait())
        for name in ("resid", "norm2t"):
            free(name, j)

        def product(n):
            r.residb[:, col(n)] = r.xv[tok(j), col(n)].astype(F32) + dot(r.mixb[...], r.wo[:, col(n)], 1, 0)

        each(width // 256, product)

        def one(m):
            r.n2b[tok(m, 32), :] = norm_rows(r.residb[tok(m, 32), :])

        each(TILE // 32, one)
        transposed(r.n2b, r.tb2)
        for name in ("resid", "norm2t"):
            store(name, j).start()

    def tile_inner(j, lo, hi):
        def one(n):
            n = n + lo
            first = dot(r.n2b[...], r.w1[:, col(n)], 1, 0)
            second = dot(r.n2b[...], r.w2[:, col(n)], 1, 0)
            inner = (first * second).astype(BF16)
            r.firstb[:, col(n)] = first.astype(BF16)
            r.secondb[:, col(n)] = second.astype(BF16)
            r.innerb[:, col(n)] = inner
            r.innertb[col(n), :] = inner.T

        each(hi - lo, one)

    half = ff // 512 * 256
    halves = (pl.ds(0, half), pl.ds(half, ff - half))

    def up_stores(j, h):
        cols = halves[h]
        sem = lambda name: r.osem.at[results.index(name)]
        copies = [
            pltpu.make_async_copy(by_rows[name](j).at[:, cols], getattr(r, name).at[tok(j), cols], sem(name))
            for name in ("first", "second", "inner")]
        return copies + [
            pltpu.make_async_copy(r.innertb.at[cols], r.innert.at[cols, tok(j)], sem("innert"))]

    def tile_up(j, h):
        if h == 0:
            @pl.when(j == 0)
            def _():
                loads[6].wait()
                loads[7].wait()

            for name in ("first", "second", "inner", "innert"):
                free(name, j)
        tile_inner(j, (0, half // 256)[h], (half // 256, ff // 256)[h])
        for copy in up_stores(j, h):
            copy.start()

    x_load(0).start()
    loads[0].start()
    loads[1].start()

    per = n_scan // blocks // 2

    def slot(n, carry):
        pl.when(n < blocks)(lambda: tile_keys(n))

        @pl.when(n == 0)
        def _():
            pl.semaphore_wait(bar, 1 + jnp.where(z < top, 1, 0) + jnp.where(z > 0, 1, 0))

        @pl.when((n >= blocks) & (n < 2 * blocks))
        def _():
            tile_query(n - blocks)
            for m in range(per_block):
                tile_scores((n - blocks) * per_block + m)

        scan(n)
        w = n - WAIT - per // 2 + 1
        j, m = w // per, w % per
        live = (w >= 0) & (j < blocks)
        pl.when((w >= per) & (j <= blocks) & (m == 0))(lambda: tile_up(j - 1, 1))
        pl.when(live & (m == 0))(lambda: tile_mixed(j, 0))

        @pl.when(live & (m == 2))
        def _():
            tile_mixed(j, 1)
            tile_resid(j)

        pl.when(live & (m == 3))(lambda: tile_up(j, 0))
        return carry

    lax.fori_loop(0, n_scan // 2 + WAIT + 2, slot, 0)
    whole = pltpu.make_async_copy(r.pre, r.prefix, r.osem.at[results.index("prefix")])
    whole.start()
    for name in results[:-1]:
        store(name, blocks - 1).wait()
    whole.wait()


def forward_fast(blk, seqs, tokens, weights):
    w_query, w_key, w_value, w_gate, w_out, out_gain, w_first, w_second, w_third = weights
    rows, width = tokens.shape
    ff = w_first.shape[1]
    pairs = width // (2 * HEAD)
    cut = 2
    n_scan = seqs * pairs // cut

    def v(*shape, dtype=BF16):
        return pltpu.VMEM(shape, dtype)

    def sem(*shape):
        return pltpu.SemaphoreType.DMA(shape)

    wide, tall = (rows, width), (width, ff)
    chunks = (n_scan, cut, HEAD, 2 * HEAD)
    scratch = dict(
        xv=v(*wide), gv=v(1, width, dtype=F32), wq=v(width, width), wk=v(width, width), wv=v(width, width),
        wg=v(width, width), wo=v(width, width), w1=v(*tall), w2=v(*tall), nrm=v(*wide), kb=v(*wide),
        vb=v(*wide), qb=v(*wide), gb=v(*wide), intra=v(*wide, dtype=F32), keyb=v(TILE, width),
        queryb=v(TILE, width), attnb=v(TILE, width), mixb=v(TILE, width), residb=v(TILE, width, dtype=F32),
        n2b=v(TILE, width), firstb=v(TILE, ff), secondb=v(TILE, ff), innerb=v(TILE, ff),
        tb0=v(width, TILE), tb1=v(width, TILE), tb2=v(width, TILE), innertb=v(ff, TILE),
        held=v(*chunks, dtype=F32), sums=v(*chunks, dtype=F32), other=v(*chunks, dtype=F32), pre=v(*chunks),
        sz=sem(n_scan), rz=sem(n_scan), sx=sem(n_scan), rx=sem(n_scan), lsem=sem(8),
        xsem=sem(rows // TILE), osem=sem(16),
    )
    turned = (width, rows)
    outs = dict(
        k=wide, v=wide, key=wide, normt=turned, q=wide, gate=wide, query=wide, attn=wide, mixedt=turned,
        resid=wide, norm2t=turned, first=(rows, ff), second=(rows, ff), inner=(rows, ff),
        innert=(ff, rows), prefix=chunks)
    ins = dict(
        tokens=tokens, gain=out_gain.reshape(1, width), w_query=w_query, w_key=w_key, w_value=w_value,
        w_gate=w_gate, w_out=w_out, w_first=w_first, w_second=w_second)
    results = tuple(outs)
    anywhere = pl.BlockSpec(memory_space=pl.ANY)
    made = pl.pallas_call(
        functools.partial(forward_kernel, blk // 2, seqs, (*ins, *outs, *scratch), results),
        out_shape=[
            jax.ShapeDtypeStruct(shape, F32 if name == "resid" else BF16) for name, shape in outs.items()
        ],
        in_specs=[anywhere] * len(ins),
        out_specs=[anywhere] * len(outs),
        scratch_shapes=list(scratch.values()),
        compiler_params=pltpu.CompilerParams(
            collective_id=4, has_side_effects=True, vmem_limit_bytes=60 * MIB),
        cost_estimate=pl.CostEstimate(flops=26 * 2**30, bytes_accessed=80 * MIB, transcendentals=0),
    )(*ins.values())
    f = dict(zip(results, made))
    f["prefix"] = f["prefix"].reshape(seqs, pairs, HEAD, 2 * HEAD)
    return f


def back_kernel(outer, seqs, names, *refs):
    r = Named(names, refs)
    rows, width = r.tokens.shape
    ff = r.first.shape[1]
    span, pairs = rows // seqs, width // (2 * HEAD)
    n_tall, n_wide, n_square = ff // 256, ff // 128, 20
    chunks = n_tall + n_wide + n_square
    at_wide, at_square = n_tall, n_tall + n_wide
    blocks = rows // TILE

    b, k = lax.axis_index("batch"), lax.axis_index("blk")
    y, c = b // 2, b % 2
    z, x = k // 2, k % 2
    ox, oy = 1 - x, 1 - y
    top = outer - 1
    zr = top - z
    to_core, to_y, to_x = {"batch": y * 2 + 1 - c}, {"batch": oy * 2 + c}, {"blk": z * 2 + ox}
    to_up = {"blk": jnp.minimum(z + 1, top) * 2 + x}
    to_down = {"blk": jnp.maximum(z - 1, 0) * 2 + x}
    to_z = [{"blk": (z + d) % outer * 2 + x} for d in range(1, outer)]

    peers = [to_core, to_y, to_x] + to_z
    bar = pltpu.get_barrier_semaphore()
    for d in peers:
        pl.semaphore_signal(bar, inc=1, device_id=d, device_id_type=MESH)

    def remote(src, dst, s, t, dev):
        return pltpu.make_async_remote_copy(
            src_ref=src, dst_ref=dst, send_sem=s, recv_sem=t, device_id=dev, device_id_type=MESH)

    def link(kind, i, src, dst, dev):
        return remote(src, dst.at[i % LAND], r.ssem.at[kind, i % LAND], r.rsem.at[kind, i % LAND], dev)

    def at(i, *where):
        return r.acc.at[(i % ACC,) + where]

    every = slice(None)

    def core_copy(i):
        return link(CORE, i, r.tbuf.at[i % 2], r.core_rx, to_core)

    def xa_copy(w, i):
        return link(XA, i, at(i, every, ox, every, w.a), r.xa.at[:, :, :, w.top_a], to_x)

    def ya_copy(w, i):
        return link(YA, i, at(i, every, x, oy, w.a), r.ya.at[:, :, w.top_a], to_y)

    def yb_copy(w, i):
        return link(YB, i, at(i, every, every, oy, w.b), r.yb.at[:, :, :, w.top_b], to_y)

    def xb_copy(w, i):
        return link(XB, i, at(i, every, ox, y, w.b), r.xb.at[:, :, w.top_b], to_x)

    def xc_copy(w, i):
        return link(XC, i, at(i, z, ox, every, w.c), r.xc.at[:, :, w.top_c], to_x)

    def yc_copy(w, i):
        return link(YC, i, at(i, z, x, oy, w.c), r.yc.at[:, w.top_c], to_y)

    def y_share(i):
        f = i % FIN
        return remote(r.fin.at[f, y], r.fin.at[f, y], r.ygs.at[f], r.ygr.at[f], to_y)

    def part_ab(w, i, s):
        return at(i, s, x, y, w.ab)

    def part_c(w, i, s):
        return at(i, s, every, every, w.c)

    def land_ab(w, i, d, n):
        return r.zab.at[i % LAND, d, n - 1, w.ab]

    def land_c(w, i, d, n):
        return r.zc.at[i % LAND, d, n - 1, :, :, w.top_c]

    AB, CC = (0, part_ab, land_ab), (1, part_c, land_c)

    def hop(group, w, i, n, up, s):
        g, part, land = group
        d = 0 if up else 1
        sem = (g, d, n - 1, i % LAND)
        return remote(part(w, i, s), land(w, i, d, n), r.zss.at[sem], r.zrs.at[sem],
                      to_up if up else to_down)

    def z_each(group, w, i, n, act):
        up = hop(group, w, i, n, True, jnp.minimum(outer - n + z, top))
        down = hop(group, w, i, n, False, jnp.maximum(n - 1 - zr, 0))
        pl.when((z <= n - 1) & (z < top))(lambda: act(up))
        pl.when((zr <= n - 1) & (z > 0))(lambda: act(down))

    def z_send(group, w, i, n):
        z_each(group, w, i, n, lambda copy: copy.start())

    def z_sent(group, w, i, n):
        z_each(group, w, i, n, lambda copy: copy.wait_send())

    def add(ref, landed):
        ref[...] = ref[...] + landed[...]

    def z_take(group, w, i, n):
        g, part, land = group

        def take(up, s):
            hop(group, w, i, n, up, s).wait_recv()
            add(part(w, i, s), land(w, i, 0 if up else 1, n))

        pl.when((z > 0) & (z <= n))(lambda: take(True, jnp.clip(outer - n + z - 1, 0, top)))
        pl.when((z < top) & (zr <= n))(lambda: take(False, jnp.clip(n - zr, 0, top)))

    BOTH = (Way(32, 16, 16), Way(0, 48, 16))
    spare = (at_wide + SPARE[0], at_wide + SPARE[1])

    def places(i, act):
        f = r.fin.at[i % FIN]

        @pl.when(i < at_wide)
        def _():
            for yy in range(2):
                for blk in range(2):
                    col = pl.multiple_of(c * (width // 2) + (yy * 2 + blk) * 128, 128)
                    act(f.at[yy, pl.ds(blk * 32, 32)], r.tall.at[pl.ds(i * 32, 32), pl.ds(col, 128)])

        @pl.when((i >= at_wide) & (i < at_square))
        def _():
            j, h = (i - at_wide) // 2, (i - at_wide) % 2
            col = pl.multiple_of(c * (ff // 2) + j * 128, 128)
            for yy in range(2):
                act(f.at[yy], r.wide.at[yy, pl.ds(h * 64, 64), pl.ds(col, 128)])

        @pl.when(i >= at_square)
        def _():
            j = i - at_square
            m, u, h = j // 4, j // 2 % 2, j % 2
            for yy in range(2):
                col = pl.multiple_of(c * (width // 2) + u * 256 + yy * 128, 128)
                act(f.at[yy], r.square.at[m, pl.ds(h * 64, 64), pl.ds(col, 128)])

    def cores(w, i):
        core_copy(i).wait_recv()
        core_copy(i).wait_send()
        add(at(i), r.core_rx.at[i % LAND])
        if w.a is not None:
            xa_copy(w, i).start()
        yb_copy(w, i).start()
        z_send(CC, w, i, 1)

    def second(w, i):
        yb_copy(w, i).wait_recv()
        add(at(i, every, every, y, w.b), r.yb.at[i % LAND, :, :, w.top_b])
        xb_copy(w, i).start()
        if w.a is not None:
            xa_copy(w, i).wait_recv()
            add(at(i, every, x, every, w.a), r.xa.at[i % LAND, :, :, w.top_a])
            ya_copy(w, i).start()
        z_take(CC, w, i, 1)
        z_send(CC, w, i, 2)
        if w.a is not None:
            xa_copy(w, i).wait_send()
        yb_copy(w, i).wait_send()
        z_sent(CC, w, i, 1)

    def third(w, i):
        xb_copy(w, i).wait_recv()
        add(at(i, every, x, y, w.b), r.xb.at[i % LAND, :, w.top_b])
        if w.a is not None:
            ya_copy(w, i).wait_recv()
            add(at(i, every, x, y, w.a), r.ya.at[i % LAND, :, w.top_a])
        z_send(AB, w, i, 1)
        z_take(CC, w, i, 2)
        z_send(CC, w, i, 3)
        xb_copy(w, i).wait_send()
        if w.a is not None:
            ya_copy(w, i).wait_send()
        z_sent(CC, w, i, 2)

    def fourth(w, i):
        z_take(AB, w, i, 1)
        z_send(AB, w, i, 2)
        z_take(CC, w, i, 3)
        xc_copy(w, i).start()
        z_sent(AB, w, i, 1)
        z_sent(CC, w, i, 3)

    def fifth(w, i):
        z_take(AB, w, i, 2)
        z_send(AB, w, i, 3)
        xc_copy(w, i).wait_recv()
        add(at(i, z, x, every, w.c), r.xc.at[i % LAND, :, w.top_c])
        yc_copy(w, i).start()
        z_sent(AB, w, i, 2)
        xc_copy(w, i).wait_send()

    def sixth(w, i):
        yc_copy(w, i).wait_recv()
        z_take(AB, w, i, 3)
        f = i % FIN
        r.fin[f, y, w.ab] = r.acc[i % ACC, z, x, y, w.ab]
        r.fin[f, y, w.c] = r.acc[i % ACC, z, x, y, w.c] + r.yc[i % LAND, w.top_c]
        y_share(i).start()
        z_sent(AB, w, i, 3)
        yc_copy(w, i).wait_send()

    def seventh(w, i):
        y_share(i).wait_recv()
        y_share(i).wait_send()
        f = i % FIN

        def go(src, dst):
            remote(src, dst, r.csem.at[f], r.crem.at[f], to_core).start()
            pltpu.make_async_copy(src, dst, r.osem.at[f]).start()

        places(i, go)

    def last(w, i):
        f = i % FIN
        whole = r.fin.at[f]
        copy = remote(whole, whole, r.csem.at[f], r.crem.at[f], to_core)
        copy.wait_send()
        copy.wait_recv()
        pltpu.make_async_copy(whole, whole, r.osem.at[f]).wait()

    ORDER = range(2, 9)
    stages = (None, cores, second, third, fourth, fifth, sixth, seventh, last)

    def advance(t, some, ways):
        for n in some:
            i = t - n
            live = (i >= 0) & (i < chunks - QUICK)
            if n >= 7:
                pl.when(live)(functools.partial(stages[n], None, i))
                continue
            if len(ways) == 2:
                spared = (i >= spare[0]) & (i < spare[1])
                pl.when(spared)(functools.partial(stages[n], ways[1], i))
                live = live & ~spared
            pl.when(live)(functools.partial(stages[n], ways[0], i))

    def z_straight(group, i, act):
        w = BOTH[0]
        g, part, _ = group
        land = (r.qab, r.qc)[g].at[i % 2]
        for d in range(1, outer):
            sem = (g, d - 1, i % 2)
            act(remote(part(w, i, (z + d) % outer), land.at[d - 1], r.qss.at[sem], r.qrs.at[sem],
                       to_z[d - 1]))

    def z_arrived(group, i):
        w = BOTH[0]
        g, part, _ = group
        land = (r.qab, r.qc)[g].at[i % 2]
        z_straight(group, i, lambda copy: copy.wait_recv())
        total = land[0]
        for d in range(1, outer - 1):
            total = total + land[d]
        ref = part(w, i, z)
        ref[...] = ref[...] + total
        z_straight(group, i, lambda copy: copy.wait_send())

    def quick_xc(i):
        w, m = BOTH[0], i % 2
        return remote(at(i, z, ox, every, w.c), r.qxc.at[m], r.qks.at[0, m], r.qkr.at[0, m], to_x)

    def quick_yc(i):
        w, m = BOTH[0], i % 2
        return remote(at(i, z, x, oy, w.c), r.qyc.at[m], r.qks.at[1, m], r.qkr.at[1, m], to_y)

    def quick_cores(i):
        w = BOTH[0]
        core_copy(i).wait_recv()
        core_copy(i).wait_send()
        add(at(i), r.core_rx.at[i % LAND])
        xa_copy(w, i).start()
        yb_copy(w, i).start()
        z_straight(CC, i, lambda copy: copy.start())

    def quick_second(i):
        w = BOTH[0]
        yb_copy(w, i).wait_recv()
        add(at(i, every, every, y, w.b), r.yb.at[i % LAND, :, :, w.top_b])
        xb_copy(w, i).start()
        z_arrived(CC, i)
        quick_xc(i).start()
        xa_copy(w, i).wait_recv()
        add(at(i, every, x, every, w.a), r.xa.at[i % LAND, :, :, w.top_a])
        ya_copy(w, i).start()
        xa_copy(w, i).wait_send()
        yb_copy(w, i).wait_send()

    def quick_third(i):
        w = BOTH[0]
        quick_xc(i).wait_recv()
        add(at(i, z, x, every, w.c), r.qxc.at[i % 2])
        quick_yc(i).start()
        xb_copy(w, i).wait_recv()
        add(at(i, every, x, y, w.b), r.xb.at[i % LAND, :, w.top_b])
        ya_copy(w, i).wait_recv()
        add(at(i, every, x, y, w.a), r.ya.at[i % LAND, :, w.top_a])
        z_straight(AB, i, lambda copy: copy.start())
        for copy in (xb_copy(w, i), ya_copy(w, i), quick_xc(i)):
            copy.wait_send()

    def quick_fourth(i):
        w = BOTH[0]
        quick_yc(i).wait_recv()
        z_arrived(AB, i)
        f = i % FIN
        r.fin[f, y, w.ab] = r.acc[i % ACC, z, x, y, w.ab]
        r.fin[f, y, w.c] = r.acc[i % ACC, z, x, y, w.c] + r.qyc[i % 2]
        y_share(i).start()
        quick_yc(i).wait_send()

    quick = (None, quick_cores, quick_second, quick_third, quick_fourth,
             functools.partial(seventh, None), functools.partial(last, None))

    def finish_chunks(t, some):
        for n in some:
            i = t - n
            pl.when((i >= chunks - QUICK) & (i < chunks))(functools.partial(quick[n], i))

    def send_first(t, ways=BOTH):
        advance(t, (1,), ways)

    def move(t, ways=BOTH):
        advance(t, ORDER, ways)

    def make(t, fill):
        fill(1 - c, r.tbuf.at[t % 2])
        core_copy(t).start()
        fill(c, r.acc.at[t % ACC])

    def fill_tall(lhs):
        def fill(half, dst):
            for yy in range(2):
                col = pl.multiple_of(half * (width // 2) + yy * 256, 256)
                res = dot(lhs, r.dyv[:, pl.ds(col, 256)], 1, 0).reshape(4, 2, 32, 256)
                for blk in range(2):
                    dst[:, :, yy, pl.ds(blk * 32, 32), :] = res[..., blk * 128:(blk + 1) * 128]
        return fill

    def left_rows(ref, h):
        return ref[:, h].reshape(8 * 64, rows)

    def fill_two(left, h, take):
        def fill(half, dst):
            res = dot(left_rows(left, h), take(half), 1, 0).reshape(4, 2, 64, 256)
            dst[:, :, 0] = res[..., :128]
            dst[:, :, 1] = res[..., 128:]
        return fill

    def make_wide(t):
        i = t - at_wide
        j, h = i // 2, i % 2

        def take(half):
            col = pl.ds(pl.multiple_of(half * (ff // 2) + j * 128, 128), 128)
            return jnp.concatenate([r.dfs[0, :, col], r.dfs[1, :, col]], axis=1)

        make(t, fill_two(r.at0, h, take))

    def make_square(t, base, left, right):
        i = t - base
        u, h = i // 2, i % 2

        def take(half):
            return right(pl.ds(pl.multiple_of(half * (width // 2) + u * 256, 256), 256))

        make(t, fill_two(left, h, take))

    zz, xx = zr, ox
    n_scan = r.sums.shape[0]
    halves = n_scan // seqs
    scan_at = at_wide

    def along(i):
        return remote(r.sums.at[i], r.held.at[i], r.sz.at[i], r.rz.at[i], to_down)

    def across(i, src):
        return remote(src.at[i], r.other.at[i], r.sx.at[i], r.rx.at[i], to_x)

    def owned(i):
        return i % 2 == xx

    def pass_on(i):
        across(i, r.other).wait_recv()
        pl.when(zz > 0)(lambda: along(i).wait_recv())

        @pl.when(zz == 0)
        def _():
            r.held[i] = jnp.zeros_like(r.held[i])

        @pl.when(xx == 0)
        def _():
            mine = r.held[i] + r.sums[i]
            r.dstate[i] = r.held[i].astype(BF16)
            r.sums[i] = mine + r.other[i]
            r.other[i] = mine
            across(i, r.other).start()

        @pl.when(xx == 1)
        def _():
            mine = r.held[i] + r.other[i]
            r.dstate[i] = mine.astype(BF16)
            r.sums[i] = mine + r.sums[i]
            across(i, r.held).start()

        pl.when(zz < top)(lambda: along(i).start())

    def finish(i):
        @pl.when(owned(i))
        def _():
            pl.when(zz < top)(lambda: along(i).wait_send())

        @pl.when(~owned(i))
        def _():
            across(i, r.sums).wait_recv()
            r.dstate[i] = r.other[i].astype(BF16)

        across(i, r.sums).wait_send()

    def scan(t):
        i = t - scan_at
        pl.when((i >= 0) & (i < n_scan) & ~owned(i))(lambda: across(i, r.sums).start())
        j = i - 1 - zz
        pl.when((j >= 0) & (j < n_scan) & owned(j))(lambda: pass_on(j))
        pl.when((j >= 2) & (j < n_scan + 2))(lambda: finish(j - 2))

    def span_of(start, size, step):
        return pl.ds(start if isinstance(start, int) else pl.multiple_of(start, step), size)

    def tok(j, n=TILE):
        return span_of(j * n, n, n)

    def tile_inner(j, w3, w1, w2, first, second):
        def block(m, carry):
            at_rows = tok(m, 512)
            din = dot(r.dyv[at_rows, :], w3[...], 1, 1)
            one = (din * second[at_rows, :].astype(F32)).astype(BF16)
            two = (din * first[at_rows, :].astype(F32)).astype(BF16)
            cols = pl.ds(pl.multiple_of(j * 256, 256), 256)
            r.dfs[0, at_rows, cols] = one
            r.dfs[1, at_rows, cols] = two
            for n in range(width // 256):
                to = pl.ds(n * 256, 256)
                res = dot(one, w1[to, :], 1, 1) + dot(two, w2[to, :], 1, 1)
                r.dn2[at_rows, to] = r.dn2[at_rows, to] + res
            return carry

        for m in range(rows // 512):
            block(m, 0)

    def tile_resid(j, resid, gate, attn, q, w_out, gain, dmix):
        def one(m, carry):
            here, sub = pl.ds(pl.multiple_of(j * TILE + m * 32, 32), 32), tok(m, 32)
            value = resid[sub, :]
            grad = r.dn2[here, :]
            scale = lax.rsqrt(jnp.mean(value * value, axis=-1, keepdims=True) + EPS)
            out = r.dyv[here, :].astype(F32) + norm_back(grad, value, scale)
            r.dn2[here, :] = out
            r.dlow[here, :] = out.astype(BF16)
            return carry

        for m in range(TILE // 32):
            one(m, 0)
        for n in range(width // 256):
            to = pl.ds(n * 256, 256)
            dmix[:, to] = dot(r.dlow[tok(j), :], w_out[to, :], 1, 1)

        def two(m, carry):
            here, sub = pl.ds(pl.multiple_of(j * TILE + m * 32, 32), 32), tok(m, 32)
            av = attn[sub, :].astype(F32)
            scale = lax.rsqrt(jnp.mean(av * av, axis=-1, keepdims=True) + EPS)
            unit = av * scale
            act, der = silu_parts(gate[sub, :].astype(F32))
            dm = dmix[sub, :]
            ds = dm * act
            r.dgate[here, :] = (dm * (unit * gain[...]) * der).astype(BF16)
            r.gacc[...] = r.gacc[...] + jnp.sum((ds * unit).reshape(4, 8, width), axis=0)
            r.dattn[here, :] = norm_back(ds * gain[...], av, scale).astype(BF16)
            return carry

        for m in range(TILE // 32):
            two(m, 0)

        def states(m, carry):
            s = j * (TILE // span) + m
            for p in range(pairs):
                lanes = pl.ds(p * 2 * HEAD, 2 * HEAD)
                grad = r.dattn[tok(s, span), lanes]
                per = pairs // halves
                r.sums[s * halves + p // per, p % per] = pick_heads(dot(q[tok(m, span), lanes], grad, 0, 0))
            return carry

        for m in range(TILE // span):
            states(m, 0)

    def tile_attn(s, q_ref, k_ref, v_ref, query, key, prefix_ref):
        causal = causal_pair(span)
        here = tok(s, span)
        for p in range(pairs):
            lanes = pl.ds(p * 2 * HEAD, 2 * HEAD)
            q, k, v, g = q_ref[:, lanes], k_ref[:, lanes], v_ref[:, lanes], r.dattn[here, lanes]
            k2, v2 = two_heads(k), two_heads(v)
            per = pairs // halves
            prefix, dstate = two_heads(prefix_ref[p]), two_heads(r.dstate[s * halves + p // per, p % per])
            scores = jnp.where(causal, dot(q, k2, 1, 1), 0.0).astype(BF16)
            dscores = jnp.where(causal, dot(g, v2, 1, 1), 0.0).astype(BF16)
            dq = dot(dscores, k2, 1, 0) + dot(g, prefix, 1, 1)
            dk = pick_heads(dot(dscores, q, 0, 0)) + dot(v, dstate, 1, 1)
            dv = pick_heads(dot(scores, g, 0, 0)) + dot(k, dstate, 1, 0)
            r.dfs[0, here, lanes] = (dq * silu_parts(query[:, lanes].astype(F32))[1]).astype(BF16)
            r.dfs[0, here, pl.ds(width + p * 2 * HEAD, 2 * HEAD)] = (
                dk * silu_parts(key[:, lanes].astype(F32))[1]).astype(BF16)
            r.dfs[1, here, lanes] = dv.astype(BF16)

    parts = [
        lambda at_rows, cols: r.dfs[0, at_rows, cols],
        lambda at_rows, cols: r.dfs[0, at_rows, pl.ds(width + cols.start, cols.size)],
        lambda at_rows, cols: r.dfs[1, at_rows, cols],
    ]
    dq_cols = lambda cols: r.dfs[0, :, cols]
    dk_cols = lambda cols: r.dfs[0, :, pl.ds(width + cols.start, cols.size)]
    dv_cols = lambda cols: r.dfs[1, :, cols]

    def load(src, dst, n):
        return pltpu.make_async_copy(src, dst, r.lsem.at[n])

    def dma(*shape):
        return pltpu.SemaphoreType.DMA(shape)

    def ring(shape, dtype):
        return pltpu.VMEM((2,) + shape, dtype)

    def steps(count, one):
        def go(j, carry):
            one(j)
            return carry

        lax.fori_loop(0, count, go, 0)

    dy_load = load(r.dy, r.dyv, 0)
    norm2_load = load(r.norm2t, r.at0, 1)
    mixed_load = load(r.mixedt, r.at1, 2)
    norm_load = load(r.normt, r.at0, 3)

    def segment0(left, w3, w1, w2, first, second, sems):
        cols = lambda ref: lambda j: ref.at[:, pl.ds(pl.multiple_of(j * 256, 256), 256)]
        s_left = Stream(lambda j: r.innert.at[:, pl.ds(pl.multiple_of(j * 32, 32), 32)], left, sems.at[0])
        tiles = [
            Stream(lambda j: r.w_third.at[pl.ds(pl.multiple_of(j * 256, 256), 256)], w3, sems.at[1]),
            Stream(cols(r.w_first), w1, sems.at[2]),
            Stream(cols(r.w_second), w2, sems.at[3]),
            Stream(cols(r.first), first, sems.at[4]),
            Stream(cols(r.second), second, sems.at[5]),
        ]
        s_left.start(0)
        dy_load.start()
        r.dn2[...] = jnp.zeros_like(r.dn2)
        r.gacc[...] = jnp.zeros_like(r.gacc)
        dy_load.wait()
        for s in tiles:
            s.start(0)
        norm2_load.start()
        pl.semaphore_wait(bar, len(peers))

        def one(j):
            send_first(j, BOTH[:1])
            make(j, fill_tall(s_left.get(j, n_tall)[...].reshape(8 * 32, rows)))
            tile_inner(j, *(s.get(j, n_tall) for s in tiles))
            move(j, BOTH[:1])

        steps(n_tall, one)
        norm2_load.wait()

    pl.run_scoped(
        segment0, ring((8, 32, rows), BF16), ring((256, width), BF16), ring((width, 256), BF16),
        ring((width, 256), BF16), ring((rows, 256), BF16), ring((rows, 256), BF16), dma(6, 2))

    def segment1(resid, gate, attn, q, w_out, gain, dmix, sems, wsem):
        blk = lambda ref: lambda j: ref.at[tok(j)]
        tiles = [
            Stream(blk(ref), buf, sems.at[n])
            for n, (ref, buf) in enumerate(((r.resid, resid), (r.gate, gate), (r.attn, attn), (r.q, q)))
        ]
        w_load = pltpu.make_async_copy(r.w_out, w_out, wsem.at[0])
        g_load = pltpu.make_async_copy(r.gain, gain, wsem.at[1])
        w_load.start()
        g_load.start()
        for s in tiles:
            s.start(0)
        w_load.wait()
        g_load.wait()

        def one(j):
            t = at_wide + j
            send_first(t)
            make_wide(t)
            rs, ga, at_, qs = (s.get(j, blocks) for s in tiles)
            tile_resid(j, rs, ga, at_, qs, w_out, gain, dmix)
            move(t)
            scan(t)

        steps(blocks, one)

    pl.run_scoped(
        segment1, ring((TILE, width), F32), ring((TILE, width), BF16), ring((TILE, width), BF16),
        ring((TILE, width), BF16), pltpu.VMEM((width, width), BF16), pltpu.VMEM((1, width), F32),
        pltpu.VMEM((TILE, width), F32), dma(4, 2), dma(2))

    def gain_sum(t):
        base = at_wide + blocks
        hops = [to_core, to_y, to_x]

        def swap(n):
            return remote(r.gbuf, r.gland.at[n], r.gs.at[n], r.gr.at[n], hops[n])

        def spread(d):
            return remote(r.gbuf, r.gland.at[2 + d], r.gs.at[2 + d], r.gr.at[2 + d], to_z[d - 1])

        @pl.when(t == base)
        def _():
            total = jnp.sum(r.gacc[...], axis=0, keepdims=True)
            for n in range(8):
                r.gbuf[pl.ds(n, 1), :] = total[:, n * 128:(n + 1) * 128]
            swap(0).start()

        for n in range(3):
            @pl.when(t == base + 2 + 2 * n)
            def _(n=n):
                swap(n).wait()
                r.gbuf[...] = r.gbuf[...] + r.gland[n]
                if n < 2:
                    swap(n + 1).start()
                else:
                    for d in range(1, outer):
                        spread(d).start()

        @pl.when(t == base + 8)
        def _():
            for d in range(1, outer):
                spread(d).wait()
            for d in range(1, outer):
                r.gbuf[...] = r.gbuf[...] + r.gland[2 + d]
            pltpu.make_async_copy(r.gbuf, r.dgain, r.lsem.at[4]).start()

        pl.when(t == base + 10)(lambda: pltpu.make_async_copy(r.gbuf, r.dgain, r.lsem.at[4]).wait())

    n2 = n_wide - blocks
    n_out = blocks * (width // 256)

    def segment2(w3, inner, resid, out, sems, osem):
        per = width // 256
        cols = lambda j: pl.ds(pl.multiple_of(j % per * 256, 256), 256)
        s_w3 = Stream(lambda j: r.w_third.at[:, cols(j)], w3, sems.at[0])
        s_resid = Stream(lambda j: r.resid.at[tok(j // per), cols(j)], resid, sems.at[1])
        s_inner = Stream(lambda n: r.inner.at[tok(n)], inner, sems.at[2])

        def store(j):
            return pltpu.make_async_copy(out.at[j % 2], r.output.at[tok(j // per), cols(j)], osem.at[j % 2])

        mixed_load.start()
        for s in (s_w3, s_resid, s_inner):
            s.start(0)

        def one(j):
            t = at_wide + blocks + j
            send_first(t)
            make_wide(t)

            @pl.when(j < n_out)
            def _():
                w, res = s_w3.get(j, n_out), s_resid.get(j, n_out)

                @pl.when(j % per == 0)
                def _():
                    s_inner.get(j // per, blocks)

                pl.when(j >= 2)(lambda: store(j - 2).wait())
                prod = dot(inner[j // per % 2], w[...], 1, 0)
                out[j % 2] = (res[...] + prod).astype(BF16)
                store(j).start()

            move(t)
            scan(t)
            gain_sum(t)

        steps(n2, one)
        store(n_out - 2).wait()
        store(n_out - 1).wait()
        mixed_load.wait()

    pl.run_scoped(
        segment2, ring((ff, 256), BF16), ring((TILE, ff), BF16), ring((TILE, 256), F32),
        ring((TILE, 256), BF16), dma(3, 2), dma(2))

    def segment3(q, k, v, query, key, prefix, sems):
        blk = lambda ref: lambda j: ref.at[tok(j, span)]
        tiles = [
            Stream(blk(ref), buf, sems.at[n])
            for n, (ref, buf) in enumerate(((r.q, q), (r.k, k), (r.v, v), (r.query, query), (r.key, key)))
        ]
        tiles.append(Stream(lambda j: r.prefix.at[j], prefix, sems.at[5]))
        norm_load.start()
        for s in tiles:
            s.start(0)

        def one(j):
            t = at_square + j
            send_first(t)
            pl.when(j < 4)(lambda: make_square(t, at_square, r.at1, lambda cols: r.dlow[:, cols]))
            pl.when(j == 4)(lambda: norm_load.wait())
            pl.when(j >= 4)(lambda: make_square(t, at_square + 4, r.at0, lambda cols: r.dgate[:, cols]))
            tile_attn(j, *(s.get(j, seqs) for s in tiles))
            move(t)

        steps(8, one)

    pl.run_scoped(
        segment3, *[ring((span, width), BF16)] * 5, ring((pairs, HEAD, 2 * HEAD), BF16), dma(6, 2))

    def segment4(wq, wk, wv, wg, total, xs, out, sems, xsem, osem):
        nn = width // 256
        rowsblk = lambda ref: lambda n: ref.at[pl.ds(pl.multiple_of(n * 256, 256), 256)]
        weights = [
            Stream(rowsblk(ref), buf, sems.at[n])
            for n, (ref, buf) in enumerate(
                ((r.w_query, wq), (r.w_key, wk), (r.w_value, wv), (r.w_gate, wg)))
        ]
        s_x = Stream(lambda j: r.tokens.at[tok(j)], xs, xsem)
        for s in weights:
            s.start(0)
        s_x.start(0)

        def product(j):
            n, m = j // 2, j % 2
            slot = n % 2

            @pl.when(m == 0)
            def _():
                for s in weights:
                    s.get(n, nn)

            here = tok(m, rows // 2)
            full = pl.ds(0, width)
            res = dot(r.dgate[here, :], wg[slot], 1, 1)
            for part, w in zip(parts, (wq, wk, wv)):
                res = res + dot(part(here, full), w[slot], 1, 1)
            total[here, pl.ds(pl.multiple_of(n * 256, 256), 256)] = res

        def store(j):
            return pltpu.make_async_copy(out.at[j % 2], r.dtokens.at[tok(j)], osem.at[j % 2])

        def finish_rows(j):
            xb = s_x.get(j, blocks)
            pl.when(j >= 2)(lambda: store(j - 2).wait())

            def one(m, carry):
                here, sub = pl.ds(pl.multiple_of(j * TILE + m * 32, 32), 32), tok(m, 32)
                xv = xb[sub, :].astype(F32)
                scale = lax.rsqrt(jnp.mean(xv * xv, axis=-1, keepdims=True) + EPS)
                out[j % 2, sub, :] = r.dn2[here, :] + norm_back(total[here, :], xv, scale)
                return carry

            for m in range(TILE // 32):
                one(m, 0)
            store(j).start()

        def one(j):
            t = at_square + 8 + j
            send_first(t, BOTH[:1])
            finish_chunks(t, (1,))
            pl.when(j < 4)(lambda: make_square(t, at_square + 8, r.at0, dq_cols))
            pl.when((j >= 4) & (j < 8))(lambda: make_square(t, at_square + 12, r.at0, dk_cols))
            pl.when(j >= 8)(lambda: make_square(t, at_square + 16, r.at0, dv_cols))
            pl.when(j < 2 * nn)(lambda: product(j))
            pl.when(j >= 2 * nn)(lambda: finish_rows(j - 2 * nn))
            move(t, BOTH[:1])

        steps(12, one)
        store(blocks - 2).wait()
        store(blocks - 1).wait()

    pl.run_scoped(
        segment4, *[ring((256, width), BF16)] * 4, pltpu.VMEM((rows, width), F32),
        ring((TILE, width), BF16), ring((TILE, width), F32), dma(4, 2), dma(2), dma(2))

    def rest(j):
        t = chunks + j
        finish_chunks(t, (1,))
        finish_chunks(t, range(2, len(quick)))
        move(t, BOTH[:1])

    steps(len(quick) - 1, rest)


def back(args, seqs, blk):
    rows, width = args["tokens"].shape
    ff = args["first"].shape[1]
    pairs = width // (2 * HEAD)
    anywhere = pl.BlockSpec(memory_space=pl.ANY)
    cut = 4

    def v(*shape, dtype=F32):
        return pltpu.VMEM(shape, dtype)

    def sem(*shape):
        return pltpu.SemaphoreType.DMA(shape)

    n_scan = seqs * 2
    chunk = (4, 2, 2, 64, 128)
    scratch = dict(
        tbuf=v(2, *chunk), core_rx=v(LAND, *chunk), acc=v(ACC, *chunk), xa=v(LAND, 4, 2, 32, 128),
        ya=v(LAND, 4, 32, 128), yb=v(LAND, 4, 2, 56, 128), xb=v(LAND, 4, 56, 128),
        xc=v(LAND, 2, 16, 128), yc=v(LAND, 16, 128), zab=v(LAND, 2, 3, 56, 128),
        zc=v(LAND, 2, 3, 2, 2, 16, 128), fin=v(FIN, 2, 64, 128),
        ssem=sem(7, LAND), rsem=sem(7, LAND), zss=sem(2, 2, 3, LAND), zrs=sem(2, 2, 3, LAND),
        osem=sem(FIN), csem=sem(FIN), crem=sem(FIN), ygs=sem(FIN), ygr=sem(FIN),
        dyv=v(rows, width, dtype=BF16), dfs=v(2, rows, ff, dtype=BF16), dn2=v(rows, width),
        dlow=v(rows, width, dtype=BF16), dgate=v(rows, width, dtype=BF16),
        dattn=v(rows, width, dtype=BF16), at0=v(8, 2, 64, rows, dtype=BF16),
        at1=v(8, 2, 64, rows, dtype=BF16), held=v(n_scan, cut, HEAD, 128), sums=v(n_scan, cut, HEAD, 128),
        other=v(n_scan, cut, HEAD, 128), dstate=v(n_scan, cut, HEAD, 128, dtype=BF16),
        sz=sem(n_scan), rz=sem(n_scan), sx=sem(n_scan), rx=sem(n_scan),
        gacc=v(8, width), gbuf=v(8, 128), gland=v(6, 8, 128), gs=sem(6), gr=sem(6), lsem=sem(5),
        qab=v(2, 3, 48, 128), qc=v(2, 3, 2, 2, 16, 128), qss=sem(2, 3, 2), qrs=sem(2, 3, 2),
        qxc=v(2, 2, 16, 128), qyc=v(2, 16, 128), qks=sem(2, 2), qkr=sem(2, 2),
    )
    args = dict(args)
    args["innert"] = args["innert"].reshape(8, ff // 8, rows)
    for name in ("normt", "norm2t", "mixedt"):
        args[name] = args[name].reshape(8, 2, 64, rows)
    args["gain"] = args["gain"].reshape(1, width)
    outs = dict(
        output=((rows, width), BF16), dtokens=((rows, width), F32), tall=((ff // 8, width), F32),
        wide=((2, width // 8, ff), F32), square=((5, width // 8, width), F32), dgain=((8, 128), F32),
    )
    return pl.pallas_call(
        functools.partial(back_kernel, blk // 2, seqs, (*args, *outs, *scratch)),
        out_shape=[jax.ShapeDtypeStruct(*of) for of in outs.values()],
        in_specs=[anywhere] * len(args),
        out_specs=[anywhere] * len(outs),
        scratch_shapes=list(scratch.values()),
        compiler_params=pltpu.CompilerParams(
            collective_id=3, has_side_effects=True, vmem_limit_bytes=60 * MIB),
        cost_estimate=pl.CostEstimate(flops=60 * 2**30, bytes_accessed=200 * MIB, transcendentals=0),
    )(*args.values())


def rms(value):
    return lax.rsqrt(jnp.mean(value * value, axis=-1, keepdims=True) + EPS)


def forward(blk, seqs, xf, weights):
    w_query, w_key, w_value, w_gate, w_out, out_gain, w_first, w_second, w_third = weights
    normed = (xf * rms(xf)).astype(BF16)
    key = project(normed, w_key)
    value = project(normed, w_value)
    k, v = silu_parts(key)[0].astype(BF16), value.astype(BF16)
    prefix = entering(local_states(k, v, seqs), blk, False)
    query = project(normed, w_query)
    gate = project(normed, w_gate)
    q = silu_parts(query)[0].astype(BF16)
    attn = attention(q, k, v, prefix, seqs)
    mixed = (attn * rms(attn) * out_gain * silu_parts(gate)[0]).astype(BF16)
    resid = xf + project(mixed, w_out)
    normed2 = (resid * rms(resid)).astype(BF16)
    first = project(normed2, w_first)
    second = project(normed2, w_second)
    inner = (first * second).astype(BF16)
    return dict(
        normed=normed, query=query, key=key, gate=gate, q=q, k=k, v=v, prefix=prefix, attn=attn,
        mixed=mixed, resid=resid, normed2=normed2, first=first, second=second, inner=inner)


def backward_plain(blk, seqs, xf, grad_top, f, weights):
    w_query, w_key, w_value, w_gate, w_out, out_gain, w_first, w_second, w_third = weights
    output = (f["resid"] + project(f["inner"], w_third)).astype(BF16)
    grad_w3 = weight_grad(f["inner"], grad_top)
    grad_inner = back_project(grad_top, w_third)
    grad_one = (grad_inner * f["second"]).astype(BF16)
    grad_two = (grad_inner * f["first"]).astype(BF16)
    grad_w1 = weight_grad(f["normed2"], grad_one)
    grad_w2 = weight_grad(f["normed2"], grad_two)
    grad_normed2 = back_project(grad_one, w_first) + back_project(grad_two, w_second)
    resid, attn = f["resid"], f["attn"]
    grad_resid = grad_top.astype(F32) + norm_back(grad_normed2, resid, rms(resid))
    grad_resid_low = grad_resid.astype(BF16)
    grad_wo = weight_grad(f["mixed"], grad_resid_low)
    grad_mixed = back_project(grad_resid_low, w_out)
    gate_act, gate_der = silu_parts(f["gate"])
    rattn = rms(attn)
    unit_attn = attn * rattn
    grad_scaled = grad_mixed * gate_act
    grad_gate_low = (grad_mixed * (unit_attn * out_gain) * gate_der).astype(BF16)
    grad_gain = jnp.sum(grad_scaled * unit_attn, axis=0)
    grad_attn = norm_back(grad_scaled * out_gain, attn, rattn).astype(BF16)
    q, k, v, prefix = f["q"], f["k"], f["v"], f["prefix"]
    dstate = entering(local_states(q, grad_attn, seqs), blk, True)
    grad_fq, grad_fk, grad_vv = attention_back(q, k, v, grad_attn, prefix, dstate, seqs)
    grad_query_low = (grad_fq * silu_parts(f["query"])[1]).astype(BF16)
    grad_key_low = (grad_fk * silu_parts(f["key"])[1]).astype(BF16)
    grad_value_low = grad_vv.astype(BF16)
    normed = f["normed"]
    grads = [weight_grad(normed, g) for g in (grad_query_low, grad_key_low, grad_value_low, grad_gate_low)]
    grads += [grad_wo, grad_gain, grad_w1, grad_w2, grad_w3]
    grad_normed = back_project(grad_query_low, w_query) + back_project(grad_key_low, w_key)
    grad_normed = (
        grad_normed + back_project(grad_value_low, w_value) + back_project(grad_gate_low, w_gate)
    )
    grad_input = grad_resid + norm_back(grad_normed, xf, rms(xf))
    summed = [
        lax.psum(lax.psum_scatter(g, "blk", scatter_dimension=0, tiled=True), "batch") for g in grads]
    return output, grad_input, summed


def laid_out(output, grad_input, tall, wide, square, dgain):
    arrays = (output, grad_input, tall, wide, square, dgain)
    squares, wides = square.shape[0], wide.shape[0]
    shapes = [square.shape[1:]] * squares + [wide.shape[1:]] * wides + [(1, dgain.shape[1])]
    types = [F32] * len(shapes) + [output.dtype, grad_input.dtype, F32]
    shapes += [output.shape, grad_input.shape, tall.shape]
    cuts = [1] * squares + [2] * wides + [1, 2, 4, 2]

    def kernel(output, grad_input, tall, wide, square, dgain, *rest):
        outs, bufs = rest[:len(shapes)], rest[len(shapes):2 * len(shapes)]
        sem_in, sem_out = rest[2 * len(shapes):]
        k = lax.axis_index("blk")
        ins = [square.at[n] for n in range(squares)] + [wide.at[n] for n in range(wides)]
        ins += [dgain.at[pl.ds(k, 1)], output, grad_input, tall]
        loads, stores = [], []
        for src, buf, dst, cut in zip(ins, bufs, outs, cuts):
            step = dst.shape[0] // cut
            for n in range(cut):
                part = pl.ds(n * step, step)
                m = len(loads)
                loads.append(pltpu.make_async_copy(src.at[part], buf.at[part], sem_in.at[m]))
                stores.append(pltpu.make_async_copy(buf.at[part], dst.at[part], sem_out.at[m]))
        for copy in loads:
            copy.start()
        for load, store in zip(loads, stores):
            load.wait()
            store.start()
        for copy in stores:
            copy.wait()

    anywhere = pl.BlockSpec(memory_space=pl.ANY)
    outs = pl.pallas_call(
        kernel,
        out_shape=[jax.ShapeDtypeStruct(*of) for of in zip(shapes, types)],
        in_specs=[anywhere] * len(arrays),
        out_specs=[anywhere] * len(shapes),
        scratch_shapes=[pltpu.VMEM(*of) for of in zip(shapes, types)]
        + [pltpu.SemaphoreType.DMA((sum(cuts),))] * 2,
        compiler_params=pltpu.CompilerParams(vmem_limit_bytes=60 * MIB),
    )(*arrays)
    return outs[:squares], outs[squares:squares + wides], *outs[squares + wides:]


def backward(blk, seqs, tokens, grad_top, f, weights):
    w_query, w_key, w_value, w_gate, w_out, gain, w_first, w_second, w_third = weights
    args = dict(
        tokens=tokens, dy=grad_top, gain=gain, w_query=w_query, w_key=w_key, w_value=w_value,
        w_gate=w_gate, w_out=w_out, w_first=w_first, w_second=w_second, w_third=w_third)
    args.update(f)
    output, grad_input, tall, wide, square, dgain = back(args, seqs, blk)
    (so, sg, sq, sk, sv), (s1, s2), sgain, output, grad_input, tall = laid_out(
        output, grad_input, tall, wide, square, dgain)
    return output, grad_input, [sq, sk, sv, sg, so, sgain.reshape(-1), s1, s2, tall]


def body(sizes, tokens, cotangent, *weights):
    batch, blk = sizes
    seqs, span, width = tokens.shape
    rows = seqs * span
    low = tokens.reshape(rows, width)
    xf = low.astype(F32)
    grad_top = cotangent.reshape(rows, width)
    ff = weights[-1].shape[0]
    if (batch, blk, rows, span, width, ff % 256) == (4, 8, 1024, 128, 1024, 0):
        f = forward_fast(blk, seqs, low, weights)
        output, grad_input, grads = backward(blk, seqs, low, grad_top, f, weights)
    else:
        f = forward(blk, seqs, xf, weights)
        output, grad_input, grads = backward_plain(blk, seqs, xf, grad_top, f, weights)
    shape = (seqs, span, width)
    return (output.reshape(shape), grad_input.reshape(shape), *grads)


def solution(mesh):
    rows = P("batch", "blk", None)
    cut = P("blk", None)
    return jax.shard_map(
        functools.partial(body, (mesh.shape["batch"], mesh.shape["blk"])),
        mesh=mesh,
        in_specs=(rows, rows) + (P(),) * 9,
        out_specs=(rows, rows) + (cut,) * 5 + (P("blk"),) + (cut,) * 3,
        check_vma=False,
    )
```

```python
import functools

import jax
import jax.numpy as jnp
from jax import lax
from jax.experimental import pallas as pl
from jax.experimental.pallas import tpu as pltpu
from jax.sharding import PartitionSpec as P

HEAD = 64
EPS = 1e-06
MESH = pl.DeviceIdType.MESH
F32 = jnp.float32
BF16 = jnp.bfloat16
MIB = 2**20


def silu_parts(pre):
    sig = jax.nn.sigmoid(pre)
    return (pre * sig, sig * (1.0 + pre * (1.0 - sig)))


def norm_back(grad, value, scale):
    inner = jnp.mean(grad * value, axis=-1, keepdims=True)
    return scale * grad - value * (scale * scale * scale) * inner


def project(left, weight):
    return jnp.dot(left, weight, preferred_element_type=F32)


def weight_grad(left, right):
    return jnp.einsum("td,tf->df", left, right, preferred_element_type=F32)


def back_project(grad, weight):
    return jnp.einsum("tf,df->td", grad, weight, preferred_element_type=F32)


def dot(a, b, ca, cb):
    return lax.dot_general(a, b, (((ca,), (cb,)), ((), ())), preferred_element_type=F32)


def low_lanes(shape):
    return lax.broadcasted_iota(jnp.int32, shape, len(shape) - 1) < HEAD


def two_heads(x):
    low = low_lanes(x.shape)
    zero = jnp.zeros_like(x)
    return jnp.concatenate([jnp.where(low, x, zero), jnp.where(low, zero, x)], axis=0)


def pick_heads(x):
    half = x.shape[0] // 2
    return jnp.where(low_lanes((half, x.shape[1])), x[:half], x[half:])


def causal_pair(span):
    t = lax.broadcasted_iota(jnp.int32, (span, 2 * span), 0)
    u = lax.broadcasted_iota(jnp.int32, (span, 2 * span), 1)
    return t >= u % span


def pair_of(ref, p):
    return ref[:, pl.ds(p * 2 * HEAD, 2 * HEAD)]


def state_kernel(left_ref, right_ref, out_ref):
    for p in range(out_ref.shape[1]):
        out_ref[0, p] = pick_heads(dot(pair_of(left_ref, p), pair_of(right_ref, p), 0, 0))


def attn_kernel(q_ref, k_ref, v_ref, prefix_ref, out_ref):
    span = q_ref.shape[0]
    causal = causal_pair(span)
    for p in range(prefix_ref.shape[1]):
        q, k2, v2 = pair_of(q_ref, p), two_heads(pair_of(k_ref, p)), two_heads(pair_of(v_ref, p))
        scores = jnp.where(causal, dot(q, k2, 1, 1), 0.0).astype(BF16)
        prefix = two_heads(prefix_ref[0, p])
        out_ref[:, pl.ds(p * 2 * HEAD, 2 * HEAD)] = dot(scores, v2, 1, 0) + dot(q, prefix, 1, 0)


def attn_back_kernel(q_ref, k_ref, v_ref, g_ref, prefix_ref, dstate_ref, dq_ref, dk_ref, dv_ref):
    span = q_ref.shape[0]
    causal = causal_pair(span)
    for p in range(prefix_ref.shape[1]):
        q, k, v, g = (pair_of(r, p) for r in (q_ref, k_ref, v_ref, g_ref))
        k2, v2 = two_heads(k), two_heads(v)
        prefix, dstate = two_heads(prefix_ref[0, p]), two_heads(dstate_ref[0, p])
        scores = jnp.where(causal, dot(q, k2, 1, 1), 0.0).astype(BF16)
        dscores = jnp.where(causal, dot(g, v2, 1, 1), 0.0).astype(BF16)
        lanes = pl.ds(p * 2 * HEAD, 2 * HEAD)
        dq_ref[:, lanes] = dot(dscores, k2, 1, 0) + dot(g, prefix, 1, 1)
        dk_ref[:, lanes] = pick_heads(dot(dscores, q, 0, 0)) + dot(v, dstate, 1, 1)
        dv_ref[:, lanes] = pick_heads(dot(scores, g, 0, 0)) + dot(k, dstate, 1, 0)


def rows_spec(span, width):
    return pl.BlockSpec((span, width), lambda s: (s, 0))


def state_spec(pairs):
    return pl.BlockSpec((1, pairs, HEAD, 2 * HEAD), lambda s: (s, 0, 0, 0))


def local_states(left, right, seqs):
    rows, width = left.shape
    span, pairs = rows // seqs, width // (2 * HEAD)
    return pl.pallas_call(
        state_kernel,
        grid=(seqs,),
        in_specs=[rows_spec(span, width)] * 2,
        out_specs=state_spec(pairs),
        out_shape=jax.ShapeDtypeStruct((seqs, pairs, HEAD, 2 * HEAD), F32),
    )(left, right)


def attention(q, k, v, prefix, seqs):
    rows, width = q.shape
    span, pairs = rows // seqs, width // (2 * HEAD)
    return pl.pallas_call(
        attn_kernel,
        grid=(seqs,),
        in_specs=[rows_spec(span, width)] * 3 + [state_spec(pairs)],
        out_specs=rows_spec(span, width),
        out_shape=jax.ShapeDtypeStruct((rows, width), F32),
    )(q, k, v, prefix)


def attention_back(q, k, v, g, prefix, dstate, seqs):
    rows, width = q.shape
    span, pairs = rows // seqs, width // (2 * HEAD)
    return pl.pallas_call(
        attn_back_kernel,
        grid=(seqs,),
        in_specs=[rows_spec(span, width)] * 4 + [state_spec(pairs)] * 2,
        out_specs=[rows_spec(span, width)] * 3,
        out_shape=[jax.ShapeDtypeStruct((rows, width), F32)] * 3,
    )(q, k, v, g, prefix, dstate)


def scan_kernel(outer, reverse, s_ref, out_ref, held, summed, other, zs, zr, xs, xr):
    chunks = s_ref.shape[0]
    k = lax.axis_index("blk")
    z, x = k // 2, k % 2
    if reverse:
        zz, xx = outer - 1 - z, 1 - x
        after, before = jnp.maximum(z - 1, 0), jnp.minimum(z + 1, outer - 1)
    else:
        zz, xx = z, x
        after, before = jnp.minimum(z + 1, outer - 1), jnp.maximum(z - 1, 0)
    nxt, prv, side = {"blk": after * 2 + x}, {"blk": before * 2 + x}, {"blk": z * 2 + 1 - x}
    first, last = zz == 0, zz == outer - 1

    bar = pltpu.get_barrier_semaphore()
    pl.semaphore_signal(bar, inc=1, device_id=side, device_id_type=MESH)
    pl.when(~last)(lambda: pl.semaphore_signal(bar, inc=1, device_id=nxt, device_id_type=MESH))
    pl.when(~first)(lambda: pl.semaphore_signal(bar, inc=1, device_id=prv, device_id_type=MESH))
    pl.semaphore_wait(bar, 1 + jnp.where(last, 0, 1) + jnp.where(first, 0, 1))

    def along(i):
        return pltpu.make_async_remote_copy(
            src_ref=summed.at[i], dst_ref=held.at[i], send_sem=zs.at[i], recv_sem=zr.at[i],
            device_id=nxt, device_id_type=MESH)

    def across(i, src):
        return pltpu.make_async_remote_copy(
            src_ref=src.at[i], dst_ref=other.at[i], send_sem=xs.at[i], recv_sem=xr.at[i],
            device_id=side, device_id_type=MESH)

    def pass_on(i):
        pl.when(~first)(lambda: along(i).wait_recv())

        @pl.when(first)
        def _():
            held[i] = jnp.zeros_like(held[i])

        summed[i] = held[i] + s_ref[i]
        pl.when(~last)(lambda: along(i).start())
        pl.when(xx == 0)(lambda: across(i, summed).start())
        pl.when(xx == 1)(lambda: across(i, held).start())

    def finish(i):
        across(i, held).wait_recv()
        out_ref[i] = (held[i] + other[i]).astype(out_ref.dtype)

    def step(i, carry):
        pl.when(i < chunks)(lambda: pass_on(i))
        pl.when(i > 0)(lambda: finish(i - 1))
        return carry

    lax.fori_loop(0, chunks + 1, step, 0)

    def drain(i, carry):
        pl.when(~last)(lambda: along(i).wait_send())
        across(i, held).wait_send()
        return carry

    lax.fori_loop(0, chunks, drain, 0)


def entering(states, blk, reverse):
    seqs, pairs, head, lanes = states.shape
    per = max(1, pairs // 2)
    shape = (seqs * pairs // per, per, head, lanes)
    vmem = pl.BlockSpec(memory_space=pltpu.VMEM)
    sems = [pltpu.SemaphoreType.DMA((shape[0],))] * 4
    out = pl.pallas_call(
        functools.partial(scan_kernel, blk // 2, reverse),
        out_shape=jax.ShapeDtypeStruct(shape, BF16),
        in_specs=[vmem],
        out_specs=vmem,
        scratch_shapes=[pltpu.VMEM(shape, F32)] * 3 + sems,
        compiler_params=pltpu.CompilerParams(
            collective_id=2 if reverse else 1, has_side_effects=True, vmem_limit_bytes=24 * MIB),
    )(states.reshape(shape))
    return out.reshape(states.shape)


LAND, FIN, ACC = 4, 8, 10
CORE, XA, YA, YB, XB, XC, YC = range(7)
TILE = 256


SPARE = (2, 19)
QUICK = 2


class Way:
    def __init__(self, a, b, c):
        self.a = pl.ds(0, a) if a else None
        self.b, self.c = pl.ds(a, b), pl.ds(a + b, c)
        self.ab, self.top_a = pl.ds(0, a + b), pl.ds(0, max(a, 8))
        self.top_b, self.top_c = pl.ds(0, b), pl.ds(0, c)


class Named:
    def __init__(self, names, refs):
        self.__dict__.update(zip(names, refs))


class Stream:
    def __init__(self, block, buf, sem):
        self.block, self.buf, self.sem = block, buf, sem

    def copy(self, j):
        return pltpu.make_async_copy(self.block(j), self.buf.at[j % 2], self.sem.at[j % 2])

    def start(self, j):
        self.copy(j).start()

    def get(self, j, count):
        self.copy(j).wait()
        pl.when(j + 1 < count)(lambda: self.start(j + 1))
        return self.buf.at[j % 2]


LAG, WAIT, OFFER = 1, 8, (0, 1, 4, 8)


def forward_kernel(outer, seqs, names, results, *refs):
    r = Named(names, refs)
    rows, width = r.tokens.shape
    ff = r.w_first.shape[1]
    span, pairs = rows // seqs, width // (2 * HEAD)
    blocks, per_block = rows // TILE, TILE // span
    n_scan, cut = r.sums.shape[:2]
    per_seq = pairs // cut

    k = lax.axis_index("blk")
    z, x = k // 2, k % 2
    top = outer - 1
    side = {"blk": z * 2 + 1 - x}
    above, below = {"blk": jnp.minimum(z + 1, top) * 2 + x}, {"blk": jnp.maximum(z - 1, 0) * 2 + x}
    bar = pltpu.get_barrier_semaphore()
    pl.semaphore_signal(bar, inc=1, device_id=side, device_id_type=MESH)
    pl.when(z < top)(lambda: pl.semaphore_signal(bar, inc=1, device_id=above, device_id_type=MESH))
    pl.when(z > 0)(lambda: pl.semaphore_signal(bar, inc=1, device_id=below, device_id_type=MESH))

    def span_of(start, size, step):
        return pl.ds(start if isinstance(start, int) else pl.multiple_of(start, step), size)

    def tok(j, n=TILE):
        return span_of(j * n, n, n)

    loads = [
        pltpu.make_async_copy(src, dst, r.lsem.at[n])
        for n, (src, dst) in enumerate((
            (r.w_key, r.wk), (r.w_value, r.wv), (r.w_query, r.wq), (r.w_gate, r.wg), (r.gain, r.gv),
            (r.w_out, r.wo), (r.w_first, r.w1), (r.w_second, r.w2)))
    ]

    def x_load(j):
        return pltpu.make_async_copy(r.tokens.at[tok(j)], r.xv.at[tok(j)], r.xsem.at[j])

    by_rows = dict(
        k=lambda j: r.kb.at[tok(j)], v=lambda j: r.vb.at[tok(j)], q=lambda j: r.qb.at[tok(j)],
        gate=lambda j: r.gb.at[tok(j)], key=lambda j: r.keyb, query=lambda j: r.queryb,
        attn=lambda j: r.attnb, resid=lambda j: r.residb, first=lambda j: r.firstb,
        second=lambda j: r.secondb, inner=lambda j: r.innerb)
    by_cols = dict(normt=r.tb0, mixedt=r.tb1, norm2t=r.tb2, innert=r.innertb)

    def store(name, j):
        sem = r.osem.at[results.index(name)]
        out = getattr(r, name)
        if name in by_rows:
            return pltpu.make_async_copy(by_rows[name](j), out.at[tok(j)], sem)
        return pltpu.make_async_copy(by_cols[name], out.at[:, tok(j)], sem)

    def free(name, j):
        pl.when(j > 0)(lambda: store(name, j - 1).wait())

    def remote(src, dst, s, t, dev):
        return pltpu.make_async_remote_copy(
            src_ref=src, dst_ref=dst, send_sem=s, recv_sem=t, device_id=dev, device_id_type=MESH)

    def along(i):
        return remote(r.sums.at[i], r.held.at[i], r.sz.at[i], r.rz.at[i], above)

    def across(i, src):
        return remote(src.at[i], r.other.at[i], r.sx.at[i], r.rx.at[i], side)

    def owned(i):
        return i % 2 == x

    def pass_on(i):
        across(i, r.other).wait_recv()
        pl.when(z > 0)(lambda: along(i).wait_recv())

        @pl.when(z == 0)
        def _():
            r.held[i] = jnp.zeros_like(r.held[i])

        @pl.when(x == 0)
        def _():
            mine = r.held[i] + r.sums[i]
            r.pre[i] = r.held[i].astype(BF16)
            r.sums[i] = mine + r.other[i]
            r.other[i] = mine
            across(i, r.other).start()

        @pl.when(x == 1)
        def _():
            mine = r.held[i] + r.other[i]
            r.pre[i] = mine.astype(BF16)
            r.sums[i] = mine + r.sums[i]
            across(i, r.held).start()

        pl.when(z < top)(lambda: along(i).start())

    def finish(i):
        @pl.when(owned(i))
        def _():
            pl.when(z < top)(lambda: along(i).wait_send())

        @pl.when(~owned(i))
        def _():
            across(i, r.sums).wait_recv()
            r.pre[i] = r.other[i].astype(BF16)

        across(i, r.sums).wait_send()

    def scan(n):
        per_tile = n_scan // blocks
        for j in range(blocks):
            @pl.when(n == OFFER[j])
            def _(j=j):
                for g in range(per_tile):
                    i = j * per_tile + g
                    pl.when(~owned(i))(lambda: across(i, r.sums).start())

        i = (n - 1 - LAG * z) * 2

        @pl.when((i >= 0) & (i < n_scan))
        def _():
            for g in range(2):
                pl.when(owned(i + g))(lambda: pass_on(i + g))

        q = (n - WAIT) * 2

        @pl.when((q >= 0) & (q < n_scan))
        def _():
            for g in range(2):
                finish(q + g)

    def transposed(src, dst):
        for n in range(dst.shape[0] // 128):
            cols = pl.ds(n * 128, 128)
            dst[cols, :] = src[:, cols].T

    def norm_rows(value):
        return (value * lax.rsqrt(jnp.mean(value * value, axis=-1, keepdims=True) + EPS)).astype(BF16)

    def each(count, one):
        for m in range(count):
            one(m)

    def rows_of(j, m):
        return span_of(j * TILE + m * 32, 32, 32)

    def col(n):
        return span_of(n * 256, 256, 256)

    def tile_keys(j):
        x_load(j).wait()

        @pl.when(j == 0)
        def _():
            loads[0].wait()
            loads[1].wait()
            for n in range(1, blocks):
                x_load(n).start()
            for copy in loads[2:]:
                copy.start()

        for name in ("key", "k", "v"):
            free(name, j)

        def one(m):
            r.nrm[rows_of(j, m), :] = norm_rows(r.xv[rows_of(j, m), :].astype(F32))

        each(TILE // 32, one)

        def product(n):
            key = dot(r.nrm[tok(j), :], r.wk[:, col(n)], 1, 0)
            r.keyb[:, col(n)] = key.astype(BF16)
            r.kb[tok(j), col(n)] = silu_parts(key)[0].astype(BF16)
            r.vb[tok(j), col(n)] = dot(r.nrm[tok(j), :], r.wv[:, col(n)], 1, 0).astype(BF16)

        each(width // 256, product)

        def states(m):
            s = j * per_block + m
            for p in range(pairs):
                lanes = pl.ds(p * 2 * HEAD, 2 * HEAD)
                here = tok(s, span)
                r.sums[s * per_seq + p // cut, p % cut] = pick_heads(dot(r.kb[here, lanes], r.vb[here, lanes], 0, 0))

        each(per_block, states)
        for name in ("key", "k", "v"):
            store(name, j).start()

    def tile_query(j):
        @pl.when(j == 0)
        def _():
            loads[2].wait()
            loads[3].wait()

        for name in ("query", "q", "gate", "normt"):
            free(name, j)

        def product(n):
            query = dot(r.nrm[tok(j), :], r.wq[:, col(n)], 1, 0)
            r.queryb[:, col(n)] = query.astype(BF16)
            r.qb[tok(j), col(n)] = silu_parts(query)[0].astype(BF16)
            r.gb[tok(j), col(n)] = dot(r.nrm[tok(j), :], r.wg[:, col(n)], 1, 0).astype(BF16)

        each(width // 256, product)
        transposed(r.nrm.at[tok(j)], r.tb0)
        for name in ("query", "q", "gate", "normt"):
            store(name, j).start()

    def tile_scores(s):
        causal = causal_pair(span)
        here = tok(s, span)
        for p in range(pairs):
            lanes = pl.ds(p * 2 * HEAD, 2 * HEAD)
            q, k2, v2 = r.qb[here, lanes], two_heads(r.kb[here, lanes]), two_heads(r.vb[here, lanes])
            scores = jnp.where(causal, dot(q, k2, 1, 1), 0.0).astype(BF16)
            r.intra[here, lanes] = dot(scores, v2, 1, 0)

    def tile_mixed(j, m):
        if m == 0:
            pl.when(j == 0)(lambda: loads[4].wait())
            for name in ("attn", "mixedt"):
                free(name, j)
        s = j * per_block + m
        here = tok(s, span)
        for p in range(pairs):
            lanes = pl.ds(p * 2 * HEAD, 2 * HEAD)
            prefix = two_heads(r.pre[s * per_seq + p // cut, p % cut])
            r.intra[here, lanes] = r.intra[here, lanes] + dot(r.qb[here, lanes], prefix, 1, 0)
        for n in range(m * span // 32, (m + 1) * span // 32):
            av = r.intra[rows_of(j, n), :]
            scale = lax.rsqrt(jnp.mean(av * av, axis=-1, keepdims=True) + EPS)
            act = silu_parts(r.gb[rows_of(j, n), :].astype(F32))[0]
            r.attnb[tok(n, 32), :] = av.astype(BF16)
            r.mixb[tok(n, 32), :] = (av * scale * r.gv[...] * act).astype(BF16)
        for n in range(width // 128):
            r.tb1[pl.ds(n * 128, 128), tok(m, span)] = r.mixb[tok(m, span), pl.ds(n * 128, 128)].T
        if m == per_block - 1:
            for name in ("attn", "mixedt"):
                store(name, j).start()

    def tile_resid(j):
        pl.when(j == 0)(lambda: loads[5].wait())
        for name in ("resid", "norm2t"):
            free(name, j)

        def product(n):
            r.residb[:, col(n)] = r.xv[tok(j), col(n)].astype(F32) + dot(r.mixb[...], r.wo[:, col(n)], 1, 0)

        each(width // 256, product)

        def one(m):
            r.n2b[tok(m, 32), :] = norm_rows(r.residb[tok(m, 32), :])

        each(TILE // 32, one)
        transposed(r.n2b, r.tb2)
        for name in ("resid", "norm2t"):
            store(name, j).start()

    def tile_inner(j, lo, hi):
        def one(n):
            n = n + lo
            first = dot(r.n2b[...], r.w1[:, col(n)], 1, 0)
            second = dot(r.n2b[...], r.w2[:, col(n)], 1, 0)
            inner = (first * second).astype(BF16)
            r.firstb[:, col(n)] = first.astype(BF16)
            r.secondb[:, col(n)] = second.astype(BF16)
            r.innerb[:, col(n)] = inner
            r.innertb[col(n), :] = inner.T

        each(hi - lo, one)

    half = ff // 512 * 256
    halves = (pl.ds(0, half), pl.ds(half, ff - half))

    def up_stores(j, h):
        cols = halves[h]
        sem = lambda name: r.osem.at[results.index(name)]
        copies = [
            pltpu.make_async_copy(by_rows[name](j).at[:, cols], getattr(r, name).at[tok(j), cols], sem(name))
            for name in ("first", "second", "inner")]
        return copies + [
            pltpu.make_async_copy(r.innertb.at[cols], r.innert.at[cols, tok(j)], sem("innert"))]

    def tile_up(j, h):
        if h == 0:
            @pl.when(j == 0)
            def _():
                loads[6].wait()
                loads[7].wait()

            for name in ("first", "second", "inner", "innert"):
                free(name, j)
        tile_inner(j, (0, half // 256)[h], (half // 256, ff // 256)[h])
        for copy in up_stores(j, h):
            copy.start()

    x_load(0).start()
    loads[0].start()
    loads[1].start()

    per = n_scan // blocks // 2

    def slot(n, carry):
        pl.when(n < blocks)(lambda: tile_keys(n))

        @pl.when(n == 0)
        def _():
            pl.semaphore_wait(bar, 1 + jnp.where(z < top, 1, 0) + jnp.where(z > 0, 1, 0))

        @pl.when((n >= blocks) & (n < 2 * blocks))
        def _():
            tile_query(n - blocks)
            for m in range(per_block):
                tile_scores((n - blocks) * per_block + m)

        scan(n)
        w = n - WAIT - per // 2 + 1
        j, m = w // per, w % per
        live = (w >= 0) & (j < blocks)
        pl.when((w >= per) & (j <= blocks) & (m == 0))(lambda: tile_up(j - 1, 1))
        pl.when(live & (m == 0))(lambda: tile_mixed(j, 0))

        @pl.when(live & (m == 2))
        def _():
            tile_mixed(j, 1)
            tile_resid(j)

        pl.when(live & (m == 3))(lambda: tile_up(j, 0))
        return carry

    lax.fori_loop(0, n_scan // 2 + WAIT + 2, slot, 0)
    whole = pltpu.make_async_copy(r.pre, r.prefix, r.osem.at[results.index("prefix")])
    whole.start()
    for name in results[:-1]:
        store(name, blocks - 1).wait()
    whole.wait()


def forward_fast(blk, seqs, tokens, weights):
    w_query, w_key, w_value, w_gate, w_out, out_gain, w_first, w_second, w_third = weights
    rows, width = tokens.shape
    ff = w_first.shape[1]
    pairs = width // (2 * HEAD)
    cut = 2
    n_scan = seqs * pairs // cut

    def v(*shape, dtype=BF16):
        return pltpu.VMEM(shape, dtype)

    def sem(*shape):
        return pltpu.SemaphoreType.DMA(shape)

    wide, tall = (rows, width), (width, ff)
    chunks = (n_scan, cut, HEAD, 2 * HEAD)
    scratch = dict(
        xv=v(*wide), gv=v(1, width, dtype=F32), wq=v(width, width), wk=v(width, width), wv=v(width, width),
        wg=v(width, width), wo=v(width, width), w1=v(*tall), w2=v(*tall), nrm=v(*wide), kb=v(*wide),
        vb=v(*wide), qb=v(*wide), gb=v(*wide), intra=v(*wide, dtype=F32), keyb=v(TILE, width),
        queryb=v(TILE, width), attnb=v(TILE, width), mixb=v(TILE, width), residb=v(TILE, width, dtype=F32),
        n2b=v(TILE, width), firstb=v(TILE, ff), secondb=v(TILE, ff), innerb=v(TILE, ff),
        tb0=v(width, TILE), tb1=v(width, TILE), tb2=v(width, TILE), innertb=v(ff, TILE),
        held=v(*chunks, dtype=F32), sums=v(*chunks, dtype=F32), other=v(*chunks, dtype=F32), pre=v(*chunks),
        sz=sem(n_scan), rz=sem(n_scan), sx=sem(n_scan), rx=sem(n_scan), lsem=sem(8),
        xsem=sem(rows // TILE), osem=sem(16),
    )
    turned = (width, rows)
    outs = dict(
        k=wide, v=wide, key=wide, normt=turned, q=wide, gate=wide, query=wide, attn=wide, mixedt=turned,
        resid=wide, norm2t=turned, first=(rows, ff), second=(rows, ff), inner=(rows, ff),
        innert=(ff, rows), prefix=chunks)
    ins = dict(
        tokens=tokens, gain=out_gain.reshape(1, width), w_query=w_query, w_key=w_key, w_value=w_value,
        w_gate=w_gate, w_out=w_out, w_first=w_first, w_second=w_second)
    results = tuple(outs)
    anywhere = pl.BlockSpec(memory_space=pl.ANY)
    made = pl.pallas_call(
        functools.partial(forward_kernel, blk // 2, seqs, (*ins, *outs, *scratch), results),
        out_shape=[
            jax.ShapeDtypeStruct(shape, F32 if name == "resid" else BF16) for name, shape in outs.items()
        ],
        in_specs=[anywhere] * len(ins),
        out_specs=[anywhere] * len(outs),
        scratch_shapes=list(scratch.values()),
        compiler_params=pltpu.CompilerParams(
            collective_id=4, has_side_effects=True, vmem_limit_bytes=60 * MIB),
        cost_estimate=pl.CostEstimate(flops=26 * 2**30, bytes_accessed=80 * MIB, transcendentals=0),
    )(*ins.values())
    f = dict(zip(results, made))
    f["prefix"] = f["prefix"].reshape(seqs, pairs, HEAD, 2 * HEAD)
    return f


def back_kernel(outer, seqs, names, *refs):
    r = Named(names, refs)
    rows, width = r.tokens.shape
    ff = r.first.shape[1]
    span, pairs = rows // seqs, width // (2 * HEAD)
    n_tall, n_wide, n_square = ff // 256, ff // 128, 20
    chunks = n_tall + n_wide + n_square
    at_wide, at_square = n_tall, n_tall + n_wide
    blocks = rows // TILE

    b, k = lax.axis_index("batch"), lax.axis_index("blk")
    y, c = b // 2, b % 2
    z, x = k // 2, k % 2
    ox, oy = 1 - x, 1 - y
    top = outer - 1
    zr = top - z
    to_core, to_y, to_x = {"batch": y * 2 + 1 - c}, {"batch": oy * 2 + c}, {"blk": z * 2 + ox}
    to_up = {"blk": jnp.minimum(z + 1, top) * 2 + x}
    to_down = {"blk": jnp.maximum(z - 1, 0) * 2 + x}
    to_z = [{"blk": (z + d) % outer * 2 + x} for d in range(1, outer)]

    peers = [to_core, to_y, to_x] + to_z
    bar = pltpu.get_barrier_semaphore()
    for d in peers:
        pl.semaphore_signal(bar, inc=1, device_id=d, device_id_type=MESH)

    def remote(src, dst, s, t, dev):
        return pltpu.make_async_remote_copy(
            src_ref=src, dst_ref=dst, send_sem=s, recv_sem=t, device_id=dev, device_id_type=MESH)

    def link(kind, i, src, dst, dev):
        return remote(src, dst.at[i % LAND], r.ssem.at[kind, i % LAND], r.rsem.at[kind, i % LAND], dev)

    def at(i, *where):
        return r.acc.at[(i % ACC,) + where]

    every = slice(None)

    def core_copy(i):
        return link(CORE, i, r.tbuf.at[i % 2], r.core_rx, to_core)

    def xa_copy(w, i):
        return link(XA, i, at(i, every, ox, every, w.a), r.xa.at[:, :, :, w.top_a], to_x)

    def ya_copy(w, i):
        return link(YA, i, at(i, every, x, oy, w.a), r.ya.at[:, :, w.top_a], to_y)

    def yb_copy(w, i):
        return link(YB, i, at(i, every, every, oy, w.b), r.yb.at[:, :, :, w.top_b], to_y)

    def xb_copy(w, i):
        return link(XB, i, at(i, every, ox, y, w.b), r.xb.at[:, :, w.top_b], to_x)

    def xc_copy(w, i):
        return link(XC, i, at(i, z, ox, every, w.c), r.xc.at[:, :, w.top_c], to_x)

    def yc_copy(w, i):
        return link(YC, i, at(i, z, x, oy, w.c), r.yc.at[:, w.top_c], to_y)

    def y_share(i):
        f = i % FIN
        return remote(r.fin.at[f, y], r.fin.at[f, y], r.ygs.at[f], r.ygr.at[f], to_y)

    def part_ab(w, i, s):
        return at(i, s, x, y, w.ab)

    def part_c(w, i, s):
        return at(i, s, every, every, w.c)

    def land_ab(w, i, d, n):
        return r.zab.at[i % LAND, d, n - 1, w.ab]

    def land_c(w, i, d, n):
        return r.zc.at[i % LAND, d, n - 1, :, :, w.top_c]

    AB, CC = (0, part_ab, land_ab), (1, part_c, land_c)

    def hop(group, w, i, n, up, s):
        g, part, land = group
        d = 0 if up else 1
        sem = (g, d, n - 1, i % LAND)
        return remote(part(w, i, s), land(w, i, d, n), r.zss.at[sem], r.zrs.at[sem],
                      to_up if up else to_down)

    def z_each(group, w, i, n, act):
        up = hop(group, w, i, n, True, jnp.minimum(outer - n + z, top))
        down = hop(group, w, i, n, False, jnp.maximum(n - 1 - zr, 0))
        pl.when((z <= n - 1) & (z < top))(lambda: act(up))
        pl.when((zr <= n - 1) & (z > 0))(lambda: act(down))

    def z_send(group, w, i, n):
        z_each(group, w, i, n, lambda copy: copy.start())

    def z_sent(group, w, i, n):
        z_each(group, w, i, n, lambda copy: copy.wait_send())

    def add(ref, landed):
        ref[...] = ref[...] + landed[...]

    def z_take(group, w, i, n):
        g, part, land = group

        def take(up, s):
            hop(group, w, i, n, up, s).wait_recv()
            add(part(w, i, s), land(w, i, 0 if up else 1, n))

        pl.when((z > 0) & (z <= n))(lambda: take(True, jnp.clip(outer - n + z - 1, 0, top)))
        pl.when((z < top) & (zr <= n))(lambda: take(False, jnp.clip(n - zr, 0, top)))

    BOTH = (Way(32, 16, 16), Way(0, 48, 16))
    spare = (at_wide + SPARE[0], at_wide + SPARE[1])

    def places(i, act):
        f = r.fin.at[i % FIN]

        @pl.when(i < at_wide)
        def _():
            for yy in range(2):
                for blk in range(2):
                    col = pl.multiple_of(c * (width // 2) + (yy * 2 + blk) * 128, 128)
                    act(f.at[yy, pl.ds(blk * 32, 32)], r.tall.at[pl.ds(i * 32, 32), pl.ds(col, 128)])

        @pl.when((i >= at_wide) & (i < at_square))
        def _():
            j, h = (i - at_wide) // 2, (i - at_wide) % 2
            col = pl.multiple_of(c * (ff // 2) + j * 128, 128)
            for yy in range(2):
                act(f.at[yy], r.wide.at[yy, pl.ds(h * 64, 64), pl.ds(col, 128)])

        @pl.when(i >= at_square)
        def _():
            j = i - at_square
            m, u, h = j // 4, j // 2 % 2, j % 2
            for yy in range(2):
                col = pl.multiple_of(c * (width // 2) + u * 256 + yy * 128, 128)
                act(f.at[yy], r.square.at[m, pl.ds(h * 64, 64), pl.ds(col, 128)])

    def cores(w, i):
        core_copy(i).wait_recv()
        core_copy(i).wait_send()
        add(at(i), r.core_rx.at[i % LAND])
        if w.a is not None:
            xa_copy(w, i).start()
        yb_copy(w, i).start()
        z_send(CC, w, i, 1)

    def second(w, i):
        yb_copy(w, i).wait_recv()
        add(at(i, every, every, y, w.b), r.yb.at[i % LAND, :, :, w.top_b])
        xb_copy(w, i).start()
        if w.a is not None:
            xa_copy(w, i).wait_recv()
            add(at(i, every, x, every, w.a), r.xa.at[i % LAND, :, :, w.top_a])
            ya_copy(w, i).start()
        z_take(CC, w, i, 1)
        z_send(CC, w, i, 2)
        if w.a is not None:
            xa_copy(w, i).wait_send()
        yb_copy(w, i).wait_send()
        z_sent(CC, w, i, 1)

    def third(w, i):
        xb_copy(w, i).wait_recv()
        add(at(i, every, x, y, w.b), r.xb.at[i % LAND, :, w.top_b])
        if w.a is not None:
            ya_copy(w, i).wait_recv()
            add(at(i, every, x, y, w.a), r.ya.at[i % LAND, :, w.top_a])
        z_send(AB, w, i, 1)
        z_take(CC, w, i, 2)
        z_send(CC, w, i, 3)
        xb_copy(w, i).wait_send()
        if w.a is not None:
            ya_copy(w, i).wait_send()
        z_sent(CC, w, i, 2)

    def fourth(w, i):
        z_take(AB, w, i, 1)
        z_send(AB, w, i, 2)
        z_take(CC, w, i, 3)
        xc_copy(w, i).start()
        z_sent(AB, w, i, 1)
        z_sent(CC, w, i, 3)

    def fifth(w, i):
        z_take(AB, w, i, 2)
        z_send(AB, w, i, 3)
        xc_copy(w, i).wait_recv()
        add(at(i, z, x, every, w.c), r.xc.at[i % LAND, :, w.top_c])
        yc_copy(w, i).start()
        z_sent(AB, w, i, 2)
        xc_copy(w, i).wait_send()

    def sixth(w, i):
        yc_copy(w, i).wait_recv()
        z_take(AB, w, i, 3)
        f = i % FIN
        r.fin[f, y, w.ab] = r.acc[i % ACC, z, x, y, w.ab]
        r.fin[f, y, w.c] = r.acc[i % ACC, z, x, y, w.c] + r.yc[i % LAND, w.top_c]
        y_share(i).start()
        z_sent(AB, w, i, 3)
        yc_copy(w, i).wait_send()

    def seventh(w, i):
        y_share(i).wait_recv()
        y_share(i).wait_send()
        f = i % FIN

        def go(src, dst):
            remote(src, dst, r.csem.at[f], r.crem.at[f], to_core).start()
            pltpu.make_async_copy(src, dst, r.osem.at[f]).start()

        places(i, go)

    def last(w, i):
        f = i % FIN
        whole = r.fin.at[f]
        copy = remote(whole, whole, r.csem.at[f], r.crem.at[f], to_core)
        copy.wait_send()
        copy.wait_recv()
        pltpu.make_async_copy(whole, whole, r.osem.at[f]).wait()

    ORDER = range(2, 9)
    stages = (None, cores, second, third, fourth, fifth, sixth, seventh, last)

    def advance(t, some, ways):
        for n in some:
            i = t - n
            live = (i >= 0) & (i < chunks - QUICK)
            if n >= 7:
                pl.when(live)(functools.partial(stages[n], None, i))
                continue
            if len(ways) == 2:
                spared = (i >= spare[0]) & (i < spare[1])
                pl.when(spared)(functools.partial(stages[n], ways[1], i))
                live = live & ~spared
            pl.when(live)(functools.partial(stages[n], ways[0], i))

    def z_straight(group, i, act):
        w = BOTH[0]
        g, part, _ = group
        land = (r.qab, r.qc)[g].at[i % 2]
        for d in range(1, outer):
            sem = (g, d - 1, i % 2)
            act(remote(part(w, i, (z + d) % outer), land.at[d - 1], r.qss.at[sem], r.qrs.at[sem],
                       to_z[d - 1]))

    def z_arrived(group, i):
        w = BOTH[0]
        g, part, _ = group
        land = (r.qab, r.qc)[g].at[i % 2]
        z_straight(group, i, lambda copy: copy.wait_recv())
        total = land[0]
        for d in range(1, outer - 1):
            total = total + land[d]
        ref = part(w, i, z)
        ref[...] = ref[...] + total
        z_straight(group, i, lambda copy: copy.wait_send())

    def quick_xc(i):
        w, m = BOTH[0], i % 2
        return remote(at(i, z, ox, every, w.c), r.qxc.at[m], r.qks.at[0, m], r.qkr.at[0, m], to_x)

    def quick_yc(i):
        w, m = BOTH[0], i % 2
        return remote(at(i, z, x, oy, w.c), r.qyc.at[m], r.qks.at[1, m], r.qkr.at[1, m], to_y)

    def quick_cores(i):
        w = BOTH[0]
        core_copy(i).wait_recv()
        core_copy(i).wait_send()
        add(at(i), r.core_rx.at[i % LAND])
        xa_copy(w, i).start()
        yb_copy(w, i).start()
        z_straight(CC, i, lambda copy: copy.start())

    def quick_second(i):
        w = BOTH[0]
        yb_copy(w, i).wait_recv()
        add(at(i, every, every, y, w.b), r.yb.at[i % LAND, :, :, w.top_b])
        xb_copy(w, i).start()
        z_arrived(CC, i)
        quick_xc(i).start()
        xa_copy(w, i).wait_recv()
        add(at(i, every, x, every, w.a), r.xa.at[i % LAND, :, :, w.top_a])
        ya_copy(w, i).start()
        xa_copy(w, i).wait_send()
        yb_copy(w, i).wait_send()

    def quick_third(i):
        w = BOTH[0]
        quick_xc(i).wait_recv()
        add(at(i, z, x, every, w.c), r.qxc.at[i % 2])
        quick_yc(i).start()
        xb_copy(w, i).wait_recv()
        add(at(i, every, x, y, w.b), r.xb.at[i % LAND, :, w.top_b])
        ya_copy(w, i).wait_recv()
        add(at(i, every, x, y, w.a), r.ya.at[i % LAND, :, w.top_a])
        z_straight(AB, i, lambda copy: copy.start())
        for copy in (xb_copy(w, i), ya_copy(w, i), quick_xc(i)):
            copy.wait_send()

    def quick_fourth(i):
        w = BOTH[0]
        quick_yc(i).wait_recv()
        z_arrived(AB, i)
        f = i % FIN
        r.fin[f, y, w.ab] = r.acc[i % ACC, z, x, y, w.ab]
        r.fin[f, y, w.c] = r.acc[i % ACC, z, x, y, w.c] + r.qyc[i % 2]
        y_share(i).start()
        quick_yc(i).wait_send()

    quick = (None, quick_cores, quick_second, quick_third, quick_fourth,
             functools.partial(seventh, None), functools.partial(last, None))

    def finish_chunks(t, some):
        for n in some:
            i = t - n
            pl.when((i >= chunks - QUICK) & (i < chunks))(functools.partial(quick[n], i))

    def send_first(t, ways=BOTH):
        advance(t, (1,), ways)

    def move(t, ways=BOTH):
        advance(t, ORDER, ways)

    def make(t, fill):
        fill(1 - c, r.tbuf.at[t % 2])
        core_copy(t).start()
        fill(c, r.acc.at[t % ACC])

    def fill_tall(lhs):
        def fill(half, dst):
            for yy in range(2):
                col = pl.multiple_of(half * (width // 2) + yy * 256, 256)
                res = dot(lhs, r.dyv[:, pl.ds(col, 256)], 1, 0).reshape(4, 2, 32, 256)
                for blk in range(2):
                    dst[:, :, yy, pl.ds(blk * 32, 32), :] = res[..., blk * 128:(blk + 1) * 128]
        return fill

    def left_rows(ref, h):
        return ref[:, h].reshape(8 * 64, rows)

    def fill_two(left, h, take):
        def fill(half, dst):
            res = dot(left_rows(left, h), take(half), 1, 0).reshape(4, 2, 64, 256)
            dst[:, :, 0] = res[..., :128]
            dst[:, :, 1] = res[..., 128:]
        return fill

    def make_wide(t):
        i = t - at_wide
        j, h = i // 2, i % 2

        def take(half):
            col = pl.ds(pl.multiple_of(half * (ff // 2) + j * 128, 128), 128)
            return jnp.concatenate([r.dfs[0, :, col], r.dfs[1, :, col]], axis=1)

        make(t, fill_two(r.at0, h, take))

    def make_square(t, base, left, right):
        i = t - base
        u, h = i // 2, i % 2

        def take(half):
            return right(pl.ds(pl.multiple_of(half * (width // 2) + u * 256, 256), 256))

        make(t, fill_two(left, h, take))

    zz, xx = zr, ox
    n_scan = r.sums.shape[0]
    halves = n_scan // seqs
    scan_at = at_wide

    def along(i):
        return remote(r.sums.at[i], r.held.at[i], r.sz.at[i], r.rz.at[i], to_down)

    def across(i, src):
        return remote(src.at[i], r.other.at[i], r.sx.at[i], r.rx.at[i], to_x)

    def owned(i):
        return i % 2 == xx

    def pass_on(i):
        across(i, r.other).wait_recv()
        pl.when(zz > 0)(lambda: along(i).wait_recv())

        @pl.when(zz == 0)
        def _():
            r.held[i] = jnp.zeros_like(r.held[i])

        @pl.when(xx == 0)
        def _():
            mine = r.held[i] + r.sums[i]
            r.dstate[i] = r.held[i].astype(BF16)
            r.sums[i] = mine + r.other[i]
            r.other[i] = mine
            across(i, r.other).start()

        @pl.when(xx == 1)
        def _():
            mine = r.held[i] + r.other[i]
            r.dstate[i] = mine.astype(BF16)
            r.sums[i] = mine + r.sums[i]
            across(i, r.held).start()

        pl.when(zz < top)(lambda: along(i).start())

    def finish(i):
        @pl.when(owned(i))
        def _():
            pl.when(zz < top)(lambda: along(i).wait_send())

        @pl.when(~owned(i))
        def _():
            across(i, r.sums).wait_recv()
            r.dstate[i] = r.other[i].astype(BF16)

        across(i, r.sums).wait_send()

    def scan(t):
        i = t - scan_at
        pl.when((i >= 0) & (i < n_scan) & ~owned(i))(lambda: across(i, r.sums).start())
        j = i - 1 - zz
        pl.when((j >= 0) & (j < n_scan) & owned(j))(lambda: pass_on(j))
        pl.when((j >= 2) & (j < n_scan + 2))(lambda: finish(j - 2))

    def span_of(start, size, step):
        return pl.ds(start if isinstance(start, int) else pl.multiple_of(start, step), size)

    def tok(j, n=TILE):
        return span_of(j * n, n, n)

    def tile_inner(j, w3, w1, w2, first, second):
        def block(m, carry):
            at_rows = tok(m, 512)
            din = dot(r.dyv[at_rows, :], w3[...], 1, 1)
            one = (din * second[at_rows, :].astype(F32)).astype(BF16)
            two = (din * first[at_rows, :].astype(F32)).astype(BF16)
            cols = pl.ds(pl.multiple_of(j * 256, 256), 256)
            r.dfs[0, at_rows, cols] = one
            r.dfs[1, at_rows, cols] = two
            for n in range(width // 256):
                to = pl.ds(n * 256, 256)
                res = dot(one, w1[to, :], 1, 1) + dot(two, w2[to, :], 1, 1)
                r.dn2[at_rows, to] = r.dn2[at_rows, to] + res
            return carry

        for m in range(rows // 512):
            block(m, 0)

    def tile_resid(j, resid, gate, attn, q, w_out, gain, dmix):
        def one(m, carry):
            here, sub = pl.ds(pl.multiple_of(j * TILE + m * 32, 32), 32), tok(m, 32)
            value = resid[sub, :]
            grad = r.dn2[here, :]
            scale = lax.rsqrt(jnp.mean(value * value, axis=-1, keepdims=True) + EPS)
            out = r.dyv[here, :].astype(F32) + norm_back(grad, value, scale)
            r.dn2[here, :] = out
            r.dlow[here, :] = out.astype(BF16)
            return carry

        for m in range(TILE // 32):
            one(m, 0)
        for n in range(width // 256):
            to = pl.ds(n * 256, 256)
            dmix[:, to] = dot(r.dlow[tok(j), :], w_out[to, :], 1, 1)

        def two(m, carry):
            here, sub = pl.ds(pl.multiple_of(j * TILE + m * 32, 32), 32), tok(m, 32)
            av = attn[sub, :].astype(F32)
            scale = lax.rsqrt(jnp.mean(av * av, axis=-1, keepdims=True) + EPS)
            unit = av * scale
            act, der = silu_parts(gate[sub, :].astype(F32))
            dm = dmix[sub, :]
            ds = dm * act
            r.dgate[here, :] = (dm * (unit * gain[...]) * der).astype(BF16)
            r.gacc[...] = r.gacc[...] + jnp.sum((ds * unit).reshape(4, 8, width), axis=0)
            r.dattn[here, :] = norm_back(ds * gain[...], av, scale).astype(BF16)
            return carry

        for m in range(TILE // 32):
            two(m, 0)

        def states(m, carry):
            s = j * (TILE // span) + m
            for p in range(pairs):
                lanes = pl.ds(p * 2 * HEAD, 2 * HEAD)
                grad = r.dattn[tok(s, span), lanes]
                per = pairs // halves
                r.sums[s * halves + p // per, p % per] = pick_heads(dot(q[tok(m, span), lanes], grad, 0, 0))
            return carry

        for m in range(TILE // span):
            states(m, 0)

    def tile_attn(s, q_ref, k_ref, v_ref, query, key, prefix_ref):
        causal = causal_pair(span)
        here = tok(s, span)
        for p in range(pairs):
            lanes = pl.ds(p * 2 * HEAD, 2 * HEAD)
            q, k, v, g = q_ref[:, lanes], k_ref[:, lanes], v_ref[:, lanes], r.dattn[here, lanes]
            k2, v2 = two_heads(k), two_heads(v)
            per = pairs // halves
            prefix, dstate = two_heads(prefix_ref[p]), two_heads(r.dstate[s * halves + p // per, p % per])
            scores = jnp.where(causal, dot(q, k2, 1, 1), 0.0).astype(BF16)
            dscores = jnp.where(causal, dot(g, v2, 1, 1), 0.0).astype(BF16)
            dq = dot(dscores, k2, 1, 0) + dot(g, prefix, 1, 1)
            dk = pick_heads(dot(dscores, q, 0, 0)) + dot(v, dstate, 1, 1)
            dv = pick_heads(dot(scores, g, 0, 0)) + dot(k, dstate, 1, 0)
            r.dfs[0, here, lanes] = (dq * silu_parts(query[:, lanes].astype(F32))[1]).astype(BF16)
            r.dfs[0, here, pl.ds(width + p * 2 * HEAD, 2 * HEAD)] = (
                dk * silu_parts(key[:, lanes].astype(F32))[1]).astype(BF16)
            r.dfs[1, here, lanes] = dv.astype(BF16)

    parts = [
        lambda at_rows, cols: r.dfs[0, at_rows, cols],
        lambda at_rows, cols: r.dfs[0, at_rows, pl.ds(width + cols.start, cols.size)],
        lambda at_rows, cols: r.dfs[1, at_rows, cols],
    ]
    dq_cols = lambda cols: r.dfs[0, :, cols]
    dk_cols = lambda cols: r.dfs[0, :, pl.ds(width + cols.start, cols.size)]
    dv_cols = lambda cols: r.dfs[1, :, cols]

    def load(src, dst, n):
        return pltpu.make_async_copy(src, dst, r.lsem.at[n])

    def dma(*shape):
        return pltpu.SemaphoreType.DMA(shape)

    def ring(shape, dtype):
        return pltpu.VMEM((2,) + shape, dtype)

    def steps(count, one):
        def go(j, carry):
            one(j)
            return carry

        lax.fori_loop(0, count, go, 0)

    dy_load = load(r.dy, r.dyv, 0)
    norm2_load = load(r.norm2t, r.at0, 1)
    mixed_load = load(r.mixedt, r.at1, 2)
    norm_load = load(r.normt, r.at0, 3)

    def segment0(left, w3, w1, w2, first, second, sems):
        cols = lambda ref: lambda j: ref.at[:, pl.ds(pl.multiple_of(j * 256, 256), 256)]
        s_left = Stream(lambda j: r.innert.at[:, pl.ds(pl.multiple_of(j * 32, 32), 32)], left, sems.at[0])
        tiles = [
            Stream(lambda j: r.w_third.at[pl.ds(pl.multiple_of(j * 256, 256), 256)], w3, sems.at[1]),
            Stream(cols(r.w_first), w1, sems.at[2]),
            Stream(cols(r.w_second), w2, sems.at[3]),
            Stream(cols(r.first), first, sems.at[4]),
            Stream(cols(r.second), second, sems.at[5]),
        ]
        s_left.start(0)
        dy_load.start()
        r.dn2[...] = jnp.zeros_like(r.dn2)
        r.gacc[...] = jnp.zeros_like(r.gacc)
        dy_load.wait()
        for s in tiles:
            s.start(0)
        norm2_load.start()
        pl.semaphore_wait(bar, len(peers))

        def one(j):
            send_first(j, BOTH[:1])
            make(j, fill_tall(s_left.get(j, n_tall)[...].reshape(8 * 32, rows)))
            tile_inner(j, *(s.get(j, n_tall) for s in tiles))
            move(j, BOTH[:1])

        steps(n_tall, one)
        norm2_load.wait()

    pl.run_scoped(
        segment0, ring((8, 32, rows), BF16), ring((256, width), BF16), ring((width, 256), BF16),
        ring((width, 256), BF16), ring((rows, 256), BF16), ring((rows, 256), BF16), dma(6, 2))

    def segment1(resid, gate, attn, q, w_out, gain, dmix, sems, wsem):
        blk = lambda ref: lambda j: ref.at[tok(j)]
        tiles = [
            Stream(blk(ref), buf, sems.at[n])
            for n, (ref, buf) in enumerate(((r.resid, resid), (r.gate, gate), (r.attn, attn), (r.q, q)))
        ]
        w_load = pltpu.make_async_copy(r.w_out, w_out, wsem.at[0])
        g_load = pltpu.make_async_copy(r.gain, gain, wsem.at[1])
        w_load.start()
        g_load.start()
        for s in tiles:
            s.start(0)

        def one(j):
            t = at_wide + j
            send_first(t)
            make_wide(t)

            @pl.when(j == 0)
            def _():
                w_load.wait()
                g_load.wait()

            rs, ga, at_, qs = (s.get(j, blocks) for s in tiles)
            tile_resid(j, rs, ga, at_, qs, w_out, gain, dmix)
            move(t)
            scan(t)

        steps(blocks, one)

    pl.run_scoped(
        segment1, ring((TILE, width), F32), ring((TILE, width), BF16), ring((TILE, width), BF16),
        ring((TILE, width), BF16), pltpu.VMEM((width, width), BF16), pltpu.VMEM((1, width), F32),
        pltpu.VMEM((TILE, width), F32), dma(4, 2), dma(2))

    def gain_sum(t):
        base = at_wide + blocks
        hops = [to_core, to_y, to_x]

        def swap(n):
            return remote(r.gbuf, r.gland.at[n], r.gs.at[n], r.gr.at[n], hops[n])

        def spread(d):
            return remote(r.gbuf, r.gland.at[2 + d], r.gs.at[2 + d], r.gr.at[2 + d], to_z[d - 1])

        @pl.when(t == base)
        def _():
            total = jnp.sum(r.gacc[...], axis=0, keepdims=True)
            for n in range(8):
                r.gbuf[pl.ds(n, 1), :] = total[:, n * 128:(n + 1) * 128]
            swap(0).start()

        for n in range(3):
            @pl.when(t == base + 2 + 2 * n)
            def _(n=n):
                swap(n).wait()
                r.gbuf[...] = r.gbuf[...] + r.gland[n]
                if n < 2:
                    swap(n + 1).start()
                else:
                    for d in range(1, outer):
                        spread(d).start()

        @pl.when(t == base + 8)
        def _():
            for d in range(1, outer):
                spread(d).wait()
            for d in range(1, outer):
                r.gbuf[...] = r.gbuf[...] + r.gland[2 + d]
            pltpu.make_async_copy(r.gbuf, r.dgain, r.lsem.at[4]).start()

        pl.when(t == base + 10)(lambda: pltpu.make_async_copy(r.gbuf, r.dgain, r.lsem.at[4]).wait())

    n2 = n_wide - blocks
    n_out = blocks * (width // 256)

    def segment2(w3, inner, resid, out, sems, osem):
        per = width // 256
        cols = lambda j: pl.ds(pl.multiple_of(j % per * 256, 256), 256)
        s_w3 = Stream(lambda j: r.w_third.at[:, cols(j)], w3, sems.at[0])
        s_resid = Stream(lambda j: r.resid.at[tok(j // per), cols(j)], resid, sems.at[1])
        s_inner = Stream(lambda n: r.inner.at[tok(n)], inner, sems.at[2])

        def store(j):
            return pltpu.make_async_copy(out.at[j % 2], r.output.at[tok(j // per), cols(j)], osem.at[j % 2])

        mixed_load.start()
        for s in (s_w3, s_resid, s_inner):
            s.start(0)

        def one(j):
            t = at_wide + blocks + j
            send_first(t)
            make_wide(t)

            @pl.when(j < n_out)
            def _():
                w, res = s_w3.get(j, n_out), s_resid.get(j, n_out)

                @pl.when(j % per == 0)
                def _():
                    s_inner.get(j // per, blocks)

                pl.when(j >= 2)(lambda: store(j - 2).wait())
                prod = dot(inner[j // per % 2], w[...], 1, 0)
                out[j % 2] = (res[...] + prod).astype(BF16)
                store(j).start()

            move(t)
            scan(t)
            gain_sum(t)

        steps(n2, one)
        store(n_out - 2).wait()
        store(n_out - 1).wait()
        mixed_load.wait()

    pl.run_scoped(
        segment2, ring((ff, 256), BF16), ring((TILE, ff), BF16), ring((TILE, 256), F32),
        ring((TILE, 256), BF16), dma(3, 2), dma(2))

    def segment3(q, k, v, query, key, prefix, sems):
        blk = lambda ref: lambda j: ref.at[tok(j, span)]
        tiles = [
            Stream(blk(ref), buf, sems.at[n])
            for n, (ref, buf) in enumerate(((r.q, q), (r.k, k), (r.v, v), (r.query, query), (r.key, key)))
        ]
        tiles.append(Stream(lambda j: r.prefix.at[j], prefix, sems.at[5]))
        norm_load.start()
        for s in tiles:
            s.start(0)

        def one(j):
            t = at_square + j
            send_first(t)
            pl.when(j < 4)(lambda: make_square(t, at_square, r.at1, lambda cols: r.dlow[:, cols]))
            pl.when(j == 4)(lambda: norm_load.wait())
            pl.when(j >= 4)(lambda: make_square(t, at_square + 4, r.at0, lambda cols: r.dgate[:, cols]))
            tile_attn(j, *(s.get(j, seqs) for s in tiles))
            move(t)

        steps(8, one)

    pl.run_scoped(
        segment3, *[ring((span, width), BF16)] * 5, ring((pairs, HEAD, 2 * HEAD), BF16), dma(6, 2))

    def rest(j):
        t = chunks + j
        finish_chunks(t, (1,))
        finish_chunks(t, range(2, len(quick)))
        move(t, BOTH[:1])

    def segment4(wq, wk, wv, wg, total, xs, out, sems, xsem, osem):
        nn = width // 256
        rowsblk = lambda ref: lambda n: ref.at[pl.ds(pl.multiple_of(n * 256, 256), 256)]
        weights = [
            Stream(rowsblk(ref), buf, sems.at[n])
            for n, (ref, buf) in enumerate(
                ((r.w_query, wq), (r.w_key, wk), (r.w_value, wv), (r.w_gate, wg)))
        ]
        s_x = Stream(lambda j: r.tokens.at[tok(j)], xs, xsem)
        for s in weights:
            s.start(0)
        s_x.start(0)

        def product(j):
            n, m = j // 2, j % 2
            slot = n % 2

            @pl.when(m == 0)
            def _():
                for s in weights:
                    s.get(n, nn)

            here = tok(m, rows // 2)
            full = pl.ds(0, width)
            res = dot(r.dgate[here, :], wg[slot], 1, 1)
            for part, w in zip(parts, (wq, wk, wv)):
                res = res + dot(part(here, full), w[slot], 1, 1)
            total[here, pl.ds(pl.multiple_of(n * 256, 256), 256)] = res

        def store(j):
            return pltpu.make_async_copy(out.at[j % 2], r.dtokens.at[tok(j)], osem.at[j % 2])

        def finish_rows(j):
            xb = s_x.get(j, blocks)
            pl.when(j >= 2)(lambda: store(j - 2).wait())

            def one(m, carry):
                here, sub = pl.ds(pl.multiple_of(j * TILE + m * 32, 32), 32), tok(m, 32)
                xv = xb[sub, :].astype(F32)
                scale = lax.rsqrt(jnp.mean(xv * xv, axis=-1, keepdims=True) + EPS)
                out[j % 2, sub, :] = r.dn2[here, :] + norm_back(total[here, :], xv, scale)
                return carry

            for m in range(TILE // 32):
                one(m, 0)
            store(j).start()

        def one(j):
            t = at_square + 8 + j
            send_first(t, BOTH[:1])
            finish_chunks(t, (1,))
            pl.when(j < 4)(lambda: make_square(t, at_square + 8, r.at0, dq_cols))
            pl.when((j >= 4) & (j < 8))(lambda: make_square(t, at_square + 12, r.at0, dk_cols))
            pl.when(j >= 8)(lambda: make_square(t, at_square + 16, r.at0, dv_cols))
            pl.when(j < 2 * nn)(lambda: product(j))
            pl.when(j >= 2 * nn)(lambda: finish_rows(j - 2 * nn))
            move(t, BOTH[:1])

        steps(12, one)
        steps(len(quick) - 1, rest)
        store(blocks - 2).wait()
        store(blocks - 1).wait()

    pl.run_scoped(
        segment4, *[ring((256, width), BF16)] * 4, pltpu.VMEM((rows, width), F32),
        ring((TILE, width), BF16), ring((TILE, width), F32), dma(4, 2), dma(2), dma(2))


def back(args, seqs, blk):
    rows, width = args["tokens"].shape
    ff = args["first"].shape[1]
    pairs = width // (2 * HEAD)
    anywhere = pl.BlockSpec(memory_space=pl.ANY)
    cut = 4

    def v(*shape, dtype=F32):
        return pltpu.VMEM(shape, dtype)

    def sem(*shape):
        return pltpu.SemaphoreType.DMA(shape)

    n_scan = seqs * 2
    chunk = (4, 2, 2, 64, 128)
    scratch = dict(
        tbuf=v(2, *chunk), core_rx=v(LAND, *chunk), acc=v(ACC, *chunk), xa=v(LAND, 4, 2, 32, 128),
        ya=v(LAND, 4, 32, 128), yb=v(LAND, 4, 2, 56, 128), xb=v(LAND, 4, 56, 128),
        xc=v(LAND, 2, 16, 128), yc=v(LAND, 16, 128), zab=v(LAND, 2, 3, 56, 128),
        zc=v(LAND, 2, 3, 2, 2, 16, 128), fin=v(FIN, 2, 64, 128),
        ssem=sem(7, LAND), rsem=sem(7, LAND), zss=sem(2, 2, 3, LAND), zrs=sem(2, 2, 3, LAND),
        osem=sem(FIN), csem=sem(FIN), crem=sem(FIN), ygs=sem(FIN), ygr=sem(FIN),
        dyv=v(rows, width, dtype=BF16), dfs=v(2, rows, ff, dtype=BF16), dn2=v(rows, width),
        dlow=v(rows, width, dtype=BF16), dgate=v(rows, width, dtype=BF16),
        dattn=v(rows, width, dtype=BF16), at0=v(8, 2, 64, rows, dtype=BF16),
        at1=v(8, 2, 64, rows, dtype=BF16), held=v(n_scan, cut, HEAD, 128), sums=v(n_scan, cut, HEAD, 128),
        other=v(n_scan, cut, HEAD, 128), dstate=v(n_scan, cut, HEAD, 128, dtype=BF16),
        sz=sem(n_scan), rz=sem(n_scan), sx=sem(n_scan), rx=sem(n_scan),
        gacc=v(8, width), gbuf=v(8, 128), gland=v(6, 8, 128), gs=sem(6), gr=sem(6), lsem=sem(5),
        qab=v(2, 3, 48, 128), qc=v(2, 3, 2, 2, 16, 128), qss=sem(2, 3, 2), qrs=sem(2, 3, 2),
        qxc=v(2, 2, 16, 128), qyc=v(2, 16, 128), qks=sem(2, 2), qkr=sem(2, 2),
    )
    args = dict(args)
    args["innert"] = args["innert"].reshape(8, ff // 8, rows)
    for name in ("normt", "norm2t", "mixedt"):
        args[name] = args[name].reshape(8, 2, 64, rows)
    args["gain"] = args["gain"].reshape(1, width)
    outs = dict(
        output=((rows, width), BF16), dtokens=((rows, width), F32), tall=((ff // 8, width), F32),
        wide=((2, width // 8, ff), F32), square=((5, width // 8, width), F32), dgain=((8, 128), F32),
    )
    return pl.pallas_call(
        functools.partial(back_kernel, blk // 2, seqs, (*args, *outs, *scratch)),
        out_shape=[jax.ShapeDtypeStruct(*of) for of in outs.values()],
        in_specs=[anywhere] * len(args),
        out_specs=[anywhere] * len(outs),
        scratch_shapes=list(scratch.values()),
        compiler_params=pltpu.CompilerParams(
            collective_id=3, has_side_effects=True, vmem_limit_bytes=60 * MIB),
        cost_estimate=pl.CostEstimate(flops=60 * 2**30, bytes_accessed=200 * MIB, transcendentals=0),
    )(*args.values())


def rms(value):
    return lax.rsqrt(jnp.mean(value * value, axis=-1, keepdims=True) + EPS)


def forward(blk, seqs, xf, weights):
    w_query, w_key, w_value, w_gate, w_out, out_gain, w_first, w_second, w_third = weights
    normed = (xf * rms(xf)).astype(BF16)
    key = project(normed, w_key)
    value = project(normed, w_value)
    k, v = silu_parts(key)[0].astype(BF16), value.astype(BF16)
    prefix = entering(local_states(k, v, seqs), blk, False)
    query = project(normed, w_query)
    gate = project(normed, w_gate)
    q = silu_parts(query)[0].astype(BF16)
    attn = attention(q, k, v, prefix, seqs)
    mixed = (attn * rms(attn) * out_gain * silu_parts(gate)[0]).astype(BF16)
    resid = xf + project(mixed, w_out)
    normed2 = (resid * rms(resid)).astype(BF16)
    first = project(normed2, w_first)
    second = project(normed2, w_second)
    inner = (first * second).astype(BF16)
    return dict(
        normed=normed, query=query, key=key, gate=gate, q=q, k=k, v=v, prefix=prefix, attn=attn,
        mixed=mixed, resid=resid, normed2=normed2, first=first, second=second, inner=inner)


def backward_plain(blk, seqs, xf, grad_top, f, weights):
    w_query, w_key, w_value, w_gate, w_out, out_gain, w_first, w_second, w_third = weights
    output = (f["resid"] + project(f["inner"], w_third)).astype(BF16)
    grad_w3 = weight_grad(f["inner"], grad_top)
    grad_inner = back_project(grad_top, w_third)
    grad_one = (grad_inner * f["second"]).astype(BF16)
    grad_two = (grad_inner * f["first"]).astype(BF16)
    grad_w1 = weight_grad(f["normed2"], grad_one)
    grad_w2 = weight_grad(f["normed2"], grad_two)
    grad_normed2 = back_project(grad_one, w_first) + back_project(grad_two, w_second)
    resid, attn = f["resid"], f["attn"]
    grad_resid = grad_top.astype(F32) + norm_back(grad_normed2, resid, rms(resid))
    grad_resid_low = grad_resid.astype(BF16)
    grad_wo = weight_grad(f["mixed"], grad_resid_low)
    grad_mixed = back_project(grad_resid_low, w_out)
    gate_act, gate_der = silu_parts(f["gate"])
    rattn = rms(attn)
    unit_attn = attn * rattn
    grad_scaled = grad_mixed * gate_act
    grad_gate_low = (grad_mixed * (unit_attn * out_gain) * gate_der).astype(BF16)
    grad_gain = jnp.sum(grad_scaled * unit_attn, axis=0)
    grad_attn = norm_back(grad_scaled * out_gain, attn, rattn).astype(BF16)
    q, k, v, prefix = f["q"], f["k"], f["v"], f["prefix"]
    dstate = entering(local_states(q, grad_attn, seqs), blk, True)
    grad_fq, grad_fk, grad_vv = attention_back(q, k, v, grad_attn, prefix, dstate, seqs)
    grad_query_low = (grad_fq * silu_parts(f["query"])[1]).astype(BF16)
    grad_key_low = (grad_fk * silu_parts(f["key"])[1]).astype(BF16)
    grad_value_low = grad_vv.astype(BF16)
    normed = f["normed"]
    grads = [weight_grad(normed, g) for g in (grad_query_low, grad_key_low, grad_value_low, grad_gate_low)]
    grads += [grad_wo, grad_gain, grad_w1, grad_w2, grad_w3]
    grad_normed = back_project(grad_query_low, w_query) + back_project(grad_key_low, w_key)
    grad_normed = (
        grad_normed + back_project(grad_value_low, w_value) + back_project(grad_gate_low, w_gate)
    )
    grad_input = grad_resid + norm_back(grad_normed, xf, rms(xf))
    summed = [
        lax.psum(lax.psum_scatter(g, "blk", scatter_dimension=0, tiled=True), "batch") for g in grads]
    return output, grad_input, summed


def laid_out(output, grad_input, tall, wide, square, dgain):
    arrays = (output, grad_input, tall, wide, square, dgain)
    squares, wides = square.shape[0], wide.shape[0]
    shapes = [square.shape[1:]] * squares + [wide.shape[1:]] * wides + [(1, dgain.shape[1])]
    types = [F32] * len(shapes) + [output.dtype, grad_input.dtype, F32]
    shapes += [output.shape, grad_input.shape, tall.shape]
    cuts = [1] * squares + [2] * wides + [1, 2, 4, 2]

    def kernel(output, grad_input, tall, wide, square, dgain, *rest):
        outs, bufs = rest[:len(shapes)], rest[len(shapes):2 * len(shapes)]
        sem_in, sem_out = rest[2 * len(shapes):]
        k = lax.axis_index("blk")
        ins = [square.at[n] for n in range(squares)] + [wide.at[n] for n in range(wides)]
        ins += [dgain.at[pl.ds(k, 1)], output, grad_input, tall]
        loads, stores = [], []
        for src, buf, dst, cut in zip(ins, bufs, outs, cuts):
            step = dst.shape[0] // cut
            for n in range(cut):
                part = pl.ds(n * step, step)
                m = len(loads)
                loads.append(pltpu.make_async_copy(src.at[part], buf.at[part], sem_in.at[m]))
                stores.append(pltpu.make_async_copy(buf.at[part], dst.at[part], sem_out.at[m]))
        for copy in loads:
            copy.start()
        for load, store in zip(loads, stores):
            load.wait()
            store.start()
        for copy in stores:
            copy.wait()

    anywhere = pl.BlockSpec(memory_space=pl.ANY)
    outs = pl.pallas_call(
        kernel,
        out_shape=[jax.ShapeDtypeStruct(*of) for of in zip(shapes, types)],
        in_specs=[anywhere] * len(arrays),
        out_specs=[anywhere] * len(shapes),
        scratch_shapes=[pltpu.VMEM(*of) for of in zip(shapes, types)]
        + [pltpu.SemaphoreType.DMA((sum(cuts),))] * 2,
        compiler_params=pltpu.CompilerParams(vmem_limit_bytes=60 * MIB),
    )(*arrays)
    return outs[:squares], outs[squares:squares + wides], *outs[squares + wides:]


def backward(blk, seqs, tokens, grad_top, f, weights):
    w_query, w_key, w_value, w_gate, w_out, gain, w_first, w_second, w_third = weights
    args = dict(
        tokens=tokens, dy=grad_top, gain=gain, w_query=w_query, w_key=w_key, w_value=w_value,
        w_gate=w_gate, w_out=w_out, w_first=w_first, w_second=w_second, w_third=w_third)
    args.update(f)
    output, grad_input, tall, wide, square, dgain = back(args, seqs, blk)
    (so, sg, sq, sk, sv), (s1, s2), sgain, output, grad_input, tall = laid_out(
        output, grad_input, tall, wide, square, dgain)
    return output, grad_input, [sq, sk, sv, sg, so, sgain.reshape(-1), s1, s2, tall]


def body(sizes, tokens, cotangent, *weights):
    batch, blk = sizes
    seqs, span, width = tokens.shape
    rows = seqs * span
    low = tokens.reshape(rows, width)
    xf = low.astype(F32)
    grad_top = cotangent.reshape(rows, width)
    ff = weights[-1].shape[0]
    if (batch, blk, rows, span, width, ff % 256) == (4, 8, 1024, 128, 1024, 0):
        f = forward_fast(blk, seqs, low, weights)
        output, grad_input, grads = backward(blk, seqs, low, grad_top, f, weights)
    else:
        f = forward(blk, seqs, xf, weights)
        output, grad_input, grads = backward_plain(blk, seqs, xf, grad_top, f, weights)
    shape = (seqs, span, width)
    return (output.reshape(shape), grad_input.reshape(shape), *grads)


def solution(mesh):
    rows = P("batch", "blk", None)
    cut = P("blk", None)
    return jax.shard_map(
        functools.partial(body, (mesh.shape["batch"], mesh.shape["blk"])),
        mesh=mesh,
        in_specs=(rows, rows) + (P(),) * 9,
        out_specs=(rows, rows) + (cut,) * 5 + (P("blk"),) + (cut,) * 3,
        check_vma=False,
    )
```

```python
import functools

import jax
import jax.numpy as jnp
from jax import lax
from jax.experimental import pallas as pl
from jax.experimental.pallas import tpu as pltpu
from jax.sharding import PartitionSpec as P

HEAD = 64
EPS = 1e-06
MESH = pl.DeviceIdType.MESH
F32 = jnp.float32
BF16 = jnp.bfloat16
MIB = 2**20


def silu_parts(pre):
    sig = jax.nn.sigmoid(pre)
    return (pre * sig, sig * (1.0 + pre * (1.0 - sig)))


def norm_back(grad, value, scale):
    inner = jnp.mean(grad * value, axis=-1, keepdims=True)
    return scale * grad - value * (scale * scale * scale) * inner


def project(left, weight):
    return jnp.dot(left, weight, preferred_element_type=F32)


def weight_grad(left, right):
    return jnp.einsum("td,tf->df", left, right, preferred_element_type=F32)


def back_project(grad, weight):
    return jnp.einsum("tf,df->td", grad, weight, preferred_element_type=F32)


def dot(a, b, ca, cb):
    return lax.dot_general(a, b, (((ca,), (cb,)), ((), ())), preferred_element_type=F32)


def low_lanes(shape):
    return lax.broadcasted_iota(jnp.int32, shape, len(shape) - 1) < HEAD


def two_heads(x):
    low = low_lanes(x.shape)
    zero = jnp.zeros_like(x)
    return jnp.concatenate([jnp.where(low, x, zero), jnp.where(low, zero, x)], axis=0)


def pick_heads(x):
    half = x.shape[0] // 2
    return jnp.where(low_lanes((half, x.shape[1])), x[:half], x[half:])


def causal_pair(span):
    t = lax.broadcasted_iota(jnp.int32, (span, 2 * span), 0)
    u = lax.broadcasted_iota(jnp.int32, (span, 2 * span), 1)
    return t >= u % span


def pair_of(ref, p):
    return ref[:, pl.ds(p * 2 * HEAD, 2 * HEAD)]


def state_kernel(left_ref, right_ref, out_ref):
    for p in range(out_ref.shape[1]):
        out_ref[0, p] = pick_heads(dot(pair_of(left_ref, p), pair_of(right_ref, p), 0, 0))


def attn_kernel(q_ref, k_ref, v_ref, prefix_ref, out_ref):
    span = q_ref.shape[0]
    causal = causal_pair(span)
    for p in range(prefix_ref.shape[1]):
        q, k2, v2 = pair_of(q_ref, p), two_heads(pair_of(k_ref, p)), two_heads(pair_of(v_ref, p))
        scores = jnp.where(causal, dot(q, k2, 1, 1), 0.0).astype(BF16)
        prefix = two_heads(prefix_ref[0, p])
        out_ref[:, pl.ds(p * 2 * HEAD, 2 * HEAD)] = dot(scores, v2, 1, 0) + dot(q, prefix, 1, 0)


def attn_back_kernel(q_ref, k_ref, v_ref, g_ref, prefix_ref, dstate_ref, dq_ref, dk_ref, dv_ref):
    span = q_ref.shape[0]
    causal = causal_pair(span)
    for p in range(prefix_ref.shape[1]):
        q, k, v, g = (pair_of(r, p) for r in (q_ref, k_ref, v_ref, g_ref))
        k2, v2 = two_heads(k), two_heads(v)
        prefix, dstate = two_heads(prefix_ref[0, p]), two_heads(dstate_ref[0, p])
        scores = jnp.where(causal, dot(q, k2, 1, 1), 0.0).astype(BF16)
        dscores = jnp.where(causal, dot(g, v2, 1, 1), 0.0).astype(BF16)
        lanes = pl.ds(p * 2 * HEAD, 2 * HEAD)
        dq_ref[:, lanes] = dot(dscores, k2, 1, 0) + dot(g, prefix, 1, 1)
        dk_ref[:, lanes] = pick_heads(dot(dscores, q, 0, 0)) + dot(v, dstate, 1, 1)
        dv_ref[:, lanes] = pick_heads(dot(scores, g, 0, 0)) + dot(k, dstate, 1, 0)


def rows_spec(span, width):
    return pl.BlockSpec((span, width), lambda s: (s, 0))


def state_spec(pairs):
    return pl.BlockSpec((1, pairs, HEAD, 2 * HEAD), lambda s: (s, 0, 0, 0))


def local_states(left, right, seqs):
    rows, width = left.shape
    span, pairs = rows // seqs, width // (2 * HEAD)
    return pl.pallas_call(
        state_kernel,
        grid=(seqs,),
        in_specs=[rows_spec(span, width)] * 2,
        out_specs=state_spec(pairs),
        out_shape=jax.ShapeDtypeStruct((seqs, pairs, HEAD, 2 * HEAD), F32),
    )(left, right)


def attention(q, k, v, prefix, seqs):
    rows, width = q.shape
    span, pairs = rows // seqs, width // (2 * HEAD)
    return pl.pallas_call(
        attn_kernel,
        grid=(seqs,),
        in_specs=[rows_spec(span, width)] * 3 + [state_spec(pairs)],
        out_specs=rows_spec(span, width),
        out_shape=jax.ShapeDtypeStruct((rows, width), F32),
    )(q, k, v, prefix)


def attention_back(q, k, v, g, prefix, dstate, seqs):
    rows, width = q.shape
    span, pairs = rows // seqs, width // (2 * HEAD)
    return pl.pallas_call(
        attn_back_kernel,
        grid=(seqs,),
        in_specs=[rows_spec(span, width)] * 4 + [state_spec(pairs)] * 2,
        out_specs=[rows_spec(span, width)] * 3,
        out_shape=[jax.ShapeDtypeStruct((rows, width), F32)] * 3,
    )(q, k, v, g, prefix, dstate)


def scan_kernel(outer, reverse, s_ref, out_ref, held, summed, other, zs, zr, xs, xr):
    chunks = s_ref.shape[0]
    k = lax.axis_index("blk")
    z, x = k // 2, k % 2
    if reverse:
        zz, xx = outer - 1 - z, 1 - x
        after, before = jnp.maximum(z - 1, 0), jnp.minimum(z + 1, outer - 1)
    else:
        zz, xx = z, x
        after, before = jnp.minimum(z + 1, outer - 1), jnp.maximum(z - 1, 0)
    nxt, prv, side = {"blk": after * 2 + x}, {"blk": before * 2 + x}, {"blk": z * 2 + 1 - x}
    first, last = zz == 0, zz == outer - 1

    bar = pltpu.get_barrier_semaphore()
    pl.semaphore_signal(bar, inc=1, device_id=side, device_id_type=MESH)
    pl.when(~last)(lambda: pl.semaphore_signal(bar, inc=1, device_id=nxt, device_id_type=MESH))
    pl.when(~first)(lambda: pl.semaphore_signal(bar, inc=1, device_id=prv, device_id_type=MESH))
    pl.semaphore_wait(bar, 1 + jnp.where(last, 0, 1) + jnp.where(first, 0, 1))

    def along(i):
        return pltpu.make_async_remote_copy(
            src_ref=summed.at[i], dst_ref=held.at[i], send_sem=zs.at[i], recv_sem=zr.at[i],
            device_id=nxt, device_id_type=MESH)

    def across(i, src):
        return pltpu.make_async_remote_copy(
            src_ref=src.at[i], dst_ref=other.at[i], send_sem=xs.at[i], recv_sem=xr.at[i],
            device_id=side, device_id_type=MESH)

    def pass_on(i):
        pl.when(~first)(lambda: along(i).wait_recv())

        @pl.when(first)
        def _():
            held[i] = jnp.zeros_like(held[i])

        summed[i] = held[i] + s_ref[i]
        pl.when(~last)(lambda: along(i).start())
        pl.when(xx == 0)(lambda: across(i, summed).start())
        pl.when(xx == 1)(lambda: across(i, held).start())

    def finish(i):
        across(i, held).wait_recv()
        out_ref[i] = (held[i] + other[i]).astype(out_ref.dtype)

    def step(i, carry):
        pl.when(i < chunks)(lambda: pass_on(i))
        pl.when(i > 0)(lambda: finish(i - 1))
        return carry

    lax.fori_loop(0, chunks + 1, step, 0)

    def drain(i, carry):
        pl.when(~last)(lambda: along(i).wait_send())
        across(i, held).wait_send()
        return carry

    lax.fori_loop(0, chunks, drain, 0)


def entering(states, blk, reverse):
    seqs, pairs, head, lanes = states.shape
    per = max(1, pairs // 2)
    shape = (seqs * pairs // per, per, head, lanes)
    vmem = pl.BlockSpec(memory_space=pltpu.VMEM)
    sems = [pltpu.SemaphoreType.DMA((shape[0],))] * 4
    out = pl.pallas_call(
        functools.partial(scan_kernel, blk // 2, reverse),
        out_shape=jax.ShapeDtypeStruct(shape, BF16),
        in_specs=[vmem],
        out_specs=vmem,
        scratch_shapes=[pltpu.VMEM(shape, F32)] * 3 + sems,
        compiler_params=pltpu.CompilerParams(
            collective_id=2 if reverse else 1, has_side_effects=True, vmem_limit_bytes=24 * MIB),
    )(states.reshape(shape))
    return out.reshape(states.shape)


LAND, FIN, ACC = 4, 8, 10
CORE, XA, YA, YB, XB, XC, YC = range(7)
TILE = 256


SPARE = (2, 19)
QUICK = 2


class Way:
    def __init__(self, a, b, c):
        self.a = pl.ds(0, a) if a else None
        self.b, self.c = pl.ds(a, b), pl.ds(a + b, c)
        self.ab, self.top_a = pl.ds(0, a + b), pl.ds(0, max(a, 8))
        self.top_b, self.top_c = pl.ds(0, b), pl.ds(0, c)


class Named:
    def __init__(self, names, refs):
        self.__dict__.update(zip(names, refs))


class Stream:
    def __init__(self, block, buf, sem):
        self.block, self.buf, self.sem = block, buf, sem

    def copy(self, j):
        return pltpu.make_async_copy(self.block(j), self.buf.at[j % 2], self.sem.at[j % 2])

    def start(self, j):
        self.copy(j).start()

    def get(self, j, count):
        self.copy(j).wait()
        pl.when(j + 1 < count)(lambda: self.start(j + 1))
        return self.buf.at[j % 2]


LAG, WAIT, OFFER = 1, 8, (0, 1, 4, 8)


def forward_kernel(outer, seqs, names, results, *refs):
    r = Named(names, refs)
    rows, width = r.tokens.shape
    ff = r.w_first.shape[1]
    span, pairs = rows // seqs, width // (2 * HEAD)
    blocks, per_block = rows // TILE, TILE // span
    n_scan, cut = r.sums.shape[:2]
    per_seq = pairs // cut

    k = lax.axis_index("blk")
    z, x = k // 2, k % 2
    top = outer - 1
    side = {"blk": z * 2 + 1 - x}
    above, below = {"blk": jnp.minimum(z + 1, top) * 2 + x}, {"blk": jnp.maximum(z - 1, 0) * 2 + x}
    bar = pltpu.get_barrier_semaphore()
    pl.semaphore_signal(bar, inc=1, device_id=side, device_id_type=MESH)
    pl.when(z < top)(lambda: pl.semaphore_signal(bar, inc=1, device_id=above, device_id_type=MESH))
    pl.when(z > 0)(lambda: pl.semaphore_signal(bar, inc=1, device_id=below, device_id_type=MESH))

    def span_of(start, size, step):
        return pl.ds(start if isinstance(start, int) else pl.multiple_of(start, step), size)

    def tok(j, n=TILE):
        return span_of(j * n, n, n)

    loads = [
        pltpu.make_async_copy(src, dst, r.lsem.at[n])
        for n, (src, dst) in enumerate((
            (r.w_key, r.wk), (r.w_value, r.wv), (r.w_query, r.wq), (r.w_gate, r.wg), (r.gain, r.gv),
            (r.w_out, r.wo), (r.w_first, r.w1), (r.w_second, r.w2)))
    ]

    def x_load(j):
        return pltpu.make_async_copy(r.tokens.at[tok(j)], r.xv.at[tok(j)], r.xsem.at[j])

    by_rows = dict(
        k=lambda j: r.kb.at[tok(j)], v=lambda j: r.vb.at[tok(j)], q=lambda j: r.qb.at[tok(j)],
        gate=lambda j: r.gb.at[tok(j)], key=lambda j: r.keyb, query=lambda j: r.queryb,
        attn=lambda j: r.attnb, resid=lambda j: r.residb, first=lambda j: r.firstb,
        second=lambda j: r.secondb, inner=lambda j: r.innerb)
    by_cols = dict(normt=r.tb0, mixedt=r.tb1, norm2t=r.tb2, innert=r.innertb)

    def store(name, j):
        sem = r.osem.at[results.index(name)]
        out = getattr(r, name)
        if name in by_rows:
            return pltpu.make_async_copy(by_rows[name](j), out.at[tok(j)], sem)
        return pltpu.make_async_copy(by_cols[name], out.at[:, tok(j)], sem)

    def free(name, j):
        pl.when(j > 0)(lambda: store(name, j - 1).wait())

    def remote(src, dst, s, t, dev):
        return pltpu.make_async_remote_copy(
            src_ref=src, dst_ref=dst, send_sem=s, recv_sem=t, device_id=dev, device_id_type=MESH)

    def along(i):
        return remote(r.sums.at[i], r.held.at[i], r.sz.at[i], r.rz.at[i], above)

    def across(i, src):
        return remote(src.at[i], r.other.at[i], r.sx.at[i], r.rx.at[i], side)

    def owned(i):
        return i % 2 == x

    def pass_on(i):
        across(i, r.other).wait_recv()
        pl.when(z > 0)(lambda: along(i).wait_recv())

        @pl.when(z == 0)
        def _():
            r.held[i] = jnp.zeros_like(r.held[i])

        @pl.when(x == 0)
        def _():
            mine = r.held[i] + r.sums[i]
            r.pre[i] = r.held[i].astype(BF16)
            r.sums[i] = mine + r.other[i]
            r.other[i] = mine
            across(i, r.other).start()

        @pl.when(x == 1)
        def _():
            mine = r.held[i] + r.other[i]
            r.pre[i] = mine.astype(BF16)
            r.sums[i] = mine + r.sums[i]
            across(i, r.held).start()

        pl.when(z < top)(lambda: along(i).start())

    def finish(i):
        @pl.when(owned(i))
        def _():
            pl.when(z < top)(lambda: along(i).wait_send())

        @pl.when(~owned(i))
        def _():
            across(i, r.sums).wait_recv()
            r.pre[i] = r.other[i].astype(BF16)

        across(i, r.sums).wait_send()

    def scan(n):
        per_tile = n_scan // blocks
        for j in range(blocks):
            @pl.when(n == OFFER[j])
            def _(j=j):
                for g in range(per_tile):
                    i = j * per_tile + g
                    pl.when(~owned(i))(lambda: across(i, r.sums).start())

        i = (n - 1 - LAG * z) * 2

        @pl.when((i >= 0) & (i < n_scan))
        def _():
            for g in range(2):
                pl.when(owned(i + g))(lambda: pass_on(i + g))

        q = (n - WAIT) * 2

        @pl.when((q >= 0) & (q < n_scan))
        def _():
            for g in range(2):
                finish(q + g)

    def transposed(src, dst):
        for n in range(dst.shape[0] // 128):
            cols = pl.ds(n * 128, 128)
            dst[cols, :] = src[:, cols].T

    def norm_rows(value):
        return (value * lax.rsqrt(jnp.mean(value * value, axis=-1, keepdims=True) + EPS)).astype(BF16)

    def each(count, one):
        for m in range(count):
            one(m)

    def rows_of(j, m):
        return span_of(j * TILE + m * 32, 32, 32)

    def col(n):
        return span_of(n * 256, 256, 256)

    def tile_keys(j):
        x_load(j).wait()

        @pl.when(j == 0)
        def _():
            loads[0].wait()
            loads[1].wait()
            for n in range(1, blocks):
                x_load(n).start()
            for copy in loads[2:]:
                copy.start()

        for name in ("key", "k", "v"):
            free(name, j)

        def one(m):
            r.nrm[rows_of(j, m), :] = norm_rows(r.xv[rows_of(j, m), :].astype(F32))

        each(TILE // 32, one)

        def product(n):
            key = dot(r.nrm[tok(j), :], r.wk[:, col(n)], 1, 0)
            r.keyb[:, col(n)] = key.astype(BF16)
            r.kb[tok(j), col(n)] = silu_parts(key)[0].astype(BF16)
            r.vb[tok(j), col(n)] = dot(r.nrm[tok(j), :], r.wv[:, col(n)], 1, 0).astype(BF16)

        each(width // 256, product)

        def states(m):
            s = j * per_block + m
            for p in range(pairs):
                lanes = pl.ds(p * 2 * HEAD, 2 * HEAD)
                here = tok(s, span)
                r.sums[s * per_seq + p // cut, p % cut] = pick_heads(dot(r.kb[here, lanes], r.vb[here, lanes], 0, 0))

        each(per_block, states)
        for name in ("key", "k", "v"):
            store(name, j).start()

    def tile_query(j):
        @pl.when(j == 0)
        def _():
            loads[2].wait()
            loads[3].wait()

        for name in ("query", "q", "gate", "normt"):
            free(name, j)

        def product(n):
            query = dot(r.nrm[tok(j), :], r.wq[:, col(n)], 1, 0)
            r.queryb[:, col(n)] = query.astype(BF16)
            r.qb[tok(j), col(n)] = silu_parts(query)[0].astype(BF16)
            r.gb[tok(j), col(n)] = dot(r.nrm[tok(j), :], r.wg[:, col(n)], 1, 0).astype(BF16)

        each(width // 256, product)
        transposed(r.nrm.at[tok(j)], r.tb0)
        for name in ("query", "q", "gate", "normt"):
            store(name, j).start()

    def tile_scores(s):
        causal = causal_pair(span)
        here = tok(s, span)
        for p in range(pairs):
            lanes = pl.ds(p * 2 * HEAD, 2 * HEAD)
            q, k2, v2 = r.qb[here, lanes], two_heads(r.kb[here, lanes]), two_heads(r.vb[here, lanes])
            scores = jnp.where(causal, dot(q, k2, 1, 1), 0.0).astype(BF16)
            r.intra[here, lanes] = dot(scores, v2, 1, 0)

    def tile_mixed(j, m):
        if m == 0:
            pl.when(j == 0)(lambda: loads[4].wait())
            for name in ("attn", "mixedt"):
                free(name, j)
        s = j * per_block + m
        here = tok(s, span)
        for p in range(pairs):
            lanes = pl.ds(p * 2 * HEAD, 2 * HEAD)
            prefix = two_heads(r.pre[s * per_seq + p // cut, p % cut])
            r.intra[here, lanes] = r.intra[here, lanes] + dot(r.qb[here, lanes], prefix, 1, 0)
        for n in range(m * span // 32, (m + 1) * span // 32):
            av = r.intra[rows_of(j, n), :]
            scale = lax.rsqrt(jnp.mean(av * av, axis=-1, keepdims=True) + EPS)
            act = silu_parts(r.gb[rows_of(j, n), :].astype(F32))[0]
            r.attnb[tok(n, 32), :] = av.astype(BF16)
            r.mixb[tok(n, 32), :] = (av * scale * r.gv[...] * act).astype(BF16)
        for n in range(width // 128):
            r.tb1[pl.ds(n * 128, 128), tok(m, span)] = r.mixb[tok(m, span), pl.ds(n * 128, 128)].T
        if m == per_block - 1:
            for name in ("attn", "mixedt"):
                store(name, j).start()

    def tile_resid(j):
        pl.when(j == 0)(lambda: loads[5].wait())
        for name in ("resid", "norm2t"):
            free(name, j)

        def product(n):
            r.residb[:, col(n)] = r.xv[tok(j), col(n)].astype(F32) + dot(r.mixb[...], r.wo[:, col(n)], 1, 0)

        each(width // 256, product)

        def one(m):
            r.n2b[tok(m, 32), :] = norm_rows(r.residb[tok(m, 32), :])

        each(TILE // 32, one)
        transposed(r.n2b, r.tb2)
        for name in ("resid", "norm2t"):
            store(name, j).start()

    def tile_inner(j, lo, hi):
        def one(n):
            n = n + lo
            first = dot(r.n2b[...], r.w1[:, col(n)], 1, 0)
            second = dot(r.n2b[...], r.w2[:, col(n)], 1, 0)
            inner = (first * second).astype(BF16)
            r.firstb[:, col(n)] = first.astype(BF16)
            r.secondb[:, col(n)] = second.astype(BF16)
            r.innerb[:, col(n)] = inner
            r.innertb[col(n), :] = inner.T

        each(hi - lo, one)

    half = ff // 512 * 256
    halves = (pl.ds(0, half), pl.ds(half, ff - half))

    def up_stores(j, h):
        cols = halves[h]
        sem = lambda name: r.osem.at[results.index(name)]
        copies = [
            pltpu.make_async_copy(by_rows[name](j).at[:, cols], getattr(r, name).at[tok(j), cols], sem(name))
            for name in ("first", "second", "inner")]
        return copies + [
            pltpu.make_async_copy(r.innertb.at[cols], r.innert.at[cols, tok(j)], sem("innert"))]

    def tile_up(j, h):
        if h == 0:
            @pl.when(j == 0)
            def _():
                loads[6].wait()
                loads[7].wait()

            for name in ("first", "second", "inner", "innert"):
                free(name, j)
        tile_inner(j, (0, half // 256)[h], (half // 256, ff // 256)[h])
        for copy in up_stores(j, h):
            copy.start()

    x_load(0).start()
    loads[0].start()
    loads[1].start()

    per = n_scan // blocks // 2

    def slot(n, carry):
        pl.when(n < blocks)(lambda: tile_keys(n))

        @pl.when(n == 0)
        def _():
            pl.semaphore_wait(bar, 1 + jnp.where(z < top, 1, 0) + jnp.where(z > 0, 1, 0))

        @pl.when((n >= blocks) & (n < 2 * blocks))
        def _():
            tile_query(n - blocks)
            for m in range(per_block):
                tile_scores((n - blocks) * per_block + m)

        scan(n)
        w = n - WAIT - per // 2 + 1
        j, m = w // per, w % per
        live = (w >= 0) & (j < blocks)
        pl.when((w >= per) & (j <= blocks) & (m == 0))(lambda: tile_up(j - 1, 1))
        pl.when(live & (m == 0))(lambda: tile_mixed(j, 0))

        @pl.when(live & (m == 2))
        def _():
            tile_mixed(j, 1)
            tile_resid(j)

        pl.when(live & (m == 3))(lambda: tile_up(j, 0))
        return carry

    lax.fori_loop(0, n_scan // 2 + WAIT + 2, slot, 0)
    whole = pltpu.make_async_copy(r.pre, r.prefix, r.osem.at[results.index("prefix")])
    whole.start()
    for name in results[:-1]:
        store(name, blocks - 1).wait()
    whole.wait()


def forward_fast(blk, seqs, tokens, weights):
    w_query, w_key, w_value, w_gate, w_out, out_gain, w_first, w_second, w_third = weights
    rows, width = tokens.shape
    ff = w_first.shape[1]
    pairs = width // (2 * HEAD)
    cut = 2
    n_scan = seqs * pairs // cut

    def v(*shape, dtype=BF16):
        return pltpu.VMEM(shape, dtype)

    def sem(*shape):
        return pltpu.SemaphoreType.DMA(shape)

    wide, tall = (rows, width), (width, ff)
    chunks = (n_scan, cut, HEAD, 2 * HEAD)
    scratch = dict(
        xv=v(*wide), gv=v(1, width, dtype=F32), wq=v(width, width), wk=v(width, width), wv=v(width, width),
        wg=v(width, width), wo=v(width, width), w1=v(*tall), w2=v(*tall), nrm=v(*wide), kb=v(*wide),
        vb=v(*wide), qb=v(*wide), gb=v(*wide), intra=v(*wide, dtype=F32), keyb=v(TILE, width),
        queryb=v(TILE, width), attnb=v(TILE, width), mixb=v(TILE, width), residb=v(TILE, width, dtype=F32),
        n2b=v(TILE, width), firstb=v(TILE, ff), secondb=v(TILE, ff), innerb=v(TILE, ff),
        tb0=v(width, TILE), tb1=v(width, TILE), tb2=v(width, TILE), innertb=v(ff, TILE),
        held=v(*chunks, dtype=F32), sums=v(*chunks, dtype=F32), other=v(*chunks, dtype=F32), pre=v(*chunks),
        sz=sem(n_scan), rz=sem(n_scan), sx=sem(n_scan), rx=sem(n_scan), lsem=sem(8),
        xsem=sem(rows // TILE), osem=sem(16),
    )
    turned = (width, rows)
    outs = dict(
        k=wide, v=wide, key=wide, normt=turned, q=wide, gate=wide, query=wide, attn=wide, mixedt=turned,
        resid=wide, norm2t=turned, first=(rows, ff), second=(rows, ff), inner=(rows, ff),
        innert=(ff, rows), prefix=chunks)
    ins = dict(
        tokens=tokens, gain=out_gain.reshape(1, width), w_query=w_query, w_key=w_key, w_value=w_value,
        w_gate=w_gate, w_out=w_out, w_first=w_first, w_second=w_second)
    results = tuple(outs)
    anywhere = pl.BlockSpec(memory_space=pl.ANY)
    made = pl.pallas_call(
        functools.partial(forward_kernel, blk // 2, seqs, (*ins, *outs, *scratch), results),
        out_shape=[
            jax.ShapeDtypeStruct(shape, F32 if name == "resid" else BF16) for name, shape in outs.items()
        ],
        in_specs=[anywhere] * len(ins),
        out_specs=[anywhere] * len(outs),
        scratch_shapes=list(scratch.values()),
        compiler_params=pltpu.CompilerParams(
            collective_id=4, has_side_effects=True, vmem_limit_bytes=60 * MIB),
        cost_estimate=pl.CostEstimate(flops=26 * 2**30, bytes_accessed=80 * MIB, transcendentals=0),
    )(*ins.values())
    f = dict(zip(results, made))
    f["prefix"] = f["prefix"].reshape(seqs, pairs, HEAD, 2 * HEAD)
    return f


def back_kernel(outer, seqs, names, *refs):
    r = Named(names, refs)
    rows, width = r.tokens.shape
    ff = r.first.shape[1]
    span, pairs = rows // seqs, width // (2 * HEAD)
    n_tall, n_wide, n_square = ff // 256, ff // 128, 20
    chunks = n_tall + n_wide + n_square
    at_wide, at_square = n_tall, n_tall + n_wide
    blocks = rows // TILE

    b, k = lax.axis_index("batch"), lax.axis_index("blk")
    y, c = b // 2, b % 2
    z, x = k // 2, k % 2
    ox, oy = 1 - x, 1 - y
    top = outer - 1
    zr = top - z
    to_core, to_y, to_x = {"batch": y * 2 + 1 - c}, {"batch": oy * 2 + c}, {"blk": z * 2 + ox}
    to_up = {"blk": jnp.minimum(z + 1, top) * 2 + x}
    to_down = {"blk": jnp.maximum(z - 1, 0) * 2 + x}
    to_z = [{"blk": (z + d) % outer * 2 + x} for d in range(1, outer)]

    peers = [to_core, to_y, to_x] + to_z
    bar = pltpu.get_barrier_semaphore()
    for d in peers:
        pl.semaphore_signal(bar, inc=1, device_id=d, device_id_type=MESH)

    def remote(src, dst, s, t, dev):
        return pltpu.make_async_remote_copy(
            src_ref=src, dst_ref=dst, send_sem=s, recv_sem=t, device_id=dev, device_id_type=MESH)

    def link(kind, i, src, dst, dev):
        return remote(src, dst.at[i % LAND], r.ssem.at[kind, i % LAND], r.rsem.at[kind, i % LAND], dev)

    def at(i, *where):
        return r.acc.at[(i % ACC,) + where]

    every = slice(None)

    def core_copy(i):
        return link(CORE, i, r.tbuf.at[i % 2], r.core_rx, to_core)

    def xa_copy(w, i):
        return link(XA, i, at(i, every, ox, every, w.a), r.xa.at[:, :, :, w.top_a], to_x)

    def ya_copy(w, i):
        return link(YA, i, at(i, every, x, oy, w.a), r.ya.at[:, :, w.top_a], to_y)

    def yb_copy(w, i):
        return link(YB, i, at(i, every, every, oy, w.b), r.yb.at[:, :, :, w.top_b], to_y)

    def xb_copy(w, i):
        return link(XB, i, at(i, every, ox, y, w.b), r.xb.at[:, :, w.top_b], to_x)

    def xc_copy(w, i):
        return link(XC, i, at(i, z, ox, every, w.c), r.xc.at[:, :, w.top_c], to_x)

    def yc_copy(w, i):
        return link(YC, i, at(i, z, x, oy, w.c), r.yc.at[:, w.top_c], to_y)

    def y_share(i):
        f = i % FIN
        return remote(r.fin.at[f, y], r.fin.at[f, y], r.ygs.at[f], r.ygr.at[f], to_y)

    def part_ab(w, i, s):
        return at(i, s, x, y, w.ab)

    def part_c(w, i, s):
        return at(i, s, every, every, w.c)

    def land_ab(w, i, d, n):
        return r.zab.at[i % LAND, d, n - 1, w.ab]

    def land_c(w, i, d, n):
        return r.zc.at[i % LAND, d, n - 1, :, :, w.top_c]

    AB, CC = (0, part_ab, land_ab), (1, part_c, land_c)

    def hop(group, w, i, n, up, s):
        g, part, land = group
        d = 0 if up else 1
        sem = (g, d, n - 1, i % LAND)
        return remote(part(w, i, s), land(w, i, d, n), r.zss.at[sem], r.zrs.at[sem],
                      to_up if up else to_down)

    def z_each(group, w, i, n, act):
        up = hop(group, w, i, n, True, jnp.minimum(outer - n + z, top))
        down = hop(group, w, i, n, False, jnp.maximum(n - 1 - zr, 0))
        pl.when((z <= n - 1) & (z < top))(lambda: act(up))
        pl.when((zr <= n - 1) & (z > 0))(lambda: act(down))

    def z_send(group, w, i, n):
        z_each(group, w, i, n, lambda copy: copy.start())

    def z_sent(group, w, i, n):
        z_each(group, w, i, n, lambda copy: copy.wait_send())

    def add(ref, landed):
        ref[...] = ref[...] + landed[...]

    def z_take(group, w, i, n):
        g, part, land = group

        def take(up, s):
            hop(group, w, i, n, up, s).wait_recv()
            add(part(w, i, s), land(w, i, 0 if up else 1, n))

        pl.when((z > 0) & (z <= n))(lambda: take(True, jnp.clip(outer - n + z - 1, 0, top)))
        pl.when((z < top) & (zr <= n))(lambda: take(False, jnp.clip(n - zr, 0, top)))

    BOTH = (Way(32, 16, 16), Way(0, 48, 16))
    spare = (at_wide + SPARE[0], at_wide + SPARE[1])

    def places(i, act):
        f = r.fin.at[i % FIN]

        @pl.when(i < at_wide)
        def _():
            for yy in range(2):
                for blk in range(2):
                    col = pl.multiple_of(c * (width // 2) + (yy * 2 + blk) * 128, 128)
                    act(f.at[yy, pl.ds(blk * 32, 32)], r.tall.at[pl.ds(i * 32, 32), pl.ds(col, 128)])

        @pl.when((i >= at_wide) & (i < at_square))
        def _():
            j, h = (i - at_wide) // 2, (i - at_wide) % 2
            col = pl.multiple_of(c * (ff // 2) + j * 128, 128)
            for yy in range(2):
                act(f.at[yy], r.wide.at[yy, pl.ds(h * 64, 64), pl.ds(col, 128)])

        @pl.when(i >= at_square)
        def _():
            j = i - at_square
            m, u, h = j // 4, j // 2 % 2, j % 2
            for yy in range(2):
                col = pl.multiple_of(c * (width // 2) + u * 256 + yy * 128, 128)
                act(f.at[yy], r.square.at[m, pl.ds(h * 64, 64), pl.ds(col, 128)])

    def cores(w, i):
        core_copy(i).wait_recv()
        core_copy(i).wait_send()
        add(at(i), r.core_rx.at[i % LAND])
        if w.a is not None:
            xa_copy(w, i).start()
        yb_copy(w, i).start()
        z_send(CC, w, i, 1)

    def second(w, i):
        yb_copy(w, i).wait_recv()
        add(at(i, every, every, y, w.b), r.yb.at[i % LAND, :, :, w.top_b])
        xb_copy(w, i).start()
        if w.a is not None:
            xa_copy(w, i).wait_recv()
            add(at(i, every, x, every, w.a), r.xa.at[i % LAND, :, :, w.top_a])
            ya_copy(w, i).start()
        z_take(CC, w, i, 1)
        z_send(CC, w, i, 2)
        if w.a is not None:
            xa_copy(w, i).wait_send()
        yb_copy(w, i).wait_send()
        z_sent(CC, w, i, 1)

    def third(w, i):
        xb_copy(w, i).wait_recv()
        add(at(i, every, x, y, w.b), r.xb.at[i % LAND, :, w.top_b])
        if w.a is not None:
            ya_copy(w, i).wait_recv()
            add(at(i, every, x, y, w.a), r.ya.at[i % LAND, :, w.top_a])
        z_send(AB, w, i, 1)
        z_take(CC, w, i, 2)
        z_send(CC, w, i, 3)
        xb_copy(w, i).wait_send()
        if w.a is not None:
            ya_copy(w, i).wait_send()
        z_sent(CC, w, i, 2)

    def fourth(w, i):
        z_take(AB, w, i, 1)
        z_send(AB, w, i, 2)
        z_take(CC, w, i, 3)
        xc_copy(w, i).start()
        z_sent(AB, w, i, 1)
        z_sent(CC, w, i, 3)

    def fifth(w, i):
        z_take(AB, w, i, 2)
        z_send(AB, w, i, 3)
        xc_copy(w, i).wait_recv()
        add(at(i, z, x, every, w.c), r.xc.at[i % LAND, :, w.top_c])
        yc_copy(w, i).start()
        z_sent(AB, w, i, 2)
        xc_copy(w, i).wait_send()

    def sixth(w, i):
        yc_copy(w, i).wait_recv()
        z_take(AB, w, i, 3)
        f = i % FIN
        r.fin[f, y, w.ab] = r.acc[i % ACC, z, x, y, w.ab]
        r.fin[f, y, w.c] = r.acc[i % ACC, z, x, y, w.c] + r.yc[i % LAND, w.top_c]
        y_share(i).start()
        z_sent(AB, w, i, 3)
        yc_copy(w, i).wait_send()

    def seventh(w, i):
        y_share(i).wait_recv()
        y_share(i).wait_send()
        f = i % FIN

        def go(src, dst):
            remote(src, dst, r.csem.at[f], r.crem.at[f], to_core).start()
            pltpu.make_async_copy(src, dst, r.osem.at[f]).start()

        places(i, go)

    def last(w, i):
        f = i % FIN
        whole = r.fin.at[f]
        copy = remote(whole, whole, r.csem.at[f], r.crem.at[f], to_core)
        copy.wait_send()
        copy.wait_recv()
        pltpu.make_async_copy(whole, whole, r.osem.at[f]).wait()

    ORDER = range(2, 9)
    stages = (None, cores, second, third, fourth, fifth, sixth, seventh, last)

    def advance(t, some, ways):
        for n in some:
            i = t - n
            live = (i >= 0) & (i < chunks - QUICK)
            if n >= 7:
                pl.when(live)(functools.partial(stages[n], None, i))
                continue
            if len(ways) == 2:
                spared = (i >= spare[0]) & (i < spare[1])
                pl.when(spared)(functools.partial(stages[n], ways[1], i))
                live = live & ~spared
            pl.when(live)(functools.partial(stages[n], ways[0], i))

    def z_straight(group, i, act):
        w = BOTH[0]
        g, part, _ = group
        land = (r.qab, r.qc)[g].at[i % 2]
        for d in range(1, outer):
            sem = (g, d - 1, i % 2)
            act(remote(part(w, i, (z + d) % outer), land.at[d - 1], r.qss.at[sem], r.qrs.at[sem],
                       to_z[d - 1]))

    def z_arrived(group, i):
        w = BOTH[0]
        g, part, _ = group
        land = (r.qab, r.qc)[g].at[i % 2]
        z_straight(group, i, lambda copy: copy.wait_recv())
        total = land[0]
        for d in range(1, outer - 1):
            total = total + land[d]
        ref = part(w, i, z)
        ref[...] = ref[...] + total
        z_straight(group, i, lambda copy: copy.wait_send())

    def quick_xc(i):
        w, m = BOTH[0], i % 2
        return remote(at(i, z, ox, every, w.c), r.qxc.at[m], r.qks.at[0, m], r.qkr.at[0, m], to_x)

    def quick_yc(i):
        w, m = BOTH[0], i % 2
        return remote(at(i, z, x, oy, w.c), r.qyc.at[m], r.qks.at[1, m], r.qkr.at[1, m], to_y)

    def quick_cores(i):
        w = BOTH[0]
        core_copy(i).wait_recv()
        core_copy(i).wait_send()
        add(at(i), r.core_rx.at[i % LAND])
        xa_copy(w, i).start()
        yb_copy(w, i).start()
        z_straight(CC, i, lambda copy: copy.start())

    def quick_second(i):
        w = BOTH[0]
        yb_copy(w, i).wait_recv()
        add(at(i, every, every, y, w.b), r.yb.at[i % LAND, :, :, w.top_b])
        xb_copy(w, i).start()
        z_arrived(CC, i)
        quick_xc(i).start()
        xa_copy(w, i).wait_recv()
        add(at(i, every, x, every, w.a), r.xa.at[i % LAND, :, :, w.top_a])
        ya_copy(w, i).start()
        xa_copy(w, i).wait_send()
        yb_copy(w, i).wait_send()

    def quick_third(i):
        w = BOTH[0]
        quick_xc(i).wait_recv()
        add(at(i, z, x, every, w.c), r.qxc.at[i % 2])
        quick_yc(i).start()
        xb_copy(w, i).wait_recv()
        add(at(i, every, x, y, w.b), r.xb.at[i % LAND, :, w.top_b])
        ya_copy(w, i).wait_recv()
        add(at(i, every, x, y, w.a), r.ya.at[i % LAND, :, w.top_a])
        z_straight(AB, i, lambda copy: copy.start())
        for copy in (xb_copy(w, i), ya_copy(w, i), quick_xc(i)):
            copy.wait_send()

    def quick_fourth(i):
        w = BOTH[0]
        quick_yc(i).wait_recv()
        z_arrived(AB, i)
        f = i % FIN
        r.fin[f, y, w.ab] = r.acc[i % ACC, z, x, y, w.ab]
        r.fin[f, y, w.c] = r.acc[i % ACC, z, x, y, w.c] + r.qyc[i % 2]
        y_share(i).start()
        quick_yc(i).wait_send()

    quick = (None, quick_cores, quick_second, quick_third, quick_fourth,
             functools.partial(seventh, None), functools.partial(last, None))

    def finish_chunks(t, some):
        for n in some:
            i = t - n
            pl.when((i >= chunks - QUICK) & (i < chunks))(functools.partial(quick[n], i))

    def send_first(t, ways=BOTH):
        advance(t, (1,), ways)

    def move(t, ways=BOTH):
        advance(t, ORDER, ways)

    def make(t, fill):
        fill(1 - c, r.tbuf.at[t % 2])
        core_copy(t).start()
        fill(c, r.acc.at[t % ACC])

    def fill_tall(lhs):
        def fill(half, dst):
            for yy in range(2):
                col = pl.multiple_of(half * (width // 2) + yy * 256, 256)
                res = dot(lhs, r.dyv[:, pl.ds(col, 256)], 1, 0).reshape(4, 2, 32, 256)
                for blk in range(2):
                    dst[:, :, yy, pl.ds(blk * 32, 32), :] = res[..., blk * 128:(blk + 1) * 128]
        return fill

    def left_rows(ref, h):
        return ref[:, h].reshape(8 * 64, rows)

    def fill_two(left, h, take):
        def fill(half, dst):
            res = dot(left_rows(left, h), take(half), 1, 0).reshape(4, 2, 64, 256)
            dst[:, :, 0] = res[..., :128]
            dst[:, :, 1] = res[..., 128:]
        return fill

    def make_wide(t):
        i = t - at_wide
        j, h = i // 2, i % 2

        def take(half):
            col = pl.ds(pl.multiple_of(half * (ff // 2) + j * 128, 128), 128)
            return jnp.concatenate([r.dfs[0, :, col], r.dfs[1, :, col]], axis=1)

        make(t, fill_two(r.at0, h, take))

    def make_square(t, base, left, right):
        i = t - base
        u, h = i // 2, i % 2

        def take(half):
            return right(pl.ds(pl.multiple_of(half * (width // 2) + u * 256, 256), 256))

        make(t, fill_two(left, h, take))

    zz, xx = zr, ox
    n_scan = r.sums.shape[0]
    halves = n_scan // seqs
    scan_at = at_wide

    def along(i):
        return remote(r.sums.at[i], r.held.at[i], r.sz.at[i], r.rz.at[i], to_down)

    def across(i, src):
        return remote(src.at[i], r.other.at[i], r.sx.at[i], r.rx.at[i], to_x)

    def owned(i):
        return i % 2 == xx

    def pass_on(i):
        across(i, r.other).wait_recv()
        pl.when(zz > 0)(lambda: along(i).wait_recv())

        @pl.when(zz == 0)
        def _():
            r.held[i] = jnp.zeros_like(r.held[i])

        @pl.when(xx == 0)
        def _():
            mine = r.held[i] + r.sums[i]
            r.dstate[i] = r.held[i].astype(BF16)
            r.sums[i] = mine + r.other[i]
            r.other[i] = mine
            across(i, r.other).start()

        @pl.when(xx == 1)
        def _():
            mine = r.held[i] + r.other[i]
            r.dstate[i] = mine.astype(BF16)
            r.sums[i] = mine + r.sums[i]
            across(i, r.held).start()

        pl.when(zz < top)(lambda: along(i).start())

    def finish(i):
        @pl.when(owned(i))
        def _():
            pl.when(zz < top)(lambda: along(i).wait_send())

        @pl.when(~owned(i))
        def _():
            across(i, r.sums).wait_recv()
            r.dstate[i] = r.other[i].astype(BF16)

        across(i, r.sums).wait_send()

    def scan(t):
        i = t - scan_at
        pl.when((i >= 0) & (i < n_scan) & ~owned(i))(lambda: across(i, r.sums).start())
        j = i - 1 - zz
        pl.when((j >= 0) & (j < n_scan) & owned(j))(lambda: pass_on(j))
        pl.when((j >= 2) & (j < n_scan + 2))(lambda: finish(j - 2))

    def span_of(start, size, step):
        return pl.ds(start if isinstance(start, int) else pl.multiple_of(start, step), size)

    def tok(j, n=TILE):
        return span_of(j * n, n, n)

    def tile_inner(j, w3, w1, w2, first, second):
        def block(m, carry):
            at_rows = tok(m, 512)
            din = dot(r.dyv[at_rows, :], w3[...], 1, 1)
            one = (din * second[at_rows, :].astype(F32)).astype(BF16)
            two = (din * first[at_rows, :].astype(F32)).astype(BF16)
            cols = pl.ds(pl.multiple_of(j * 256, 256), 256)
            r.dfs[0, at_rows, cols] = one
            r.dfs[1, at_rows, cols] = two
            for n in range(width // 256):
                to = pl.ds(n * 256, 256)
                res = dot(one, w1[to, :], 1, 1) + dot(two, w2[to, :], 1, 1)
                r.dn2[at_rows, to] = r.dn2[at_rows, to] + res
            return carry

        for m in range(rows // 512):
            block(m, 0)

    def tile_resid(j, resid, gate, attn, q, w_out, gain, dmix):
        def one(m, carry):
            here, sub = pl.ds(pl.multiple_of(j * TILE + m * 32, 32), 32), tok(m, 32)
            value = resid[sub, :]
            grad = r.dn2[here, :]
            scale = lax.rsqrt(jnp.mean(value * value, axis=-1, keepdims=True) + EPS)
            out = r.dyv[here, :].astype(F32) + norm_back(grad, value, scale)
            r.dn2[here, :] = out
            r.dlow[here, :] = out.astype(BF16)
            return carry

        for m in range(TILE // 32):
            one(m, 0)
        for n in range(width // 256):
            to = pl.ds(n * 256, 256)
            dmix[:, to] = dot(r.dlow[tok(j), :], w_out[to, :], 1, 1)

        def two(m, carry):
            here, sub = pl.ds(pl.multiple_of(j * TILE + m * 32, 32), 32), tok(m, 32)
            av = attn[sub, :].astype(F32)
            scale = lax.rsqrt(jnp.mean(av * av, axis=-1, keepdims=True) + EPS)
            unit = av * scale
            act, der = silu_parts(gate[sub, :].astype(F32))
            dm = dmix[sub, :]
            ds = dm * act
            r.dgate[here, :] = (dm * (unit * gain[...]) * der).astype(BF16)
            r.gacc[...] = r.gacc[...] + jnp.sum((ds * unit).reshape(4, 8, width), axis=0)
            r.dattn[here, :] = norm_back(ds * gain[...], av, scale).astype(BF16)
            return carry

        for m in range(TILE // 32):
            two(m, 0)

        def states(m, carry):
            s = j * (TILE // span) + m
            for p in range(pairs):
                lanes = pl.ds(p * 2 * HEAD, 2 * HEAD)
                grad = r.dattn[tok(s, span), lanes]
                per = pairs // halves
                r.sums[s * halves + p // per, p % per] = pick_heads(dot(q[tok(m, span), lanes], grad, 0, 0))
            return carry

        for m in range(TILE // span):
            states(m, 0)

    def tile_attn(s, q_ref, k_ref, v_ref, query, key, prefix_ref):
        causal = causal_pair(span)
        here = tok(s, span)
        for p in range(pairs):
            lanes = pl.ds(p * 2 * HEAD, 2 * HEAD)
            q, k, v, g = q_ref[:, lanes], k_ref[:, lanes], v_ref[:, lanes], r.dattn[here, lanes]
            k2, v2 = two_heads(k), two_heads(v)
            per = pairs // halves
            prefix, dstate = two_heads(prefix_ref[p]), two_heads(r.dstate[s * halves + p // per, p % per])
            scores = jnp.where(causal, dot(q, k2, 1, 1), 0.0).astype(BF16)
            dscores = jnp.where(causal, dot(g, v2, 1, 1), 0.0).astype(BF16)
            dq = dot(dscores, k2, 1, 0) + dot(g, prefix, 1, 1)
            dk = pick_heads(dot(dscores, q, 0, 0)) + dot(v, dstate, 1, 1)
            dv = pick_heads(dot(scores, g, 0, 0)) + dot(k, dstate, 1, 0)
            r.dfs[0, here, lanes] = (dq * silu_parts(query[:, lanes].astype(F32))[1]).astype(BF16)
            r.dfs[0, here, pl.ds(width + p * 2 * HEAD, 2 * HEAD)] = (
                dk * silu_parts(key[:, lanes].astype(F32))[1]).astype(BF16)
            r.dfs[1, here, lanes] = dv.astype(BF16)

    parts = [
        lambda at_rows, cols: r.dfs[0, at_rows, cols],
        lambda at_rows, cols: r.dfs[0, at_rows, pl.ds(width + cols.start, cols.size)],
        lambda at_rows, cols: r.dfs[1, at_rows, cols],
    ]
    dq_cols = lambda cols: r.dfs[0, :, cols]
    dk_cols = lambda cols: r.dfs[0, :, pl.ds(width + cols.start, cols.size)]
    dv_cols = lambda cols: r.dfs[1, :, cols]

    def load(src, dst, n):
        return pltpu.make_async_copy(src, dst, r.lsem.at[n])

    def dma(*shape):
        return pltpu.SemaphoreType.DMA(shape)

    def ring(shape, dtype):
        return pltpu.VMEM((2,) + shape, dtype)

    def steps(count, one):
        def go(j, carry):
            one(j)
            return carry

        lax.fori_loop(0, count, go, 0)

    dy_load = load(r.dy, r.dyv, 0)
    norm2_load = load(r.norm2t, r.at0, 1)
    mixed_load = load(r.mixedt, r.at1, 2)
    norm_load = load(r.normt, r.at0, 3)

    def segment0(left, w3, w1, w2, first, second, sems):
        cols = lambda ref: lambda j: ref.at[:, pl.ds(pl.multiple_of(j * 256, 256), 256)]
        s_left = Stream(lambda j: r.innert.at[:, pl.ds(pl.multiple_of(j * 32, 32), 32)], left, sems.at[0])
        tiles = [
            Stream(lambda j: r.w_third.at[pl.ds(pl.multiple_of(j * 256, 256), 256)], w3, sems.at[1]),
            Stream(cols(r.w_first), w1, sems.at[2]),
            Stream(cols(r.w_second), w2, sems.at[3]),
            Stream(cols(r.first), first, sems.at[4]),
            Stream(cols(r.second), second, sems.at[5]),
        ]
        s_left.start(0)
        dy_load.start()
        r.dn2[...] = jnp.zeros_like(r.dn2)
        r.gacc[...] = jnp.zeros_like(r.gacc)
        dy_load.wait()
        for s in tiles:
            s.start(0)
        norm2_load.start()
        pl.semaphore_wait(bar, len(peers))

        def one(j):
            send_first(j, BOTH[:1])
            make(j, fill_tall(s_left.get(j, n_tall)[...].reshape(8 * 32, rows)))
            tile_inner(j, *(s.get(j, n_tall) for s in tiles))
            move(j, BOTH[:1])

        steps(n_tall, one)
        norm2_load.wait()

    pl.run_scoped(
        segment0, ring((8, 32, rows), BF16), ring((256, width), BF16), ring((width, 256), BF16),
        ring((width, 256), BF16), ring((rows, 256), BF16), ring((rows, 256), BF16), dma(6, 2))

    def segment1(resid, gate, attn, q, w_out, gain, dmix, sems, wsem):
        blk = lambda ref: lambda j: ref.at[tok(j)]
        tiles = [
            Stream(blk(ref), buf, sems.at[n])
            for n, (ref, buf) in enumerate(((r.resid, resid), (r.gate, gate), (r.attn, attn), (r.q, q)))
        ]
        w_load = pltpu.make_async_copy(r.w_out, w_out, wsem.at[0])
        g_load = pltpu.make_async_copy(r.gain, gain, wsem.at[1])
        w_load.start()
        g_load.start()
        for s in tiles:
            s.start(0)

        def one(j):
            t = at_wide + j
            send_first(t)
            make_wide(t)

            @pl.when(j == 0)
            def _():
                w_load.wait()
                g_load.wait()

            rs, ga, at_, qs = (s.get(j, blocks) for s in tiles)
            tile_resid(j, rs, ga, at_, qs, w_out, gain, dmix)
            scan(t)
            move(t)

        steps(blocks, one)

    pl.run_scoped(
        segment1, ring((TILE, width), F32), ring((TILE, width), BF16), ring((TILE, width), BF16),
        ring((TILE, width), BF16), pltpu.VMEM((width, width), BF16), pltpu.VMEM((1, width), F32),
        pltpu.VMEM((TILE, width), F32), dma(4, 2), dma(2))

    def gain_sum(t):
        base = at_wide + blocks
        hops = [to_core, to_y, to_x]

        def swap(n):
            return remote(r.gbuf, r.gland.at[n], r.gs.at[n], r.gr.at[n], hops[n])

        def spread(d):
            return remote(r.gbuf, r.gland.at[2 + d], r.gs.at[2 + d], r.gr.at[2 + d], to_z[d - 1])

        @pl.when(t == base)
        def _():
            total = jnp.sum(r.gacc[...], axis=0, keepdims=True)
            for n in range(8):
                r.gbuf[pl.ds(n, 1), :] = total[:, n * 128:(n + 1) * 128]
            swap(0).start()

        for n in range(3):
            @pl.when(t == base + 2 + 2 * n)
            def _(n=n):
                swap(n).wait()
                r.gbuf[...] = r.gbuf[...] + r.gland[n]
                if n < 2:
                    swap(n + 1).start()
                else:
                    for d in range(1, outer):
                        spread(d).start()

        @pl.when(t == base + 8)
        def _():
            for d in range(1, outer):
                spread(d).wait()
            for d in range(1, outer):
                r.gbuf[...] = r.gbuf[...] + r.gland[2 + d]
            pltpu.make_async_copy(r.gbuf, r.dgain, r.lsem.at[4]).start()

        pl.when(t == base + 10)(lambda: pltpu.make_async_copy(r.gbuf, r.dgain, r.lsem.at[4]).wait())

    n2 = n_wide - blocks
    n_out = blocks * (width // 256)

    def segment2(w3, inner, resid, out, sems, osem):
        per = width // 256
        cols = lambda j: pl.ds(pl.multiple_of(j % per * 256, 256), 256)
        s_w3 = Stream(lambda j: r.w_third.at[:, cols(j)], w3, sems.at[0])
        s_resid = Stream(lambda j: r.resid.at[tok(j // per), cols(j)], resid, sems.at[1])
        s_inner = Stream(lambda n: r.inner.at[tok(n)], inner, sems.at[2])

        def store(j):
            return pltpu.make_async_copy(out.at[j % 2], r.output.at[tok(j // per), cols(j)], osem.at[j % 2])

        mixed_load.start()
        for s in (s_w3, s_resid, s_inner):
            s.start(0)

        def one(j):
            t = at_wide + blocks + j
            send_first(t)
            make_wide(t)

            @pl.when(j < n_out)
            def _():
                w, res = s_w3.get(j, n_out), s_resid.get(j, n_out)

                @pl.when(j % per == 0)
                def _():
                    s_inner.get(j // per, blocks)

                pl.when(j >= 2)(lambda: store(j - 2).wait())
                prod = dot(inner[j // per % 2], w[...], 1, 0)
                out[j % 2] = (res[...] + prod).astype(BF16)
                store(j).start()

            scan(t)
            move(t)
            gain_sum(t)

        steps(n2, one)
        store(n_out - 2).wait()
        store(n_out - 1).wait()
        mixed_load.wait()

    pl.run_scoped(
        segment2, ring((ff, 256), BF16), ring((TILE, ff), BF16), ring((TILE, 256), F32),
        ring((TILE, 256), BF16), dma(3, 2), dma(2))

    def segment3(q, k, v, query, key, prefix, sems):
        blk = lambda ref: lambda j: ref.at[tok(j, span)]
        tiles = [
            Stream(blk(ref), buf, sems.at[n])
            for n, (ref, buf) in enumerate(((r.q, q), (r.k, k), (r.v, v), (r.query, query), (r.key, key)))
        ]
        tiles.append(Stream(lambda j: r.prefix.at[j], prefix, sems.at[5]))
        norm_load.start()
        for s in tiles:
            s.start(0)

        def one(j):
            t = at_square + j
            send_first(t)
            pl.when(j < 4)(lambda: make_square(t, at_square, r.at1, lambda cols: r.dlow[:, cols]))
            pl.when(j == 4)(lambda: norm_load.wait())
            pl.when(j >= 4)(lambda: make_square(t, at_square + 4, r.at0, lambda cols: r.dgate[:, cols]))
            tile_attn(j, *(s.get(j, seqs) for s in tiles))
            move(t)

        steps(8, one)

    pl.run_scoped(
        segment3, *[ring((span, width), BF16)] * 5, ring((pairs, HEAD, 2 * HEAD), BF16), dma(6, 2))

    def rest(j):
        t = chunks + j
        finish_chunks(t, (1,))
        finish_chunks(t, range(2, len(quick)))
        move(t, BOTH[:1])

    def segment4(wq, wk, wv, wg, total, xs, out, sems, xsem, osem):
        nn = width // 256
        rowsblk = lambda ref: lambda n: ref.at[pl.ds(pl.multiple_of(n * 256, 256), 256)]
        weights = [
            Stream(rowsblk(ref), buf, sems.at[n])
            for n, (ref, buf) in enumerate(
                ((r.w_query, wq), (r.w_key, wk), (r.w_value, wv), (r.w_gate, wg)))
        ]
        s_x = Stream(lambda j: r.tokens.at[tok(j)], xs, xsem)
        for s in weights:
            s.start(0)
        s_x.start(0)

        def product(j):
            n, m = j // 2, j % 2
            slot = n % 2

            @pl.when(m == 0)
            def _():
                for s in weights:
                    s.get(n, nn)

            here = tok(m, rows // 2)
            full = pl.ds(0, width)
            res = dot(r.dgate[here, :], wg[slot], 1, 1)
            for part, w in zip(parts, (wq, wk, wv)):
                res = res + dot(part(here, full), w[slot], 1, 1)
            total[here, pl.ds(pl.multiple_of(n * 256, 256), 256)] = res

        def store(j):
            return pltpu.make_async_copy(out.at[j % 2], r.dtokens.at[tok(j)], osem.at[j % 2])

        def finish_rows(j):
            xb = s_x.get(j, blocks)
            pl.when(j >= 2)(lambda: store(j - 2).wait())

            def one(m, carry):
                here, sub = pl.ds(pl.multiple_of(j * TILE + m * 32, 32), 32), tok(m, 32)
                xv = xb[sub, :].astype(F32)
                scale = lax.rsqrt(jnp.mean(xv * xv, axis=-1, keepdims=True) + EPS)
                out[j % 2, sub, :] = r.dn2[here, :] + norm_back(total[here, :], xv, scale)
                return carry

            for m in range(TILE // 32):
                one(m, 0)
            store(j).start()

        def one(j):
            t = at_square + 8 + j
            send_first(t, BOTH[:1])
            finish_chunks(t, (1,))
            pl.when(j < 4)(lambda: make_square(t, at_square + 8, r.at0, dq_cols))
            pl.when((j >= 4) & (j < 8))(lambda: make_square(t, at_square + 12, r.at0, dk_cols))
            pl.when(j >= 8)(lambda: make_square(t, at_square + 16, r.at0, dv_cols))
            pl.when(j < 2 * nn)(lambda: product(j))
            pl.when(j >= 2 * nn)(lambda: finish_rows(j - 2 * nn))
            move(t, BOTH[:1])

        steps(12, one)
        steps(len(quick) - 1, rest)
        store(blocks - 2).wait()
        store(blocks - 1).wait()

    pl.run_scoped(
        segment4, *[ring((256, width), BF16)] * 4, pltpu.VMEM((rows, width), F32),
        ring((TILE, width), BF16), ring((TILE, width), F32), dma(4, 2), dma(2), dma(2))


def back(args, seqs, blk):
    rows, width = args["tokens"].shape
    ff = args["first"].shape[1]
    pairs = width // (2 * HEAD)
    anywhere = pl.BlockSpec(memory_space=pl.ANY)
    cut = 4

    def v(*shape, dtype=F32):
        return pltpu.VMEM(shape, dtype)

    def sem(*shape):
        return pltpu.SemaphoreType.DMA(shape)

    n_scan = seqs * 2
    chunk = (4, 2, 2, 64, 128)
    scratch = dict(
        tbuf=v(2, *chunk), core_rx=v(LAND, *chunk), acc=v(ACC, *chunk), xa=v(LAND, 4, 2, 32, 128),
        ya=v(LAND, 4, 32, 128), yb=v(LAND, 4, 2, 56, 128), xb=v(LAND, 4, 56, 128),
        xc=v(LAND, 2, 16, 128), yc=v(LAND, 16, 128), zab=v(LAND, 2, 3, 56, 128),
        zc=v(LAND, 2, 3, 2, 2, 16, 128), fin=v(FIN, 2, 64, 128),
        ssem=sem(7, LAND), rsem=sem(7, LAND), zss=sem(2, 2, 3, LAND), zrs=sem(2, 2, 3, LAND),
        osem=sem(FIN), csem=sem(FIN), crem=sem(FIN), ygs=sem(FIN), ygr=sem(FIN),
        dyv=v(rows, width, dtype=BF16), dfs=v(2, rows, ff, dtype=BF16), dn2=v(rows, width),
        dlow=v(rows, width, dtype=BF16), dgate=v(rows, width, dtype=BF16),
        dattn=v(rows, width, dtype=BF16), at0=v(8, 2, 64, rows, dtype=BF16),
        at1=v(8, 2, 64, rows, dtype=BF16), held=v(n_scan, cut, HEAD, 128), sums=v(n_scan, cut, HEAD, 128),
        other=v(n_scan, cut, HEAD, 128), dstate=v(n_scan, cut, HEAD, 128, dtype=BF16),
        sz=sem(n_scan), rz=sem(n_scan), sx=sem(n_scan), rx=sem(n_scan),
        gacc=v(8, width), gbuf=v(8, 128), gland=v(6, 8, 128), gs=sem(6), gr=sem(6), lsem=sem(5),
        qab=v(2, 3, 48, 128), qc=v(2, 3, 2, 2, 16, 128), qss=sem(2, 3, 2), qrs=sem(2, 3, 2),
        qxc=v(2, 2, 16, 128), qyc=v(2, 16, 128), qks=sem(2, 2), qkr=sem(2, 2),
    )
    args = dict(args)
    args["innert"] = args["innert"].reshape(8, ff // 8, rows)
    for name in ("normt", "norm2t", "mixedt"):
        args[name] = args[name].reshape(8, 2, 64, rows)
    args["gain"] = args["gain"].reshape(1, width)
    outs = dict(
        output=((rows, width), BF16), dtokens=((rows, width), F32), tall=((ff // 8, width), F32),
        wide=((2, width // 8, ff), F32), square=((5, width // 8, width), F32), dgain=((8, 128), F32),
    )
    return pl.pallas_call(
        functools.partial(back_kernel, blk // 2, seqs, (*args, *outs, *scratch)),
        out_shape=[jax.ShapeDtypeStruct(*of) for of in outs.values()],
        in_specs=[anywhere] * len(args),
        out_specs=[anywhere] * len(outs),
        scratch_shapes=list(scratch.values()),
        compiler_params=pltpu.CompilerParams(
            collective_id=3, has_side_effects=True, vmem_limit_bytes=60 * MIB),
        cost_estimate=pl.CostEstimate(flops=60 * 2**30, bytes_accessed=200 * MIB, transcendentals=0),
    )(*args.values())


def rms(value):
    return lax.rsqrt(jnp.mean(value * value, axis=-1, keepdims=True) + EPS)


def forward(blk, seqs, xf, weights):
    w_query, w_key, w_value, w_gate, w_out, out_gain, w_first, w_second, w_third = weights
    normed = (xf * rms(xf)).astype(BF16)
    key = project(normed, w_key)
    value = project(normed, w_value)
    k, v = silu_parts(key)[0].astype(BF16), value.astype(BF16)
    prefix = entering(local_states(k, v, seqs), blk, False)
    query = project(normed, w_query)
    gate = project(normed, w_gate)
    q = silu_parts(query)[0].astype(BF16)
    attn = attention(q, k, v, prefix, seqs)
    mixed = (attn * rms(attn) * out_gain * silu_parts(gate)[0]).astype(BF16)
    resid = xf + project(mixed, w_out)
    normed2 = (resid * rms(resid)).astype(BF16)
    first = project(normed2, w_first)
    second = project(normed2, w_second)
    inner = (first * second).astype(BF16)
    return dict(
        normed=normed, query=query, key=key, gate=gate, q=q, k=k, v=v, prefix=prefix, attn=attn,
        mixed=mixed, resid=resid, normed2=normed2, first=first, second=second, inner=inner)


def backward_plain(blk, seqs, xf, grad_top, f, weights):
    w_query, w_key, w_value, w_gate, w_out, out_gain, w_first, w_second, w_third = weights
    output = (f["resid"] + project(f["inner"], w_third)).astype(BF16)
    grad_w3 = weight_grad(f["inner"], grad_top)
    grad_inner = back_project(grad_top, w_third)
    grad_one = (grad_inner * f["second"]).astype(BF16)
    grad_two = (grad_inner * f["first"]).astype(BF16)
    grad_w1 = weight_grad(f["normed2"], grad_one)
    grad_w2 = weight_grad(f["normed2"], grad_two)
    grad_normed2 = back_project(grad_one, w_first) + back_project(grad_two, w_second)
    resid, attn = f["resid"], f["attn"]
    grad_resid = grad_top.astype(F32) + norm_back(grad_normed2, resid, rms(resid))
    grad_resid_low = grad_resid.astype(BF16)
    grad_wo = weight_grad(f["mixed"], grad_resid_low)
    grad_mixed = back_project(grad_resid_low, w_out)
    gate_act, gate_der = silu_parts(f["gate"])
    rattn = rms(attn)
    unit_attn = attn * rattn
    grad_scaled = grad_mixed * gate_act
    grad_gate_low = (grad_mixed * (unit_attn * out_gain) * gate_der).astype(BF16)
    grad_gain = jnp.sum(grad_scaled * unit_attn, axis=0)
    grad_attn = norm_back(grad_scaled * out_gain, attn, rattn).astype(BF16)
    q, k, v, prefix = f["q"], f["k"], f["v"], f["prefix"]
    dstate = entering(local_states(q, grad_attn, seqs), blk, True)
    grad_fq, grad_fk, grad_vv = attention_back(q, k, v, grad_attn, prefix, dstate, seqs)
    grad_query_low = (grad_fq * silu_parts(f["query"])[1]).astype(BF16)
    grad_key_low = (grad_fk * silu_parts(f["key"])[1]).astype(BF16)
    grad_value_low = grad_vv.astype(BF16)
    normed = f["normed"]
    grads = [weight_grad(normed, g) for g in (grad_query_low, grad_key_low, grad_value_low, grad_gate_low)]
    grads += [grad_wo, grad_gain, grad_w1, grad_w2, grad_w3]
    grad_normed = back_project(grad_query_low, w_query) + back_project(grad_key_low, w_key)
    grad_normed = (
        grad_normed + back_project(grad_value_low, w_value) + back_project(grad_gate_low, w_gate)
    )
    grad_input = grad_resid + norm_back(grad_normed, xf, rms(xf))
    summed = [
        lax.psum(lax.psum_scatter(g, "blk", scatter_dimension=0, tiled=True), "batch") for g in grads]
    return output, grad_input, summed


def laid_out(output, grad_input, tall, wide, square, dgain):
    arrays = (output, grad_input, tall, wide, square, dgain)
    squares, wides = square.shape[0], wide.shape[0]
    shapes = [square.shape[1:]] * squares + [wide.shape[1:]] * wides + [(1, dgain.shape[1])]
    types = [F32] * len(shapes) + [output.dtype, grad_input.dtype, F32]
    shapes += [output.shape, grad_input.shape, tall.shape]
    cuts = [1] * squares + [2] * wides + [1, 2, 4, 2]

    def kernel(output, grad_input, tall, wide, square, dgain, *rest):
        outs, bufs = rest[:len(shapes)], rest[len(shapes):2 * len(shapes)]
        sem_in, sem_out = rest[2 * len(shapes):]
        k = lax.axis_index("blk")
        ins = [square.at[n] for n in range(squares)] + [wide.at[n] for n in range(wides)]
        ins += [dgain.at[pl.ds(k, 1)], output, grad_input, tall]
        loads, stores = [], []
        for src, buf, dst, cut in zip(ins, bufs, outs, cuts):
            step = dst.shape[0] // cut
            for n in range(cut):
                part = pl.ds(n * step, step)
                m = len(loads)
                loads.append(pltpu.make_async_copy(src.at[part], buf.at[part], sem_in.at[m]))
                stores.append(pltpu.make_async_copy(buf.at[part], dst.at[part], sem_out.at[m]))
        for copy in loads:
            copy.start()
        for load, store in zip(loads, stores):
            load.wait()
            store.start()
        for copy in stores:
            copy.wait()

    anywhere = pl.BlockSpec(memory_space=pl.ANY)
    outs = pl.pallas_call(
        kernel,
        out_shape=[jax.ShapeDtypeStruct(*of) for of in zip(shapes, types)],
        in_specs=[anywhere] * len(arrays),
        out_specs=[anywhere] * len(shapes),
        scratch_shapes=[pltpu.VMEM(*of) for of in zip(shapes, types)]
        + [pltpu.SemaphoreType.DMA((sum(cuts),))] * 2,
        compiler_params=pltpu.CompilerParams(vmem_limit_bytes=60 * MIB),
    )(*arrays)
    return outs[:squares], outs[squares:squares + wides], *outs[squares + wides:]


def backward(blk, seqs, tokens, grad_top, f, weights):
    w_query, w_key, w_value, w_gate, w_out, gain, w_first, w_second, w_third = weights
    args = dict(
        tokens=tokens, dy=grad_top, gain=gain, w_query=w_query, w_key=w_key, w_value=w_value,
        w_gate=w_gate, w_out=w_out, w_first=w_first, w_second=w_second, w_third=w_third)
    args.update(f)
    output, grad_input, tall, wide, square, dgain = back(args, seqs, blk)
    (so, sg, sq, sk, sv), (s1, s2), sgain, output, grad_input, tall = laid_out(
        output, grad_input, tall, wide, square, dgain)
    return output, grad_input, [sq, sk, sv, sg, so, sgain.reshape(-1), s1, s2, tall]


def body(sizes, tokens, cotangent, *weights):
    batch, blk = sizes
    seqs, span, width = tokens.shape
    rows = seqs * span
    low = tokens.reshape(rows, width)
    xf = low.astype(F32)
    grad_top = cotangent.reshape(rows, width)
    ff = weights[-1].shape[0]
    if (batch, blk, rows, span, width, ff % 256) == (4, 8, 1024, 128, 1024, 0):
        f = forward_fast(blk, seqs, low, weights)
        output, grad_input, grads = backward(blk, seqs, low, grad_top, f, weights)
    else:
        f = forward(blk, seqs, xf, weights)
        output, grad_input, grads = backward_plain(blk, seqs, xf, grad_top, f, weights)
    shape = (seqs, span, width)
    return (output.reshape(shape), grad_input.reshape(shape), *grads)


def solution(mesh):
    rows = P("batch", "blk", None)
    cut = P("blk", None)
    return jax.shard_map(
        functools.partial(body, (mesh.shape["batch"], mesh.shape["blk"])),
        mesh=mesh,
        in_specs=(rows, rows) + (P(),) * 9,
        out_specs=(rows, rows) + (cut,) * 5 + (P("blk"),) + (cut,) * 3,
        check_vma=False,
    )
```
